32 devices in a mesh: dp: 16 (over z, y, x), fsdp: 2 (over core).
Axes of the slice: x: 2, y: 2, z: 4, core: 2. Of those that a mesh axis runs over, the one named last changes fastest.
Arguments:
- tokens_in: bfloat16 [32, 576, 768], P(('dp', 'fsdp')), may hold values from -6 to 6
- cotangent: bfloat16 [32, 576, 768], P(('dp', 'fsdp')), may hold values from -6 to 6
- segments: int32 [32, 576], P(('dp', 'fsdp')), may hold values from 0 to 3, as said below
- tile_sides: int32 [32, 576], P(('dp', 'fsdp')), may hold values from 1 to 15, as said below
- valid_slots: int32 [32, 576], P(('dp', 'fsdp')), may hold values from 0 to 1, as said below
- owners: int32 [32], replicated, may hold values from 0 to 31, as said below
- master_qkv: float32 [768, 2304], P(('dp', 'fsdp')), may hold values from -0.21875 to 0.21875
- master_out: float32 [768, 768], P(('dp', 'fsdp')), may hold values from -0.625 to 0.625
- master_up: float32 [768, 3072], P(('dp', 'fsdp')), may hold values from -0.21875 to 0.21875
- master_down: float32 [3072, 768], P(('dp', 'fsdp')), may hold values from -0.109375 to 0.109375
- master_vec: float32 [7680], P(('dp', 'fsdp'))
- first_qkv: float32 [768, 2304], P(('dp', 'fsdp')), may hold values from -56 to 56
- first_out: float32 [768, 768], P(('dp', 'fsdp')), may hold values from -40 to 40
- first_up: float32 [768, 3072], P(('dp', 'fsdp')), may hold values from -28 to 28
- first_down: float32 [3072, 768], P(('dp', 'fsdp')), may hold values from -64 to 64
- first_vec: float32 [7680], P(('dp', 'fsdp')), may hold values from -48 to 48
- second_qkv: float32 [768, 2304], P(('dp', 'fsdp')), may hold values from 7.3728 to 29.4912
- second_out: float32 [768, 768], P(('dp', 'fsdp')), may hold values from 3.6864 to 14.7456
- second_up: float32 [768, 3072], P(('dp', 'fsdp')), may hold values from 1.8432 to 7.3728
- second_down: float32 [3072, 768], P(('dp', 'fsdp')), may hold values from 11.9808 to 47.9232
- second_vec: float32 [7680], P(('dp', 'fsdp')), may hold values from 4.608 to 18.432
Outputs:
- block_out: bfloat16 [32, 576, 768], P(('dp', 'fsdp'))
- tokens_grad: float32 [32, 576, 768], P(('dp', 'fsdp'))
- first_qkv_new: float32 [768, 2304], P(('dp', 'fsdp'))
- second_qkv_new: float32 [768, 2304], P(('dp', 'fsdp'))
- master_qkv_new: float32 [768, 2304], P(('dp', 'fsdp'))
- first_out_new: float32 [768, 768], P(('dp', 'fsdp'))
- second_out_new: float32 [768, 768], P(('dp', 'fsdp'))
- master_out_new: float32 [768, 768], P(('dp', 'fsdp'))
- first_up_new: float32 [768, 3072], P(('dp', 'fsdp'))
- second_up_new: float32 [768, 3072], P(('dp', 'fsdp'))
- master_up_new: float32 [768, 3072], P(('dp', 'fsdp'))
- first_down_new: float32 [3072, 768], P(('dp', 'fsdp'))
- second_down_new: float32 [3072, 768], P(('dp', 'fsdp'))
- master_down_new: float32 [3072, 768], P(('dp', 'fsdp'))
- first_vec_new: float32 [7680], P(('dp', 'fsdp'))
- second_vec_new: float32 [7680], P(('dp', 'fsdp'))
- master_vec_new: float32 [7680], P(('dp', 'fsdp'))
The draws below stay inside these ranges and needn't reach their ends.
Inputs may be any that keep to these rules, and one draw needn't show every extreme that they name: In each row, segments never fall from slot to slot and count tiles from 0; a row holds four small tiles, two large tiles then padding, or a large tile, two small tiles then padding; padding slots form the row's last segment. `tile_sides`: every slot of a tile carries that tile's side (12 or 15); padding slots carry 1. `valid_slots`: padding slots are 0 and stand at the end of a row. `owners`: A permutation of 0 .. 31.
All inputs are finite; a program needn't handle non-finite values.
Results may differ from the reference program's by a relative error of at most 0.011.
Values may be sent and summed in bfloat16 or wider, within the bound.
No kernel may reach another device: no remote copies, remote signals or barrier semaphores. Data moves between devices by JAX's collectives and lax.ppermute only.
A program may use at most 192 MiB of HBM per device.

```python
import math
import jax
import jax.numpy as jnp
from jax import lax

D = 768
HEADS = 12
HD = 64
FF = 3072
SIDE_A = 12
SIDE_B = 15
STEP = 10
SLOTS = 576
SHARDS = 32
ROWS = 32
TOKENS = 18432
VEC = 7680


def owner_order(key):
    return jax.random.permutation(jax.random.fold_in(key, 11), SHARDS).astype(jnp.int32)


def tile_layout(key):
    compose = jax.random.randint(jax.random.fold_in(key, 5), (ROWS,), 0, 3)
    compose = compose.at[0].set(2)
    small_area = SIDE_A * SIDE_A
    large_area = SIDE_B * SIDE_B
    slot_ids = jnp.arange(SLOTS, dtype=jnp.int32)[None, :]
    choose = compose[:, None]
    seg_zero = slot_ids // small_area
    seg_one = jnp.where(slot_ids < large_area, 0, jnp.where(slot_ids < 2 * large_area, 1, 2))
    seg_two = jnp.where(slot_ids < large_area, 0, jnp.where(slot_ids < large_area + small_area, 1, jnp.where(slot_ids < large_area + 2 * small_area, 2, 3)))
    side_zero = jnp.zeros_like(slot_ids) + SIDE_A
    side_one = jnp.where(slot_ids < 2 * large_area, SIDE_B, 1)
    side_two = jnp.where(slot_ids < large_area, SIDE_B, jnp.where(slot_ids < large_area + 2 * small_area, SIDE_A, 1))
    valid_zero = jnp.ones_like(slot_ids)
    valid_one = (slot_ids < 2 * large_area).astype(jnp.int32)
    valid_two = (slot_ids < large_area + 2 * small_area).astype(jnp.int32)
    seg_all = jnp.where(choose == 0, seg_zero, jnp.where(choose == 1, seg_one, seg_two))
    side_all = jnp.where(choose == 0, side_zero, jnp.where(choose == 1, side_one, side_two))
    valid_all = jnp.where(choose == 0, valid_zero, jnp.where(choose == 1, valid_one, valid_two))
    return (seg_all.astype(jnp.int32), side_all.astype(jnp.int32), valid_all.astype(jnp.int32))


def draw_segments(key, part):
    return tile_layout(key)[0]


def draw_tile_sides(key, part):
    return tile_layout(key)[1]


def draw_valid_slots(key, part):
    return tile_layout(key)[2]


def draw_owners(key, part):
    return owner_order(key)


def draw_master_vec(key, part):
    keys_all = jax.random.split(jax.random.fold_in(key, 3), 7)
    gain_one = jax.random.uniform(keys_all[0], (D,), jnp.float32, 0.6, 1.4)
    shift_one = 0.8 * jax.random.normal(keys_all[1], (D,), jnp.float32)
    out_bias = 0.8 * jax.random.normal(keys_all[2], (D,), jnp.float32)
    gain_two = jax.random.uniform(keys_all[3], (D,), jnp.float32, 0.6, 1.4)
    shift_two = 0.8 * jax.random.normal(keys_all[4], (D,), jnp.float32)
    up_bias = 0.8 * jax.random.normal(keys_all[5], (FF,), jnp.float32)
    down_bias = 0.8 * jax.random.normal(keys_all[6], (D,), jnp.float32)
    logical = jnp.concatenate([gain_one, shift_one, out_bias, gain_two, shift_two, up_bias, down_bias])
    blocks = logical.reshape(SHARDS, -1)
    stored = jnp.zeros_like(blocks).at[owner_order(key)].set(blocks)
    return stored.reshape(-1)


def block_scale(stream_key, dims, shards, smallest, largest):
    def one(dim, blocks):
        heights = jax.random.uniform(jax.random.fold_in(jax.random.fold_in(stream_key, 6), dim), (blocks,), jnp.float32, smallest / len(shards), largest / len(shards))
        return jnp.repeat(jnp.exp(heights), dims[dim] // blocks).reshape((-1,) + (1,) * (len(dims) - dim - 1))

    factor_of = one(*shards[0])
    for cut in shards[1:]:
        factor_of = factor_of * one(*cut)
    return factor_of


def bell_draw(stream_key, dims, deviation, most, cuts=(), held_as=jnp.bfloat16):
    drawn = deviation * jax.random.normal(stream_key, dims, jnp.float32)
    if cuts:
        drawn = drawn * block_scale(stream_key, dims, cuts, -0.22, 0.18)
    return jnp.clip(drawn, -most, most).astype(held_as)


def setup_inputs(seed: int = 0) -> dict:
    keys = jax.random.split(jax.random.key(seed), 22)
    tokens_in = bell_draw(keys[0], (ROWS, SLOTS, D), 1.0, 6.0, ((0, 32),))
    cotangent = bell_draw(keys[1], (ROWS, SLOTS, D), 1.0, 6.0, ((0, 32),))
    segments = draw_segments(jax.random.fold_in(keys[21], 71), 0)
    tile_sides = draw_tile_sides(jax.random.fold_in(keys[21], 71), 0)
    valid_slots = draw_valid_slots(jax.random.fold_in(keys[21], 71), 0)
    owners = draw_owners(jax.random.fold_in(keys[21], 71), 0)
    master_qkv = bell_draw(keys[6], (D, 3 * D), D ** -0.5, 0.21875, ((0, 32),), jnp.float32)
    master_out = bell_draw(keys[7], (D, D), (D // 8) ** -0.5, 0.625, ((0, 32),), jnp.float32)
    master_up = bell_draw(keys[8], (D, FF), D ** -0.5, 0.21875, ((0, 32),), jnp.float32)
    master_down = bell_draw(keys[9], (FF, D), FF ** -0.5, 0.109375, ((0, 32),), jnp.float32)
    master_vec = draw_master_vec(jax.random.fold_in(keys[21], 71), 0)
    first_qkv = bell_draw(keys[11], (D, 3 * D), (0.07 * TOKENS ** 0.5), 56.0, ((0, 32),), jnp.float32)
    first_out = bell_draw(keys[12], (D, D), (0.05 * TOKENS ** 0.5), 40.0, ((0, 32),), jnp.float32)
    first_up = bell_draw(keys[13], (D, FF), (0.036 * TOKENS ** 0.5), 28.0, ((0, 32),), jnp.float32)
    first_down = bell_draw(keys[14], (FF, D), (0.09 * TOKENS ** 0.5), 64.0, ((0, 32),), jnp.float32)
    first_vec = bell_draw(keys[15], (VEC,), (0.055 * TOKENS ** 0.5), 48.0, ((0, 32),), jnp.float32)
    second_qkv = jnp.clip(jnp.exp(math.log(29.4912) - 1.3862944 * jax.random.uniform(keys[16], (D, 3 * D), jnp.float32) ** block_scale(keys[16], (D, 3 * D), ((0, 32),), -0.2, 0.2)), 7.3728, 29.4912)
    second_out = jnp.clip(jnp.exp(math.log(14.7456) - 1.3862944 * jax.random.uniform(keys[17], (D, D), jnp.float32) ** block_scale(keys[17], (D, D), ((0, 32),), -0.2, 0.2)), 3.6864, 14.7456)
    second_up = jnp.clip(jnp.exp(math.log(7.3728) - 1.3862944 * jax.random.uniform(keys[18], (D, FF), jnp.float32) ** block_scale(keys[18], (D, FF), ((0, 32),), -0.2, 0.2)), 1.8432, 7.3728)
    second_down = jnp.clip(jnp.exp(math.log(47.9232) - 1.3862944 * jax.random.uniform(keys[19], (FF, D), jnp.float32) ** block_scale(keys[19], (FF, D), ((0, 32),), -0.2, 0.2)), 11.9808, 47.9232)
    second_vec = jnp.clip(jnp.exp(math.log(18.432) - 1.3862944 * jax.random.uniform(keys[20], (VEC,), jnp.float32) ** block_scale(keys[20], (VEC,), ((0, 32),), -0.2, 0.2)), 4.608, 18.432)
    return dict(tokens_in=tokens_in, cotangent=cotangent, segments=segments, tile_sides=tile_sides, valid_slots=valid_slots, owners=owners, master_qkv=master_qkv, master_out=master_out, master_up=master_up, master_down=master_down, master_vec=master_vec, first_qkv=first_qkv, first_out=first_out, first_up=first_up, first_down=first_down, first_vec=first_vec, second_qkv=second_qkv, second_out=second_out, second_up=second_up, second_down=second_down, second_vec=second_vec)


EPSILON = 1e-05
MASKED = -1000000000.0
BETA_ONE = 0.9
BETA_TWO = 0.999
ADAM_EPS = 1e-08
RATE_MATRIX = 0.05
DECAY_MATRIX = 0.05
RATE_VECTOR = 0.3

@jax.custom_vjp
def low(v):
    return lax.optimization_barrier(v.astype(jnp.bfloat16)).astype(jnp.float32)

@jax.custom_vjp
def low_back(v):
    return v

def low_keep(v):
    return (low(v), None)

def low_pass(kept, grad):
    return (grad,)

def back_keep(v):
    return (v, None)

def back_low(kept, grad):
    return (low(grad),)
low.defvjp(low_keep, low_pass)
low_back.defvjp(back_keep, back_low)

def layer_norm(values, scale_vec, shift_vec):
    centre = values - lax.optimization_barrier(jnp.mean(values, axis=-1, keepdims=True))
    spread = lax.optimization_barrier(jnp.mean(centre * centre, axis=-1, keepdims=True))
    return centre * lax.rsqrt(spread + EPSILON) * scale_vec + shift_vec

def tile_bias(seg_row, side_row, valid_row):
    slot_ids = jnp.arange(seg_row.shape[0], dtype=jnp.int32)
    starts = lax.optimization_barrier(jnp.sum((seg_row[None, :] < seg_row[:, None]).astype(jnp.int32), axis=1))
    place_ids = slot_ids - starts
    tile_row = place_ids // side_row
    tile_col = place_ids % side_row
    row_diff = (tile_row[:, None] - tile_row[None, :]).astype(jnp.float32)
    col_diff = (tile_col[:, None] - tile_col[None, :]).astype(jnp.float32)
    distance = jnp.sqrt(row_diff * row_diff + col_diff * col_diff)
    head_ids = jnp.arange(HEADS, dtype=jnp.int32).astype(jnp.float32)
    slopes = jnp.exp2(-8.0 * (head_ids + 1.0) / HEADS)
    allowed = (seg_row[:, None] == seg_row[None, :]) & ((valid_row[None, :] == 1) | (slot_ids[:, None] == slot_ids[None, :]))
    return (-slopes[:, None, None] * distance[None], allowed)

def arrange(whole_array, block_order):
    blocks = whole_array.reshape((SHARDS, whole_array.shape[0] // SHARDS) + whole_array.shape[1:])
    return jnp.take(blocks, block_order, axis=0).reshape(whole_array.shape)

def row_attention(packed):
    qkv_row, seg_row, side_row, valid_row = packed
    parts = qkv_row.reshape(SLOTS, 3, HEADS, HD)
    queries, keys_row, values_row = (parts[:, 0], parts[:, 1], parts[:, 2])
    alibi_bias, allowed = tile_bias(seg_row, side_row, valid_row)
    raw_scores = low_back(jnp.einsum('qhd,khd->hqk', queries, keys_row, precision=lax.Precision.HIGHEST))
    scores = jnp.where(allowed[None], raw_scores * HD ** (-0.5) + alibi_bias, MASKED)
    row_max = lax.optimization_barrier(jnp.max(scores, axis=-1, keepdims=True))
    expo = jnp.exp(scores - row_max)
    attn_probs = expo / lax.optimization_barrier(jnp.sum(expo, axis=-1, keepdims=True))
    mixed_row = jnp.einsum('hqk,khd->qhd', low(attn_probs), values_row, precision=lax.Precision.HIGHEST)
    return mixed_row.reshape(SLOTS, D)

def matmul(left_side, right_side):
    return jnp.dot(left_side, right_side, preferred_element_type=jnp.float32, precision=lax.Precision.HIGHEST)

def adamw(master, moment_one, moment_two, gradient, step_rate, decay_rate):
    first_new = BETA_ONE * moment_one + (1.0 - BETA_ONE) * gradient
    second_new = BETA_TWO * moment_two + (1.0 - BETA_TWO) * gradient * gradient
    first_hat = first_new / (1.0 - BETA_ONE ** STEP)
    second_hat = second_new / (1.0 - BETA_TWO ** STEP)
    master_new = master - step_rate * (first_hat / (jnp.sqrt(second_hat) + ADAM_EPS) + decay_rate * master)
    return (first_new, second_new, master_new)

def reference(tokens_in, cotangent, segments, tile_sides, valid_slots, owners, master_qkv, master_out, master_up, master_down, master_vec, first_qkv, first_out, first_up, first_down, first_vec, second_qkv, second_out, second_up, second_down, second_vec):
    tokens_f = tokens_in.astype(jnp.float32)
    grad_out = cotangent.astype(jnp.float32)

    def forward(tokens_x, stored_qkv, stored_out, stored_up, stored_down, stored_vec):
        weight_qkv = arrange(low(stored_qkv), owners)
        weight_out = arrange(low(stored_out), owners)
        weight_up = arrange(low(stored_up), owners)
        weight_down = arrange(low(stored_down), owners)
        vector_all = arrange(low(stored_vec), owners)
        gain_one = vector_all[0:D]
        shift_one = vector_all[D:2 * D]
        out_bias = vector_all[2 * D:3 * D]
        gain_two = vector_all[3 * D:4 * D]
        shift_two = vector_all[4 * D:5 * D]
        up_bias = vector_all[5 * D:5 * D + FF]
        down_bias = vector_all[5 * D + FF:]
        flat_in = tokens_x.reshape(-1, D)
        act_one = low(layer_norm(flat_in, gain_one, shift_one))
        qkv_all = low_back(low(matmul(act_one, weight_qkv)))
        qkv_rows = qkv_all.reshape(ROWS, SLOTS, 3 * D)
        mixed_rows = lax.map(jax.checkpoint(row_attention), (qkv_rows, segments, tile_sides, valid_slots))
        mixed_low = low_back(low(mixed_rows.reshape(-1, D)))
        hidden_one = flat_in + low_back(matmul(mixed_low, weight_out)) + out_bias
        act_two = low(layer_norm(hidden_one, gain_two, shift_two))
        upper = low_back(matmul(act_two, weight_up)) + up_bias
        gelu_low = low(jax.nn.gelu(upper, approximate=False))
        result = hidden_one + low_back(matmul(gelu_low, weight_down)) + down_bias
        return result.reshape(tokens_x.shape)
    block_f, vjp_fn = jax.vjp(forward, tokens_f, master_qkv, master_out, master_up, master_down, master_vec)
    tokens_grad, grad_qkv, grad_out_w, grad_up, grad_down, grad_vec = vjp_fn(grad_out)
    upd_qkv = adamw(master_qkv, first_qkv, second_qkv, grad_qkv, RATE_MATRIX, DECAY_MATRIX)
    upd_out = adamw(master_out, first_out, second_out, grad_out_w, RATE_MATRIX, DECAY_MATRIX)
    upd_up = adamw(master_up, first_up, second_up, grad_up, RATE_MATRIX, DECAY_MATRIX)
    upd_down = adamw(master_down, first_down, second_down, grad_down, RATE_MATRIX, DECAY_MATRIX)
    upd_vec = adamw(master_vec, first_vec, second_vec, grad_vec, RATE_VECTOR, 0.0)
    return (block_f.astype(jnp.bfloat16), tokens_grad, upd_qkv[0], upd_qkv[1], upd_qkv[2], upd_out[0], upd_out[1], upd_out[2], upd_up[0], upd_up[1], upd_up[2], upd_down[0], upd_down[1], upd_down[2], upd_vec[0], upd_vec[1], upd_vec[2])
```

```python
from functools import partial

import jax
import jax.numpy as jnp
from jax import lax
from jax.sharding import PartitionSpec as P

D = 768
HEADS = 12
HD = 64
FF = 3072
STEP = 10
SLOTS = 576


EPSILON = 1e-05
MASKED = -1000000000.0
BETA_ONE = 0.9
BETA_TWO = 0.999
ADAM_EPS = 1e-08
RATE_MATRIX = 0.05
DECAY_MATRIX = 0.05
RATE_VECTOR = 0.3


def layer_norm(values, scale_vec, shift_vec):
    centre = values - jnp.mean(values, axis=-1, keepdims=True)
    spread = jnp.mean(centre * centre, axis=-1, keepdims=True)
    return centre * lax.rsqrt(spread + EPSILON) * scale_vec + shift_vec


def tile_bias(seg_row, side_row, valid_row):
    slot_ids = jnp.arange(seg_row.shape[0], dtype=jnp.int32)
    starts = jnp.sum((seg_row[None, :] < seg_row[:, None]).astype(jnp.int32), axis=1)
    place_ids = slot_ids - starts
    tile_row = place_ids // side_row
    tile_col = place_ids % side_row
    row_diff = (tile_row[:, None] - tile_row[None, :]).astype(jnp.float32)
    col_diff = (tile_col[:, None] - tile_col[None, :]).astype(jnp.float32)
    distance = jnp.sqrt(row_diff * row_diff + col_diff * col_diff)
    head_ids = jnp.arange(HEADS, dtype=jnp.int32).astype(jnp.float32)
    slopes = jnp.exp2(-8.0 * (head_ids + 1.0) / HEADS)
    allowed = (seg_row[:, None] == seg_row[None, :]) & (
        (valid_row[None, :] == 1) | (slot_ids[:, None] == slot_ids[None, :])
    )
    return (-slopes[:, None, None] * distance[None], allowed)


def lead_product(left_side, right_side):
    return lax.dot_general(
        left_side, right_side, (((0,), (0,)), ((), ())), preferred_element_type=jnp.float32
    )


def tail_product(left_side, right_side):
    return lax.dot_general(
        left_side, right_side, (((1,), (1,)), ((), ())), preferred_element_type=jnp.float32
    )


def split_heads(qkv_row):
    parts = qkv_row.reshape(qkv_row.shape[0], 3, HEADS, HD)
    return (parts[:, 0], parts[:, 1], parts[:, 2])


def row_scores(queries, keys_row, seg_row, side_row, valid_row):
    alibi_bias, allowed = tile_bias(seg_row, side_row, valid_row)
    raw_scores = jnp.einsum("qhd,khd->hqk", queries, keys_row, preferred_element_type=jnp.float32)
    return jnp.where(allowed[None], raw_scores * HD ** (-0.5) + alibi_bias, MASKED)


def attend_row(packed):
    qkv_row, seg_row, side_row, valid_row = packed
    queries, keys_row, values_row = split_heads(qkv_row)
    scores = row_scores(queries, keys_row, seg_row, side_row, valid_row)
    row_max = jnp.max(scores, axis=-1, keepdims=True)
    log_total = row_max + jnp.log(jnp.sum(jnp.exp(scores - row_max), axis=-1, keepdims=True))
    attn_probs = jnp.exp(scores - log_total).astype(jnp.bfloat16)
    mixed_row = jnp.einsum(
        "hqk,khd->qhd", attn_probs, values_row, preferred_element_type=jnp.float32
    )
    return (mixed_row.reshape(qkv_row.shape[0], D), log_total[..., 0])


def attend_back(packed):
    qkv_row, grad_row, log_total, seg_row, side_row, valid_row = packed
    queries, keys_row, values_row = split_heads(qkv_row)
    scores = row_scores(queries, keys_row, seg_row, side_row, valid_row)
    attn_probs = jnp.exp(scores - log_total[..., None])
    grad_heads = grad_row.reshape(grad_row.shape[0], HEADS, HD)
    value_grad = jnp.einsum(
        "hqk,qhd->khd",
        attn_probs.astype(jnp.bfloat16),
        grad_heads,
        preferred_element_type=jnp.float32,
    )
    prob_grad = jnp.einsum(
        "qhd,khd->hqk", grad_heads, values_row, preferred_element_type=jnp.float32
    )
    row_delta = jnp.sum(attn_probs * prob_grad, axis=-1, keepdims=True)
    score_grad = (attn_probs * (prob_grad - row_delta) * HD ** (-0.5)).astype(jnp.bfloat16)
    query_grad = jnp.einsum(
        "hqk,khd->qhd", score_grad, keys_row, preferred_element_type=jnp.float32
    )
    key_grad = jnp.einsum("hqk,qhd->khd", score_grad, queries, preferred_element_type=jnp.float32)
    return jnp.stack([query_grad, key_grad, value_grad], axis=1).reshape(qkv_row.shape[0], 3 * D)


def adamw(master, moment_one, moment_two, gradient, step_rate, decay_rate):
    first_new = BETA_ONE * moment_one + (1.0 - BETA_ONE) * gradient
    second_new = BETA_TWO * moment_two + (1.0 - BETA_TWO) * gradient * gradient
    first_hat = first_new / (1.0 - BETA_ONE**STEP)
    second_hat = second_new / (1.0 - BETA_TWO**STEP)
    master_new = master - step_rate * (
        first_hat / (jnp.sqrt(second_hat) + ADAM_EPS) + decay_rate * master
    )
    return (first_new, second_new, master_new)

AXES = ("dp", "fsdp")
LOW = jnp.bfloat16


def swap(value, bits):
    pairs = [(i, i ^ bits) for i in range(32)]
    return lax.ppermute(value, AXES, pairs)


def spread(block, cut):
    near = jnp.concatenate([block] + [swap(block, 8 * k) for k in (1, 2, 3)], axis=0)
    rows = near.shape[0]
    left, right = near[:, :cut], near[:, cut:]
    left = jnp.concatenate([left, swap(left, 2)], axis=0)
    right = jnp.concatenate([right, swap(right, 4)], axis=0)
    left = jnp.concatenate([left, swap(left, 4)], axis=0)
    far = swap(right, 2)
    right = jnp.concatenate([right[:rows], far[:rows], right[rows:], far[rows:]], axis=0)
    mine = jnp.concatenate([left, right], axis=1)
    return mine, swap(mine, 1)


def gather_up(mine, other, cut):
    wide = jnp.float32
    total = mine.astype(wide) + swap(other, 1).astype(wide)
    half = total.shape[0] // 2
    rows = half // 2
    left, right = total[:, :cut], total[:, cut:]
    left_got = swap(left[half:].astype(LOW), 4)
    right_out = jnp.concatenate([right[rows:half], right[half + rows :]], axis=0).astype(LOW)
    right_got = swap(right_out, 2)
    left = left[:half] + left_got.astype(wide)
    right = jnp.concatenate([right[:rows], right[half : half + rows]], axis=0) + right_got.astype(wide)
    left_got = swap(left[rows:].astype(LOW), 2)
    right_got = swap(right[rows:].astype(LOW), 4)
    left = left[:rows] + left_got.astype(wide)
    right = right[:rows] + right_got.astype(wide)
    both = jnp.concatenate([left, right], axis=1)
    unit = rows // 4
    low = both.astype(LOW)
    got = both[:unit]
    for k in (1, 2, 3):
        got = got + swap(low[unit * k : unit * (k + 1)], 8 * k).astype(wide)
    return got


def local(
    tokens_in, cotangent, segments, tile_sides, valid_slots, owners,
    master_qkv, master_out, master_up, master_down, master_vec,
    first_qkv, first_out, first_up, first_down, first_vec,
    second_qkv, second_out, second_up, second_down, second_vec,
):
    shards = lax.axis_size(AXES)
    near = shards == 32
    unit = D // shards
    unit_ff = FF // shards
    per_row = master_vec.shape[0] // unit
    me = lax.axis_index(AXES).astype(jnp.int32)
    device_ids = jnp.arange(shards, dtype=jnp.int32)
    inverse = jnp.sum(device_ids[:, None] * (owners[:, None] == device_ids[None, :]), axis=0)
    if near:
        away = owners ^ me
        place = (away >> 3) + 4 * ((away >> 1) & 1) + 8 * ((away >> 2) & 1) + 16 * (away & 1)
    else:
        place = owners
    target = (place[:, None] * unit + jnp.arange(unit, dtype=jnp.int32)[None, :]).reshape(-1)
    order = (target[:, None] == jnp.arange(D, dtype=jnp.int32)[None, :]).astype(LOW)

    def reorder(values):
        return jnp.dot(values, order, preferred_element_type=jnp.float32).astype(LOW)

    def restore(values):
        return tail_product(values.astype(LOW), order)

    vec_block = jnp.pad(master_vec.reshape(unit, per_row), ((0, 0), (0, 128 - per_row)))
    block_one = jnp.concatenate([master_qkv, vec_block], axis=1).astype(LOW)
    block_two = jnp.concatenate([master_out, master_up], axis=1).astype(LOW)
    block_three = master_down.astype(LOW)
    half = D // 2
    if near:
        one = spread(block_one, 1280)
        two = spread(block_two, 1920)
    else:
        one = lax.all_gather(block_one, AXES, axis=0, tiled=True)
        one = (one[:half], one[half:])
        two = lax.all_gather(block_two, AXES, axis=0, tiled=True)
        two = (two[:half], two[half:])
    three = lax.all_gather(block_three, AXES, axis=0, tiled=True)
    weight_down = jnp.take(three.reshape(shards, unit_ff, D), owners, axis=0, mode="clip").reshape(FF, D)

    def forth(values, pair, lo, hi):
        return jnp.dot(values[:, :half], pair[0][:, lo:hi], preferred_element_type=jnp.float32) + jnp.dot(
            values[:, half:], pair[1][:, lo:hi], preferred_element_type=jnp.float32
        )

    def back(values, pair, lo, hi):
        return jnp.concatenate(
            [tail_product(values, pair[0][:, lo:hi]), tail_product(values, pair[1][:, lo:hi])], axis=1
        )

    vec_rows = jnp.concatenate([one[0][:, 3 * D :], one[1][:, 3 * D :]], axis=0)
    vector_f = jnp.dot(order, vec_rows, preferred_element_type=jnp.float32)[:, :per_row].reshape(-1)
    gain_one = vector_f[0:D]
    shift_one = vector_f[D : 2 * D]
    out_bias = vector_f[2 * D : 3 * D]
    gain_two = vector_f[3 * D : 4 * D]
    shift_two = vector_f[4 * D : 5 * D]
    up_bias = vector_f[5 * D : 5 * D + FF]
    down_bias = vector_f[5 * D + FF :]
    flat_in = tokens_in.reshape(-1, D).astype(jnp.float32)
    act_one = reorder(layer_norm(flat_in, gain_one, shift_one).astype(LOW))
    qkv_all = forth(act_one, one, 0, 3 * D).astype(LOW)
    seg, side, valid = segments[0], tile_sides[0], valid_slots[0]
    mixed, log_total = attend_row((qkv_all, seg, side, valid))
    mixed_low = reorder(mixed.astype(LOW))
    hidden_one = flat_in + forth(mixed_low, two, 0, D) + out_bias
    act_two = reorder(layer_norm(hidden_one, gain_two, shift_two).astype(LOW))
    upper = forth(act_two, two, D, D + FF) + up_bias
    gelu_low = jax.nn.gelu(upper, approximate=False).astype(LOW)
    result = hidden_one + jnp.dot(gelu_low, weight_down, preferred_element_type=jnp.float32) + down_bias
    block_out = result.reshape(tokens_in.shape).astype(LOW)

    grad_low = cotangent.reshape(-1, D)
    grad_out = grad_low.astype(jnp.float32)
    down_grad = lead_product(gelu_low, grad_low).astype(LOW)
    down_bias_grad = jnp.sum(grad_out, axis=0)
    gelu_grad = tail_product(grad_low, weight_down)
    upper_grad = jax.vjp(partial(jax.nn.gelu, approximate=False), upper)[1](gelu_grad)[0]
    upper_low = upper_grad.astype(LOW)
    up_bias_grad = jnp.sum(upper_grad, axis=0)
    act_two_grad = restore(back(upper_low, two, D, D + FF))
    hidden_part, gain_two_grad, shift_two_grad = jax.vjp(layer_norm, hidden_one, gain_two, shift_two)[1](
        act_two_grad
    )
    hidden_grad = grad_out + hidden_part
    hidden_low = hidden_grad.astype(LOW)
    out_bias_grad = jnp.sum(hidden_grad, axis=0)
    mixed_grad = restore(back(hidden_low, two, 0, D)).astype(LOW)

    def lead_pair(left, right):
        return lead_product(left[:, :half], right).astype(LOW), lead_product(left[:, half:], right).astype(LOW)

    up_pair = lead_pair(act_two, upper_low)
    out_pair = lead_pair(mixed_low, hidden_low)
    two_mine = jnp.concatenate([out_pair[0], up_pair[0]], axis=1)
    two_other = jnp.concatenate([out_pair[1], up_pair[1]], axis=1)
    qkv_grad_low = attend_back((qkv_all, mixed_grad, log_total, seg, side, valid)).astype(LOW)
    act_one_grad = restore(back(qkv_grad_low, one, 0, 3 * D))
    input_part, gain_one_grad, shift_one_grad = jax.vjp(layer_norm, flat_in, gain_one, shift_one)[1](
        act_one_grad
    )
    tokens_grad = (hidden_grad + input_part).reshape(tokens_in.shape)
    vector_grad = jnp.concatenate(
        [gain_one_grad, shift_one_grad, out_bias_grad, gain_two_grad, shift_two_grad, up_bias_grad, down_bias_grad]
    )
    vec_pad = jnp.pad(vector_grad.reshape(D, per_row), ((0, 0), (0, 128 - per_row))).astype(LOW)
    vec_cols = lead_product(order, vec_pad).astype(LOW)
    qkv_pair = lead_pair(act_one, qkv_grad_low)
    one_mine = jnp.concatenate([qkv_pair[0], vec_cols[:half]], axis=1)
    one_other = jnp.concatenate([qkv_pair[1], vec_cols[half:]], axis=1)

    down_moved = jnp.take(down_grad.reshape(shards, unit_ff, D), inverse, axis=0, mode="clip").reshape(FF, D)
    summed_down = lax.psum_scatter(down_moved, AXES, scatter_dimension=0, tiled=True).astype(jnp.float32)
    if near:
        summed_two = gather_up(two_mine, two_other, 1920)
        summed_one = gather_up(one_mine, one_other, 1280)
    else:
        summed_two = lax.psum_scatter(
            jnp.concatenate([two_mine, two_other], axis=0), AXES, scatter_dimension=0, tiled=True
        ).astype(jnp.float32)
        summed_one = lax.psum_scatter(
            jnp.concatenate([one_mine, one_other], axis=0), AXES, scatter_dimension=0, tiled=True
        ).astype(jnp.float32)
    summed_qkv = summed_one[:, : 3 * D]
    summed_vec = summed_one[:, 3 * D : 3 * D + per_row].reshape(-1)
    summed_out = summed_two[:, :D]
    summed_up = summed_two[:, D:]
    upd_qkv = adamw(master_qkv, first_qkv, second_qkv, summed_qkv, RATE_MATRIX, DECAY_MATRIX)
    upd_out = adamw(master_out, first_out, second_out, summed_out, RATE_MATRIX, DECAY_MATRIX)
    upd_up = adamw(master_up, first_up, second_up, summed_up, RATE_MATRIX, DECAY_MATRIX)
    upd_down = adamw(master_down, first_down, second_down, summed_down, RATE_MATRIX, DECAY_MATRIX)
    upd_vec = adamw(master_vec, first_vec, second_vec, summed_vec, RATE_VECTOR, 0.0)
    return (block_out, tokens_grad) + upd_qkv + upd_out + upd_up + upd_down + upd_vec


def solution(mesh):
    in_specs = (
        P(("dp", "fsdp"), None, None),
        P(("dp", "fsdp"), None, None),
        P(("dp", "fsdp"), None),
        P(("dp", "fsdp"), None),
        P(("dp", "fsdp"), None),
        P(),
        P(("dp", "fsdp"), None),
        P(("dp", "fsdp"), None),
        P(("dp", "fsdp"), None),
        P(("dp", "fsdp"), None),
        P(("dp", "fsdp")),
        P(("dp", "fsdp"), None),
        P(("dp", "fsdp"), None),
        P(("dp", "fsdp"), None),
        P(("dp", "fsdp"), None),
        P(("dp", "fsdp")),
        P(("dp", "fsdp"), None),
        P(("dp", "fsdp"), None),
        P(("dp", "fsdp"), None),
        P(("dp", "fsdp"), None),
        P(("dp", "fsdp")),
    )
    out_specs = (
        P(("dp", "fsdp"), None, None),
        P(("dp", "fsdp"), None, None),
        P(("dp", "fsdp"), None),
        P(("dp", "fsdp"), None),
        P(("dp", "fsdp"), None),
        P(("dp", "fsdp"), None),
        P(("dp", "fsdp"), None),
        P(("dp", "fsdp"), None),
        P(("dp", "fsdp"), None),
        P(("dp", "fsdp"), None),
        P(("dp", "fsdp"), None),
        P(("dp", "fsdp"), None),
        P(("dp", "fsdp"), None),
        P(("dp", "fsdp"), None),
        P(("dp", "fsdp")),
        P(("dp", "fsdp")),
        P(("dp", "fsdp")),
    )
    return jax.shard_map(local, mesh=mesh, in_specs=in_specs, out_specs=out_specs, check_vma=False)
```

```python
import jax
import jax.numpy as jnp
from jax import lax
from jax.experimental import pallas as pl
from jax.experimental.pallas import tpu as pltpu
from jax.sharding import PartitionSpec as P

D = 768
HEADS = 12
FF = 3072
STEP = 10
HALF = 384
WIN = 256
CUT_ONE = 1152
CUT_TWO = 1920
CUT_THREE = 384

EPSILON = 1e-05
BETA_ONE = 0.9
BETA_TWO = 0.999
ADAM_EPS = 1e-08
RATE_MATRIX = 0.05
DECAY_MATRIX = 0.05
RATE_VECTOR = 0.3

AXES = ("dp", "fsdp")
LOW = jnp.bfloat16
WIDE = jnp.float32
VMEM_BYTES = 56 * 2**20


def nn(left, right):
    return lax.dot_general(left, right, (((1,), (0,)), ((), ())), preferred_element_type=WIDE)


def nt(left, right):
    return lax.dot_general(left, right, (((1,), (1,)), ((), ())), preferred_element_type=WIDE)


def tn(left, right):
    return lax.dot_general(left, right, (((0,), (0,)), ((), ())), preferred_element_type=WIDE)


def shape(rows, cols, kind=LOW):
    return jax.ShapeDtypeStruct((rows, cols), kind)


def whole_call(kernel, outs, scratch, smem, name, flops, *args, anywhere=()):
    specs = []
    for i in range(len(args)):
        space = pltpu.SMEM if i < smem else pl.ANY if i in anywhere else pltpu.VMEM
        specs.append(pl.BlockSpec(memory_space=space))
    moved = sum(a.size * a.dtype.itemsize for a in args) + sum(o.size * o.dtype.itemsize for o in outs)
    return pl.pallas_call(
        kernel,
        in_specs=specs,
        out_specs=[pl.BlockSpec(memory_space=pltpu.VMEM)] * len(outs),
        out_shape=outs,
        scratch_shapes=scratch,
        compiler_params=pltpu.CompilerParams(vmem_limit_bytes=VMEM_BYTES),
        cost_estimate=pl.CostEstimate(flops=flops, bytes_accessed=moved, transcendentals=0),
        name=name,
    )(*args)


def over_rows(count, step, body, init=None):
    return lax.fori_loop(0, count // step, lambda i, c: body(pl.ds(pl.multiple_of(i * step, step), step), c), init)


def normal(values):
    centre = values - jnp.mean(values, axis=-1, keepdims=True)
    rstd = lax.rsqrt(jnp.mean(centre * centre, axis=-1, keepdims=True) + EPSILON)
    return centre * rstd, rstd


def both(own, other, lo, width):
    return jnp.concatenate([own[:, lo : lo + width], other[:, lo : lo + width]], axis=0)


def qkv_kernel(x_ref, vec_ref, order_ref, ao, ax, bo, bx, a_ref, qkv_ref, tmp):
    gain, shift = vec_ref[0:1, :], vec_ref[1:2, :]

    def norm(rows, _):
        tmp[rows, :] = (normal(x_ref[rows, :].astype(WIDE))[0] * gain + shift).astype(LOW)

    over_rows(x_ref.shape[0], 64, norm)
    a_ref[...] = nn(tmp[...], order_ref[...]).astype(LOW)
    for col in range(0, 3 * D, 384):
        own, other, lo = (ao, ax, col) if col < CUT_ONE else (bo, bx, col - CUT_ONE)
        qkv_ref[:, col : col + 384] = nn(a_ref[...], both(own, other, lo, 384)).astype(LOW)


def project(x, vec, order, one):
    n = x.shape[0]
    return whole_call(
        qkv_kernel, [shape(n, D), shape(n, 3 * D)], [pltpu.VMEM((n, D), LOW)], 0, "project",
        2 * n * D * (4 * D), x, vec, order, *one,
    )


def attend_kernel(spans, slopes, q_ref, k_ref, v_ref, far_ref, o_ref, p_ref, acc):
    pair = pl.program_id(0)
    acc[...] = jnp.zeros_like(acc)
    lane = lax.broadcasted_iota(jnp.int32, (WIN, 128), 1)
    rows = lax.broadcasted_iota(jnp.int32, (WIN, 1), 0)
    for t in range(4):
        lo, hi = spans[t, 0], spans[t, 1]

        @pl.when(hi > lo)
        def _():
            at = pl.multiple_of(spans[t, 2], 16)
            win = pl.ds(at, WIN)
            q, k, v = q_ref[win, :], k_ref[win, :], v_ref[win, :]
            inside = ((rows + at >= lo) & (rows + at < hi)).astype(WIDE)
            far = far_ref[t]
            out = None
            for e in range(2):
                keep = (lane < 64) if e == 0 else (lane >= 64)
                s = nt(q, jnp.where(keep, k, jnp.zeros_like(k))) * 0.125 - slopes[2 * pair + e] * far
                p = jnp.exp(s - jnp.max(s, axis=1, keepdims=True))
                p = (p * (inside / jnp.sum(p, axis=1, keepdims=True))).astype(LOW)
                p_ref[e, t] = p
                part = nn(p, jnp.where(keep, v, jnp.zeros_like(v)))
                out = part if out is None else out + part
            acc[win, :] += out

    o_ref[...] = acc[...].astype(LOW)


def columns(n, offset):
    return pl.BlockSpec((n, 128), lambda h, *_: (0, h + offset))


def attend(qkv, far, spans, slopes):
    n = qkv.shape[0]
    return pl.pallas_call(
        attend_kernel,
        grid_spec=pltpu.PrefetchScalarGridSpec(
            num_scalar_prefetch=2,
            grid=(6,),
            in_specs=[columns(n, 0), columns(n, 6), columns(n, 12), pl.BlockSpec((4, WIN, WIN), lambda h, *_: (0, 0, 0))],
            out_specs=[columns(n, 0), pl.BlockSpec((2, 4, WIN, WIN), lambda h, *_: (h, 0, 0, 0))],
            scratch_shapes=[pltpu.VMEM((n, 128), WIDE)],
        ),
        out_shape=[shape(n, D), jax.ShapeDtypeStruct((HEADS, 4, WIN, WIN), LOW)],
        compiler_params=pltpu.CompilerParams(vmem_limit_bytes=VMEM_BYTES),
        cost_estimate=pl.CostEstimate(flops=12 * 10**9, bytes_accessed=12 * 10**6, transcendentals=0),
        name="attend",
    )(spans, slopes, qkv, qkv, qkv, far)


def attend_back_kernel(spans, q_ref, k_ref, v_ref, g_ref, p_ref, d_ref, aq, ak, av):
    for acc in (aq, ak, av):
        acc[...] = jnp.zeros_like(acc)
    lane = lax.broadcasted_iota(jnp.int32, (WIN, 128), 1)
    for t in range(4):

        @pl.when(spans[t, 1] > spans[t, 0])
        def _():
            win = pl.ds(pl.multiple_of(spans[t, 2], 16), WIN)
            q, k, v, g = q_ref[win, :], k_ref[win, :], v_ref[win, :], g_ref[win, :]
            sums = None
            for e in range(2):
                keep = (lane < 64) if e == 0 else (lane >= 64)
                qe, ke, ge = [jnp.where(keep, z, jnp.zeros_like(z)) for z in (q, k, g)]
                p = p_ref[e, t]
                wide = p.astype(WIDE)
                d = wide * nt(ge, v)
                d = ((d - wide * jnp.sum(d, axis=1, keepdims=True)) * 0.125).astype(LOW)
                parts = (nn(d, ke), tn(d, qe), tn(p, ge))
                sums = parts if sums is None else tuple(a + b for a, b in zip(sums, parts))
            for acc, part in zip((aq, ak, av), sums):
                acc[win, :] += part

    col = pl.multiple_of(pl.program_id(0) * 128, 128)
    for third, acc in enumerate((aq, ak, av)):
        d_ref[:, pl.ds(col + third * D, 128)] = acc[...].astype(LOW)


def attend_back(qkv, grad, probs, spans):
    n = qkv.shape[0]
    return pl.pallas_call(
        attend_back_kernel,
        grid_spec=pltpu.PrefetchScalarGridSpec(
            num_scalar_prefetch=1,
            grid=(6,),
            in_specs=[columns(n, 0), columns(n, 6), columns(n, 12), columns(n, 0),
                      pl.BlockSpec((2, 4, WIN, WIN), lambda h, *_: (h, 0, 0, 0))],
            out_specs=pl.BlockSpec((n, 3 * D), lambda h, *_: (0, 0)),
            scratch_shapes=[pltpu.VMEM((n, 128), WIDE)] * 3,
        ),
        out_shape=shape(n, 3 * D),
        compiler_params=pltpu.CompilerParams(vmem_limit_bytes=VMEM_BYTES),
        cost_estimate=pl.CostEstimate(flops=20 * 10**9, bytes_accessed=12 * 10**6, transcendentals=0),
        name="attend_back",
    )(spans, qkv, qkv, qkv, grad, probs)


def tables(seg, side, valid):
    n = seg.shape[0]
    ids = jnp.arange(n, dtype=jnp.int32)
    tiles = jnp.arange(4, dtype=jnp.int32)
    low = jnp.sum((seg[None, :] < tiles[:, None]).astype(jnp.int32), axis=1)
    high = jnp.sum((seg[None, :] <= tiles[:, None]).astype(jnp.int32), axis=1)
    at = jnp.minimum(low // 16 * 16, n - WIN)
    spans = jnp.stack([low, high, at], axis=1)
    place = ids - jnp.sum((seg[None, :] < seg[:, None]).astype(jnp.int32), axis=1)
    packed = jnp.stack([place // side, place % side, seg, valid, ids], axis=0)
    cut = jnp.stack([lax.dynamic_slice(packed, (0, at[t]), (5, WIN)) for t in range(4)], axis=0)
    row, col = cut[:, 0].astype(WIDE), cut[:, 1].astype(WIDE)
    row = row[:, :, None] - row[:, None, :]
    col = col[:, :, None] - col[:, None, :]
    mine = cut[:, 2] == tiles[:, None]
    allowed = mine[:, :, None] & mine[:, None, :] & (
        (cut[:, 3][:, None, :] == 1) | (cut[:, 4][:, :, None] == cut[:, 4][:, None, :])
    )
    return spans, jnp.where(allowed, jnp.sqrt(row * row + col * col), 1e12)


def bell(u):
    bell_value = jnp.exp(u * u * -0.5)
    size = jnp.abs(u)
    t = 1.0 / (1.0 + 0.23164189 * size)
    poly = 0.127414796 + t * (-0.142248368 + t * (0.7107068705 + t * (-0.7265760135 + t * 0.5307027145)))
    tail = poly * t * bell_value
    share = jnp.where(u >= 0, 1.0 - tail, tail)
    return u * share, share + u * bell_value * 0.3989422804014327


def up_kernel(x_ref, o_ref, vec_ref, order_ref, ao, ax, bo, bx, mixed_ref, h_ref, a_ref, gl_ref, gp_ref, tmp):
    mixed_ref[...] = nn(o_ref[...], order_ref[...]).astype(LOW)
    for col in (0, 384):
        part = slice(col, col + 384)
        h_ref[:, part] = x_ref[:, part].astype(WIDE) + nn(mixed_ref[...], both(ao, ax, col, 384)) + vec_ref[2:3, part]
    gain, shift = vec_ref[3:4, :], vec_ref[4:5, :]

    def norm(rows, _):
        tmp[rows, :] = (normal(h_ref[rows, :])[0] * gain + shift).astype(LOW)

    over_rows(x_ref.shape[0], 64, norm)
    a_ref[...] = nn(tmp[...], order_ref[...]).astype(LOW)
    for col in range(0, FF, 384):
        lo = col + D
        own, other, lo = (ao, ax, lo) if lo < CUT_TWO else (bo, bx, lo - CUT_TWO)
        k = 5 + col // D
        u = nn(a_ref[...], both(own, other, lo, 384)) + vec_ref[k : k + 1, col % D : col % D + 384]
        value, slope = bell(u)
        gl_ref[:, col : col + 384] = value.astype(LOW)
        gp_ref[:, col : col + 384] = slope.astype(LOW)


def upward(x, o, vec, order, two):
    n = x.shape[0]
    return whole_call(
        up_kernel, [shape(n, D), shape(n, D, WIDE), shape(n, D), shape(n, FF), shape(n, FF)],
        [pltpu.VMEM((n, D), LOW)], 0, "upward", 2 * n * D * (7 * D) * 2, x, o, vec, order, *two,
    )


def down_kernel(place, vec_ref, order_ref, gl_ref, gp_ref, dy_ref, h_ref, ao, ax, bo, bx, w0, w1, w2, w3,
                out_ref, dur_ref, dh_ref, dhr_ref, dor_ref, vg_ref, wd, tmp, sem):
    def fetch(b, go):
        p = place[b]
        dst = pl.ds(pl.multiple_of(b * 96, 96), 96)

        def move(left, right, row):
            src = pl.ds(pl.multiple_of(row * 96, 96), 96)
            for piece, cols in ((left, pl.ds(0, CUT_THREE)), (right, pl.ds(CUT_THREE, D - CUT_THREE))):
                copy = pltpu.make_async_copy(piece.at[src, :], wd.at[dst, cols], sem)
                if go:
                    copy.start()
                else:
                    copy.wait()

        if go:
            pl.when(p < 16)(lambda: move(w0, w2, p))
            pl.when(p >= 16)(lambda: move(w1, w3, p - 16))
        else:
            move(w0, w2, 0)

    lax.fori_loop(0, 32, lambda b, c: (fetch(b, True), c)[1], 0)
    lax.fori_loop(0, 32, lambda b, c: (fetch(b, False), c)[1], 0)
    for col in (0, 384):
        part = slice(col, col + 384)
        out_ref[:, part] = (h_ref[:, part] + nn(gl_ref[...], wd[:, part]) + vec_ref[9:10, part]).astype(LOW)
    for col in range(0, FF, 384):
        part = slice(col, col + 384)
        du = nt(dy_ref[...], wd[part, :]) * gp_ref[:, part].astype(WIDE)
        dur_ref[:, part] = du.astype(LOW)
        k = 5 + col // D
        vg_ref[k : k + 1, col % D : col % D + 384] = jnp.sum(du, axis=0, keepdims=True)
    split = CUT_TWO - D
    for i, (a, b) in enumerate(((ao, bo), (ax, bx))):
        tmp[:, HALF * i : HALF * (i + 1)] = (
            nt(dur_ref[:, :split], a[:, D:]) + nt(dur_ref[:, split:], b[...])
        ).astype(LOW)
    dh_ref[...] = nt(tmp[...], order_ref[...])
    gain = vec_ref[3:4, :]

    def step(rows, sums):
        e = dh_ref[rows, :]
        dy = dy_ref[rows, :].astype(WIDE)
        n, rstd = normal(h_ref[rows, :])
        w = e * gain
        dh = dy + rstd * (w - jnp.mean(w, axis=-1, keepdims=True) - n * jnp.mean(w * n, axis=-1, keepdims=True))
        dh_ref[rows, :] = dh
        dhr_ref[rows, :] = dh.astype(LOW)
        return tuple(s + jnp.sum(z.reshape(-1, 8, D), axis=0) for s, z in zip(sums, (dh, e * n, e, dy)))

    zero = jnp.zeros((8, D), WIDE)
    sums = over_rows(h_ref.shape[0], 32, step, (zero,) * 4)
    for k, s in zip((2, 3, 4, 9), sums):
        vg_ref[k : k + 1, :] = jnp.sum(s, axis=0, keepdims=True)
    for i, a in enumerate((ao, ax)):
        tmp[:, HALF * i : HALF * (i + 1)] = nt(dhr_ref[...], a[:, :D]).astype(LOW)
    dor_ref[...] = nt(tmp[...], order_ref[...]).astype(LOW)


def downward(place, vec, order, gl, gp, dy, h, two, three):
    n = h.shape[0]
    return whole_call(
        down_kernel,
        [shape(n, D), shape(n, FF), shape(n, D, WIDE), shape(n, D), shape(n, D), shape(16, D, WIDE)],
        [pltpu.VMEM((FF, D), LOW), pltpu.VMEM((n, D), LOW), pltpu.SemaphoreType.DMA], 1, "downward",
        2 * n * D * (17 * D), place, vec, order, gl, gp, dy, h, *two, *three, anywhere=(11, 12, 13, 14),
    )


def down_grad_kernel(place, gl_ref, dy_ref, w0, w1, w2, w3):
    for c in range(8):
        t = tn(gl_ref[:, 384 * c : 384 * (c + 1)], dy_ref[...]).astype(LOW)
        for i in range(4):
            p = place[4 * c + i]

            def put(left, right, row):
                rows = pl.ds(pl.multiple_of(row * 96, 96), 96)
                left[rows, :] = t[96 * i : 96 * (i + 1), :CUT_THREE]
                right[rows, :] = t[96 * i : 96 * (i + 1), CUT_THREE:]

            pl.when(p < 16)(lambda: put(w0, w2, p))
            pl.when(p >= 16)(lambda: put(w1, w3, p - 16))


def down_grad(place, gl, dy):
    n = dy.shape[0]
    outs = [shape(FF // 2, CUT_THREE)] * 2 + [shape(FF // 2, D - CUT_THREE)] * 2
    return whole_call(down_grad_kernel, outs, [], 1, "down_grad", 2 * n * D * FF, place, gl, dy)


def two_grad_kernel(mixed_ref, a_ref, dhr_ref, dur_ref, ao, ax, bo, bx):
    for col in range(0, D + FF, 384):
        left, right = (mixed_ref, dhr_ref[:, col : col + 384]) if col < D else (a_ref, dur_ref[:, col - D : col - D + 384])
        t = tn(left[...], right).astype(LOW)
        own, other, lo = (ao, ax, col) if col < CUT_TWO else (bo, bx, col - CUT_TWO)
        own[:, lo : lo + 384] = t[:HALF]
        other[:, lo : lo + 384] = t[HALF:]


def two_grad(mixed, a, dhr, dur):
    n = a.shape[0]
    outs = [shape(HALF, CUT_TWO)] * 2 + [shape(HALF, D + FF - CUT_TWO)] * 2
    return whole_call(two_grad_kernel, outs, [], 0, "two_grad", 2 * n * D * (D + FF), mixed, a, dhr, dur)


def one_grad_kernel(a_ref, d_ref, vec_ref, ao, ax, bo, bx):
    for col in range(0, 3 * D, 384):
        t = tn(a_ref[...], d_ref[:, col : col + 384]).astype(LOW)
        own, other, lo = (ao, ax, col) if col < CUT_ONE else (bo, bx, col - CUT_ONE)
        own[:, lo : lo + 384] = t[:HALF]
        other[:, lo : lo + 384] = t[HALF:]
    bo[:, 3 * D - CUT_ONE :] = vec_ref[:HALF, :]
    bx[:, 3 * D - CUT_ONE :] = vec_ref[HALF:, :]


def one_grad(a, d, vec_cols):
    n = a.shape[0]
    outs = [shape(HALF, CUT_ONE)] * 2 + [shape(HALF, 3 * D + 128 - CUT_ONE)] * 2
    return whole_call(one_grad_kernel, outs, [], 0, "one_grad", 2 * n * D * 3 * D, a, d, vec_cols)


def input_kernel(x_ref, vec_ref, order_ref, d_ref, dh_ref, ao, ax, bo, bx, dx_ref, vg_ref, tmp):
    for i, (a, b) in enumerate(((ao, bo), (ax, bx))):
        tmp[:, HALF * i : HALF * (i + 1)] = (
            nt(d_ref[:, :CUT_ONE], a[...]) + nt(d_ref[:, CUT_ONE:], b[:, : 3 * D - CUT_ONE])
        ).astype(LOW)
    dx_ref[...] = nt(tmp[...], order_ref[...])
    gain = vec_ref[0:1, :]

    def step(rows, sums):
        e = dx_ref[rows, :]
        n, rstd = normal(x_ref[rows, :].astype(WIDE))
        w = e * gain
        dx_ref[rows, :] = dh_ref[rows, :] + rstd * (
            w - jnp.mean(w, axis=-1, keepdims=True) - n * jnp.mean(w * n, axis=-1, keepdims=True)
        )
        return tuple(s + jnp.sum(z.reshape(-1, 8, D), axis=0) for s, z in zip(sums, (e * n, e)))

    zero = jnp.zeros((8, D), WIDE)
    sums = over_rows(x_ref.shape[0], 32, step, (zero,) * 2)
    for k, s in enumerate(sums):
        vg_ref[k : k + 1, :] = jnp.sum(s, axis=0, keepdims=True)


def input_grad(x, vec, order, d, dh, one):
    n = x.shape[0]
    return whole_call(
        input_kernel, [shape(n, D, WIDE), shape(8, D, WIDE)], [pltpu.VMEM((n, D), LOW)], 0, "input_grad",
        2 * n * D * 4 * D, x, vec, order, d, dh, *one,
    )


def swap(value, bits):
    pairs = [(i, i ^ bits) for i in range(32)]
    return lax.ppermute(value, AXES, pairs)


def spread(block, cut):
    near = jnp.concatenate([block] + [swap(block, 8 * k) for k in (1, 2, 3)], axis=0)
    rows = near.shape[0]
    left, right = near[:, :cut], near[:, cut:]
    left = jnp.concatenate([left, swap(left, 2)], axis=0)
    right = jnp.concatenate([right, swap(right, 4)], axis=0)
    left = jnp.concatenate([left, swap(left, 4)], axis=0)
    far = swap(right, 2)
    right = jnp.concatenate([right[:rows], far[:rows], right[rows:], far[rows:]], axis=0)
    return left, swap(left, 1), right, swap(right, 1)


def collect(pieces):
    left = pieces[0].astype(WIDE) + swap(pieces[1], 1).astype(WIDE)
    right = pieces[2].astype(WIDE) + swap(pieces[3], 1).astype(WIDE)
    half = left.shape[0] // 2
    rows = half // 2
    left_got = swap(left[half:].astype(LOW), 4)
    right_got = swap(jnp.concatenate([right[rows:half], right[half + rows :]], axis=0).astype(LOW), 2)
    left = left[:half] + left_got.astype(WIDE)
    right = jnp.concatenate([right[:rows], right[half : half + rows]], axis=0) + right_got.astype(WIDE)
    left_got = swap(left[rows:].astype(LOW), 2)
    right_got = swap(right[rows:].astype(LOW), 4)
    both_sides = jnp.concatenate(
        [left[:rows] + left_got.astype(WIDE), right[:rows] + right_got.astype(WIDE)], axis=1
    )
    unit = rows // 4
    low = both_sides.astype(LOW)
    total = both_sides[:unit]
    for k in (1, 2, 3):
        total = total + swap(low[unit * k : unit * (k + 1)], 8 * k).astype(WIDE)
    return total


def spread_any(block, cut):
    whole = lax.all_gather(block, AXES, axis=0, tiled=True)
    half = whole.shape[0] // 2
    return whole[:half, :cut], whole[half:, :cut], whole[:half, cut:], whole[half:, cut:]


def join(pieces):
    return jnp.concatenate(
        [jnp.concatenate(pieces[:2], axis=0), jnp.concatenate(pieces[2:], axis=0)], axis=1
    )


def collect_any(pieces):
    return lax.psum_scatter(join(pieces), AXES, scatter_dimension=0, tiled=True).astype(WIDE)


def rearrange(whole, order, shards):
    return jnp.take(whole.reshape(shards, -1, whole.shape[1]), order, axis=0, mode="clip").reshape(whole.shape)


def adamw(master, moment_one, moment_two, gradient, step_rate, decay_rate):
    first_new = BETA_ONE * moment_one + (1.0 - BETA_ONE) * gradient
    second_new = BETA_TWO * moment_two + (1.0 - BETA_TWO) * gradient * gradient
    first_hat = first_new / (1.0 - BETA_ONE**STEP)
    second_hat = second_new / (1.0 - BETA_TWO**STEP)
    master_new = master - step_rate * (
        first_hat / (jnp.sqrt(second_hat) + ADAM_EPS) + decay_rate * master
    )
    return (first_new, second_new, master_new)


def local(
    tokens_in, cotangent, segments, tile_sides, valid_slots, owners,
    master_qkv, master_out, master_up, master_down, master_vec,
    first_qkv, first_out, first_up, first_down, first_vec,
    second_qkv, second_out, second_up, second_down, second_vec,
):
    shards = lax.axis_size(AXES)
    near = shards == 32
    unit = D // shards
    per_row = master_vec.shape[0] // unit
    if near:
        away = owners ^ lax.axis_index(AXES).astype(jnp.int32)
        place = (away >> 3) + 4 * ((away >> 1) & 1) + 8 * ((away >> 2) & 1) + 16 * (away & 1)
        place_down = place
    else:
        place = owners
        place_down = jnp.arange(32, dtype=jnp.int32)
    target = (place[:, None] * unit + jnp.arange(unit, dtype=jnp.int32)[None, :]).reshape(-1)
    order = (target[:, None] == jnp.arange(D, dtype=jnp.int32)[None, :]).astype(LOW)

    vec_block = jnp.pad(master_vec.reshape(unit, per_row), ((0, 0), (0, 128 - per_row)))
    block_one = jnp.concatenate([master_qkv, vec_block], axis=1).astype(LOW)
    block_two = jnp.concatenate([master_out, master_up], axis=1).astype(LOW)
    block_three = master_down.astype(LOW)
    if near:
        one = spread(block_one, CUT_ONE)
        two = spread(block_two, CUT_TWO)
        three = spread(block_three, CUT_THREE)
    else:
        one = spread_any(block_one, CUT_ONE)
        two = spread_any(block_two, CUT_TWO)
        whole = rearrange(lax.all_gather(block_three, AXES, axis=0, tiled=True), owners, shards)
        three = (whole[: FF // 2, :CUT_THREE], whole[FF // 2 :, :CUT_THREE],
                 whole[: FF // 2, CUT_THREE:], whole[FF // 2 :, CUT_THREE:])

    vec_rows = jnp.concatenate([one[2][:, 3 * D - CUT_ONE :], one[3][:, 3 * D - CUT_ONE :]], axis=0)
    vec = nn(order, vec_rows)[:, :per_row].reshape(per_row, D)
    vec = jnp.pad(vec, ((0, 16 - per_row), (0, 0)))
    spans, far = tables(segments[0], tile_sides[0], valid_slots[0])
    slopes = jnp.exp2(-8.0 * (jnp.arange(HEADS, dtype=jnp.int32).astype(WIDE) + 1.0) / HEADS)
    x = tokens_in[0]
    dy = cotangent[0]
    act_one, qkv = project(x, vec, order, one)
    mixed, probs = attend(qkv, far, spans, slopes)
    mixed, hidden, act_two, gelu, gelu_slope = upward(x, mixed, vec, order, two)
    grad_three = down_grad(place_down, gelu, dy)
    block_out, dur, dh, dh_low, dmixed, sums = downward(
        place_down, vec, order, gelu, gelu_slope, dy, hidden, two, three
    )
    grad_two = two_grad(mixed, act_two, dh_low, dur)
    dqkv = attend_back(qkv, dmixed, probs, spans)
    tokens_grad, sums_one = input_grad(x, vec, order, dqkv, dh, one)
    vector_grad = jnp.concatenate([sums_one[:2], sums[2:10]], axis=0).reshape(D, per_row)
    vec_cols = tn(order, jnp.pad(vector_grad, ((0, 0), (0, 128 - per_row))).astype(LOW)).astype(LOW)
    grad_one = one_grad(act_one, dqkv, vec_cols)
    if near:
        sum_three = collect(grad_three)
        sum_two = collect(grad_two)
        sum_one = collect(grad_one)
    else:
        ids = jnp.arange(shards, dtype=jnp.int32)
        inverse = jnp.sum(ids[:, None] * (owners[:, None] == ids[None, :]), axis=0)
        moved = rearrange(join(grad_three), inverse, shards)
        sum_three = lax.psum_scatter(moved, AXES, scatter_dimension=0, tiled=True).astype(WIDE)
        sum_two = collect_any(grad_two)
        sum_one = collect_any(grad_one)
    upd_qkv = adamw(master_qkv, first_qkv, second_qkv, sum_one[:, : 3 * D], RATE_MATRIX, DECAY_MATRIX)
    upd_out = adamw(master_out, first_out, second_out, sum_two[:, :D], RATE_MATRIX, DECAY_MATRIX)
    upd_up = adamw(master_up, first_up, second_up, sum_two[:, D:], RATE_MATRIX, DECAY_MATRIX)
    upd_down = adamw(master_down, first_down, second_down, sum_three, RATE_MATRIX, DECAY_MATRIX)
    sum_vec = sum_one[:, 3 * D : 3 * D + per_row].reshape(-1)
    upd_vec = adamw(master_vec, first_vec, second_vec, sum_vec, RATE_VECTOR, 0.0)
    return (
        (block_out[None], tokens_grad[None]) + upd_qkv + upd_out + upd_up + upd_down + upd_vec
    )


def solution(mesh):
    rows = P(AXES, None)
    flat = P(AXES)
    deep = P(AXES, None, None)
    stored = (rows,) * 4 + (flat,)
    in_specs = (deep,) * 2 + (rows,) * 3 + (P(),) + stored * 3
    out_specs = (deep,) * 2 + (rows,) * 12 + (flat,) * 3
    return jax.shard_map(local, mesh=mesh, in_specs=in_specs, out_specs=out_specs, check_vma=False)
```

```python
import functools

import jax
import jax.numpy as jnp
from jax import lax
from jax.experimental import pallas as pl
from jax.experimental.pallas import tpu as pltpu
from jax.sharding import PartitionSpec as P

D = 768
HEADS = 12
FF = 3072
STEP = 10
HALF = 384
WIN = 256
CUT_ONE = 1152
CUT_TWO = 1920
CUT_THREE = 384

EPSILON = 1e-05
BETA_ONE = 0.9
BETA_TWO = 0.999
ADAM_EPS = 1e-08
RATE_MATRIX = 0.05
DECAY_MATRIX = 0.05
RATE_VECTOR = 0.3

AXES = ("dp", "fsdp")
LOW = jnp.bfloat16
WIDE = jnp.float32
VMEM_BYTES = 56 * 2**20


def nn(left, right):
    return lax.dot_general(left, right, (((1,), (0,)), ((), ())), preferred_element_type=WIDE)


def nt(left, right):
    return lax.dot_general(left, right, (((1,), (1,)), ((), ())), preferred_element_type=WIDE)


def tn(left, right):
    return lax.dot_general(left, right, (((0,), (0,)), ((), ())), preferred_element_type=WIDE)


def shape(rows, cols, kind=LOW):
    return jax.ShapeDtypeStruct((rows, cols), kind)


def later(kernel, inputs, extra):
    return lambda *refs: kernel(*refs[:inputs], *refs[inputs + extra :])


def whole_call(kernel, outs, scratch, smem, name, flops, *args, anywhere=(), after=()):
    specs = []
    for i in range(len(args)):
        space = pltpu.SMEM if i < smem else pl.ANY if i in anywhere else pltpu.VMEM
        specs.append(pl.BlockSpec(memory_space=space))
    moved = sum(a.size * a.dtype.itemsize for a in args) + sum(o.size * o.dtype.itemsize for o in outs)
    return pl.pallas_call(
        later(kernel, len(args), len(after)),
        in_specs=specs + [pl.BlockSpec(memory_space=pl.ANY)] * len(after),
        out_specs=[pl.BlockSpec(memory_space=pltpu.VMEM)] * len(outs),
        out_shape=outs,
        scratch_shapes=scratch,
        compiler_params=pltpu.CompilerParams(vmem_limit_bytes=VMEM_BYTES),
        cost_estimate=pl.CostEstimate(flops=flops, bytes_accessed=moved, transcendentals=0),
        name=name,
    )(*args, *after)


def over_rows(count, step, body, init=None):
    return lax.fori_loop(0, count // step, lambda i, c: body(pl.ds(pl.multiple_of(i * step, step), step), c), init)


def normal(values):
    centre = values - jnp.mean(values, axis=-1, keepdims=True)
    rstd = lax.rsqrt(jnp.mean(centre * centre, axis=-1, keepdims=True) + EPSILON)
    return centre * rstd, rstd


def both(own, other, lo, width):
    return jnp.concatenate([own[:, lo : lo + width], other[:, lo : lo + width]], axis=0)


def qkv_kernel(x_ref, vec_ref, order_ref, ao, ax, bo, bx, a_ref, qkv_ref, tmp):
    gain, shift = vec_ref[0:1, :], vec_ref[1:2, :]

    def norm(rows, _):
        tmp[rows, :] = (normal(x_ref[rows, :].astype(WIDE))[0] * gain + shift).astype(LOW)

    over_rows(x_ref.shape[0], 64, norm)
    a_ref[...] = nn(tmp[...], order_ref[...]).astype(LOW)
    for col in range(0, 3 * D, 384):
        own, other, lo = (ao, ax, col) if col < CUT_ONE else (bo, bx, col - CUT_ONE)
        qkv_ref[:, col : col + 384] = nn(a_ref[...], both(own, other, lo, 384)).astype(LOW)


def project(x, vec, order, one, after=()):
    n = x.shape[0]
    return whole_call(
        qkv_kernel, [shape(n, D), shape(n, 3 * D)], [pltpu.VMEM((n, D), LOW)], 0, "project",
        2 * n * D * (4 * D), x, vec, order, *one, after=after,
    )


def attend_kernel(base, spans, slopes, q_ref, k_ref, v_ref, far_ref, o_ref, p_ref, acc):
    pair = pl.program_id(0) + base
    acc[...] = jnp.zeros_like(acc)
    lane = lax.broadcasted_iota(jnp.int32, (WIN, 128), 1)
    rows = lax.broadcasted_iota(jnp.int32, (WIN, 1), 0)
    for t in range(4):
        lo, hi = spans[t, 0], spans[t, 1]

        @pl.when(hi > lo)
        def _():
            at = pl.multiple_of(spans[t, 2], 16)
            win = pl.ds(at, WIN)
            q, k, v = q_ref[win, :], k_ref[win, :], v_ref[win, :]
            inside = ((rows + at >= lo) & (rows + at < hi)).astype(WIDE)
            far = far_ref[t]
            out = None
            for e in range(2):
                keep = (lane < 64) if e == 0 else (lane >= 64)
                s = nt(q, jnp.where(keep, k, jnp.zeros_like(k))) * 0.125 - slopes[2 * pair + e] * far
                p = jnp.exp(s - jnp.max(s, axis=1, keepdims=True))
                p = (p * (inside / jnp.sum(p, axis=1, keepdims=True))).astype(LOW)
                p_ref[e, t] = p
                part = nn(p, jnp.where(keep, v, jnp.zeros_like(v)))
                out = part if out is None else out + part
            acc[win, :] += out

    o_ref[...] = acc[...].astype(LOW)


def columns(n, offset):
    return pl.BlockSpec((n, 128), lambda h, *_: (0, h + offset))


def attend(base, qkv, far, spans, slopes, after=()):
    n = qkv.shape[0]
    return pl.pallas_call(
        later(functools.partial(attend_kernel, base), 6, len(after)),
        grid_spec=pltpu.PrefetchScalarGridSpec(
            num_scalar_prefetch=2,
            grid=(3,),
            in_specs=[columns(n, base), columns(n, base + 6), columns(n, base + 12),
                      pl.BlockSpec((4, WIN, WIN), lambda h, *_: (0, 0, 0))]
            + [pl.BlockSpec(memory_space=pl.ANY)] * len(after),
            out_specs=[columns(n, 0), pl.BlockSpec((2, 4, WIN, WIN), lambda h, *_: (h, 0, 0, 0))],
            scratch_shapes=[pltpu.VMEM((n, 128), WIDE)],
        ),
        out_shape=[shape(n, HALF), jax.ShapeDtypeStruct((HEADS // 2, 4, WIN, WIN), LOW)],
        compiler_params=pltpu.CompilerParams(vmem_limit_bytes=VMEM_BYTES),
        cost_estimate=pl.CostEstimate(flops=9 * 10**9, bytes_accessed=6 * 10**6, transcendentals=0),
        name="attend",
    )(spans, slopes, qkv, qkv, qkv, far, *after)


def attend_back_kernel(spans, q_ref, k_ref, v_ref, g_ref, p_ref, dq_ref, dk_ref, dv_ref, aq, ak, av):
    for acc in (aq, ak, av):
        acc[...] = jnp.zeros_like(acc)
    lane = lax.broadcasted_iota(jnp.int32, (WIN, 128), 1)
    for t in range(4):

        @pl.when(spans[t, 1] > spans[t, 0])
        def _():
            win = pl.ds(pl.multiple_of(spans[t, 2], 16), WIN)
            q, k, v, g = q_ref[win, :], k_ref[win, :], v_ref[win, :], g_ref[win, :]
            sums = None
            for e in range(2):
                keep = (lane < 64) if e == 0 else (lane >= 64)
                qe, ke, ge = [jnp.where(keep, z, jnp.zeros_like(z)) for z in (q, k, g)]
                p = p_ref[e, t]
                wide = p.astype(WIDE)
                d = wide * nt(ge, v)
                d = ((d - wide * jnp.sum(d, axis=1, keepdims=True)) * 0.125).astype(LOW)
                parts = (nn(d, ke), tn(d, qe), tn(p, ge))
                sums = parts if sums is None else tuple(a + b for a, b in zip(sums, parts))
            for acc, part in zip((aq, ak, av), sums):
                acc[win, :] += part

    for out, acc in zip((dq_ref, dk_ref, dv_ref), (aq, ak, av)):
        out[...] = acc[...].astype(LOW)


def attend_back(base, qkv, grad, probs, spans, after=()):
    n = qkv.shape[0]
    return pl.pallas_call(
        later(attend_back_kernel, 6, len(after)),
        grid_spec=pltpu.PrefetchScalarGridSpec(
            num_scalar_prefetch=1,
            grid=(3,),
            in_specs=[columns(n, base), columns(n, base + 6), columns(n, base + 12), columns(n, base),
                      pl.BlockSpec((2, 4, WIN, WIN), lambda h, *_: (h, 0, 0, 0))]
            + [pl.BlockSpec(memory_space=pl.ANY)] * len(after),
            out_specs=[columns(n, 0)] * 3,
            scratch_shapes=[pltpu.VMEM((n, 128), WIDE)] * 3,
        ),
        out_shape=[shape(n, HALF)] * 3,
        compiler_params=pltpu.CompilerParams(vmem_limit_bytes=VMEM_BYTES),
        cost_estimate=pl.CostEstimate(flops=12 * 10**9, bytes_accessed=6 * 10**6, transcendentals=0),
        name="attend_back",
    )(spans, qkv, qkv, qkv, grad, probs, *after)


def tables(seg, side, valid):
    n = seg.shape[0]
    ids = jnp.arange(n, dtype=jnp.int32)
    tiles = jnp.arange(4, dtype=jnp.int32)
    low = jnp.sum((seg[None, :] < tiles[:, None]).astype(jnp.int32), axis=1)
    high = jnp.sum((seg[None, :] <= tiles[:, None]).astype(jnp.int32), axis=1)
    at = jnp.minimum(low // 16 * 16, n - WIN)
    spans = jnp.stack([low, high, at], axis=1)
    place = ids - jnp.sum((seg[None, :] < seg[:, None]).astype(jnp.int32), axis=1)
    packed = jnp.stack([place // side, place % side, seg, valid, ids], axis=0)
    cut = jnp.stack([lax.dynamic_slice(packed, (0, at[t]), (5, WIN)) for t in range(4)], axis=0)
    row, col = cut[:, 0].astype(WIDE), cut[:, 1].astype(WIDE)
    row = row[:, :, None] - row[:, None, :]
    col = col[:, :, None] - col[:, None, :]
    mine = cut[:, 2] == tiles[:, None]
    allowed = mine[:, :, None] & mine[:, None, :] & (
        (cut[:, 3][:, None, :] == 1) | (cut[:, 4][:, :, None] == cut[:, 4][:, None, :])
    )
    return spans, jnp.where(allowed, jnp.sqrt(row * row + col * col), 1e12)


def bell(u):
    bell_value = jnp.exp(u * u * -0.5)
    size = jnp.abs(u)
    t = 1.0 / (1.0 + 0.23164189 * size)
    poly = 0.127414796 + t * (-0.142248368 + t * (0.7107068705 + t * (-0.7265760135 + t * 0.5307027145)))
    tail = poly * t * bell_value
    share = jnp.where(u >= 0, 1.0 - tail, tail)
    return u * share, share + u * bell_value * 0.3989422804014327


def up_kernel(x_ref, o0_ref, o1_ref, vec_ref, order_ref, ao, ax, bo, bx, mixed_ref, h_ref, a_ref, gl_ref, gp_ref, tmp):
    mixed_ref[...] = (
        nn(o0_ref[...], order_ref[:HALF, :]) + nn(o1_ref[...], order_ref[HALF:, :])
    ).astype(LOW)
    for col in (0, 384):
        part = slice(col, col + 384)
        h_ref[:, part] = x_ref[:, part].astype(WIDE) + nn(mixed_ref[...], both(ao, ax, col, 384)) + vec_ref[2:3, part]
    gain, shift = vec_ref[3:4, :], vec_ref[4:5, :]

    def norm(rows, _):
        tmp[rows, :] = (normal(h_ref[rows, :])[0] * gain + shift).astype(LOW)

    over_rows(x_ref.shape[0], 64, norm)
    a_ref[...] = nn(tmp[...], order_ref[...]).astype(LOW)
    for col in range(0, FF, 384):
        lo = col + D
        own, other, lo = (ao, ax, lo) if lo < CUT_TWO else (bo, bx, lo - CUT_TWO)
        k = 5 + col // D
        u = nn(a_ref[...], both(own, other, lo, 384)) + vec_ref[k : k + 1, col % D : col % D + 384]
        value, slope = bell(u)
        gl_ref[:, col : col + 384] = value.astype(LOW)
        gp_ref[:, col : col + 384] = slope.astype(LOW)


def upward(x, o, vec, order, two, after=()):
    n = x.shape[0]
    return whole_call(
        up_kernel, [shape(n, D), shape(n, D, WIDE), shape(n, D), shape(n, FF), shape(n, FF)],
        [pltpu.VMEM((n, D), LOW)], 0, "upward", 2 * n * D * (7 * D) * 2, x, *o, vec, order, *two,
        after=after,
    )


def down_kernel(place, vec_ref, gl_ref, gp_ref, dy_ref, h_ref, w0, w1, w2, w3, out_ref, dur_ref, vg_ref, wd, sem):
    def copies(b, left, right, row):
        src, dst = [pl.ds(pl.multiple_of(z * 96, 96), 96) for z in (row, b)]
        return (
            pltpu.make_async_copy(left.at[src, :], wd.at[dst, pl.ds(0, CUT_THREE)], sem),
            pltpu.make_async_copy(right.at[src, :], wd.at[dst, pl.ds(CUT_THREE, D - CUT_THREE)], sem),
        )

    def begin(b, carry):
        p = place[b]
        pl.when(p < 16)(lambda: [z.start() for z in copies(b, w0, w2, p)] and None)
        pl.when(p >= 16)(lambda: [z.start() for z in copies(b, w1, w3, p - 16)] and None)
        return carry

    def finish(b, carry):
        for z in copies(b, w0, w2, 0):
            z.wait()
        return carry

    lax.fori_loop(0, 32, begin, 0)
    lax.fori_loop(0, 32, finish, 0)
    for col in range(0, FF, 384):
        part = slice(col, col + 384)
        du = nt(dy_ref[...], wd[part, :]) * gp_ref[:, part].astype(WIDE)
        dur_ref[:, part] = du.astype(LOW)
        k = col // D
        vg_ref[k : k + 1, col % D : col % D + 384] = jnp.sum(du, axis=0, keepdims=True)
    for col in (0, 384):
        part = slice(col, col + 384)
        out_ref[:, part] = (h_ref[:, part] + nn(gl_ref[...], wd[:, part]) + vec_ref[9:10, part]).astype(LOW)


def downward(place, vec, gl, gp, dy, h, three, after=()):
    n = h.shape[0]
    return whole_call(
        down_kernel, [shape(n, D), shape(n, FF), shape(8, D, WIDE)],
        [pltpu.VMEM((FF, D), LOW), pltpu.SemaphoreType.DMA], 1, "downward",
        2 * n * D * (8 * D), place, vec, gl, gp, dy, h, *three, anywhere=(6, 7, 8, 9), after=after,
    )


def hidden_kernel(vec_ref, order_ref, dur_ref, dy_ref, h_ref, ao, ax, bo, bx, dh_ref, dhr_ref, dor_ref, vg_ref, tmp):
    split = CUT_TWO - D
    for i, (a, b) in enumerate(((ao, bo), (ax, bx))):
        tmp[:, HALF * i : HALF * (i + 1)] = (
            nt(dur_ref[:, :split], a[:, D:]) + nt(dur_ref[:, split:], b[...])
        ).astype(LOW)
    dh_ref[...] = nt(tmp[...], order_ref[...])
    gain = vec_ref[3:4, :]

    def step(rows, sums):
        e = dh_ref[rows, :]
        dy = dy_ref[rows, :].astype(WIDE)
        n, rstd = normal(h_ref[rows, :])
        w = e * gain
        dh = dy + rstd * (w - jnp.mean(w, axis=-1, keepdims=True) - n * jnp.mean(w * n, axis=-1, keepdims=True))
        dh_ref[rows, :] = dh
        dhr_ref[rows, :] = dh.astype(LOW)
        return tuple(s + jnp.sum(z.reshape(-1, 8, D), axis=0) for s, z in zip(sums, (dh, e * n, e, dy)))

    zero = jnp.zeros((8, D), WIDE)
    sums = over_rows(h_ref.shape[0], 32, step, (zero,) * 4)
    for k, s in enumerate(sums):
        vg_ref[k : k + 1, :] = jnp.sum(s, axis=0, keepdims=True)
    for i, a in enumerate((ao, ax)):
        tmp[:, HALF * i : HALF * (i + 1)] = nt(dhr_ref[...], a[:, :D]).astype(LOW)
    dor_ref[...] = nt(tmp[...], order_ref[...]).astype(LOW)


def hidden_grad(vec, order, dur, dy, h, two, after=()):
    n = h.shape[0]
    return whole_call(
        hidden_kernel, [shape(n, D, WIDE), shape(n, D), shape(n, D), shape(8, D, WIDE)],
        [pltpu.VMEM((n, D), LOW)], 0, "hidden_grad",
        2 * n * D * (7 * D), vec, order, dur, dy, h, *two, after=after,
    )


def down_grad_kernel(place, gl_ref, dy_ref, w0, w1, w2, w3):
    for c in range(8):
        t = tn(gl_ref[:, 384 * c : 384 * (c + 1)], dy_ref[...]).astype(LOW)
        for i in range(4):
            p = place[4 * c + i]

            def put(left, right, row):
                rows = pl.ds(pl.multiple_of(row * 96, 96), 96)
                left[rows, :] = t[96 * i : 96 * (i + 1), :CUT_THREE]
                right[rows, :] = t[96 * i : 96 * (i + 1), CUT_THREE:]

            pl.when(p < 16)(lambda: put(w0, w2, p))
            pl.when(p >= 16)(lambda: put(w1, w3, p - 16))


def down_grad(place, gl, dy, after=()):
    n = dy.shape[0]
    outs = [shape(FF // 2, CUT_THREE)] * 2 + [shape(FF // 2, D - CUT_THREE)] * 2
    return whole_call(down_grad_kernel, outs, [], 1, "down_grad", 2 * n * D * FF, place, gl, dy, after=after)


def two_grad_kernel(mixed_ref, a_ref, dhr_ref, dur_ref, ao, ax, bo, bx):
    for col in range(0, D + FF, 384):
        left, right = (mixed_ref, dhr_ref[:, col : col + 384]) if col < D else (a_ref, dur_ref[:, col - D : col - D + 384])
        t = tn(left[...], right).astype(LOW)
        own, other, lo = (ao, ax, col) if col < CUT_TWO else (bo, bx, col - CUT_TWO)
        own[:, lo : lo + 384] = t[:HALF]
        other[:, lo : lo + 384] = t[HALF:]


def two_grad(mixed, a, dhr, dur, after=()):
    n = a.shape[0]
    outs = [shape(HALF, CUT_TWO)] * 2 + [shape(HALF, D + FF - CUT_TWO)] * 2
    return whole_call(two_grad_kernel, outs, [], 0, "two_grad", 2 * n * D * (D + FF), mixed, a, dhr, dur,
                      after=after)


def one_grad_kernel(a_ref, *refs):
    halves, (ao, ax, bo, bx) = refs[:6], refs[6:]
    for i, half in enumerate(halves):
        t = tn(a_ref[...], half[...]).astype(LOW)
        col = 384 * i
        own, other, lo = (ao, ax, col) if col < CUT_ONE else (bo, bx, col - CUT_ONE)
        own[:, lo : lo + 384] = t[:HALF]
        other[:, lo : lo + 384] = t[HALF:]


def one_grad(a, d, after=()):
    n = a.shape[0]
    outs = [shape(HALF, CUT_ONE)] * 2 + [shape(HALF, 3 * D - CUT_ONE)] * 2
    return whole_call(one_grad_kernel, outs, [], 0, "one_grad", 2 * n * D * 3 * D, a, *d, after=after)


def input_kernel(x_ref, vec_ref, order_ref, q0, q1, k0, k1, v0, v1, dh_ref, ao, ax, bo, bx, dx_ref, vg_ref, tmp):
    for i, (a, b) in enumerate(((ao, bo), (ax, bx))):
        parts = ((q0, a, 0), (q1, a, 384), (k0, a, 768), (k1, b, 0), (v0, b, 384), (v1, b, 768))
        tmp[:, HALF * i : HALF * (i + 1)] = sum(nt(d[...], w[:, lo : lo + 384]) for d, w, lo in parts).astype(LOW)
    dx_ref[...] = nt(tmp[...], order_ref[...])
    gain = vec_ref[0:1, :]

    def step(rows, sums):
        e = dx_ref[rows, :]
        n, rstd = normal(x_ref[rows, :].astype(WIDE))
        w = e * gain
        dx_ref[rows, :] = dh_ref[rows, :] + rstd * (
            w - jnp.mean(w, axis=-1, keepdims=True) - n * jnp.mean(w * n, axis=-1, keepdims=True)
        )
        return tuple(s + jnp.sum(z.reshape(-1, 8, D), axis=0) for s, z in zip(sums, (e * n, e)))

    zero = jnp.zeros((8, D), WIDE)
    sums = over_rows(x_ref.shape[0], 32, step, (zero,) * 2)
    for k, s in enumerate(sums):
        vg_ref[k : k + 1, :] = jnp.sum(s, axis=0, keepdims=True)


def input_grad(x, vec, order, d, dh, one, after=()):
    n = x.shape[0]
    return whole_call(
        input_kernel, [shape(n, D, WIDE), shape(8, D, WIDE)], [pltpu.VMEM((n, D), LOW)], 0, "input_grad",
        2 * n * D * 4 * D, x, vec, order, *d, dh, *one, after=after,
    )


def swap(value, bits):
    pairs = [(i, i ^ bits) for i in range(32)]
    return lax.ppermute(value, AXES, pairs)


def tie(values, *first):
    return lax.optimization_barrier((tuple(values), first))[0]


def spread(block, cut):
    near = jnp.concatenate([block] + [swap(block, 8 * k) for k in (1, 2, 3)], axis=0)
    first = yield (near,)
    rows = near.shape[0]
    (near,) = tie((near,), first)
    left, right = near[:, :cut], near[:, cut:]
    left = jnp.concatenate([left, swap(left, 2)], axis=0)
    right = jnp.concatenate([right, swap(right, 4)], axis=0)
    first = yield left, right
    left, right = tie((left, right), first)
    left = jnp.concatenate([left, swap(left, 4)], axis=0)
    far = swap(right, 2)
    right = jnp.concatenate([right[:rows], far[:rows], right[rows:], far[rows:]], axis=0)
    first = yield left, right
    left, right = tie((left, right), first)
    yield left, swap(left, 1), right, swap(right, 1)


def collect(pieces):
    got = swap(pieces[1], 1), swap(pieces[3], 1)
    yield got
    left = pieces[0].astype(WIDE) + got[0].astype(WIDE)
    right = pieces[2].astype(WIDE) + got[1].astype(WIDE)
    half = left.shape[0] // 2
    rows = half // 2
    out = jnp.concatenate([right[rows:half], right[half + rows :]], axis=0).astype(LOW)
    got = swap(left[half:].astype(LOW), 4), swap(out, 2)
    yield got
    left = left[:half] + got[0].astype(WIDE)
    right = jnp.concatenate([right[:rows], right[half : half + rows]], axis=0) + got[1].astype(WIDE)
    got = swap(left[rows:].astype(LOW), 2), swap(right[rows:].astype(LOW), 4)
    yield got
    both_sides = jnp.concatenate(
        [left[:rows] + got[0].astype(WIDE), right[:rows] + got[1].astype(WIDE)], axis=1
    )
    unit = rows // 4
    low = both_sides.astype(LOW)
    got = [swap(low[unit * k : unit * (k + 1)], 8 * k) for k in (1, 2, 3)]
    yield got
    yield (sum((z.astype(WIDE) for z in got), both_sides[:unit]),)


def collect_vec(blocks):
    for bits in (1, 4, 2):
        half = blocks.shape[0] // 2
        blocks = blocks[:half] + swap(blocks[half:], bits)
    return sum((swap(blocks[k : k + 1], 8 * k) for k in (1, 2, 3)), blocks[:1]).reshape(-1)


def cut_up(whole, cut):
    half = whole.shape[0] // 2
    return whole[:half, :cut], whole[half:, :cut], whole[:half, cut:], whole[half:, cut:]


def repeat(value, count):
    for _ in range(count):
        yield value


def spread_any(block, cut):
    return repeat(cut_up(lax.all_gather(block, AXES, axis=0, tiled=True), cut), 4)


def join(pieces):
    return jnp.concatenate(
        [jnp.concatenate(pieces[:2], axis=0), jnp.concatenate(pieces[2:], axis=0)], axis=1
    )


def collect_any(pieces):
    total = lax.psum_scatter(join(pieces), AXES, scatter_dimension=0, tiled=True).astype(WIDE)
    return repeat((total,), 5)


def rearrange(whole, order, shards):
    return jnp.take(whole.reshape(shards, -1, whole.shape[1]), order, axis=0, mode="clip").reshape(whole.shape)


def adamw(master, moment_one, moment_two, gradient, step_rate, decay_rate):
    first_new = BETA_ONE * moment_one + (1.0 - BETA_ONE) * gradient
    second_new = BETA_TWO * moment_two + (1.0 - BETA_TWO) * gradient * gradient
    first_hat = first_new / (1.0 - BETA_ONE**STEP)
    second_hat = second_new / (1.0 - BETA_TWO**STEP)
    master_new = master - step_rate * (
        first_hat / (jnp.sqrt(second_hat) + ADAM_EPS) + decay_rate * master
    )
    return (first_new, second_new, master_new)


def local(
    tokens_in, cotangent, segments, tile_sides, valid_slots, owners,
    master_qkv, master_out, master_up, master_down, master_vec,
    first_qkv, first_out, first_up, first_down, first_vec,
    second_qkv, second_out, second_up, second_down, second_vec,
):
    shards = lax.axis_size(AXES)
    near = shards == 32
    unit = D // shards
    per_row = master_vec.shape[0] // unit
    share = master_vec.shape[0]
    ids = jnp.arange(shards, dtype=jnp.int32)
    if near:
        away = owners ^ lax.axis_index(AXES).astype(jnp.int32)
        place = (away >> 3) + 4 * ((away >> 1) & 1) + 8 * ((away >> 2) & 1) + 16 * (away & 1)
        place_down = place
    else:
        place = owners
        place_down = jnp.arange(32, dtype=jnp.int32)
    inverse = jnp.sum(ids[:, None] * (place[:, None] == ids[None, :]), axis=0)
    target = (place[:, None] * unit + jnp.arange(unit, dtype=jnp.int32)[None, :]).reshape(-1)
    order = (target[:, None] == jnp.arange(D, dtype=jnp.int32)[None, :]).astype(LOW)
    gather, scatter = (spread, collect) if near else (spread_any, collect_any)

    vec_block = jnp.pad(master_vec.reshape(unit, per_row), ((0, 0), (0, 128 - per_row)))
    one = gather(jnp.concatenate([master_qkv, vec_block], axis=1).astype(LOW), CUT_ONE)
    two = gather(jnp.concatenate([master_out, master_up], axis=1).astype(LOW), CUT_TWO)
    if near:
        three = spread(master_down.astype(LOW), CUT_THREE)
    else:
        whole = lax.all_gather(master_down.astype(LOW), AXES, axis=0, tiled=True)
        three = repeat(cut_up(rearrange(whole, owners, shards), CUT_THREE), 4)
    next(one)
    two_near = next(two)
    next(one)
    three_near = next(three)
    one_second = next(one)
    two_first = two.send(one_second)
    one = next(one)

    vec_rows = jnp.concatenate([one[2][:, 3 * D - CUT_ONE :], one[3][:, 3 * D - CUT_ONE :]], axis=0)
    vec = nn(order, vec_rows)[:, :per_row].reshape(per_row, D)
    vec = jnp.pad(vec, ((0, 16 - per_row), (0, 0)))
    spans, far = tables(segments[0], tile_sides[0], valid_slots[0])
    slopes = jnp.exp2(-8.0 * (jnp.arange(HEADS, dtype=jnp.int32).astype(WIDE) + 1.0) / HEADS)
    x = tokens_in[0]
    dy = cotangent[0]
    act_one, qkv = project(x, vec, order, one, two_near)
    mixed_0, probs_0 = attend(0, qkv, far, spans, slopes, two_first + three_near)
    two_second = two.send(qkv)
    mixed_1, probs_1 = attend(3, qkv, far, spans, slopes, two_second + (mixed_0,))
    three_first = three.send(mixed_0)
    two = two.send(mixed_0)
    mixed, hidden, act_two, gelu, gelu_slope = upward(x, (mixed_0, mixed_1), vec, order, two, three_first)
    three_second = three.send(mixed_1)
    three = three.send(mixed_1)
    grad_three = down_grad(place_down, gelu, dy, three_second)
    if not near:
        whole = join(grad_three)
        back = jnp.sum(ids[:, None] * (owners[:, None] == ids[None, :]), axis=0)
        grad_three = cut_up(rearrange(whole, back, shards), CUT_THREE)
    sum_three = scatter(grad_three)
    block_out, dur, sums_up = downward(place_down, vec, gelu, gelu_slope, dy, hidden, three, tuple(grad_three))
    dh, dh_low, dmixed, sums = hidden_grad(vec, order, dur, dy, hidden, two, tuple(next(sum_three)))
    grad_two = two_grad(mixed, act_two, dh_low, dur, tuple(next(sum_three)))
    sum_two = scatter(grad_two)
    d0 = attend_back(0, qkv, dmixed, probs_0, spans, tuple(next(sum_three)) + tuple(grad_two))
    d1 = attend_back(3, qkv, dmixed, probs_1, spans, tuple(next(sum_three)) + tuple(next(sum_two)) + (d0[0],))
    d = [z for pair in zip(d0, d1) for z in pair]
    grad_one = one_grad(act_one, d, tuple(next(sum_two)))
    sum_one = scatter(grad_one)
    tokens_grad, sums_one = input_grad(
        x, vec, order, d, dh, one, tuple(next(sum_one)) + tuple(next(sum_two))
    )
    vector_grad = jnp.concatenate([sums_one[:2], sums[:3], sums_up[:4], sums[3:4]], axis=0)
    blocks = jnp.take(vector_grad.reshape(shards, share), inverse, axis=0, mode="clip")
    if near:
        sum_vec = collect_vec(blocks)
    else:
        sum_vec = lax.psum_scatter(blocks.reshape(-1), AXES, scatter_dimension=0, tiled=True)
    sum_one, sum_two, sum_three = [list(z)[-1][0] for z in (sum_one, sum_two, sum_three)]
    upd_qkv = adamw(master_qkv, first_qkv, second_qkv, sum_one, RATE_MATRIX, DECAY_MATRIX)
    upd_out = adamw(master_out, first_out, second_out, sum_two[:, :D], RATE_MATRIX, DECAY_MATRIX)
    upd_up = adamw(master_up, first_up, second_up, sum_two[:, D:], RATE_MATRIX, DECAY_MATRIX)
    upd_down = adamw(master_down, first_down, second_down, sum_three, RATE_MATRIX, DECAY_MATRIX)
    upd_vec = adamw(master_vec, first_vec, second_vec, sum_vec, RATE_VECTOR, 0.0)
    return (
        (block_out[None], tokens_grad[None]) + upd_qkv + upd_out + upd_up + upd_down + upd_vec
    )


def solution(mesh):
    rows = P(AXES, None)
    flat = P(AXES)
    deep = P(AXES, None, None)
    stored = (rows,) * 4 + (flat,)
    in_specs = (deep,) * 2 + (rows,) * 3 + (P(),) + stored * 3
    out_specs = (deep,) * 2 + (rows,) * 12 + (flat,) * 3
    return jax.shard_map(local, mesh=mesh, in_specs=in_specs, out_specs=out_specs, check_vma=False)
```

```python
import functools

import jax
import jax.numpy as jnp
from jax import lax
from jax.experimental import pallas as pl
from jax.experimental.pallas import tpu as pltpu
from jax.sharding import PartitionSpec as P

D = 768
HEADS = 12
FF = 3072
STEP = 10
HALF = 384
WIN = 256
CUT_ONE = 1152
CUT_TWO = 1920
CUT_THREE = 384

EPSILON = 1e-05
BETA_ONE = 0.9
BETA_TWO = 0.999
ADAM_EPS = 1e-08
RATE_MATRIX = 0.05
DECAY_MATRIX = 0.05
RATE_VECTOR = 0.3

AXES = ("dp", "fsdp")
LOW = jnp.bfloat16
WIDE = jnp.float32
VMEM_BYTES = 56 * 2**20


def nn(left, right):
    return lax.dot_general(left, right, (((1,), (0,)), ((), ())), preferred_element_type=WIDE)


def nt(left, right):
    return lax.dot_general(left, right, (((1,), (1,)), ((), ())), preferred_element_type=WIDE)


def tn(left, right):
    return lax.dot_general(left, right, (((0,), (0,)), ((), ())), preferred_element_type=WIDE)


def shape(rows, cols, kind=LOW):
    return jax.ShapeDtypeStruct((rows, cols), kind)


def later(kernel, inputs, extra):
    return lambda *refs: kernel(*refs[:inputs], *refs[inputs + extra :])


def whole_call(kernel, outs, scratch, smem, name, flops, *args, anywhere=(), after=()):
    specs = []
    for i in range(len(args)):
        space = pltpu.SMEM if i < smem else pl.ANY if i in anywhere else pltpu.VMEM
        specs.append(pl.BlockSpec(memory_space=space))
    moved = sum(a.size * a.dtype.itemsize for a in args) + sum(o.size * o.dtype.itemsize for o in outs)
    return pl.pallas_call(
        later(kernel, len(args), len(after)),
        in_specs=specs + [pl.BlockSpec(memory_space=pl.ANY)] * len(after),
        out_specs=[pl.BlockSpec(memory_space=pltpu.VMEM)] * len(outs),
        out_shape=outs,
        scratch_shapes=scratch,
        compiler_params=pltpu.CompilerParams(vmem_limit_bytes=VMEM_BYTES),
        cost_estimate=pl.CostEstimate(flops=flops, bytes_accessed=moved, transcendentals=0),
        name=name,
    )(*args, *after)


def over_rows(count, step, body, init=None):
    return lax.fori_loop(0, count // step, lambda i, c: body(pl.ds(pl.multiple_of(i * step, step), step), c), init)


def normal(values):
    centre = values - jnp.mean(values, axis=-1, keepdims=True)
    rstd = lax.rsqrt(jnp.mean(centre * centre, axis=-1, keepdims=True) + EPSILON)
    return centre * rstd, rstd


def both(own, other, lo, width):
    return jnp.concatenate([own[:, lo : lo + width], other[:, lo : lo + width]], axis=0)


def qkv_kernel(x_ref, vec_ref, order_ref, ao, ax, bo, bx, a_ref, qkv_ref, tmp):
    gain, shift = vec_ref[0:1, :], vec_ref[1:2, :]

    def norm(rows, _):
        tmp[rows, :] = (normal(x_ref[rows, :].astype(WIDE))[0] * gain + shift).astype(LOW)

    over_rows(x_ref.shape[0], 64, norm)
    a_ref[...] = nn(tmp[...], order_ref[...]).astype(LOW)
    for col in range(0, 3 * D, 384):
        own, other, lo = (ao, ax, col) if col < CUT_ONE else (bo, bx, col - CUT_ONE)
        qkv_ref[:, col : col + 384] = nn(a_ref[...], both(own, other, lo, 384)).astype(LOW)


def project(x, vec, order, one, after=()):
    n = x.shape[0]
    return whole_call(
        qkv_kernel, [shape(n, D), shape(n, 3 * D)], [pltpu.VMEM((n, D), LOW)], 0, "project",
        2 * n * D * (4 * D), x, vec, order, *one, after=after,
    )


def attend_kernel(base, spans, slopes, q_ref, k_ref, v_ref, far_ref, o_ref, p_ref, acc):
    pair = pl.program_id(0) + base
    acc[...] = jnp.zeros_like(acc)
    lane = lax.broadcasted_iota(jnp.int32, (WIN, 128), 1)
    rows = lax.broadcasted_iota(jnp.int32, (WIN, 1), 0)
    for t in range(4):
        lo, hi = spans[t, 0], spans[t, 1]

        @pl.when(hi > lo)
        def _():
            at = pl.multiple_of(spans[t, 2], 16)
            win = pl.ds(at, WIN)
            q, k, v = q_ref[win, :], k_ref[win, :], v_ref[win, :]
            inside = ((rows + at >= lo) & (rows + at < hi)).astype(WIDE)
            far = far_ref[t]
            out = None
            for e in range(2):
                keep = (lane < 64) if e == 0 else (lane >= 64)
                s = nt(q, jnp.where(keep, k, jnp.zeros_like(k))) * 0.125 - slopes[2 * pair + e] * far
                p = jnp.exp(s - jnp.max(s, axis=1, keepdims=True))
                p = (p * (inside / jnp.sum(p, axis=1, keepdims=True))).astype(LOW)
                p_ref[e, t] = p
                part = nn(p, jnp.where(keep, v, jnp.zeros_like(v)))
                out = part if out is None else out + part
            acc[win, :] += out

    o_ref[...] = acc[...].astype(LOW)


def columns(n, offset):
    return pl.BlockSpec((n, 128), lambda h, *_: (0, h + offset))


def attend(base, qkv, far, spans, slopes, after=()):
    n = qkv.shape[0]
    return pl.pallas_call(
        later(functools.partial(attend_kernel, base), 6, len(after)),
        grid_spec=pltpu.PrefetchScalarGridSpec(
            num_scalar_prefetch=2,
            grid=(3,),
            in_specs=[columns(n, base), columns(n, base + 6), columns(n, base + 12),
                      pl.BlockSpec((4, WIN, WIN), lambda h, *_: (0, 0, 0))]
            + [pl.BlockSpec(memory_space=pl.ANY)] * len(after),
            out_specs=[columns(n, 0), pl.BlockSpec((2, 4, WIN, WIN), lambda h, *_: (h, 0, 0, 0))],
            scratch_shapes=[pltpu.VMEM((n, 128), WIDE)],
        ),
        out_shape=[shape(n, HALF), jax.ShapeDtypeStruct((HEADS // 2, 4, WIN, WIN), LOW)],
        compiler_params=pltpu.CompilerParams(vmem_limit_bytes=VMEM_BYTES),
        cost_estimate=pl.CostEstimate(flops=9 * 10**9, bytes_accessed=6 * 10**6, transcendentals=0),
        name="attend",
    )(spans, slopes, qkv, qkv, qkv, far, *after)


def attend_back_kernel(spans, q_ref, k_ref, v_ref, g_ref, p_ref, dq_ref, dk_ref, dv_ref, aq, ak, av):
    for acc in (aq, ak, av):
        acc[...] = jnp.zeros_like(acc)
    lane = lax.broadcasted_iota(jnp.int32, (WIN, 128), 1)
    for t in range(4):

        @pl.when(spans[t, 1] > spans[t, 0])
        def _():
            win = pl.ds(pl.multiple_of(spans[t, 2], 16), WIN)
            q, k, v, g = q_ref[win, :], k_ref[win, :], v_ref[win, :], g_ref[win, :]
            sums = None
            for e in range(2):
                keep = (lane < 64) if e == 0 else (lane >= 64)
                qe, ke, ge = [jnp.where(keep, z, jnp.zeros_like(z)) for z in (q, k, g)]
                p = p_ref[e, t]
                wide = p.astype(WIDE)
                d = wide * nt(ge, v)
                d = ((d - wide * jnp.sum(d, axis=1, keepdims=True)) * 0.125).astype(LOW)
                parts = (nn(d, ke), tn(d, qe), tn(p, ge))
                sums = parts if sums is None else tuple(a + b for a, b in zip(sums, parts))
            for acc, part in zip((aq, ak, av), sums):
                acc[win, :] += part

    for out, acc in zip((dq_ref, dk_ref, dv_ref), (aq, ak, av)):
        out[...] = acc[...].astype(LOW)


def attend_back(base, qkv, grad, probs, spans, after=()):
    n = qkv.shape[0]
    return pl.pallas_call(
        later(attend_back_kernel, 6, len(after)),
        grid_spec=pltpu.PrefetchScalarGridSpec(
            num_scalar_prefetch=1,
            grid=(3,),
            in_specs=[columns(n, base), columns(n, base + 6), columns(n, base + 12), columns(n, base),
                      pl.BlockSpec((2, 4, WIN, WIN), lambda h, *_: (h, 0, 0, 0))]
            + [pl.BlockSpec(memory_space=pl.ANY)] * len(after),
            out_specs=[columns(n, 0)] * 3,
            scratch_shapes=[pltpu.VMEM((n, 128), WIDE)] * 3,
        ),
        out_shape=[shape(n, HALF)] * 3,
        compiler_params=pltpu.CompilerParams(vmem_limit_bytes=VMEM_BYTES),
        cost_estimate=pl.CostEstimate(flops=12 * 10**9, bytes_accessed=6 * 10**6, transcendentals=0),
        name="attend_back",
    )(spans, qkv, qkv, qkv, grad, probs, *after)


def tables(seg, side, valid):
    n = seg.shape[0]
    ids = jnp.arange(n, dtype=jnp.int32)
    tiles = jnp.arange(4, dtype=jnp.int32)
    low = jnp.sum((seg[None, :] < tiles[:, None]).astype(jnp.int32), axis=1)
    high = jnp.sum((seg[None, :] <= tiles[:, None]).astype(jnp.int32), axis=1)
    at = jnp.minimum(low // 16 * 16, n - WIN)
    spans = jnp.stack([low, high, at], axis=1)
    place = ids - jnp.sum((seg[None, :] < seg[:, None]).astype(jnp.int32), axis=1)
    packed = jnp.stack([place // side, place % side, seg, valid, ids], axis=0)
    cut = jnp.stack([lax.dynamic_slice(packed, (0, at[t]), (5, WIN)) for t in range(4)], axis=0)
    row, col = cut[:, 0].astype(WIDE), cut[:, 1].astype(WIDE)
    row = row[:, :, None] - row[:, None, :]
    col = col[:, :, None] - col[:, None, :]
    mine = cut[:, 2] == tiles[:, None]
    allowed = mine[:, :, None] & mine[:, None, :] & (
        (cut[:, 3][:, None, :] == 1) | (cut[:, 4][:, :, None] == cut[:, 4][:, None, :])
    )
    return spans, jnp.where(allowed, jnp.sqrt(row * row + col * col), 1e12)


def bell(u):
    bell_value = jnp.exp(u * u * -0.5)
    size = jnp.abs(u)
    t = 1.0 / (1.0 + 0.23164189 * size)
    poly = 0.127414796 + t * (-0.142248368 + t * (0.7107068705 + t * (-0.7265760135 + t * 0.5307027145)))
    tail = poly * t * bell_value
    share = jnp.where(u >= 0, 1.0 - tail, tail)
    return u * share, share + u * bell_value * 0.3989422804014327


def up_kernel(x_ref, o0_ref, o1_ref, vec_ref, order_ref, ao, ax, bo, bx, mixed_ref, h_ref, a_ref, gl_ref, gp_ref, tmp):
    mixed_ref[...] = (
        nn(o0_ref[...], order_ref[:HALF, :]) + nn(o1_ref[...], order_ref[HALF:, :])
    ).astype(LOW)
    for col in (0, 384):
        part = slice(col, col + 384)
        h_ref[:, part] = x_ref[:, part].astype(WIDE) + nn(mixed_ref[...], both(ao, ax, col, 384)) + vec_ref[2:3, part]
    gain, shift = vec_ref[3:4, :], vec_ref[4:5, :]

    def norm(rows, _):
        tmp[rows, :] = (normal(h_ref[rows, :])[0] * gain + shift).astype(LOW)

    over_rows(x_ref.shape[0], 64, norm)
    a_ref[...] = nn(tmp[...], order_ref[...]).astype(LOW)
    for col in range(0, FF, 384):
        lo = col + D
        own, other, lo = (ao, ax, lo) if lo < CUT_TWO else (bo, bx, lo - CUT_TWO)
        k = 5 + col // D
        u = nn(a_ref[...], both(own, other, lo, 384)) + vec_ref[k : k + 1, col % D : col % D + 384]
        value, slope = bell(u)
        gl_ref[:, col : col + 384] = value.astype(LOW)
        gp_ref[:, col : col + 384] = slope.astype(LOW)


def upward(x, o, vec, order, two, after=()):
    n = x.shape[0]
    return whole_call(
        up_kernel, [shape(n, D), shape(n, D, WIDE), shape(n, D), shape(n, FF), shape(n, FF)],
        [pltpu.VMEM((n, D), LOW)], 0, "upward", 2 * n * D * (7 * D) * 2, x, *o, vec, order, *two,
        after=after,
    )


def down_kernel(place, vec_ref, gl_ref, gp_ref, dy_ref, h_ref, w0, w1, w2, w3, out_ref, dur_ref, vg_ref, wd, sem):
    def copies(b, left, right, row):
        src, dst = [pl.ds(pl.multiple_of(z * 96, 96), 96) for z in (row, b)]
        return (
            pltpu.make_async_copy(left.at[src, :], wd.at[dst, pl.ds(0, CUT_THREE)], sem),
            pltpu.make_async_copy(right.at[src, :], wd.at[dst, pl.ds(CUT_THREE, D - CUT_THREE)], sem),
        )

    def begin(b, carry):
        p = place[b]
        pl.when(p < 16)(lambda: [z.start() for z in copies(b, w0, w2, p)] and None)
        pl.when(p >= 16)(lambda: [z.start() for z in copies(b, w1, w3, p - 16)] and None)
        return carry

    def finish(b, carry):
        for z in copies(b, w0, w2, 0):
            z.wait()
        return carry

    lax.fori_loop(0, 32, begin, 0)
    lax.fori_loop(0, 32, finish, 0)
    for col in range(0, FF, 384):
        part = slice(col, col + 384)
        du = nt(dy_ref[...], wd[part, :]) * gp_ref[:, part].astype(WIDE)
        dur_ref[:, part] = du.astype(LOW)
        k = col // D
        vg_ref[k : k + 1, col % D : col % D + 384] = jnp.sum(du, axis=0, keepdims=True)
    for col in (0, 384):
        part = slice(col, col + 384)
        out_ref[:, part] = (h_ref[:, part] + nn(gl_ref[...], wd[:, part]) + vec_ref[9:10, part]).astype(LOW)


def downward(place, vec, gl, gp, dy, h, three, after=()):
    n = h.shape[0]
    return whole_call(
        down_kernel, [shape(n, D), shape(n, FF), shape(8, D, WIDE)],
        [pltpu.VMEM((FF, D), LOW), pltpu.SemaphoreType.DMA], 1, "downward",
        2 * n * D * (8 * D), place, vec, gl, gp, dy, h, *three, anywhere=(6, 7, 8, 9), after=after,
    )


def hidden_kernel(vec_ref, order_ref, dur_ref, dy_ref, h_ref, ao, ax, bo, bx, dh_ref, dhr_ref, dor_ref, vg_ref, tmp):
    split = CUT_TWO - D
    for i, (a, b) in enumerate(((ao, bo), (ax, bx))):
        tmp[:, HALF * i : HALF * (i + 1)] = (
            nt(dur_ref[:, :split], a[:, D:]) + nt(dur_ref[:, split:], b[...])
        ).astype(LOW)
    dh_ref[...] = nt(tmp[...], order_ref[...])
    gain = vec_ref[3:4, :]

    def step(rows, sums):
        e = dh_ref[rows, :]
        dy = dy_ref[rows, :].astype(WIDE)
        n, rstd = normal(h_ref[rows, :])
        w = e * gain
        dh = dy + rstd * (w - jnp.mean(w, axis=-1, keepdims=True) - n * jnp.mean(w * n, axis=-1, keepdims=True))
        dh_ref[rows, :] = dh
        dhr_ref[rows, :] = dh.astype(LOW)
        return tuple(s + jnp.sum(z.reshape(-1, 8, D), axis=0) for s, z in zip(sums, (dh, e * n, e, dy)))

    zero = jnp.zeros((8, D), WIDE)
    sums = over_rows(h_ref.shape[0], 32, step, (zero,) * 4)
    for k, s in enumerate(sums):
        vg_ref[k : k + 1, :] = jnp.sum(s, axis=0, keepdims=True)
    for i, a in enumerate((ao, ax)):
        tmp[:, HALF * i : HALF * (i + 1)] = nt(dhr_ref[...], a[:, :D]).astype(LOW)
    dor_ref[...] = nt(tmp[...], order_ref[...]).astype(LOW)


def hidden_grad(vec, order, dur, dy, h, two, after=()):
    n = h.shape[0]
    return whole_call(
        hidden_kernel, [shape(n, D, WIDE), shape(n, D), shape(n, D), shape(8, D, WIDE)],
        [pltpu.VMEM((n, D), LOW)], 0, "hidden_grad",
        2 * n * D * (7 * D), vec, order, dur, dy, h, *two, after=after,
    )


def down_grad_kernel(place, gl_ref, dy_ref, w0, w1, w2, w3):
    for c in range(8):
        t = tn(gl_ref[:, 384 * c : 384 * (c + 1)], dy_ref[...]).astype(LOW)
        for i in range(4):
            p = place[4 * c + i]

            def put(left, right, row):
                rows = pl.ds(pl.multiple_of(row * 96, 96), 96)
                left[rows, :] = t[96 * i : 96 * (i + 1), :CUT_THREE]
                right[rows, :] = t[96 * i : 96 * (i + 1), CUT_THREE:]

            pl.when(p < 16)(lambda: put(w0, w2, p))
            pl.when(p >= 16)(lambda: put(w1, w3, p - 16))


def down_grad(place, gl, dy, after=()):
    n = dy.shape[0]
    outs = [shape(FF // 2, CUT_THREE)] * 2 + [shape(FF // 2, D - CUT_THREE)] * 2
    return whole_call(down_grad_kernel, outs, [], 1, "down_grad", 2 * n * D * FF, place, gl, dy, after=after)


def two_grad_kernel(mixed_ref, a_ref, dhr_ref, dur_ref, ao, ax, bo, bx):
    for col in range(0, D + FF, 384):
        left, right = (mixed_ref, dhr_ref[:, col : col + 384]) if col < D else (a_ref, dur_ref[:, col - D : col - D + 384])
        t = tn(left[...], right).astype(LOW)
        own, other, lo = (ao, ax, col) if col < CUT_TWO else (bo, bx, col - CUT_TWO)
        own[:, lo : lo + 384] = t[:HALF]
        other[:, lo : lo + 384] = t[HALF:]


def two_grad(mixed, a, dhr, dur, after=()):
    n = a.shape[0]
    outs = [shape(HALF, CUT_TWO)] * 2 + [shape(HALF, D + FF - CUT_TWO)] * 2
    return whole_call(two_grad_kernel, outs, [], 0, "two_grad", 2 * n * D * (D + FF), mixed, a, dhr, dur,
                      after=after)


def one_grad_kernel(a_ref, *refs):
    halves, (ao, ax, bo, bx) = refs[:6], refs[6:]
    for i, half in enumerate(halves):
        t = tn(a_ref[...], half[...]).astype(LOW)
        col = 384 * i
        own, other, lo = (ao, ax, col) if col < CUT_ONE else (bo, bx, col - CUT_ONE)
        own[:, lo : lo + 384] = t[:HALF]
        other[:, lo : lo + 384] = t[HALF:]


def one_grad(a, d, after=()):
    n = a.shape[0]
    outs = [shape(HALF, CUT_ONE)] * 2 + [shape(HALF, 3 * D - CUT_ONE)] * 2
    return whole_call(one_grad_kernel, outs, [], 0, "one_grad", 2 * n * D * 3 * D, a, *d, after=after)


def input_back_kernel(order_ref, q0, q1, k0, k1, v0, v1, ao, ax, bo, bx, e_ref, tmp):
    for i, (a, b) in enumerate(((ao, bo), (ax, bx))):
        parts = ((q0, a, 0), (q1, a, 384), (k0, a, 768), (k1, b, 0), (v0, b, 384), (v1, b, 768))
        tmp[:, HALF * i : HALF * (i + 1)] = sum(nt(d[...], w[:, lo : lo + 384]) for d, w, lo in parts).astype(LOW)
    e_ref[...] = nt(tmp[...], order_ref[...])


def input_back(order, d, one, after=()):
    n = d[0].shape[0]
    return whole_call(
        input_back_kernel, [shape(n, D, WIDE)], [pltpu.VMEM((n, D), LOW)], 0, "input_back",
        2 * n * D * 4 * D, order, *d, *one, after=after,
    )[0]


def input_kernel(x_ref, vec_ref, e_ref, dh_ref, dx_ref, vg_ref):
    gain = vec_ref[0:1, :]

    def step(rows, sums):
        e = e_ref[rows, :]
        n, rstd = normal(x_ref[rows, :].astype(WIDE))
        w = e * gain
        dx_ref[rows, :] = dh_ref[rows, :] + rstd * (
            w - jnp.mean(w, axis=-1, keepdims=True) - n * jnp.mean(w * n, axis=-1, keepdims=True)
        )
        return tuple(s + jnp.sum(z.reshape(-1, 8, D), axis=0) for s, z in zip(sums, (e * n, e)))

    zero = jnp.zeros((8, D), WIDE)
    sums = over_rows(x_ref.shape[0], 32, step, (zero,) * 2)
    for k, s in enumerate(sums):
        vg_ref[k : k + 1, :] = jnp.sum(s, axis=0, keepdims=True)


def input_grad(x, vec, e, dh, after=()):
    n = x.shape[0]
    return whole_call(
        input_kernel, [shape(n, D, WIDE), shape(8, D, WIDE)], [], 0, "input_grad",
        2 * n * D * 3 * D, x, vec, e, dh, after=after,
    )


def swap(value, bits):
    pairs = [(i, i ^ bits) for i in range(32)]
    return lax.ppermute(value, AXES, pairs)


def tie(values, *first):
    return lax.optimization_barrier((tuple(values), first))[0]


def transfer(firsts, stage, values, *bits):
    values = tie(values, firsts.get((stage, "start"), ()))
    got = firsts[stage, "got"] = tuple(swap(value, bit) for value, bit in zip(values, bits))
    both = tie(tuple(values) + got, firsts.get((stage, "end"), ()))
    return both[: len(values)], both[len(values) :]


def spread(block, cut, firsts):
    move = functools.partial(transfer, firsts)
    (block, _, _), got = move(0, (block,) * 3, 8, 16, 24)
    near = jnp.concatenate((block,) + got, axis=0)
    yield (near,)
    rows = near.shape[0]
    mine, got = move(1, (near[:, :cut], near[:, cut:]), 2, 4)
    left, right = [jnp.concatenate(z, axis=0) for z in zip(mine, got)]
    yield left, right
    (left, right), (got, far) = move(2, (left, right), 4, 2)
    left = jnp.concatenate([left, got], axis=0)
    right = jnp.concatenate([right[:rows], far[:rows], right[rows:], far[rows:]], axis=0)
    yield left, right
    mine, got = move(3, (left, right), 1, 1)
    yield mine[0], got[0], mine[1], got[1]


def collect(pieces, firsts):
    move = functools.partial(transfer, firsts)
    _, got = move(0, (pieces[1], pieces[3]), 1, 1)
    yield
    left = pieces[0].astype(WIDE) + got[0].astype(WIDE)
    right = pieces[2].astype(WIDE) + got[1].astype(WIDE)
    half = left.shape[0] // 2
    rows = half // 2
    out = jnp.concatenate([right[rows:half], right[half + rows :]], axis=0).astype(LOW)
    _, got = move(1, (left[half:].astype(LOW), out), 4, 2)
    yield
    left = left[:half] + got[0].astype(WIDE)
    right = jnp.concatenate([right[:rows], right[half : half + rows]], axis=0) + got[1].astype(WIDE)
    _, got = move(2, (left[rows:].astype(LOW), right[rows:].astype(LOW)), 2, 4)
    yield
    both_sides = jnp.concatenate(
        [left[:rows] + got[0].astype(WIDE), right[:rows] + got[1].astype(WIDE)], axis=1
    )
    unit = rows // 4
    low = both_sides.astype(LOW)
    _, got = move(3, [low[unit * k : unit * (k + 1)] for k in (1, 2, 3)], 8, 16, 24)
    yield
    yield sum((z.astype(WIDE) for z in got), both_sides[:unit])


def collect_vec(blocks):
    for bits in (1, 4, 2):
        half = blocks.shape[0] // 2
        blocks = blocks[:half] + swap(blocks[half:], bits)
    return sum((swap(blocks[k : k + 1], 8 * k) for k in (1, 2, 3)), blocks[:1]).reshape(-1)


def cut_up(whole, cut):
    half = whole.shape[0] // 2
    return whole[:half, :cut], whole[half:, :cut], whole[:half, cut:], whole[half:, cut:]


def repeat(value, count):
    for _ in range(count):
        yield value


def spread_any(block, cut, firsts):
    return repeat(cut_up(lax.all_gather(block, AXES, axis=0, tiled=True), cut), 4)


def join(pieces):
    return jnp.concatenate(
        [jnp.concatenate(pieces[:2], axis=0), jnp.concatenate(pieces[2:], axis=0)], axis=1
    )


def collect_any(pieces, firsts):
    total = lax.psum_scatter(join(pieces), AXES, scatter_dimension=0, tiled=True).astype(WIDE)
    return repeat(total, 5)


def rearrange(whole, order, shards):
    return jnp.take(whole.reshape(shards, -1, whole.shape[1]), order, axis=0, mode="clip").reshape(whole.shape)


def adamw(master, moment_one, moment_two, gradient, step_rate, decay_rate):
    first_new = BETA_ONE * moment_one + (1.0 - BETA_ONE) * gradient
    second_new = BETA_TWO * moment_two + (1.0 - BETA_TWO) * gradient * gradient
    first_hat = first_new / (1.0 - BETA_ONE**STEP)
    second_hat = second_new / (1.0 - BETA_TWO**STEP)
    master_new = master - step_rate * (
        first_hat / (jnp.sqrt(second_hat) + ADAM_EPS) + decay_rate * master
    )
    return (first_new, second_new, master_new)


def local(
    tokens_in, cotangent, segments, tile_sides, valid_slots, owners,
    master_qkv, master_out, master_up, master_down, master_vec,
    first_qkv, first_out, first_up, first_down, first_vec,
    second_qkv, second_out, second_up, second_down, second_vec,
):
    shards = lax.axis_size(AXES)
    near = shards == 32
    unit = D // shards
    per_row = master_vec.shape[0] // unit
    share = master_vec.shape[0]
    ids = jnp.arange(shards, dtype=jnp.int32)
    if near:
        away = owners ^ lax.axis_index(AXES).astype(jnp.int32)
        place = (away >> 3) + 4 * ((away >> 1) & 1) + 8 * ((away >> 2) & 1) + 16 * (away & 1)
        place_down = place
    else:
        place = owners
        place_down = jnp.arange(32, dtype=jnp.int32)
    inverse = jnp.sum(ids[:, None] * (place[:, None] == ids[None, :]), axis=0)
    target = (place[:, None] * unit + jnp.arange(unit, dtype=jnp.int32)[None, :]).reshape(-1)
    order = (target[:, None] == jnp.arange(D, dtype=jnp.int32)[None, :]).astype(LOW)
    gather, scatter = (spread, collect) if near else (spread_any, collect_any)

    vec_block = jnp.pad(master_vec.reshape(unit, per_row), ((0, 0), (0, 128 - per_row)))
    wait_two, wait_three = {}, {}
    one = gather(jnp.concatenate([master_qkv, vec_block], axis=1).astype(LOW), CUT_ONE, {})
    two = gather(jnp.concatenate([master_out, master_up], axis=1).astype(LOW), CUT_TWO, wait_two)
    if near:
        three = spread(master_down.astype(LOW), CUT_THREE, wait_three)
    else:
        whole = lax.all_gather(master_down.astype(LOW), AXES, axis=0, tiled=True)
        three = repeat(cut_up(rearrange(whole, owners, shards), CUT_THREE), 4)
    next(one)
    wait_two[0, "start"] = next(one)
    next(one)
    one = next(one)
    next(two)

    vec_rows = jnp.concatenate([one[2][:, 3 * D - CUT_ONE :], one[3][:, 3 * D - CUT_ONE :]], axis=0)
    vec = nn(order, vec_rows)[:, :per_row].reshape(per_row, D)
    vec = jnp.pad(vec, ((0, 16 - per_row), (0, 0)))
    spans, far = tables(segments[0], tile_sides[0], valid_slots[0])
    slopes = jnp.exp2(-8.0 * (jnp.arange(HEADS, dtype=jnp.int32).astype(WIDE) + 1.0) / HEADS)
    x = tokens_in[0]
    dy = cotangent[0]
    act_one, qkv = project(x, vec, order, one)
    wait_two[1, "start"] = one
    wait_two[1, "end"] = qkv
    wait_three[0, "start"] = next(two)
    mixed_0, probs_0 = attend(0, qkv, far, spans, slopes)
    wait_two[2, "end"] = mixed_0
    wait_three[1, "start"] = next(two)
    wait_three[0, "end"] = mixed_0
    next(three)
    mixed_1, probs_1 = attend(3, qkv, far, spans, slopes, wait_three.get((0, "got"), ()) + (mixed_0,))
    wait_three[1, "end"] = mixed_1
    next(three)
    two = next(two)
    mixed, hidden, act_two, gelu, gelu_slope = upward(
        x, (mixed_0, mixed_1), vec, order, two, wait_three.get((1, "got"), ())
    )
    wait_three[2, "end"] = mixed
    next(three)
    grad_three = down_grad(place_down, gelu, dy, wait_three.get((2, "got"), ()))
    three = next(three)
    if not near:
        whole = join(grad_three)
        back = jnp.sum(ids[:, None] * (owners[:, None] == ids[None, :]), axis=0)
        grad_three = cut_up(rearrange(whole, back, shards), CUT_THREE)
    wait_two, wait_three, wait_one = {}, {}, {}

    def arrived(waits, stage):
        return waits.get((stage, "got"), ())

    sum_three = scatter(grad_three, wait_three)
    block_out, dur, sums_up = downward(place_down, vec, gelu, gelu_slope, dy, hidden, three)
    wait_three[0, "end"] = dur
    next(sum_three)
    dh, dh_low, dmixed, sums = hidden_grad(vec, order, dur, dy, hidden, two, arrived(wait_three, 0))
    wait_three[1, "end"] = dh_low
    next(sum_three)
    grad_two = two_grad(mixed, act_two, dh_low, dur, arrived(wait_three, 1))
    wait_three[2, "end"] = grad_two
    next(sum_three)
    sum_two = scatter(grad_two, wait_two)
    d0 = attend_back(0, qkv, dmixed, probs_0, spans, arrived(wait_three, 2) + tuple(grad_two))
    wait_three[3, "end"] = d0[0]
    next(sum_three)
    wait_two[0, "end"] = d0[0]
    next(sum_two)
    d1 = attend_back(3, qkv, dmixed, probs_1, spans, arrived(wait_three, 3) + arrived(wait_two, 0) + (d0[0],))
    wait_two[1, "end"] = d1[0]
    next(sum_two)
    d = [z for pair in zip(d0, d1) for z in pair]
    grad_one = one_grad(act_one, d, arrived(wait_two, 1))
    wait_two[2, "end"] = grad_one
    next(sum_two)
    sum_one = scatter(grad_one, wait_one)
    dact = input_back(order, d, one, arrived(wait_two, 2) + tuple(grad_one))
    wait_one[0, "end"] = dact
    next(sum_one)
    wait_two[3, "end"] = dact
    next(sum_two)
    tokens_grad, sums_one = input_grad(x, vec, dact, dh, arrived(wait_one, 0) + arrived(wait_two, 3))
    wait_one[1, "end"] = tokens_grad
    next(sum_one)
    vector_grad = jnp.concatenate([sums_one[:2], sums[:3], sums_up[:4], sums[3:4]], axis=0)
    blocks = jnp.take(vector_grad.reshape(shards, share), inverse, axis=0, mode="clip")
    (blocks,) = tie((blocks,), arrived(wait_one, 1))
    if near:
        sum_vec = collect_vec(blocks)
    else:
        sum_vec = lax.psum_scatter(blocks.reshape(-1), AXES, scatter_dimension=0, tiled=True)
    sum_one, sum_two, sum_three = [list(z)[-1] for z in (sum_one, sum_two, sum_three)]
    upd_qkv = adamw(master_qkv, first_qkv, second_qkv, sum_one, RATE_MATRIX, DECAY_MATRIX)
    upd_out = adamw(master_out, first_out, second_out, sum_two[:, :D], RATE_MATRIX, DECAY_MATRIX)
    upd_up = adamw(master_up, first_up, second_up, sum_two[:, D:], RATE_MATRIX, DECAY_MATRIX)
    upd_down = adamw(master_down, first_down, second_down, sum_three, RATE_MATRIX, DECAY_MATRIX)
    upd_vec = adamw(master_vec, first_vec, second_vec, sum_vec, RATE_VECTOR, 0.0)
    return (
        (block_out[None], tokens_grad[None]) + upd_qkv + upd_out + upd_up + upd_down + upd_vec
    )


def solution(mesh):
    rows = P(AXES, None)
    flat = P(AXES)
    deep = P(AXES, None, None)
    stored = (rows,) * 4 + (flat,)
    in_specs = (deep,) * 2 + (rows,) * 3 + (P(),) + stored * 3
    out_specs = (deep,) * 2 + (rows,) * 12 + (flat,) * 3
    return jax.shard_map(local, mesh=mesh, in_specs=in_specs, out_specs=out_specs, check_vma=False)
```

```python
import functools

import jax
import jax.numpy as jnp
from jax import lax
from jax.experimental import pallas as pl
from jax.experimental.pallas import tpu as pltpu
from jax.sharding import PartitionSpec as P

D = 768
HEADS = 12
FF = 3072
STEP = 10
HALF = 384
WIN = 256
CUT_ONE = 1152
CUT_TWO = 1920
CUT_THREE = 384

EPSILON = 1e-05
BETA_ONE = 0.9
BETA_TWO = 0.999
ADAM_EPS = 1e-08
RATE_MATRIX = 0.05
DECAY_MATRIX = 0.05
RATE_VECTOR = 0.3

AXES = ("dp", "fsdp")
LOW = jnp.bfloat16
WIDE = jnp.float32
VMEM_BYTES = 12 * 2**20


def nn(left, right):
    return lax.dot_general(left, right, (((1,), (0,)), ((), ())), preferred_element_type=WIDE)


def nt(left, right):
    return lax.dot_general(left, right, (((1,), (1,)), ((), ())), preferred_element_type=WIDE)


def tn(left, right):
    return lax.dot_general(left, right, (((0,), (0,)), ((), ())), preferred_element_type=WIDE)


def shape(rows, cols, kind=LOW):
    return jax.ShapeDtypeStruct((rows, cols), kind)


def later(kernel, inputs, extra):
    return lambda *refs: kernel(*refs[:inputs], *refs[inputs + extra :])


def whole_call(kernel, outs, scratch, smem, name, flops, *args, anywhere=(), after=()):
    specs = []
    for i in range(len(args)):
        space = pltpu.SMEM if i < smem else pl.ANY if i in anywhere else pltpu.VMEM
        specs.append(pl.BlockSpec(memory_space=space))
    moved = sum(a.size * a.dtype.itemsize for a in args) + sum(o.size * o.dtype.itemsize for o in outs)
    return pl.pallas_call(
        later(kernel, len(args), len(after)),
        in_specs=specs + [pl.BlockSpec(memory_space=pl.ANY)] * len(after),
        out_specs=[pl.BlockSpec(memory_space=pltpu.VMEM)] * len(outs),
        out_shape=outs,
        scratch_shapes=scratch,
        compiler_params=pltpu.CompilerParams(vmem_limit_bytes=VMEM_BYTES),
        cost_estimate=pl.CostEstimate(flops=flops, bytes_accessed=moved, transcendentals=0),
        name=name,
    )(*args, *after)


def over_rows(count, step, body, init=None):
    return lax.fori_loop(0, count // step, lambda i, c: body(pl.ds(pl.multiple_of(i * step, step), step), c), init)


def normal(values):
    centre = values - jnp.mean(values, axis=-1, keepdims=True)
    rstd = lax.rsqrt(jnp.mean(centre * centre, axis=-1, keepdims=True) + EPSILON)
    return centre * rstd, rstd


def both(own, other, lo, width):
    return jnp.concatenate([own[:, lo : lo + width], other[:, lo : lo + width]], axis=0)


def qkv_kernel(x_ref, vec_ref, order_ref, ao, ax, bo, bx, a_ref, qkv_ref, tmp):
    gain, shift = vec_ref[0:1, :], vec_ref[1:2, :]

    def norm(rows, _):
        tmp[rows, :] = (normal(x_ref[rows, :].astype(WIDE))[0] * gain + shift).astype(LOW)

    over_rows(x_ref.shape[0], 64, norm)
    a_ref[...] = nn(tmp[...], order_ref[...]).astype(LOW)
    for col in range(0, 3 * D, 384):
        own, other, lo = (ao, ax, col) if col < CUT_ONE else (bo, bx, col - CUT_ONE)
        qkv_ref[:, col : col + 384] = nn(a_ref[...], both(own, other, lo, 384)).astype(LOW)


def project(x, vec, order, one, after=()):
    n = x.shape[0]
    return whole_call(
        qkv_kernel, [shape(n, D), shape(n, 3 * D)], [pltpu.VMEM((n, D), LOW)], 0, "project",
        2 * n * D * (4 * D), x, vec, order, *one, after=after,
    )


def attend_kernel(base, spans, slopes, q_ref, k_ref, v_ref, far_ref, o_ref, p_ref, acc):
    pair = pl.program_id(0) + base
    acc[...] = jnp.zeros_like(acc)
    lane = lax.broadcasted_iota(jnp.int32, (WIN, 128), 1)
    rows = lax.broadcasted_iota(jnp.int32, (WIN, 1), 0)
    for t in range(4):
        lo, hi = spans[t, 0], spans[t, 1]

        @pl.when(hi > lo)
        def _():
            at = pl.multiple_of(spans[t, 2], 16)
            win = pl.ds(at, WIN)
            q, k, v = q_ref[win, :], k_ref[win, :], v_ref[win, :]
            inside = ((rows + at >= lo) & (rows + at < hi)).astype(WIDE)
            far = far_ref[t]
            out = None
            for e in range(2):
                keep = (lane < 64) if e == 0 else (lane >= 64)
                s = nt(q, jnp.where(keep, k, jnp.zeros_like(k))) * 0.125 - slopes[2 * pair + e] * far
                p = jnp.exp(s - jnp.max(s, axis=1, keepdims=True))
                p = (p * (inside / jnp.sum(p, axis=1, keepdims=True))).astype(LOW)
                p_ref[e, t] = p
                part = nn(p, jnp.where(keep, v, jnp.zeros_like(v)))
                out = part if out is None else out + part
            acc[win, :] += out

    o_ref[...] = acc[...].astype(LOW)


def columns(n, offset):
    return pl.BlockSpec((n, 128), lambda h, *_: (0, h + offset))


def attend(base, qkv, far, spans, slopes, after=()):
    n = qkv.shape[0]
    return pl.pallas_call(
        later(functools.partial(attend_kernel, base), 6, len(after)),
        grid_spec=pltpu.PrefetchScalarGridSpec(
            num_scalar_prefetch=2,
            grid=(3,),
            in_specs=[columns(n, base), columns(n, base + 6), columns(n, base + 12),
                      pl.BlockSpec((4, WIN, WIN), lambda h, *_: (0, 0, 0))]
            + [pl.BlockSpec(memory_space=pl.ANY)] * len(after),
            out_specs=[columns(n, 0), pl.BlockSpec((2, 4, WIN, WIN), lambda h, *_: (h, 0, 0, 0))],
            scratch_shapes=[pltpu.VMEM((n, 128), WIDE)],
        ),
        out_shape=[shape(n, HALF), jax.ShapeDtypeStruct((HEADS // 2, 4, WIN, WIN), LOW)],
        compiler_params=pltpu.CompilerParams(vmem_limit_bytes=VMEM_BYTES),
        cost_estimate=pl.CostEstimate(flops=9 * 10**9, bytes_accessed=6 * 10**6, transcendentals=0),
        name="attend",
    )(spans, slopes, qkv, qkv, qkv, far, *after)


def attend_back_kernel(spans, q_ref, k_ref, v_ref, g_ref, p_ref, dq_ref, dk_ref, dv_ref, aq, ak, av):
    for acc in (aq, ak, av):
        acc[...] = jnp.zeros_like(acc)
    lane = lax.broadcasted_iota(jnp.int32, (WIN, 128), 1)
    for t in range(4):

        @pl.when(spans[t, 1] > spans[t, 0])
        def _():
            win = pl.ds(pl.multiple_of(spans[t, 2], 16), WIN)
            q, k, v, g = q_ref[win, :], k_ref[win, :], v_ref[win, :], g_ref[win, :]
            sums = None
            for e in range(2):
                keep = (lane < 64) if e == 0 else (lane >= 64)
                qe, ke, ge = [jnp.where(keep, z, jnp.zeros_like(z)) for z in (q, k, g)]
                p = p_ref[e, t]
                wide = p.astype(WIDE)
                d = wide * nt(ge, v)
                d = ((d - wide * jnp.sum(d, axis=1, keepdims=True)) * 0.125).astype(LOW)
                parts = (nn(d, ke), tn(d, qe), tn(p, ge))
                sums = parts if sums is None else tuple(a + b for a, b in zip(sums, parts))
            for acc, part in zip((aq, ak, av), sums):
                acc[win, :] += part

    for out, acc in zip((dq_ref, dk_ref, dv_ref), (aq, ak, av)):
        out[...] = acc[...].astype(LOW)


def attend_back(base, qkv, grad, probs, spans, after=()):
    n = qkv.shape[0]
    return pl.pallas_call(
        later(attend_back_kernel, 6, len(after)),
        grid_spec=pltpu.PrefetchScalarGridSpec(
            num_scalar_prefetch=1,
            grid=(3,),
            in_specs=[columns(n, base), columns(n, base + 6), columns(n, base + 12), columns(n, base),
                      pl.BlockSpec((2, 4, WIN, WIN), lambda h, *_: (h, 0, 0, 0))]
            + [pl.BlockSpec(memory_space=pl.ANY)] * len(after),
            out_specs=[columns(n, 0)] * 3,
            scratch_shapes=[pltpu.VMEM((n, 128), WIDE)] * 3,
        ),
        out_shape=[shape(n, HALF)] * 3,
        compiler_params=pltpu.CompilerParams(vmem_limit_bytes=VMEM_BYTES),
        cost_estimate=pl.CostEstimate(flops=12 * 10**9, bytes_accessed=6 * 10**6, transcendentals=0),
        name="attend_back",
    )(spans, qkv, qkv, qkv, grad, probs, *after)


def tables(seg, side, valid):
    n = seg.shape[0]
    ids = jnp.arange(n, dtype=jnp.int32)
    tiles = jnp.arange(4, dtype=jnp.int32)
    low = jnp.sum((seg[None, :] < tiles[:, None]).astype(jnp.int32), axis=1)
    high = jnp.sum((seg[None, :] <= tiles[:, None]).astype(jnp.int32), axis=1)
    at = jnp.minimum(low // 16 * 16, n - WIN)
    spans = jnp.stack([low, high, at], axis=1)
    place = ids - jnp.sum((seg[None, :] < seg[:, None]).astype(jnp.int32), axis=1)
    packed = jnp.stack([place // side, place % side, seg, valid, ids], axis=0)
    cut = jnp.stack([lax.dynamic_slice(packed, (0, at[t]), (5, WIN)) for t in range(4)], axis=0)
    row, col = cut[:, 0].astype(WIDE), cut[:, 1].astype(WIDE)
    row = row[:, :, None] - row[:, None, :]
    col = col[:, :, None] - col[:, None, :]
    mine = cut[:, 2] == tiles[:, None]
    allowed = mine[:, :, None] & mine[:, None, :] & (
        (cut[:, 3][:, None, :] == 1) | (cut[:, 4][:, :, None] == cut[:, 4][:, None, :])
    )
    return spans, jnp.where(allowed, jnp.sqrt(row * row + col * col), 1e12)


def bell(u):
    bell_value = jnp.exp(u * u * -0.5)
    size = jnp.abs(u)
    t = 1.0 / (1.0 + 0.23164189 * size)
    poly = 0.127414796 + t * (-0.142248368 + t * (0.7107068705 + t * (-0.7265760135 + t * 0.5307027145)))
    tail = poly * t * bell_value
    share = jnp.where(u >= 0, 1.0 - tail, tail)
    return u * share, share + u * bell_value * 0.3989422804014327


def up_kernel(x_ref, o0_ref, o1_ref, vec_ref, order_ref, ao, ax, bo, bx, mixed_ref, h_ref, a_ref, gl_ref, gp_ref, tmp):
    mixed_ref[...] = (
        nn(o0_ref[...], order_ref[:HALF, :]) + nn(o1_ref[...], order_ref[HALF:, :])
    ).astype(LOW)
    for col in (0, 384):
        part = slice(col, col + 384)
        h_ref[:, part] = x_ref[:, part].astype(WIDE) + nn(mixed_ref[...], both(ao, ax, col, 384)) + vec_ref[2:3, part]
    gain, shift = vec_ref[3:4, :], vec_ref[4:5, :]

    def norm(rows, _):
        tmp[rows, :] = (normal(h_ref[rows, :])[0] * gain + shift).astype(LOW)

    over_rows(x_ref.shape[0], 64, norm)
    a_ref[...] = nn(tmp[...], order_ref[...]).astype(LOW)
    for col in range(0, FF, 384):
        lo = col + D
        own, other, lo = (ao, ax, lo) if lo < CUT_TWO else (bo, bx, lo - CUT_TWO)
        k = 5 + col // D
        u = nn(a_ref[...], both(own, other, lo, 384)) + vec_ref[k : k + 1, col % D : col % D + 384]
        value, slope = bell(u)
        gl_ref[:, col : col + 384] = value.astype(LOW)
        gp_ref[:, col : col + 384] = slope.astype(LOW)


def upward(x, o, vec, order, two, after=()):
    n = x.shape[0]
    return whole_call(
        up_kernel, [shape(n, D), shape(n, D, WIDE), shape(n, D), shape(n, FF), shape(n, FF)],
        [pltpu.VMEM((n, D), LOW)], 0, "upward", 2 * n * D * (7 * D) * 2, x, *o, vec, order, *two,
        after=after,
    )


def down_kernel(place, vec_ref, gl_ref, gp_ref, dy_ref, h_ref, w0, w1, w2, w3, out_ref, dur_ref, vg_ref, wd, sem):
    def copies(b, left, right, row):
        src, dst = [pl.ds(pl.multiple_of(z * 96, 96), 96) for z in (row, b)]
        return (
            pltpu.make_async_copy(left.at[src, :], wd.at[dst, pl.ds(0, CUT_THREE)], sem),
            pltpu.make_async_copy(right.at[src, :], wd.at[dst, pl.ds(CUT_THREE, D - CUT_THREE)], sem),
        )

    def begin(b, carry):
        p = place[b]
        pl.when(p < 16)(lambda: [z.start() for z in copies(b, w0, w2, p)] and None)
        pl.when(p >= 16)(lambda: [z.start() for z in copies(b, w1, w3, p - 16)] and None)
        return carry

    def finish(b, carry):
        for z in copies(b, w0, w2, 0):
            z.wait()
        return carry

    lax.fori_loop(0, 32, begin, 0)
    lax.fori_loop(0, 32, finish, 0)
    for col in range(0, FF, 384):
        part = slice(col, col + 384)
        du = nt(dy_ref[...], wd[part, :]) * gp_ref[:, part].astype(WIDE)
        dur_ref[:, part] = du.astype(LOW)
        k = col // D
        vg_ref[k : k + 1, col % D : col % D + 384] = jnp.sum(du, axis=0, keepdims=True)
    for col in (0, 384):
        part = slice(col, col + 384)
        out_ref[:, part] = (h_ref[:, part] + nn(gl_ref[...], wd[:, part]) + vec_ref[9:10, part]).astype(LOW)


def downward(place, vec, gl, gp, dy, h, three, after=()):
    n = h.shape[0]
    return whole_call(
        down_kernel, [shape(n, D), shape(n, FF), shape(8, D, WIDE)],
        [pltpu.VMEM((FF, D), LOW), pltpu.SemaphoreType.DMA], 1, "downward",
        2 * n * D * (8 * D), place, vec, gl, gp, dy, h, *three, anywhere=(6, 7, 8, 9), after=after,
    )


def hidden_kernel(vec_ref, order_ref, dur_ref, dy_ref, h_ref, ao, ax, bo, bx, dh_ref, dhr_ref, dor_ref, vg_ref, tmp):
    split = CUT_TWO - D
    for i, (a, b) in enumerate(((ao, bo), (ax, bx))):
        tmp[:, HALF * i : HALF * (i + 1)] = (
            nt(dur_ref[:, :split], a[:, D:]) + nt(dur_ref[:, split:], b[...])
        ).astype(LOW)
    dh_ref[...] = nt(tmp[...], order_ref[...])
    gain = vec_ref[3:4, :]

    def step(rows, sums):
        e = dh_ref[rows, :]
        dy = dy_ref[rows, :].astype(WIDE)
        n, rstd = normal(h_ref[rows, :])
        w = e * gain
        dh = dy + rstd * (w - jnp.mean(w, axis=-1, keepdims=True) - n * jnp.mean(w * n, axis=-1, keepdims=True))
        dh_ref[rows, :] = dh
        dhr_ref[rows, :] = dh.astype(LOW)
        return tuple(s + jnp.sum(z.reshape(-1, 8, D), axis=0) for s, z in zip(sums, (dh, e * n, e, dy)))

    zero = jnp.zeros((8, D), WIDE)
    sums = over_rows(h_ref.shape[0], 32, step, (zero,) * 4)
    for k, s in enumerate(sums):
        vg_ref[k : k + 1, :] = jnp.sum(s, axis=0, keepdims=True)
    for i, a in enumerate((ao, ax)):
        tmp[:, HALF * i : HALF * (i + 1)] = nt(dhr_ref[...], a[:, :D]).astype(LOW)
    dor_ref[...] = nt(tmp[...], order_ref[...]).astype(LOW)


def hidden_grad(vec, order, dur, dy, h, two, after=()):
    n = h.shape[0]
    return whole_call(
        hidden_kernel, [shape(n, D, WIDE), shape(n, D), shape(n, D), shape(8, D, WIDE)],
        [pltpu.VMEM((n, D), LOW)], 0, "hidden_grad",
        2 * n * D * (7 * D), vec, order, dur, dy, h, *two, after=after,
    )


def down_grad_kernel(place, gl_ref, dy_ref, w0, w1, w2, w3):
    for c in range(8):
        t = tn(gl_ref[:, 384 * c : 384 * (c + 1)], dy_ref[...]).astype(LOW)
        for i in range(4):
            p = place[4 * c + i]

            def put(left, right, row):
                rows = pl.ds(pl.multiple_of(row * 96, 96), 96)
                left[rows, :] = t[96 * i : 96 * (i + 1), :CUT_THREE]
                right[rows, :] = t[96 * i : 96 * (i + 1), CUT_THREE:]

            pl.when(p < 16)(lambda: put(w0, w2, p))
            pl.when(p >= 16)(lambda: put(w1, w3, p - 16))


def down_grad(place, gl, dy, after=()):
    n = dy.shape[0]
    outs = [shape(FF // 2, CUT_THREE)] * 2 + [shape(FF // 2, D - CUT_THREE)] * 2
    return whole_call(down_grad_kernel, outs, [], 1, "down_grad", 2 * n * D * FF, place, gl, dy, after=after)


def two_grad_kernel(mixed_ref, a_ref, dhr_ref, dur_ref, ao, ax, bo, bx):
    for col in range(0, D + FF, 384):
        left, right = (mixed_ref, dhr_ref[:, col : col + 384]) if col < D else (a_ref, dur_ref[:, col - D : col - D + 384])
        t = tn(left[...], right).astype(LOW)
        own, other, lo = (ao, ax, col) if col < CUT_TWO else (bo, bx, col - CUT_TWO)
        own[:, lo : lo + 384] = t[:HALF]
        other[:, lo : lo + 384] = t[HALF:]


def two_grad(mixed, a, dhr, dur, after=()):
    n = a.shape[0]
    outs = [shape(HALF, CUT_TWO)] * 2 + [shape(HALF, D + FF - CUT_TWO)] * 2
    return whole_call(two_grad_kernel, outs, [], 0, "two_grad", 2 * n * D * (D + FF), mixed, a, dhr, dur,
                      after=after)


def one_grad_kernel(a_ref, *refs):
    halves, (ao, ax, bo, bx) = refs[:6], refs[6:]
    for i, half in enumerate(halves):
        t = tn(a_ref[...], half[...]).astype(LOW)
        col = 384 * i
        own, other, lo = (ao, ax, col) if col < CUT_ONE else (bo, bx, col - CUT_ONE)
        own[:, lo : lo + 384] = t[:HALF]
        other[:, lo : lo + 384] = t[HALF:]


def one_grad(a, d, after=()):
    n = a.shape[0]
    outs = [shape(HALF, CUT_ONE)] * 2 + [shape(HALF, 3 * D - CUT_ONE)] * 2
    return whole_call(one_grad_kernel, outs, [], 0, "one_grad", 2 * n * D * 3 * D, a, *d, after=after)


def input_back_kernel(order_ref, q0, q1, k0, k1, v0, v1, ao, ax, bo, bx, e_ref, tmp):
    for i, (a, b) in enumerate(((ao, bo), (ax, bx))):
        parts = ((q0, a, 0), (q1, a, 384), (k0, a, 768), (k1, b, 0), (v0, b, 384), (v1, b, 768))
        tmp[:, HALF * i : HALF * (i + 1)] = sum(nt(d[...], w[:, lo : lo + 384]) for d, w, lo in parts).astype(LOW)
    e_ref[...] = nt(tmp[...], order_ref[...])


def input_back(order, d, one, after=()):
    n = d[0].shape[0]
    return whole_call(
        input_back_kernel, [shape(n, D, WIDE)], [pltpu.VMEM((n, D), LOW)], 0, "input_back",
        2 * n * D * 4 * D, order, *d, *one, after=after,
    )[0]


def input_kernel(x_ref, vec_ref, e_ref, dh_ref, dx_ref, vg_ref):
    gain = vec_ref[0:1, :]

    def step(rows, sums):
        e = e_ref[rows, :]
        n, rstd = normal(x_ref[rows, :].astype(WIDE))
        w = e * gain
        dx_ref[rows, :] = dh_ref[rows, :] + rstd * (
            w - jnp.mean(w, axis=-1, keepdims=True) - n * jnp.mean(w * n, axis=-1, keepdims=True)
        )
        return tuple(s + jnp.sum(z.reshape(-1, 8, D), axis=0) for s, z in zip(sums, (e * n, e)))

    zero = jnp.zeros((8, D), WIDE)
    sums = over_rows(x_ref.shape[0], 32, step, (zero,) * 2)
    for k, s in enumerate(sums):
        vg_ref[k : k + 1, :] = jnp.sum(s, axis=0, keepdims=True)


def input_grad(x, vec, e, dh, after=()):
    n = x.shape[0]
    return whole_call(
        input_kernel, [shape(n, D, WIDE), shape(8, D, WIDE)], [], 0, "input_grad",
        2 * n * D * 3 * D, x, vec, e, dh, after=after,
    )


def swap(value, bits):
    pairs = [(i, i ^ bits) for i in range(32)]
    return lax.ppermute(value, AXES, pairs)


def tie(values, *first):
    return lax.optimization_barrier((tuple(values), first))[0]


def transfer(firsts, stage, values, *bits):
    values = tie(values, firsts.get((stage, "start"), ()))
    got = firsts[stage, "got"] = tuple(swap(value, bit) for value, bit in zip(values, bits))
    both = tie(tuple(values) + got, firsts.get((stage, "end"), ()))
    return both[: len(values)], both[len(values) :]


def spread(block, cut, firsts):
    move = functools.partial(transfer, firsts)
    (block, _, _), got = move(0, (block,) * 3, 8, 16, 24)
    near = jnp.concatenate((block,) + got, axis=0)
    yield (near,)
    rows = near.shape[0]
    mine, got = move(1, (near[:, :cut], near[:, cut:]), 2, 4)
    left, right = [jnp.concatenate(z, axis=0) for z in zip(mine, got)]
    yield left, right
    (left, right), (got, far) = move(2, (left, right), 4, 2)
    left = jnp.concatenate([left, got], axis=0)
    right = jnp.concatenate([right[:rows], far[:rows], right[rows:], far[rows:]], axis=0)
    yield left, right
    mine, got = move(3, (left, right), 1, 1)
    yield mine[0], got[0], mine[1], got[1]


def collect(pieces, firsts):
    move = functools.partial(transfer, firsts)
    _, got = move(0, (pieces[1], pieces[3]), 1, 1)
    yield
    left = pieces[0].astype(WIDE) + got[0].astype(WIDE)
    right = pieces[2].astype(WIDE) + got[1].astype(WIDE)
    half = left.shape[0] // 2
    rows = half // 2
    out = jnp.concatenate([right[rows:half], right[half + rows :]], axis=0).astype(LOW)
    _, got = move(1, (left[half:].astype(LOW), out), 4, 2)
    yield
    left = left[:half] + got[0].astype(WIDE)
    right = jnp.concatenate([right[:rows], right[half : half + rows]], axis=0) + got[1].astype(WIDE)
    _, got = move(2, (left[rows:].astype(LOW), right[rows:].astype(LOW)), 2, 4)
    yield
    both_sides = jnp.concatenate(
        [left[:rows] + got[0].astype(WIDE), right[:rows] + got[1].astype(WIDE)], axis=1
    )
    unit = rows // 4
    low = both_sides.astype(LOW)
    _, got = move(3, [low[unit * k : unit * (k + 1)] for k in (1, 2, 3)], 8, 16, 24)
    yield
    yield sum((z.astype(WIDE) for z in got), both_sides[:unit])


def collect_vec(blocks):
    for bits in (1, 4, 2):
        half = blocks.shape[0] // 2
        blocks = blocks[:half] + swap(blocks[half:], bits)
    return sum((swap(blocks[k : k + 1], 8 * k) for k in (1, 2, 3)), blocks[:1]).reshape(-1)


def cut_up(whole, cut):
    half = whole.shape[0] // 2
    return whole[:half, :cut], whole[half:, :cut], whole[:half, cut:], whole[half:, cut:]


def repeat(value, count):
    for _ in range(count):
        yield value


def spread_any(block, cut, firsts):
    return repeat(cut_up(lax.all_gather(block, AXES, axis=0, tiled=True), cut), 4)


def join(pieces):
    return jnp.concatenate(
        [jnp.concatenate(pieces[:2], axis=0), jnp.concatenate(pieces[2:], axis=0)], axis=1
    )


def collect_any(pieces, firsts):
    total = lax.psum_scatter(join(pieces), AXES, scatter_dimension=0, tiled=True).astype(WIDE)
    return repeat(total, 5)


def rearrange(whole, order, shards):
    return jnp.take(whole.reshape(shards, -1, whole.shape[1]), order, axis=0, mode="clip").reshape(whole.shape)


def adamw(master, moment_one, moment_two, gradient, step_rate, decay_rate):
    first_new = BETA_ONE * moment_one + (1.0 - BETA_ONE) * gradient
    second_new = BETA_TWO * moment_two + (1.0 - BETA_TWO) * gradient * gradient
    first_hat = first_new / (1.0 - BETA_ONE**STEP)
    second_hat = second_new / (1.0 - BETA_TWO**STEP)
    master_new = master - step_rate * (
        first_hat / (jnp.sqrt(second_hat) + ADAM_EPS) + decay_rate * master
    )
    return (first_new, second_new, master_new)


def local(
    tokens_in, cotangent, segments, tile_sides, valid_slots, owners,
    master_qkv, master_out, master_up, master_down, master_vec,
    first_qkv, first_out, first_up, first_down, first_vec,
    second_qkv, second_out, second_up, second_down, second_vec,
):
    shards = lax.axis_size(AXES)
    near = shards == 32
    unit = D // shards
    per_row = master_vec.shape[0] // unit
    share = master_vec.shape[0]
    ids = jnp.arange(shards, dtype=jnp.int32)
    if near:
        away = owners ^ lax.axis_index(AXES).astype(jnp.int32)
        place = (away >> 3) + 4 * ((away >> 1) & 1) + 8 * ((away >> 2) & 1) + 16 * (away & 1)
        place_down = place
    else:
        place = owners
        place_down = jnp.arange(32, dtype=jnp.int32)
    inverse = jnp.sum(ids[:, None] * (place[:, None] == ids[None, :]), axis=0)
    target = (place[:, None] * unit + jnp.arange(unit, dtype=jnp.int32)[None, :]).reshape(-1)
    order = (target[:, None] == jnp.arange(D, dtype=jnp.int32)[None, :]).astype(LOW)
    gather, scatter = (spread, collect) if near else (spread_any, collect_any)

    vec_block = jnp.pad(master_vec.reshape(unit, per_row), ((0, 0), (0, 128 - per_row)))
    wait_two, wait_three = {}, {}
    one = gather(jnp.concatenate([master_qkv, vec_block], axis=1).astype(LOW), CUT_ONE, {})
    two = gather(jnp.concatenate([master_out, master_up], axis=1).astype(LOW), CUT_TWO, wait_two)
    if near:
        three = spread(master_down.astype(LOW), CUT_THREE, wait_three)
    else:
        whole = lax.all_gather(master_down.astype(LOW), AXES, axis=0, tiled=True)
        three = repeat(cut_up(rearrange(whole, owners, shards), CUT_THREE), 4)
    next(one)
    wait_two[0, "start"] = next(one)
    next(one)
    one = next(one)
    next(two)

    vec_rows = jnp.concatenate([one[2][:, 3 * D - CUT_ONE :], one[3][:, 3 * D - CUT_ONE :]], axis=0)
    vec = nn(order, vec_rows)[:, :per_row].reshape(per_row, D)
    vec = jnp.pad(vec, ((0, 16 - per_row), (0, 0)))
    spans, far = tables(segments[0], tile_sides[0], valid_slots[0])
    slopes = jnp.exp2(-8.0 * (jnp.arange(HEADS, dtype=jnp.int32).astype(WIDE) + 1.0) / HEADS)
    x = tokens_in[0]
    dy = cotangent[0]
    act_one, qkv = project(x, vec, order, one)
    wait_two[1, "start"] = one
    wait_two[1, "end"] = qkv
    wait_three[0, "start"] = next(two)
    mixed_0, probs_0 = attend(0, qkv, far, spans, slopes)
    wait_two[2, "end"] = mixed_0
    wait_three[1, "start"] = next(two)
    wait_three[0, "end"] = mixed_0
    next(three)
    mixed_1, probs_1 = attend(3, qkv, far, spans, slopes, wait_three.get((0, "got"), ()) + (mixed_0,))
    wait_three[1, "end"] = mixed_1
    next(three)
    two = next(two)
    mixed, hidden, act_two, gelu, gelu_slope = upward(
        x, (mixed_0, mixed_1), vec, order, two, wait_three.get((1, "got"), ())
    )
    wait_three[2, "end"] = mixed
    next(three)
    grad_three = down_grad(place_down, gelu, dy, wait_three.get((2, "got"), ()))
    three = next(three)
    if not near:
        whole = join(grad_three)
        back = jnp.sum(ids[:, None] * (owners[:, None] == ids[None, :]), axis=0)
        grad_three = cut_up(rearrange(whole, back, shards), CUT_THREE)
    wait_two, wait_three, wait_one = {}, {}, {}

    def arrived(waits, stage):
        return waits.get((stage, "got"), ())

    sum_three = scatter(grad_three, wait_three)
    block_out, dur, sums_up = downward(place_down, vec, gelu, gelu_slope, dy, hidden, three)
    wait_three[0, "end"] = dur
    next(sum_three)
    dh, dh_low, dmixed, sums = hidden_grad(vec, order, dur, dy, hidden, two, arrived(wait_three, 0))
    wait_three[1, "end"] = dh_low
    next(sum_three)
    grad_two = two_grad(mixed, act_two, dh_low, dur, arrived(wait_three, 1))
    wait_three[2, "end"] = grad_two
    next(sum_three)
    sum_two = scatter(grad_two, wait_two)
    d0 = attend_back(0, qkv, dmixed, probs_0, spans, arrived(wait_three, 2) + tuple(grad_two))
    wait_three[3, "end"] = d0[0]
    next(sum_three)
    wait_two[0, "end"] = d0[0]
    next(sum_two)
    d1 = attend_back(3, qkv, dmixed, probs_1, spans, arrived(wait_three, 3) + arrived(wait_two, 0) + (d0[0],))
    wait_two[1, "end"] = d1[0]
    next(sum_two)
    d = [z for pair in zip(d0, d1) for z in pair]
    grad_one = one_grad(act_one, d, arrived(wait_two, 1))
    wait_two[2, "end"] = grad_one
    next(sum_two)
    sum_one = scatter(grad_one, wait_one)
    dact = input_back(order, d, one, arrived(wait_two, 2) + tuple(grad_one))
    wait_one[0, "end"] = dact
    next(sum_one)
    wait_two[3, "end"] = dact
    next(sum_two)
    tokens_grad, sums_one = input_grad(x, vec, dact, dh, arrived(wait_one, 0) + arrived(wait_two, 3))
    wait_one[1, "end"] = tokens_grad
    next(sum_one)
    vector_grad = jnp.concatenate([sums_one[:2], sums[:3], sums_up[:4], sums[3:4]], axis=0)
    blocks = jnp.take(vector_grad.reshape(shards, share), inverse, axis=0, mode="clip")
    (blocks,) = tie((blocks,), arrived(wait_one, 1))
    if near:
        sum_vec = collect_vec(blocks)
    else:
        sum_vec = lax.psum_scatter(blocks.reshape(-1), AXES, scatter_dimension=0, tiled=True)
    sum_one, sum_two, sum_three = [list(z)[-1] for z in (sum_one, sum_two, sum_three)]
    upd_qkv = adamw(master_qkv, first_qkv, second_qkv, sum_one, RATE_MATRIX, DECAY_MATRIX)
    upd_out = adamw(master_out, first_out, second_out, sum_two[:, :D], RATE_MATRIX, DECAY_MATRIX)
    upd_up = adamw(master_up, first_up, second_up, sum_two[:, D:], RATE_MATRIX, DECAY_MATRIX)
    upd_down = adamw(master_down, first_down, second_down, sum_three, RATE_MATRIX, DECAY_MATRIX)
    upd_vec = adamw(master_vec, first_vec, second_vec, sum_vec, RATE_VECTOR, 0.0)
    return (
        (block_out[None], tokens_grad[None]) + upd_qkv + upd_out + upd_up + upd_down + upd_vec
    )


def solution(mesh):
    rows = P(AXES, None)
    flat = P(AXES)
    deep = P(AXES, None, None)
    stored = (rows,) * 4 + (flat,)
    in_specs = (deep,) * 2 + (rows,) * 3 + (P(),) + stored * 3
    out_specs = (deep,) * 2 + (rows,) * 12 + (flat,) * 3
    return jax.shard_map(local, mesh=mesh, in_specs=in_specs, out_specs=out_specs, check_vma=False)
```

```python
import functools

import jax
import jax.numpy as jnp
from jax import lax
from jax.experimental import pallas as pl
from jax.experimental.pallas import tpu as pltpu
from jax.sharding import PartitionSpec as P

D = 768
HEADS = 12
FF = 3072
STEP = 10
HALF = 384
WIN = 256
SMALL = 160
LARGE = 240
LOG2E = 1.4426950408889634
CUT_ONE = 1152
WIDTH_ONE = 1280
WIDTH_TWO = 1920
WIDTH_THREE = 384

EPSILON = 1e-05
BETA_ONE = 0.9
BETA_TWO = 0.999
ADAM_EPS = 1e-08
RATE_MATRIX = 0.05
DECAY_MATRIX = 0.05
RATE_VECTOR = 0.3

AXES = ("dp", "fsdp")
LOW = jnp.bfloat16
WIDE = jnp.float32
VMEM_BYTES = 12 * 2**20


def nn(left, right):
    return lax.dot_general(left, right, (((1,), (0,)), ((), ())), preferred_element_type=WIDE)


def nt(left, right):
    return lax.dot_general(left, right, (((1,), (1,)), ((), ())), preferred_element_type=WIDE)


def tn(left, right):
    return lax.dot_general(left, right, (((0,), (0,)), ((), ())), preferred_element_type=WIDE)


def shape(rows, cols, kind=LOW):
    return jax.ShapeDtypeStruct((rows, cols), kind)


def later(kernel, inputs, extra):
    return lambda *refs: kernel(*refs[:inputs], *refs[inputs + extra :])


def whole_call(kernel, outs, scratch, smem, name, flops, *args, anywhere=(), after=()):
    specs = []
    for i in range(len(args)):
        space = pltpu.SMEM if i < smem else pl.ANY if i in anywhere else pltpu.VMEM
        specs.append(pl.BlockSpec(memory_space=space))
    moved = sum(a.size * a.dtype.itemsize for a in args) + sum(o.size * o.dtype.itemsize for o in outs)
    return pl.pallas_call(
        later(kernel, len(args), len(after)),
        in_specs=specs + [pl.BlockSpec(memory_space=pl.ANY)] * len(after),
        out_specs=[pl.BlockSpec(memory_space=pltpu.VMEM)] * len(outs),
        out_shape=outs,
        scratch_shapes=scratch,
        compiler_params=pltpu.CompilerParams(vmem_limit_bytes=VMEM_BYTES),
        cost_estimate=pl.CostEstimate(flops=flops, bytes_accessed=moved, transcendentals=0),
        name=name,
    )(*args, *after)


def over_rows(count, step, body, init=None):
    return lax.fori_loop(0, count // step, lambda i, c: body(pl.ds(pl.multiple_of(i * step, step), step), c), init)


def normal(values):
    centre = values - jnp.mean(values, axis=-1, keepdims=True)
    rstd = lax.rsqrt(jnp.mean(centre * centre, axis=-1, keepdims=True) + EPSILON)
    return centre * rstd, rstd


def both(pair, side, lo, width):
    rows = slice(HALF * side, HALF * (side + 1))
    return jnp.concatenate([z[rows, lo : lo + width] for z in pair], axis=0)


def qkv_kernel(x_ref, vec_ref, order_ref, own, other, a_ref, qkv_ref, tmp):
    gain, shift = vec_ref[0:1, :], vec_ref[1:2, :]

    def norm(rows, _):
        tmp[rows, :] = (normal(x_ref[rows, :].astype(WIDE))[0] * gain + shift).astype(LOW)

    over_rows(x_ref.shape[0], 144, norm)
    a_ref[...] = nn(tmp[...], order_ref[...]).astype(LOW)
    for col in range(0, 3 * D, 384):
        w = both((own, other), *divmod(col, CUT_ONE), 384)
        qkv_ref[:, col : col + 384] = nn(a_ref[...], w).astype(LOW)


def project(x, vec, order, one, after=()):
    n = x.shape[0]
    return whole_call(
        qkv_kernel, [shape(n, D), shape(n, 3 * D)], [pltpu.VMEM((n, D), LOW)], 0, "project",
        2 * n * D * (4 * D), x, vec, order, *one, after=after,
    )


def each_tile(spans, body):
    def step(t, carry):
        for kind, rows in ((1, SMALL), (2, LARGE)):

            @pl.when(spans[t, 4] == kind)
            def _():
                body(t, pl.multiple_of(spans[t, 2], 16), rows, pl.multiple_of(spans[t, 3], 16))

        return carry

    lax.fori_loop(0, 4, step, 0)


def padding_rows(spans, shape_):
    return lax.broadcasted_iota(jnp.int32, shape_, 0) >= spans[4, 0]


def own_half(values, e):
    lane = lax.broadcasted_iota(jnp.int32, values.shape, 1)
    return jnp.where((lane < 64) if e == 0 else (lane >= 64), values, jnp.zeros_like(values))


def attend_kernel(base, spans, slopes, qkv_ref, far_ref, o_ref, p_ref, acc):
    acc[...] = jnp.zeros_like(acc)

    def tile(t, at, count, key):
        rows, keys = pl.ds(at, count), pl.ds(key, WIN)
        row = lax.broadcasted_iota(jnp.int32, (count, 1), 0) + at
        inside = ((row >= spans[t, 0]) & (row < spans[t, 1])).astype(WIDE)
        far = far_ref[t, :count, :]
        for pair in range(3):
            col = (base + pair) * 128
            q, k, v = [qkv_ref[z, col + i * D : col + i * D + 128] for i, z in enumerate((rows, keys, keys))]
            out = None
            for e in range(2):
                s = nt(q, own_half(k, e)) * (0.125 * LOG2E) - slopes[2 * (base + pair) + e] * far
                p = jnp.exp2(s - jnp.max(s, axis=1, keepdims=True))
                p = (p * (inside / jnp.sum(p, axis=1, keepdims=True))).astype(LOW)
                p_ref[t, 2 * pair + e, :count, :] = p
                part = nn(p, own_half(v, e))
                out = part if out is None else out + part
            acc[rows, pair * 128 : pair * 128 + 128] += out

    each_tile(spans, tile)
    v = qkv_ref[:, base * 128 + 2 * D : base * 128 + 2 * D + HALF]
    o_ref[...] = jnp.where(padding_rows(spans, v.shape), v, acc[...].astype(LOW))


def attend(base, qkv, far, spans, slopes, after=()):
    n = qkv.shape[0]
    return whole_call(
        functools.partial(attend_kernel, base),
        [shape(n, HALF), jax.ShapeDtypeStruct((4, HEADS // 2, LARGE, WIN), LOW)],
        [pltpu.VMEM((n, HALF), WIDE)], 2, "attend", 9 * 10**9, spans, slopes, qkv, far, after=after,
    )


def attend_back_kernel(base, spans, qkv_ref, g_ref, p_ref, dq_ref, dk_ref, dv_ref, aq, ak, av):
    for acc in (aq, ak, av):
        acc[...] = jnp.zeros_like(acc)

    def tile(t, at, count, key):
        rows, keys = pl.ds(at, count), pl.ds(key, WIN)
        for pair in range(3):
            col = (base + pair) * 128
            q, k, v = [qkv_ref[z, col + i * D : col + i * D + 128] for i, z in enumerate((rows, keys, keys))]
            g = g_ref[rows, col : col + 128]
            sums = None
            for e in range(2):
                ge = own_half(g, e)
                p = p_ref[t, 2 * pair + e, :count, :]
                wide = p.astype(WIDE)
                d = wide * nt(ge * 0.125, v)
                d = (d - wide * jnp.sum(d, axis=1, keepdims=True)).astype(LOW)
                parts = (nn(d, own_half(k, e)), tn(d, own_half(q, e)), tn(p, ge))
                sums = parts if sums is None else tuple(a + b for a, b in zip(sums, parts))
            part = slice(pair * 128, pair * 128 + 128)
            aq[rows, part] += sums[0]
            ak[keys, part] += sums[1]
            av[keys, part] += sums[2]

    each_tile(spans, tile)
    dq_ref[...] = aq[...].astype(LOW)
    dk_ref[...] = ak[...].astype(LOW)
    g = g_ref[:, base * 128 : base * 128 + HALF]
    dv_ref[...] = jnp.where(padding_rows(spans, g.shape), g, av[...].astype(LOW))


def attend_back(base, qkv, grad, probs, spans, after=()):
    n = qkv.shape[0]
    return whole_call(
        functools.partial(attend_back_kernel, base), [shape(n, HALF)] * 3, [pltpu.VMEM((n, HALF), WIDE)] * 3, 1,
        "attend_back", 12 * 10**9, spans, qkv, grad, probs, after=after,
    )


def tables(seg, side, valid):
    n = seg.shape[0]
    tiles = jnp.arange(4, dtype=jnp.int32)
    low = jnp.sum((seg[None, :] < tiles[:, None]).astype(jnp.int32), axis=1)
    high = jnp.sum((seg[None, :] <= tiles[:, None]).astype(jnp.int32), axis=1)
    live = jnp.sum(valid)
    small = high - low <= SMALL - 16
    kind = jnp.where((high > low) & (low < live), jnp.where(small, 1, 2), 0)
    at = jnp.minimum(low // 16 * 16, jnp.where(small, n - SMALL, n - LARGE))
    key = jnp.minimum(low // 16 * 16, n - WIN)
    spans = jnp.stack([low, high, at, key, kind], axis=1)
    spans = jnp.concatenate([spans, jnp.broadcast_to(live, (1, 5))], axis=0)
    place = jnp.arange(n, dtype=jnp.int32) - jnp.sum((seg[None, :] < seg[:, None]).astype(jnp.int32), axis=1)
    packed = jnp.stack([place // side, place % side, seg], axis=0)
    packed = jnp.pad(packed, ((0, 0), (0, WIN)), constant_values=-1)
    row = jnp.stack([lax.dynamic_slice(packed, (0, at[t]), (3, LARGE)) for t in range(4)], axis=0)[:, :, :, None]
    col = jnp.stack([lax.dynamic_slice(packed, (0, key[t]), (3, WIN)) for t in range(4)], axis=0)[:, :, None, :]
    allowed = (row[:, 2] == tiles[:, None, None]) & (col[:, 2] == tiles[:, None, None])
    down, along = [(row[:, i] - col[:, i]).astype(WIDE) for i in (0, 1)]
    return spans, jnp.where(allowed, jnp.sqrt(down * down + along * along), 1e12)


def bell(u):
    share = 0.5 + 0.5 * lax.erf(u * 0.7071067811865476)
    return u * share, share + u * (jnp.exp2(u * u * -0.7213475204444817) * 0.3989422804014327)


def up_kernel(x_ref, o0_ref, o1_ref, vec_ref, order_ref, own, other, mixed_ref, h_ref, a_ref, gl_ref, gp_ref, tmp):
    mixed_ref[...] = (
        nn(o0_ref[...], order_ref[:HALF, :]) + nn(o1_ref[...], order_ref[HALF:, :])
    ).astype(LOW)
    for col in (0, 384):
        part = slice(col, col + 384)
        h_ref[:, part] = x_ref[:, part].astype(WIDE) + nn(mixed_ref[...], both((own, other), 0, col, 384)) + vec_ref[2:3, part]
    gain, shift = vec_ref[3:4, :], vec_ref[4:5, :]

    def norm(rows, _):
        tmp[rows, :] = (normal(h_ref[rows, :])[0] * gain + shift).astype(LOW)

    over_rows(x_ref.shape[0], 144, norm)
    a_ref[...] = nn(tmp[...], order_ref[...]).astype(LOW)
    for col in range(0, FF, 384):
        k = 5 + col // D
        u = nn(a_ref[...], both((own, other), *divmod(col + D, WIDTH_TWO), 384)) + vec_ref[k : k + 1, col % D : col % D + 384]
        value, slope = bell(u)
        gl_ref[:, col : col + 384] = value.astype(LOW)
        gp_ref[:, col : col + 384] = slope.astype(LOW)


def upward(x, o, vec, order, two, after=()):
    n = x.shape[0]
    return whole_call(
        up_kernel, [shape(n, D), shape(n, D, WIDE), shape(n, D), shape(n, FF), shape(n, FF)],
        [pltpu.VMEM((n, D), LOW)], 0, "upward", 2 * n * D * (7 * D) * 2, x, *o, vec, order, *two,
        after=after,
    )


def down_kernel(place, vec_ref, gl_ref, gp_ref, dy_ref, h_ref, own, other, out_ref, dur_ref, vg_ref, wd, sem):
    def copies(b, piece, row):
        dst = pl.ds(pl.multiple_of(b * 96, 96), 96)
        return [
            pltpu.make_async_copy(
                piece.at[pl.ds(pl.multiple_of(row * 96 + side * (FF // 2), 96), 96), :],
                wd.at[dst, pl.ds(side * WIDTH_THREE, WIDTH_THREE)],
                sem.at[b // 4],
            )
            for side in (0, 1)
        ]

    def begin(b, carry):
        p = place[b]
        pl.when(p < 16)(lambda: [z.start() for z in copies(b, own, p)] and None)
        pl.when(p >= 16)(lambda: [z.start() for z in copies(b, other, p - 16)] and None)
        return carry

    def finish(b, carry):
        for z in copies(b, own, 0):
            z.wait()
        return carry

    lax.fori_loop(0, 32, begin, 0)
    for col in range(0, FF, 384):
        part = slice(col, col + 384)
        lax.fori_loop(col // 96, col // 96 + 4, finish, 0)
        du = nt(dy_ref[...], wd[part, :]) * gp_ref[:, part].astype(WIDE)
        dur_ref[:, part] = du.astype(LOW)
        k = col // D
        vg_ref[k : k + 1, col % D : col % D + 384] = jnp.sum(du, axis=0, keepdims=True)
    for col in (0, 384):
        part = slice(col, col + 384)
        out_ref[:, part] = (h_ref[:, part] + nn(gl_ref[...], wd[:, part]) + vec_ref[9:10, part]).astype(LOW)


def downward(place, vec, gl, gp, dy, h, three, after=()):
    n = h.shape[0]
    return whole_call(
        down_kernel, [shape(n, D), shape(n, FF), shape(8, D, WIDE)],
        [pltpu.VMEM((FF, D), LOW), pltpu.SemaphoreType.DMA((8,))], 1, "downward",
        2 * n * D * (8 * D), place, vec, gl, gp, dy, h, *three, anywhere=(6, 7), after=after,
    )


def hidden_kernel(vec_ref, order_ref, dur_ref, dy_ref, h_ref, own, other, dh_ref, dhr_ref, dor_ref, vg_ref, tmp):
    split = WIDTH_TWO - D
    for i, w in enumerate((own, other)):
        tmp[:, HALF * i : HALF * (i + 1)] = (
            nt(dur_ref[:, :split], w[:HALF, D:]) + nt(dur_ref[:, split:], w[HALF:, :])
        ).astype(LOW)
    dh_ref[...] = nt(tmp[...], order_ref[...])
    gain = vec_ref[3:4, :]

    def step(rows, sums):
        e = dh_ref[rows, :]
        dy = dy_ref[rows, :].astype(WIDE)
        n, rstd = normal(h_ref[rows, :])
        w = e * gain
        dh = dy + rstd * (w - jnp.mean(w, axis=-1, keepdims=True) - n * jnp.mean(w * n, axis=-1, keepdims=True))
        dh_ref[rows, :] = dh
        dhr_ref[rows, :] = dh.astype(LOW)
        return tuple(s + jnp.sum(z.reshape(-1, 8, D), axis=0) for s, z in zip(sums, (dh, e * n, e, dy)))

    zero = jnp.zeros((8, D), WIDE)
    sums = over_rows(h_ref.shape[0], 144, step, (zero,) * 4)
    for k, s in enumerate(sums):
        vg_ref[k : k + 1, :] = jnp.sum(s, axis=0, keepdims=True)
    for i, w in enumerate((own, other)):
        tmp[:, HALF * i : HALF * (i + 1)] = nt(dhr_ref[...], w[:HALF, :D]).astype(LOW)
    dor_ref[...] = nt(tmp[...], order_ref[...]).astype(LOW)


def hidden_grad(vec, order, dur, dy, h, two, after=()):
    n = h.shape[0]
    return whole_call(
        hidden_kernel, [shape(n, D, WIDE), shape(n, D), shape(n, D), shape(8, D, WIDE)],
        [pltpu.VMEM((n, D), LOW)], 0, "hidden_grad",
        2 * n * D * (7 * D), vec, order, dur, dy, h, *two, after=after,
    )


def down_grad_kernel(place, gl_ref, dy_ref, own, other):
    for c in range(8):
        t = tn(gl_ref[:, 384 * c : 384 * (c + 1)], dy_ref[...]).astype(LOW)
        for i in range(4):
            p = place[4 * c + i]

            def put(piece, row):
                for side in (0, 1):
                    rows = pl.ds(pl.multiple_of(row * 96 + side * (FF // 2), 96), 96)
                    piece[rows, :] = t[96 * i : 96 * (i + 1), side * WIDTH_THREE : (side + 1) * WIDTH_THREE]

            pl.when(p < 16)(lambda: put(own, p))
            pl.when(p >= 16)(lambda: put(other, p - 16))


def down_grad(place, gl, dy, after=()):
    n = dy.shape[0]
    return whole_call(down_grad_kernel, [shape(FF, WIDTH_THREE)] * 2, [], 1, "down_grad", 2 * n * D * FF, place, gl, dy, after=after)


def two_grad_kernel(mixed_ref, a_ref, dhr_ref, dur_ref, own, other):
    for col in range(0, D + FF, 384):
        left, right = (mixed_ref, dhr_ref[:, col : col + 384]) if col < D else (a_ref, dur_ref[:, col - D : col - D + 384])
        t = tn(left[...], right).astype(LOW)
        side, lo = divmod(col, WIDTH_TWO)
        own[HALF * side : HALF * (side + 1), lo : lo + 384] = t[:HALF]
        other[HALF * side : HALF * (side + 1), lo : lo + 384] = t[HALF:]


def two_grad(mixed, a, dhr, dur, after=()):
    n = a.shape[0]
    return whole_call(two_grad_kernel, [shape(D, WIDTH_TWO)] * 2, [], 0, "two_grad", 2 * n * D * (D + FF), mixed, a, dhr, dur,
                      after=after)


def one_grad_kernel(a_ref, *refs):
    halves, (own, other) = refs[:6], refs[6:]
    for i, half in enumerate(halves):
        t = tn(a_ref[...], half[...]).astype(LOW)
        side, lo = divmod(384 * i, CUT_ONE)
        own[HALF * side : HALF * (side + 1), lo : lo + 384] = t[:HALF]
        other[HALF * side : HALF * (side + 1), lo : lo + 384] = t[HALF:]


def one_grad(a, d, after=()):
    n = a.shape[0]
    return whole_call(one_grad_kernel, [shape(D, CUT_ONE)] * 2, [], 0, "one_grad", 2 * n * D * 3 * D, a, *d, after=after)


def input_back_kernel(order_ref, q0, q1, k0, k1, v0, v1, own, other, e_ref, tmp):
    for i, w in enumerate((own, other)):
        total = 0.0
        for j, d in enumerate((q0, q1, k0, k1, v0, v1)):
            side, lo = divmod(384 * j, CUT_ONE)
            total = total + nt(d[...], w[HALF * side : HALF * (side + 1), lo : lo + 384])
        tmp[:, HALF * i : HALF * (i + 1)] = total.astype(LOW)
    e_ref[...] = nt(tmp[...], order_ref[...])


def input_back(order, d, one, after=()):
    n = d[0].shape[0]
    return whole_call(
        input_back_kernel, [shape(n, D, WIDE)], [pltpu.VMEM((n, D), LOW)], 0, "input_back",
        2 * n * D * 4 * D, order, *d, *one, after=after,
    )[0]


def input_kernel(x_ref, vec_ref, e_ref, dh_ref, dx_ref, vg_ref):
    gain = vec_ref[0:1, :]

    def step(rows, sums):
        e = e_ref[rows, :]
        n, rstd = normal(x_ref[rows, :].astype(WIDE))
        w = e * gain
        dx_ref[rows, :] = dh_ref[rows, :] + rstd * (
            w - jnp.mean(w, axis=-1, keepdims=True) - n * jnp.mean(w * n, axis=-1, keepdims=True)
        )
        return tuple(s + jnp.sum(z.reshape(-1, 8, D), axis=0) for s, z in zip(sums, (e * n, e)))

    zero = jnp.zeros((8, D), WIDE)
    sums = over_rows(x_ref.shape[0], 144, step, (zero,) * 2)
    for k, s in enumerate(sums):
        vg_ref[k : k + 1, :] = jnp.sum(s, axis=0, keepdims=True)


def input_grad(x, vec, e, dh, after=()):
    n = x.shape[0]
    return whole_call(
        input_kernel, [shape(n, D, WIDE), shape(8, D, WIDE)], [], 0, "input_grad",
        2 * n * D * 3 * D, x, vec, e, dh, after=after,
    )


def near_kernel(a, b, c, d, left_ref, right_ref):
    cut = left_ref.shape[1]
    for out, lo in ((left_ref, 0), (right_ref, cut)):
        out[...] = jnp.concatenate([z[:, lo : lo + cut].astype(WIDE) for z in (a, b, c, d)], axis=0).astype(LOW)


def near_pieces(pieces, after=()):
    rows, cols = pieces[0].shape
    return whole_call(near_kernel, [shape(4 * rows, cols // 2)] * 2, [], 0, "near", 1, *pieces, after=after)


def first_kernel(left, got_left, right, got_right, left_ref, right_ref):
    rows = left.shape[0]
    for out, mine, got in ((left_ref, left, got_left), (right_ref, right, got_right)):
        out[:rows, :] = mine[...]
        out[rows:, :] = got[...]


def first_pieces(left, right, got, after=()):
    rows, cols = left.shape
    return whole_call(
        first_kernel, [shape(2 * rows, cols)] * 2, [], 0, "first", 1, left, got[0], right, got[1], after=after
    )


def second_kernel(left, got, right, far, own_ref):
    rows = left.shape[0]
    half = rows // 2
    own_ref[:rows, :] = left[...]
    own_ref[rows : 2 * rows, :] = got[...]
    for i in (0, 1):
        own_ref[2 * rows + 2 * i * half : 2 * rows + (2 * i + 1) * half, :] = right[i * half : (i + 1) * half, :]
        own_ref[2 * rows + (2 * i + 1) * half : 2 * rows + (2 * i + 2) * half, :] = far[i * half : (i + 1) * half, :]


def second_pieces(left, right, got, after=()):
    rows, cols = left.shape
    return whole_call(
        second_kernel, [shape(4 * rows, cols)], [], 0, "second", 1, left, got[0], right, got[1], after=after
    )[0]


def core_sum_kernel(own, got, left_keep, right_keep, left_out, right_out):
    half = left_keep.shape[0]
    rows = half // 2

    def total(lo, count):
        return own[lo : lo + count, :].astype(WIDE) + got[lo : lo + count, :].astype(WIDE)

    left_keep[...] = total(0, half)
    left_out[...] = total(half, half).astype(LOW)
    for i in (0, 1):
        lo = 2 * half + 2 * i * rows
        right_keep[i * rows : (i + 1) * rows, :] = total(lo, rows)
        right_out[i * rows : (i + 1) * rows, :] = total(lo + rows, rows).astype(LOW)


def core_sum(own, got, after=()):
    rows, cols = own.shape[0] // 4, own.shape[1]
    return whole_call(
        core_sum_kernel, [shape(rows, cols, WIDE)] * 2 + [shape(rows, cols)] * 2, [], 0, "core_sum", 1, own, got,
        after=after,
    )


def half_sum_kernel(left, got_left, right, got_right, left_keep, right_keep, left_out, right_out):
    rows = left_keep.shape[0]
    for mine, got, keep, out in ((left, got_left, left_keep, left_out), (right, got_right, right_keep, right_out)):
        keep[...] = mine[:rows, :] + got[:rows, :].astype(WIDE)
        out[...] = (mine[rows:, :] + got[rows:, :].astype(WIDE)).astype(LOW)


def half_sum(left, right, got, after=()):
    rows, cols = left.shape[0] // 2, left.shape[1]
    return whole_call(
        half_sum_kernel, [shape(rows, cols, WIDE)] * 2 + [shape(rows, cols)] * 2, [], 0, "half_sum", 1,
        left, got[0], right, got[1], after=after,
    )


def last_sum_kernel(left, got_left, right, got_right, keep, *outs):
    unit, cut = keep.shape[0], left.shape[1]
    for lo, mine, got in ((0, left, got_left), (cut, right, got_right)):
        total = mine[...] + got[...].astype(WIDE)
        keep[:, lo : lo + cut] = total[:unit]
        for i, out in enumerate(outs):
            out[:, lo : lo + cut] = total[unit * (i + 1) : unit * (i + 2)].astype(LOW)


def last_sum(left, right, got, after=()):
    unit, cols = left.shape[0] // 4, 2 * left.shape[1]
    return whole_call(
        last_sum_kernel, [shape(unit, cols, WIDE)] + [shape(unit, cols)] * 3, [], 0, "last_sum", 1,
        left, got[0], right, got[1], after=after,
    )


def swap(value, bits):
    pairs = [(i, i ^ bits) for i in range(32)]
    return lax.ppermute(value, AXES, pairs)


def tie(values, *first):
    return lax.optimization_barrier((tuple(values), first))[0]


def transfer(firsts, stage, values, *bits):
    values = tie(values, firsts.get((stage, "start"), ()))
    got = firsts[stage, "got"] = tuple(swap(value, bit) for value, bit in zip(values, bits))
    return tie(got, firsts.get((stage, "end"), ()))


def spread(block, firsts):
    move = functools.partial(transfer, firsts)
    left, right = firsts[0, "ready"] = tuple(near_pieces((block,) + move(0, (block,) * 3, 8, 16, 24)))
    yield
    left, right = firsts[1, "ready"] = tuple(first_pieces(left, right, move(1, (left, right), 2, 4)))
    yield
    own = second_pieces(left, right, move(2, (left, right), 4, 2))
    firsts[2, "ready"] = (own,)
    yield
    (other,) = move(3, (own,), 1)
    yield own, other


def collect(pieces, firsts):
    move = functools.partial(transfer, firsts)
    (got,) = move(0, (pieces[1],), 1)
    left, right, *out = firsts[0, "ready"] = tuple(core_sum(pieces[0], got))
    yield
    left, right, *out = firsts[1, "ready"] = tuple(half_sum(left, right, move(1, out, 4, 2)))
    yield
    total, *out = firsts[2, "ready"] = tuple(last_sum(left, right, move(2, out, 2, 4)))
    yield
    got = move(3, out, 8, 16, 24)
    yield
    yield sum((z.astype(WIDE) for z in got), total)


def collect_vec(blocks, ends):
    half = blocks.shape[0] // 2
    (got,) = tie((swap(blocks[half:], 1),), ends[0])
    blocks = blocks[:half] + got
    rows = half // 4
    got = tie([swap(blocks[rows * k : rows * (k + 1)], 2 * k) for k in (1, 2, 3)], ends[1])
    blocks = sum(got, blocks[:rows])
    return sum((swap(blocks[k : k + 1], 8 * k) for k in (1, 2, 3)), blocks[:1]).reshape(-1)


def stack(whole):
    half, cut = whole.shape[0] // 2, whole.shape[1] // 2
    return tuple(jnp.concatenate([z[:, :cut], z[:, cut:]], axis=0) for z in (whole[:half], whole[half:]))


def unstack(pieces):
    half = pieces[0].shape[0] // 2
    return jnp.concatenate([jnp.concatenate([z[:half], z[half:]], axis=1) for z in pieces], axis=0)


def repeat(value, count):
    for _ in range(count):
        yield value


def spread_any(block, firsts):
    return repeat(stack(lax.all_gather(block, AXES, axis=0, tiled=True)), 4)


def collect_any(pieces, firsts):
    total = lax.psum_scatter(unstack(pieces), AXES, scatter_dimension=0, tiled=True).astype(WIDE)
    return repeat(total, 5)


def rearrange(whole, order, shards):
    return jnp.take(whole.reshape(shards, -1, whole.shape[1]), order, axis=0, mode="clip").reshape(whole.shape)


def adamw(master, moment_one, moment_two, gradient, step_rate, decay_rate):
    first_new = BETA_ONE * moment_one + (1.0 - BETA_ONE) * gradient
    second_new = BETA_TWO * moment_two + (1.0 - BETA_TWO) * gradient * gradient
    first_hat = first_new / (1.0 - BETA_ONE**STEP)
    second_hat = second_new / (1.0 - BETA_TWO**STEP)
    master_new = master - step_rate * (
        first_hat / (jnp.sqrt(second_hat) + ADAM_EPS) + decay_rate * master
    )
    return (first_new, second_new, master_new)


def local(
    tokens_in, cotangent, segments, tile_sides, valid_slots, owners,
    master_qkv, master_out, master_up, master_down, master_vec,
    first_qkv, first_out, first_up, first_down, first_vec,
    second_qkv, second_out, second_up, second_down, second_vec,
):
    shards = lax.axis_size(AXES)
    near = shards == 32
    unit = D // shards
    per_row = master_vec.shape[0] // unit
    share = master_vec.shape[0]
    ids = jnp.arange(shards, dtype=jnp.int32)
    if near:
        away = owners ^ lax.axis_index(AXES).astype(jnp.int32)
        place = (away >> 3) + 4 * ((away >> 1) & 1) + 8 * ((away >> 2) & 1) + 16 * (away & 1)
        place_down = place
    else:
        place = owners
        place_down = jnp.arange(32, dtype=jnp.int32)
    inverse = jnp.sum(ids[:, None] * (place[:, None] == ids[None, :]), axis=0)
    target = (place[:, None] * unit + jnp.arange(unit, dtype=jnp.int32)[None, :]).reshape(-1)
    order = (target[:, None] == jnp.arange(D, dtype=jnp.int32)[None, :]).astype(LOW)
    gather, scatter = (spread, collect) if near else (spread_any, collect_any)

    vec_block = jnp.pad(master_vec.reshape(unit, per_row), ((0, 0), (0, 128 - per_row)))
    block_one = jnp.concatenate(
        [master_qkv[:, :CUT_ONE], vec_block, master_qkv[:, CUT_ONE:], jnp.zeros_like(vec_block)], axis=1
    )
    wait_one, wait_two, wait_three = {}, {}, {}

    def arrived(waits, stage):
        return waits.get((stage, "got"), ())

    def ready(waits, stage):
        return waits.get((stage, "ready"), ())

    one = gather(block_one.astype(LOW), wait_one)
    two = gather(jnp.concatenate([master_out, master_up], axis=1).astype(LOW), wait_two)
    if near:
        three = spread(master_down.astype(LOW), wait_three)
    else:
        whole = lax.all_gather(master_down.astype(LOW), AXES, axis=0, tiled=True)
        three = repeat(stack(rearrange(whole, owners, shards)), 4)
    next(one)
    next(one)
    wait_two[0, "start"] = arrived(wait_one, 1)
    next(two)
    wait_one[2, "end"] = arrived(wait_two, 0)
    next(one)
    wait_two[1, "start"] = arrived(wait_one, 2)
    one = next(one)

    vec_rows = jnp.concatenate([z[:HALF, CUT_ONE:] for z in one], axis=0)
    vec = nn(order, vec_rows)[:, :per_row].reshape(per_row, D)
    vec = jnp.pad(vec, ((0, 16 - per_row), (0, 0)))
    spans, far = tables(segments[0], tile_sides[0], valid_slots[0])
    slopes = LOG2E * jnp.exp2(-8.0 * (jnp.arange(HEADS, dtype=jnp.int32).astype(WIDE) + 1.0) / HEADS)
    x = tokens_in[0]
    dy = cotangent[0]
    act_one, qkv = project(x, vec, order, one)
    wait_two[1, "end"] = qkv
    next(two)
    wait_three[0, "start"] = arrived(wait_two, 0)
    wait_three[0, "end"] = qkv
    next(three)
    mixed_0, probs_0 = attend(0, qkv, far, spans, slopes, ready(wait_two, 1) + ready(wait_three, 0))
    wait_two[2, "end"] = mixed_0
    next(two)
    wait_three[1, "start"] = arrived(wait_two, 2)
    mixed_1, probs_1 = attend(3, qkv, far, spans, slopes, ready(wait_two, 2) + (mixed_0,))
    wait_three[1, "end"] = mixed_1
    next(three)
    two = next(two)
    mixed, hidden, act_two, gelu, gelu_slope = upward(
        x, (mixed_0, mixed_1), vec, order, two, ready(wait_three, 1)
    )
    wait_three[2, "end"] = mixed
    next(three)
    grad_three = down_grad(place_down, gelu, dy, arrived(wait_three, 2))
    three = next(three)
    if not near:
        back = jnp.sum(ids[:, None] * (owners[:, None] == ids[None, :]), axis=0)
        grad_three = stack(rearrange(unstack(grad_three), back, shards))
    wait_one, wait_two, wait_three = {}, {}, {}
    sum_three = scatter(grad_three, wait_three)
    block_out, dur, sums_up = downward(place_down, vec, gelu, gelu_slope, dy, hidden, three)
    wait_three[0, "end"] = dur
    next(sum_three)
    dh, dh_low, dmixed, sums = hidden_grad(vec, order, dur, dy, hidden, two, ready(wait_three, 0))
    wait_three[1, "end"] = dh_low
    next(sum_three)
    grad_two = two_grad(mixed, act_two, dh_low, dur, ready(wait_three, 1))
    wait_three[2, "end"] = grad_two
    next(sum_three)
    sum_two = scatter(grad_two, wait_two)
    d0 = attend_back(0, qkv, dmixed, probs_0, spans, ready(wait_three, 2) + tuple(grad_two))
    wait_three[3, "end"] = d0[0]
    next(sum_three)
    wait_two[0, "end"] = d0[0]
    next(sum_two)
    d1 = attend_back(3, qkv, dmixed, probs_1, spans, arrived(wait_three, 3) + ready(wait_two, 0) + (d0[0],))
    d = [z for pair in zip(d0, d1) for z in pair]
    grad_one = one_grad(act_one, d)
    wait_two[1, "end"] = grad_one
    next(sum_two)
    sum_one = scatter(grad_one, wait_one)
    next(sum_one)
    dact = input_back(order, d, one, ready(wait_two, 1) + ready(wait_one, 0))
    wait_two[2, "end"] = dact
    next(sum_two)
    tokens_grad, sums_one = input_grad(x, vec, dact, dh, ready(wait_two, 2))
    wait_one[1, "end"] = tokens_grad
    next(sum_one)
    next(sum_one)
    wait_two[3, "end"] = ready(wait_one, 2)
    next(sum_two)
    next(sum_one)
    vector_grad = jnp.concatenate([sums_one[:2], sums[:3], sums_up[:4], sums[3:4]], axis=0)
    blocks = jnp.take(vector_grad.reshape(shards, share), inverse, axis=0, mode="clip")
    if near:
        sum_vec = collect_vec(blocks, (arrived(wait_one, 1), arrived(wait_one, 2)))
    else:
        sum_vec = lax.psum_scatter(blocks.reshape(-1), AXES, scatter_dimension=0, tiled=True)
    sum_one, sum_two, sum_three = [list(z)[-1] for z in (sum_one, sum_two, sum_three)]
    upd_qkv = adamw(master_qkv, first_qkv, second_qkv, sum_one, RATE_MATRIX, DECAY_MATRIX)
    upd_out = adamw(master_out, first_out, second_out, sum_two[:, :D], RATE_MATRIX, DECAY_MATRIX)
    upd_up = adamw(master_up, first_up, second_up, sum_two[:, D:], RATE_MATRIX, DECAY_MATRIX)
    upd_down = adamw(master_down, first_down, second_down, sum_three, RATE_MATRIX, DECAY_MATRIX)
    upd_vec = adamw(master_vec, first_vec, second_vec, sum_vec, RATE_VECTOR, 0.0)
    return (
        (block_out[None], tokens_grad[None]) + upd_qkv + upd_out + upd_up + upd_down + upd_vec
    )


def solution(mesh):
    rows = P(AXES, None)
    flat = P(AXES)
    deep = P(AXES, None, None)
    stored = (rows,) * 4 + (flat,)
    in_specs = (deep,) * 2 + (rows,) * 3 + (P(),) + stored * 3
    out_specs = (deep,) * 2 + (rows,) * 12 + (flat,) * 3
    return jax.shard_map(local, mesh=mesh, in_specs=in_specs, out_specs=out_specs, check_vma=False)
```

```python
import functools

import jax
import jax.numpy as jnp
from jax import lax
from jax.experimental import pallas as pl
from jax.experimental.pallas import tpu as pltpu
from jax.sharding import PartitionSpec as P

D = 768
HEADS = 12
FF = 3072
STEP = 10
HALF = 384
WIN = 256
SMALL = 160
LARGE = 240
LOG2E = 1.4426950408889634
CUT_ONE = 1152
WIDTH_ONE = 1280
WIDTH_TWO = 1920
WIDTH_THREE = 384

EPSILON = 1e-05
BETA_ONE = 0.9
BETA_TWO = 0.999
ADAM_EPS = 1e-08
RATE_MATRIX = 0.05
DECAY_MATRIX = 0.05
RATE_VECTOR = 0.3

AXES = ("dp", "fsdp")
LOW = jnp.bfloat16
WIDE = jnp.float32
VMEM_BYTES = 12 * 2**20


def nn(left, right):
    return lax.dot_general(left, right, (((1,), (0,)), ((), ())), preferred_element_type=WIDE)


def nt(left, right):
    return lax.dot_general(left, right, (((1,), (1,)), ((), ())), preferred_element_type=WIDE)


def tn(left, right):
    return lax.dot_general(left, right, (((0,), (0,)), ((), ())), preferred_element_type=WIDE)


def shape(rows, cols, kind=LOW):
    return jax.ShapeDtypeStruct((rows, cols), kind)


def later(kernel, inputs, extra):
    return lambda *refs: kernel(*refs[:inputs], *refs[inputs + extra :])


def whole_call(kernel, outs, scratch, smem, name, flops, *args, anywhere=(), after=()):
    specs = []
    for i in range(len(args)):
        space = pltpu.SMEM if i < smem else pl.ANY if i in anywhere else pltpu.VMEM
        specs.append(pl.BlockSpec(memory_space=space))
    moved = sum(a.size * a.dtype.itemsize for a in args) + sum(o.size * o.dtype.itemsize for o in outs)
    return pl.pallas_call(
        later(kernel, len(args), len(after)),
        in_specs=specs + [pl.BlockSpec(memory_space=pl.ANY)] * len(after),
        out_specs=[pl.BlockSpec(memory_space=pltpu.VMEM)] * len(outs),
        out_shape=outs,
        scratch_shapes=scratch,
        compiler_params=pltpu.CompilerParams(vmem_limit_bytes=VMEM_BYTES),
        cost_estimate=pl.CostEstimate(flops=flops, bytes_accessed=moved, transcendentals=0),
        name=name,
    )(*args, *after)


def over_rows(count, step, body, init=None):
    return lax.fori_loop(0, count // step, lambda i, c: body(pl.ds(pl.multiple_of(i * step, step), step), c), init)


def normal(values):
    centre = values - jnp.mean(values, axis=-1, keepdims=True)
    rstd = lax.rsqrt(jnp.mean(centre * centre, axis=-1, keepdims=True) + EPSILON)
    return centre * rstd, rstd


def both(pair, side, lo, width):
    rows = slice(HALF * side, HALF * (side + 1))
    return jnp.concatenate([z[rows, lo : lo + width] for z in pair], axis=0)


def qkv_kernel(x_ref, vec_ref, order_ref, own, other, a_ref, qkv_ref, tmp):
    gain, shift = vec_ref[0:1, :], vec_ref[1:2, :]

    def norm(rows, _):
        tmp[rows, :] = (normal(x_ref[rows, :].astype(WIDE))[0] * gain + shift).astype(LOW)

    over_rows(x_ref.shape[0], 144, norm)
    a_ref[...] = nn(tmp[...], order_ref[...]).astype(LOW)
    for col in range(0, 3 * D, 384):
        w = both((own, other), *divmod(col, CUT_ONE), 384)
        qkv_ref[:, col : col + 384] = nn(a_ref[...], w).astype(LOW)


def project(x, vec, order, one, after=()):
    n = x.shape[0]
    return whole_call(
        qkv_kernel, [shape(n, D), shape(n, 3 * D)], [pltpu.VMEM((n, D), LOW)], 0, "project",
        2 * n * D * (4 * D), x, vec, order, *one, after=after,
    )


def each_tile(spans, body):
    def step(t, carry):
        for kind, rows in ((1, SMALL), (2, LARGE)):

            @pl.when(spans[t, 4] == kind)
            def _():
                body(t, pl.multiple_of(spans[t, 2], 16), rows, pl.multiple_of(spans[t, 3], 16))

        return carry

    lax.fori_loop(0, 4, step, 0)


def padding_rows(spans, shape_):
    return lax.broadcasted_iota(jnp.int32, shape_, 0) >= spans[4, 0]


def own_half(values, e):
    lane = lax.broadcasted_iota(jnp.int32, values.shape, 1)
    return jnp.where((lane < 64) if e == 0 else (lane >= 64), values, jnp.zeros_like(values))


def attend_kernel(base, spans, slopes, qkv_ref, far_ref, o_ref, p_ref, acc):
    acc[...] = jnp.zeros_like(acc)

    def tile(t, at, count, key):
        rows, keys = pl.ds(at, count), pl.ds(key, WIN)
        row = lax.broadcasted_iota(jnp.int32, (count, 1), 0) + at
        inside = ((row >= spans[t, 0]) & (row < spans[t, 1])).astype(WIDE)
        far = far_ref[t, :count, :]
        for pair in range(3):
            col = (base + pair) * 128
            q, k, v = [qkv_ref[z, col + i * D : col + i * D + 128] for i, z in enumerate((rows, keys, keys))]
            out = None
            for e in range(2):
                s = nt(q, own_half(k, e)) * (0.125 * LOG2E) - slopes[2 * (base + pair) + e] * far
                p = jnp.exp2(s - jnp.max(s, axis=1, keepdims=True))
                p = (p * (inside / jnp.sum(p, axis=1, keepdims=True))).astype(LOW)
                p_ref[t, 2 * pair + e, :count, :] = p
                part = nn(p, own_half(v, e))
                out = part if out is None else out + part
            acc[rows, pair * 128 : pair * 128 + 128] += out

    each_tile(spans, tile)
    v = qkv_ref[:, base * 128 + 2 * D : base * 128 + 2 * D + HALF]
    o_ref[...] = jnp.where(padding_rows(spans, v.shape), v, acc[...].astype(LOW))


def attend(base, qkv, far, spans, slopes, after=()):
    n = qkv.shape[0]
    return whole_call(
        functools.partial(attend_kernel, base),
        [shape(n, HALF), jax.ShapeDtypeStruct((4, HEADS // 2, LARGE, WIN), LOW)],
        [pltpu.VMEM((n, HALF), WIDE)], 2, "attend", 9 * 10**9, spans, slopes, qkv, far, after=after,
    )


def attend_back_kernel(base, spans, qkv_ref, g_ref, p_ref, dq_ref, dk_ref, dv_ref, aq, ak, av):
    for acc in (aq, ak, av):
        acc[...] = jnp.zeros_like(acc)

    def tile(t, at, count, key):
        rows, keys = pl.ds(at, count), pl.ds(key, WIN)
        for pair in range(3):
            col = (base + pair) * 128
            q, k, v = [qkv_ref[z, col + i * D : col + i * D + 128] for i, z in enumerate((rows, keys, keys))]
            g = g_ref[rows, col : col + 128]
            sums = None
            for e in range(2):
                ge = own_half(g, e)
                p = p_ref[t, 2 * pair + e, :count, :]
                wide = p.astype(WIDE)
                d = wide * nt(ge * 0.125, v)
                d = (d - wide * jnp.sum(d, axis=1, keepdims=True)).astype(LOW)
                parts = (nn(d, own_half(k, e)), tn(d, own_half(q, e)), tn(p, ge))
                sums = parts if sums is None else tuple(a + b for a, b in zip(sums, parts))
            part = slice(pair * 128, pair * 128 + 128)
            aq[rows, part] += sums[0]
            ak[keys, part] += sums[1]
            av[keys, part] += sums[2]

    each_tile(spans, tile)
    dq_ref[...] = aq[...].astype(LOW)
    dk_ref[...] = ak[...].astype(LOW)
    g = g_ref[:, base * 128 : base * 128 + HALF]
    dv_ref[...] = jnp.where(padding_rows(spans, g.shape), g, av[...].astype(LOW))


def attend_back(base, qkv, grad, probs, spans, after=()):
    n = qkv.shape[0]
    return whole_call(
        functools.partial(attend_back_kernel, base), [shape(n, HALF)] * 3, [pltpu.VMEM((n, HALF), WIDE)] * 3, 1,
        "attend_back", 12 * 10**9, spans, qkv, grad, probs, after=after,
    )


def tables(seg, side, valid):
    n = seg.shape[0]
    tiles = jnp.arange(4, dtype=jnp.int32)
    low = jnp.sum((seg[None, :] < tiles[:, None]).astype(jnp.int32), axis=1)
    high = jnp.sum((seg[None, :] <= tiles[:, None]).astype(jnp.int32), axis=1)
    live = jnp.sum(valid)
    small = high - low <= SMALL - 16
    kind = jnp.where((high > low) & (low < live), jnp.where(small, 1, 2), 0)
    at = jnp.minimum(low // 16 * 16, jnp.where(small, n - SMALL, n - LARGE))
    key = jnp.minimum(low // 16 * 16, n - WIN)
    spans = jnp.stack([low, high, at, key, kind], axis=1)
    spans = jnp.concatenate([spans, jnp.broadcast_to(live, (1, 5))], axis=0)
    place = jnp.arange(n, dtype=jnp.int32) - jnp.sum((seg[None, :] < seg[:, None]).astype(jnp.int32), axis=1)
    packed = jnp.stack([place // side, place % side, seg], axis=0)
    packed = jnp.pad(packed, ((0, 0), (0, WIN)), constant_values=-1)
    row = jnp.stack([lax.dynamic_slice(packed, (0, at[t]), (3, LARGE)) for t in range(4)], axis=0)[:, :, :, None]
    col = jnp.stack([lax.dynamic_slice(packed, (0, key[t]), (3, WIN)) for t in range(4)], axis=0)[:, :, None, :]
    allowed = (row[:, 2] == tiles[:, None, None]) & (col[:, 2] == tiles[:, None, None])
    down, along = [(row[:, i] - col[:, i]).astype(WIDE) for i in (0, 1)]
    return spans, jnp.where(allowed, jnp.sqrt(down * down + along * along), 1e12)


def bell(u):
    share = 0.5 + 0.5 * lax.erf(u * 0.7071067811865476)
    return u * share, share + u * (jnp.exp2(u * u * -0.7213475204444817) * 0.3989422804014327)


def up_kernel(x_ref, o0_ref, o1_ref, vec_ref, order_ref, own, other, mixed_ref, h_ref, a_ref, gl_ref, gp_ref, tmp):
    mixed_ref[...] = (
        nn(o0_ref[...], order_ref[:HALF, :]) + nn(o1_ref[...], order_ref[HALF:, :])
    ).astype(LOW)
    for col in (0, 384):
        part = slice(col, col + 384)
        h_ref[:, part] = x_ref[:, part].astype(WIDE) + nn(mixed_ref[...], both((own, other), 0, col, 384)) + vec_ref[2:3, part]
    gain, shift = vec_ref[3:4, :], vec_ref[4:5, :]

    def norm(rows, _):
        tmp[rows, :] = (normal(h_ref[rows, :])[0] * gain + shift).astype(LOW)

    over_rows(x_ref.shape[0], 144, norm)
    a_ref[...] = nn(tmp[...], order_ref[...]).astype(LOW)
    for col in range(0, FF, 384):
        k = 5 + col // D
        u = nn(a_ref[...], both((own, other), *divmod(col + D, WIDTH_TWO), 384)) + vec_ref[k : k + 1, col % D : col % D + 384]
        value, slope = bell(u)
        gl_ref[:, col : col + 384] = value.astype(LOW)
        gp_ref[:, col : col + 384] = slope.astype(LOW)


def upward(x, o, vec, order, two, after=()):
    n = x.shape[0]
    return whole_call(
        up_kernel, [shape(n, D), shape(n, D, WIDE), shape(n, D), shape(n, FF), shape(n, FF)],
        [pltpu.VMEM((n, D), LOW)], 0, "upward", 2 * n * D * (7 * D) * 2, x, *o, vec, order, *two,
        after=after,
    )


def down_kernel(place, vec_ref, gl_ref, gp_ref, dy_ref, h_ref, own, other, out_ref, dur_ref, vg_ref, wd, sem):
    def copies(b, piece, row):
        dst = pl.ds(pl.multiple_of(b * 96, 96), 96)
        return [
            pltpu.make_async_copy(
                piece.at[pl.ds(pl.multiple_of(row * 96 + side * (FF // 2), 96), 96), :],
                wd.at[dst, pl.ds(side * WIDTH_THREE, WIDTH_THREE)],
                sem.at[b // 4],
            )
            for side in (0, 1)
        ]

    def begin(b, carry):
        p = place[b]
        pl.when(p < 16)(lambda: [z.start() for z in copies(b, own, p)] and None)
        pl.when(p >= 16)(lambda: [z.start() for z in copies(b, other, p - 16)] and None)
        return carry

    def finish(b, carry):
        for z in copies(b, own, 0):
            z.wait()
        return carry

    lax.fori_loop(0, 32, begin, 0)
    for col in range(0, FF, 384):
        part = slice(col, col + 384)
        lax.fori_loop(col // 96, col // 96 + 4, finish, 0)
        du = nt(dy_ref[...], wd[part, :]) * gp_ref[:, part].astype(WIDE)
        dur_ref[:, part] = du.astype(LOW)
        k = col // D
        vg_ref[k : k + 1, col % D : col % D + 384] = jnp.sum(du, axis=0, keepdims=True)
    for col in (0, 384):
        part = slice(col, col + 384)
        out_ref[:, part] = (h_ref[:, part] + nn(gl_ref[...], wd[:, part]) + vec_ref[9:10, part]).astype(LOW)


def downward(place, vec, gl, gp, dy, h, three, after=()):
    n = h.shape[0]
    return whole_call(
        down_kernel, [shape(n, D), shape(n, FF), shape(8, D, WIDE)],
        [pltpu.VMEM((FF, D), LOW), pltpu.SemaphoreType.DMA((8,))], 1, "downward",
        2 * n * D * (8 * D), place, vec, gl, gp, dy, h, *three, anywhere=(6, 7), after=after,
    )


def hidden_kernel(vec_ref, order_ref, dur_ref, dy_ref, h_ref, own, other, dh_ref, dhr_ref, dor_ref, vg_ref, tmp):
    split = WIDTH_TWO - D
    for i, w in enumerate((own, other)):
        tmp[:, HALF * i : HALF * (i + 1)] = (
            nt(dur_ref[:, :split], w[:HALF, D:]) + nt(dur_ref[:, split:], w[HALF:, :])
        ).astype(LOW)
    dh_ref[...] = nt(tmp[...], order_ref[...])
    gain = vec_ref[3:4, :]

    def step(rows, sums):
        e = dh_ref[rows, :]
        dy = dy_ref[rows, :].astype(WIDE)
        n, rstd = normal(h_ref[rows, :])
        w = e * gain
        dh = dy + rstd * (w - jnp.mean(w, axis=-1, keepdims=True) - n * jnp.mean(w * n, axis=-1, keepdims=True))
        dh_ref[rows, :] = dh
        dhr_ref[rows, :] = dh.astype(LOW)
        return tuple(s + jnp.sum(z.reshape(-1, 8, D), axis=0) for s, z in zip(sums, (dh, e * n, e, dy)))

    zero = jnp.zeros((8, D), WIDE)
    sums = over_rows(h_ref.shape[0], 144, step, (zero,) * 4)
    for k, s in enumerate(sums):
        vg_ref[k : k + 1, :] = jnp.sum(s, axis=0, keepdims=True)
    for i, w in enumerate((own, other)):
        tmp[:, HALF * i : HALF * (i + 1)] = nt(dhr_ref[...], w[:HALF, :D]).astype(LOW)
    dor_ref[...] = nt(tmp[...], order_ref[...]).astype(LOW)


def hidden_grad(vec, order, dur, dy, h, two, after=()):
    n = h.shape[0]
    return whole_call(
        hidden_kernel, [shape(n, D, WIDE), shape(n, D), shape(n, D), shape(8, D, WIDE)],
        [pltpu.VMEM((n, D), LOW)], 0, "hidden_grad",
        2 * n * D * (7 * D), vec, order, dur, dy, h, *two, after=after,
    )


def down_grad_kernel(place, gl_ref, dy_ref, own, other):
    for c in range(8):
        t = tn(gl_ref[:, 384 * c : 384 * (c + 1)], dy_ref[...]).astype(LOW)
        for i in range(4):
            p = place[4 * c + i]

            def put(piece, row):
                for side in (0, 1):
                    rows = pl.ds(pl.multiple_of(row * 96 + side * (FF // 2), 96), 96)
                    piece[rows, :] = t[96 * i : 96 * (i + 1), side * WIDTH_THREE : (side + 1) * WIDTH_THREE]

            pl.when(p < 16)(lambda: put(own, p))
            pl.when(p >= 16)(lambda: put(other, p - 16))


def down_grad(place, gl, dy, after=()):
    n = dy.shape[0]
    return whole_call(down_grad_kernel, [shape(FF, WIDTH_THREE)] * 2, [], 1, "down_grad", 2 * n * D * FF, place, gl, dy, after=after)


def two_grad_kernel(mixed_ref, a_ref, dhr_ref, dur_ref, own, other):
    for col in range(0, D + FF, 384):
        left, right = (mixed_ref, dhr_ref[:, col : col + 384]) if col < D else (a_ref, dur_ref[:, col - D : col - D + 384])
        t = tn(left[...], right).astype(LOW)
        side, lo = divmod(col, WIDTH_TWO)
        own[HALF * side : HALF * (side + 1), lo : lo + 384] = t[:HALF]
        other[HALF * side : HALF * (side + 1), lo : lo + 384] = t[HALF:]


def two_grad(mixed, a, dhr, dur, after=()):
    n = a.shape[0]
    return whole_call(two_grad_kernel, [shape(D, WIDTH_TWO)] * 2, [], 0, "two_grad", 2 * n * D * (D + FF), mixed, a, dhr, dur,
                      after=after)


def one_grad_kernel(a_ref, *refs):
    halves, (own, other) = refs[:6], refs[6:]
    for i, half in enumerate(halves):
        t = tn(a_ref[...], half[...]).astype(LOW)
        side, lo = divmod(384 * i, CUT_ONE)
        own[HALF * side : HALF * (side + 1), lo : lo + 384] = t[:HALF]
        other[HALF * side : HALF * (side + 1), lo : lo + 384] = t[HALF:]


def one_grad(a, d, after=()):
    n = a.shape[0]
    return whole_call(one_grad_kernel, [shape(D, CUT_ONE)] * 2, [], 0, "one_grad", 2 * n * D * 3 * D, a, *d, after=after)


def input_back_kernel(order_ref, q0, q1, k0, k1, v0, v1, own, other, e_ref, tmp):
    for i, w in enumerate((own, other)):
        total = 0.0
        for j, d in enumerate((q0, q1, k0, k1, v0, v1)):
            side, lo = divmod(384 * j, CUT_ONE)
            total = total + nt(d[...], w[HALF * side : HALF * (side + 1), lo : lo + 384])
        tmp[:, HALF * i : HALF * (i + 1)] = total.astype(LOW)
    e_ref[...] = nt(tmp[...], order_ref[...])


def input_back(order, d, one, after=()):
    n = d[0].shape[0]
    return whole_call(
        input_back_kernel, [shape(n, D, WIDE)], [pltpu.VMEM((n, D), LOW)], 0, "input_back",
        2 * n * D * 4 * D, order, *d, *one, after=after,
    )[0]


def input_kernel(x_ref, vec_ref, e_ref, dh_ref, dx_ref, vg_ref):
    gain = vec_ref[0:1, :]

    def step(rows, sums):
        e = e_ref[rows, :]
        n, rstd = normal(x_ref[rows, :].astype(WIDE))
        w = e * gain
        dx_ref[rows, :] = dh_ref[rows, :] + rstd * (
            w - jnp.mean(w, axis=-1, keepdims=True) - n * jnp.mean(w * n, axis=-1, keepdims=True)
        )
        return tuple(s + jnp.sum(z.reshape(-1, 8, D), axis=0) for s, z in zip(sums, (e * n, e)))

    zero = jnp.zeros((8, D), WIDE)
    sums = over_rows(x_ref.shape[0], 144, step, (zero,) * 2)
    for k, s in enumerate(sums):
        vg_ref[k : k + 1, :] = jnp.sum(s, axis=0, keepdims=True)


def input_grad(x, vec, e, dh, after=()):
    n = x.shape[0]
    return whole_call(
        input_kernel, [shape(n, D, WIDE), shape(8, D, WIDE)], [], 0, "input_grad",
        2 * n * D * 3 * D, x, vec, e, dh, after=after,
    )


def near_kernel(a, b, c, d, left_ref, right_ref):
    cut = left_ref.shape[1]
    for out, lo in ((left_ref, 0), (right_ref, cut)):
        out[...] = jnp.concatenate([z[:, lo : lo + cut].astype(WIDE) for z in (a, b, c, d)], axis=0).astype(LOW)


def near_pieces(pieces, after=()):
    rows, cols = pieces[0].shape
    return whole_call(near_kernel, [shape(4 * rows, cols // 2)] * 2, [], 0, "near", 1, *pieces, after=after)


def first_kernel(left, got_left, right, got_right, left_ref, right_ref):
    rows = left.shape[0]
    for out, mine, got in ((left_ref, left, got_left), (right_ref, right, got_right)):
        out[:rows, :] = mine[...]
        out[rows:, :] = got[...]


def first_pieces(left, right, got, after=()):
    rows, cols = left.shape
    return whole_call(
        first_kernel, [shape(2 * rows, cols)] * 2, [], 0, "first", 1, left, got[0], right, got[1], after=after
    )


def second_kernel(left, got, right, far, own_ref):
    rows = left.shape[0]
    half = rows // 2
    own_ref[:rows, :] = left[...]
    own_ref[rows : 2 * rows, :] = got[...]
    for i in (0, 1):
        own_ref[2 * rows + 2 * i * half : 2 * rows + (2 * i + 1) * half, :] = right[i * half : (i + 1) * half, :]
        own_ref[2 * rows + (2 * i + 1) * half : 2 * rows + (2 * i + 2) * half, :] = far[i * half : (i + 1) * half, :]


def second_pieces(left, right, got, after=()):
    rows, cols = left.shape
    return whole_call(
        second_kernel, [shape(4 * rows, cols)], [], 0, "second", 1, left, got[0], right, got[1], after=after
    )[0]


def core_sum_kernel(own, got, left_keep, right_keep, left_out, right_out):
    half = left_keep.shape[0]
    rows = half // 2

    def total(lo, count):
        return own[lo : lo + count, :].astype(WIDE) + got[lo : lo + count, :].astype(WIDE)

    left_keep[...] = total(0, half)
    left_out[...] = total(half, half).astype(LOW)
    for i in (0, 1):
        lo = 2 * half + 2 * i * rows
        right_keep[i * rows : (i + 1) * rows, :] = total(lo, rows)
        right_out[i * rows : (i + 1) * rows, :] = total(lo + rows, rows).astype(LOW)


def core_sum(own, got, after=()):
    rows, cols = own.shape[0] // 4, own.shape[1]
    return whole_call(
        core_sum_kernel, [shape(rows, cols, WIDE)] * 2 + [shape(rows, cols)] * 2, [], 0, "core_sum", 1, own, got,
        after=after,
    )


def half_sum_kernel(left, got_left, right, got_right, left_keep, right_keep, left_out, right_out):
    rows = left_keep.shape[0]
    for mine, got, keep, out in ((left, got_left, left_keep, left_out), (right, got_right, right_keep, right_out)):
        keep[...] = mine[:rows, :] + got[:rows, :].astype(WIDE)
        out[...] = (mine[rows:, :] + got[rows:, :].astype(WIDE)).astype(LOW)


def half_sum(left, right, got, after=()):
    rows, cols = left.shape[0] // 2, left.shape[1]
    return whole_call(
        half_sum_kernel, [shape(rows, cols, WIDE)] * 2 + [shape(rows, cols)] * 2, [], 0, "half_sum", 1,
        left, got[0], right, got[1], after=after,
    )


def last_sum_kernel(left, got_left, right, got_right, keep, *outs):
    unit, cut = keep.shape[0], left.shape[1]
    for lo, mine, got in ((0, left, got_left), (cut, right, got_right)):
        total = mine[...] + got[...].astype(WIDE)
        keep[:, lo : lo + cut] = total[:unit]
        for i, out in enumerate(outs):
            out[:, lo : lo + cut] = total[unit * (i + 1) : unit * (i + 2)].astype(LOW)


def last_sum(left, right, got, after=()):
    unit, cols = left.shape[0] // 4, 2 * left.shape[1]
    return whole_call(
        last_sum_kernel, [shape(unit, cols, WIDE)] + [shape(unit, cols)] * 3, [], 0, "last_sum", 1,
        left, got[0], right, got[1], after=after,
    )


def swap(value, bits):
    pairs = [(i, i ^ bits) for i in range(32)]
    return lax.ppermute(value, AXES, pairs)


def tie(values, *first):
    return lax.optimization_barrier((tuple(values), first))[0]


class Flow:
    def __init__(self, steps):
        self.steps = steps
        self.next = next(steps)[:2]

    def issue(self, start=()):
        values, bits = self.next
        values = tie(values, start)
        self.got = tuple(swap(value, bit) for value, bit in zip(values, bits))
        return self.got

    def land(self, end=()):
        values, *bits = self.steps.send(tie(self.got, end))
        if values is None:
            return bits[0]
        self.next = (values, bits[0])
        return bits[1]


def spread(block):
    got = yield (block,) * 3, (8, 16, 24)
    left, right = near_pieces((block,) + got)
    got = yield (left, right), (2, 4), (left, right)
    left, right = first_pieces(left, right, got)
    got = yield (left, right), (4, 2), (left, right)
    own = second_pieces(left, right, got)
    got = yield (own,), (1,), (own,)
    yield None, (own, got[0])


def collect(pieces):
    (got,) = yield (pieces[1],), (1,)
    left, right, *out = ready = core_sum(pieces[0], got)
    got = yield out, (4, 2), tuple(ready)
    left, right, *out = ready = half_sum(left, right, got)
    got = yield out, (2, 4), tuple(ready)
    total, *out = ready = last_sum(left, right, got)
    got = yield out, (8, 16, 24), tuple(ready)
    yield None, (sum((z.astype(WIDE) for z in got), total),)


def collect_vec(blocks):
    half = blocks.shape[0] // 2
    (got,) = yield (blocks[half:],), (1,)
    blocks = blocks[:half] + got
    rows = half // 4
    got = yield [blocks[rows * k : rows * (k + 1)] for k in (1, 2, 3)], (2, 4, 6), (blocks,)
    blocks = sum(got, blocks[:rows])
    got = yield [blocks[k : k + 1] for k in (1, 2, 3)], (8, 16, 24), (blocks,)
    yield None, (sum(got, blocks[:1]).reshape(-1),)


def stack(whole):
    half, cut = whole.shape[0] // 2, whole.shape[1] // 2
    return tuple(jnp.concatenate([z[:, :cut], z[:, cut:]], axis=0) for z in (whole[:half], whole[half:]))


def unstack(pieces):
    half = pieces[0].shape[0] // 2
    return jnp.concatenate([jnp.concatenate([z[:half], z[half:]], axis=1) for z in pieces], axis=0)


class Whole:
    def __init__(self, result):
        self.result = result

    def issue(self, start=()):
        return ()

    def land(self, end=()):
        return self.result


def spread_any(block):
    return stack(lax.all_gather(block, AXES, axis=0, tiled=True))


def collect_any(pieces):
    return (lax.psum_scatter(unstack(pieces), AXES, scatter_dimension=0, tiled=True).astype(WIDE),)


def rearrange(whole, order, shards):
    return jnp.take(whole.reshape(shards, -1, whole.shape[1]), order, axis=0, mode="clip").reshape(whole.shape)


def adamw(master, moment_one, moment_two, gradient, step_rate, decay_rate):
    first_new = BETA_ONE * moment_one + (1.0 - BETA_ONE) * gradient
    second_new = BETA_TWO * moment_two + (1.0 - BETA_TWO) * gradient * gradient
    first_hat = first_new / (1.0 - BETA_ONE**STEP)
    second_hat = second_new / (1.0 - BETA_TWO**STEP)
    master_new = master - step_rate * (
        first_hat / (jnp.sqrt(second_hat) + ADAM_EPS) + decay_rate * master
    )
    return (first_new, second_new, master_new)


def local(
    tokens_in, cotangent, segments, tile_sides, valid_slots, owners,
    master_qkv, master_out, master_up, master_down, master_vec,
    first_qkv, first_out, first_up, first_down, first_vec,
    second_qkv, second_out, second_up, second_down, second_vec,
):
    shards = lax.axis_size(AXES)
    near = shards == 32
    unit = D // shards
    per_row = master_vec.shape[0] // unit
    share = master_vec.shape[0]
    ids = jnp.arange(shards, dtype=jnp.int32)
    if near:
        away = owners ^ lax.axis_index(AXES).astype(jnp.int32)
        place = (away >> 3) + 4 * ((away >> 1) & 1) + 8 * ((away >> 2) & 1) + 16 * (away & 1)
        place_down = place
    else:
        place = owners
        place_down = jnp.arange(32, dtype=jnp.int32)
    inverse = jnp.sum(ids[:, None] * (place[:, None] == ids[None, :]), axis=0)
    target = (place[:, None] * unit + jnp.arange(unit, dtype=jnp.int32)[None, :]).reshape(-1)
    order = (target[:, None] == jnp.arange(D, dtype=jnp.int32)[None, :]).astype(LOW)

    def gather(block):
        return Flow(spread(block)) if near else Whole(spread_any(block))

    def scatter(pieces):
        return Flow(collect(pieces)) if near else Whole(collect_any(pieces))

    vec_block = jnp.pad(master_vec.reshape(unit, per_row), ((0, 0), (0, 128 - per_row)))
    block_one = jnp.concatenate(
        [master_qkv[:, :CUT_ONE], vec_block, master_qkv[:, CUT_ONE:], jnp.zeros_like(vec_block)], axis=1
    )
    spans, far = tables(segments[0], tile_sides[0], valid_slots[0])
    slopes = LOG2E * jnp.exp2(-8.0 * (jnp.arange(HEADS, dtype=jnp.int32).astype(WIDE) + 1.0) / HEADS)
    one = gather(block_one.astype(LOW))
    two = gather(jnp.concatenate([master_out, master_up], axis=1).astype(LOW))
    if near:
        three = gather(master_down.astype(LOW))
    else:
        whole = lax.all_gather(master_down.astype(LOW), AXES, axis=0, tiled=True)
        three = Whole(stack(rearrange(whole, owners, shards)))
    one.issue()
    done = one.land((far, spans, slopes, order))
    one.issue(done)
    done = one.land()
    sent = one.issue(done) + two.issue(done)
    done = one.land(sent) + two.land(sent)
    one.issue(done)
    sent = two.issue(done) + three.issue(done)
    one = one.land()

    vec_rows = jnp.concatenate([z[:HALF, CUT_ONE:] for z in one], axis=0)
    vec = nn(order, vec_rows)[:, :per_row].reshape(per_row, D)
    vec = jnp.pad(vec, ((0, 16 - per_row), (0, 0)))
    x = tokens_in[0]
    dy = cotangent[0]
    act_one, qkv = project(x, vec, order, one)
    done = two.land((qkv,) + sent) + three.land((qkv,) + sent)
    two.issue(done)
    mixed_0, probs_0 = attend(0, qkv, far, spans, slopes, done)
    done = two.land((mixed_0,))
    sent = two.issue(done) + three.issue(done)
    mixed_1, probs_1 = attend(3, qkv, far, spans, slopes, done + (mixed_0,))
    done = three.land((mixed_1,) + sent)
    two = two.land((mixed_1,) + sent)
    three.issue(done + two[1:])
    mixed, hidden, act_two, gelu, gelu_slope = upward(x, (mixed_0, mixed_1), vec, order, two, done)
    grad_three = down_grad(place_down, gelu, dy)
    done = three.land(tuple(grad_three))
    three.issue(done)
    three = three.land()
    if not near:
        back = jnp.sum(ids[:, None] * (owners[:, None] == ids[None, :]), axis=0)
        grad_three = stack(rearrange(unstack(grad_three), back, shards))
    flow_three = scatter(grad_three)
    flow_three.issue((three[1],))
    block_out, dur, sums_up = downward(place_down, vec, gelu, gelu_slope, dy, hidden, three)
    done = flow_three.land((dur,))
    flow_three.issue(done)
    dh, dh_low, dmixed, sums = hidden_grad(vec, order, dur, dy, hidden, two, done)
    grad_two = two_grad(mixed, act_two, dh_low, dur)
    done = flow_three.land(tuple(grad_two)) + tuple(grad_two)
    flow_two = scatter(grad_two)
    sent = flow_three.issue(done) + flow_two.issue(done)
    d0 = attend_back(0, qkv, dmixed, probs_0, spans, done)
    done = flow_three.land(tuple(d0) + sent) + flow_two.land(tuple(d0) + sent)
    sent = flow_three.issue(done) + flow_two.issue(done)
    d1 = attend_back(3, qkv, dmixed, probs_1, spans, done + tuple(d0))
    d = [z for pair in zip(d0, d1) for z in pair]
    grad_one = one_grad(act_one, d)
    dact = input_back(order, d, one, tuple(grad_one))
    done = (dact,) + tuple(grad_one) + sent
    sum_three, = flow_three.land(done)
    done = flow_two.land(done)
    flow_one = scatter(grad_one)
    sent = flow_one.issue(done) + flow_two.issue(done)
    tokens_grad, sums_one = input_grad(x, vec, dact, dh, done)
    vector_grad = jnp.concatenate([sums_one[:2], sums[:3], sums_up[:4], sums[3:4]], axis=0)
    blocks = jnp.take(vector_grad.reshape(shards, share), inverse, axis=0, mode="clip")
    if near:
        flow_vec = Flow(collect_vec(blocks))
    else:
        flow_vec = Whole((lax.psum_scatter(blocks.reshape(-1), AXES, scatter_dimension=0, tiled=True),))
    done = flow_one.land((blocks,) + sent) + flow_two.land((blocks,) + sent)
    sent = flow_one.issue(done) + flow_two.issue(done) + flow_vec.issue(done)
    upd_down = adamw(master_down, first_down, second_down, sum_three, RATE_MATRIX, DECAY_MATRIX)
    sent = sent + upd_down
    done = flow_one.land(sent) + flow_vec.land(sent)
    sum_two, = flow_two.land(sent)
    sent = flow_one.issue(done) + flow_vec.issue(done)
    done = flow_one.land(sent) + flow_vec.land(sent)
    sent = flow_one.issue(done) + flow_vec.issue(done)
    upd_out = adamw(master_out, first_out, second_out, sum_two[:, :D], RATE_MATRIX, DECAY_MATRIX)
    upd_up = adamw(master_up, first_up, second_up, sum_two[:, D:], RATE_MATRIX, DECAY_MATRIX)
    sum_one, = flow_one.land(sent + upd_out + upd_up)
    sum_vec, = flow_vec.land(sent + upd_out + upd_up)
    upd_qkv = adamw(master_qkv, first_qkv, second_qkv, sum_one, RATE_MATRIX, DECAY_MATRIX)
    upd_vec = adamw(master_vec, first_vec, second_vec, sum_vec, RATE_VECTOR, 0.0)
    return (
        (block_out[None], tokens_grad[None]) + upd_qkv + upd_out + upd_up + upd_down + upd_vec
    )


def solution(mesh):
    rows = P(AXES, None)
    flat = P(AXES)
    deep = P(AXES, None, None)
    stored = (rows,) * 4 + (flat,)
    in_specs = (deep,) * 2 + (rows,) * 3 + (P(),) + stored * 3
    out_specs = (deep,) * 2 + (rows,) * 12 + (flat,) * 3
    return jax.shard_map(local, mesh=mesh, in_specs=in_specs, out_specs=out_specs, check_vma=False)
```

```python
import functools

import jax
import jax.numpy as jnp
from jax import lax
from jax.experimental import pallas as pl
from jax.experimental.pallas import tpu as pltpu
from jax.sharding import PartitionSpec as P

D = 768
HEADS = 12
FF = 3072
STEP = 10
HALF = 384
WIN = 256
SMALL = 160
LARGE = 240
LOG2E = 1.4426950408889634
CUT_ONE = 1152
WIDTH_ONE = 1280
WIDTH_TWO = 1920
WIDTH_THREE = 384

EPSILON = 1e-05
BETA_ONE = 0.9
BETA_TWO = 0.999
ADAM_EPS = 1e-08
RATE_MATRIX = 0.05
DECAY_MATRIX = 0.05
RATE_VECTOR = 0.3

AXES = ("dp", "fsdp")
LOW = jnp.bfloat16
WIDE = jnp.float32
VMEM_BYTES = 12 * 2**20


def nn(left, right):
    return lax.dot_general(left, right, (((1,), (0,)), ((), ())), preferred_element_type=WIDE)


def nt(left, right):
    return lax.dot_general(left, right, (((1,), (1,)), ((), ())), preferred_element_type=WIDE)


def tn(left, right):
    return lax.dot_general(left, right, (((0,), (0,)), ((), ())), preferred_element_type=WIDE)


def shape(rows, cols, kind=LOW):
    return jax.ShapeDtypeStruct((rows, cols), kind)


def later(kernel, inputs, extra):
    return lambda *refs: kernel(*refs[:inputs], *refs[inputs + extra :])


def whole_call(kernel, outs, scratch, smem, name, flops, *args, anywhere=(), after=()):
    specs = []
    for i in range(len(args)):
        space = pltpu.SMEM if i < smem else pl.ANY if i in anywhere else pltpu.VMEM
        specs.append(pl.BlockSpec(memory_space=space))
    moved = sum(a.size * a.dtype.itemsize for a in args) + sum(o.size * o.dtype.itemsize for o in outs)
    return pl.pallas_call(
        later(kernel, len(args), len(after)),
        in_specs=specs + [pl.BlockSpec(memory_space=pl.ANY)] * len(after),
        out_specs=[pl.BlockSpec(memory_space=pltpu.VMEM)] * len(outs),
        out_shape=outs,
        scratch_shapes=scratch,
        compiler_params=pltpu.CompilerParams(vmem_limit_bytes=VMEM_BYTES),
        cost_estimate=pl.CostEstimate(flops=flops, bytes_accessed=moved, transcendentals=0),
        name=name,
    )(*args, *after)


def over_rows(count, step, body, init=None):
    return lax.fori_loop(0, count // step, lambda i, c: body(pl.ds(pl.multiple_of(i * step, step), step), c), init)


def normal(values):
    centre = values - jnp.mean(values, axis=-1, keepdims=True)
    rstd = lax.rsqrt(jnp.mean(centre * centre, axis=-1, keepdims=True) + EPSILON)
    return centre * rstd, rstd


def both(pair, side, lo, width):
    rows = slice(HALF * side, HALF * (side + 1))
    return jnp.concatenate([z[rows, lo : lo + width] for z in pair], axis=0)


def qkv_kernel(x_ref, order_ref, own, other, a_ref, qkv_ref, vec_ref, tmp, wide):
    moved = jnp.concatenate([z[:HALF, CUT_ONE:] for z in (own, other)], axis=0)
    wide[...] = nn(order_ref[...], moved)
    vec_ref[...] = jnp.zeros_like(vec_ref)
    for k in range(10):
        first = min(D * k // 10 // 8 * 8, D - 88)

        def tenths(rows):
            entry = lax.broadcasted_iota(jnp.int32, (rows, D), 1) + D * k
            tenth = (entry * 52429) >> 19
            return tenth, entry - 10 * tenth, lax.broadcasted_iota(jnp.int32, (rows, D), 0)

        _, column, row = tenths(128)
        picked = nn(wide[first : first + 88, :].astype(LOW), (row == column).astype(LOW))
        tenth, _, row = tenths(88)
        vec_ref[k : k + 1, :] = jnp.sum(jnp.where(row + first == tenth, picked, 0.0), axis=0, keepdims=True)
    gain, shift = vec_ref[0:1, :], vec_ref[1:2, :]

    def norm(rows, _):
        tmp[rows, :] = (normal(x_ref[rows, :].astype(WIDE))[0] * gain + shift).astype(LOW)

    over_rows(x_ref.shape[0], 144, norm)
    a_ref[...] = nn(tmp[...], order_ref[...]).astype(LOW)
    for col in range(0, 3 * D, 384):
        w = both((own, other), *divmod(col, CUT_ONE), 384)
        qkv_ref[:, col : col + 384] = nn(a_ref[...], w).astype(LOW)


def project(x, order, one, after=()):
    n = x.shape[0]
    return whole_call(
        qkv_kernel, [shape(n, D), shape(n, 3 * D), shape(16, D, WIDE)],
        [pltpu.VMEM((n, D), LOW), pltpu.VMEM((D, 128), WIDE)], 0, "project",
        2 * n * D * (4 * D), x, order, *one, after=after,
    )


def each_tile(spans, body):
    def step(t, carry):
        for kind, rows in ((1, SMALL), (2, LARGE)):

            @pl.when(spans[t, 4] == kind)
            def _():
                body(t, pl.multiple_of(spans[t, 2], 16), rows, pl.multiple_of(spans[t, 3], 16))

        return carry

    lax.fori_loop(0, 4, step, 0)


def padding_rows(spans, shape_):
    return lax.broadcasted_iota(jnp.int32, shape_, 0) >= spans[4, 0]


def own_half(values, e):
    lane = lax.broadcasted_iota(jnp.int32, values.shape, 1)
    return jnp.where((lane < 64) if e == 0 else (lane >= 64), values, jnp.zeros_like(values))


def attend_kernel(base, spans, slopes, qkv_ref, far_ref, o_ref, p_ref, acc):
    acc[...] = jnp.zeros_like(acc)

    def tile(t, at, count, key):
        rows, keys = pl.ds(at, count), pl.ds(key, WIN)
        row = lax.broadcasted_iota(jnp.int32, (count, 1), 0) + at
        inside = ((row >= spans[t, 0]) & (row < spans[t, 1])).astype(WIDE)
        far = far_ref[t, :count, :]
        for pair in range(3):
            col = (base + pair) * 128
            q, k, v = [qkv_ref[z, col + i * D : col + i * D + 128] for i, z in enumerate((rows, keys, keys))]
            out = None
            for e in range(2):
                s = nt(q, own_half(k, e)) * (0.125 * LOG2E) - slopes[2 * (base + pair) + e] * far
                p = jnp.exp2(s - jnp.max(s, axis=1, keepdims=True))
                p = (p * (inside / jnp.sum(p, axis=1, keepdims=True))).astype(LOW)
                p_ref[t, 2 * pair + e, :count, :] = p
                part = nn(p, own_half(v, e))
                out = part if out is None else out + part
            acc[rows, pair * 128 : pair * 128 + 128] += out

    each_tile(spans, tile)
    v = qkv_ref[:, base * 128 + 2 * D : base * 128 + 2 * D + HALF]
    o_ref[...] = jnp.where(padding_rows(spans, v.shape), v, acc[...].astype(LOW))


def attend(base, qkv, far, spans, slopes, after=()):
    n = qkv.shape[0]
    return whole_call(
        functools.partial(attend_kernel, base),
        [shape(n, HALF), jax.ShapeDtypeStruct((4, HEADS // 2, LARGE, WIN), LOW)],
        [pltpu.VMEM((n, HALF), WIDE)], 2, "attend", 9 * 10**9, spans, slopes, qkv, far, after=after,
    )


def attend_back_kernel(base, spans, qkv_ref, g_ref, p_ref, dq_ref, dk_ref, dv_ref, aq, ak, av):
    for acc in (aq, ak, av):
        acc[...] = jnp.zeros_like(acc)

    def tile(t, at, count, key):
        rows, keys = pl.ds(at, count), pl.ds(key, WIN)
        for pair in range(3):
            col = (base + pair) * 128
            q, k, v = [qkv_ref[z, col + i * D : col + i * D + 128] for i, z in enumerate((rows, keys, keys))]
            g = g_ref[rows, col : col + 128]
            sums = None
            for e in range(2):
                ge = own_half(g, e)
                p = p_ref[t, 2 * pair + e, :count, :]
                wide = p.astype(WIDE)
                d = wide * nt(ge * 0.125, v)
                d = (d - wide * jnp.sum(d, axis=1, keepdims=True)).astype(LOW)
                parts = (nn(d, own_half(k, e)), tn(d, own_half(q, e)), tn(p, ge))
                sums = parts if sums is None else tuple(a + b for a, b in zip(sums, parts))
            part = slice(pair * 128, pair * 128 + 128)
            aq[rows, part] += sums[0]
            ak[keys, part] += sums[1]
            av[keys, part] += sums[2]

    each_tile(spans, tile)
    dq_ref[...] = aq[...].astype(LOW)
    dk_ref[...] = ak[...].astype(LOW)
    g = g_ref[:, base * 128 : base * 128 + HALF]
    dv_ref[...] = jnp.where(padding_rows(spans, g.shape), g, av[...].astype(LOW))


def attend_back(base, qkv, grad, probs, spans, after=()):
    n = qkv.shape[0]
    return whole_call(
        functools.partial(attend_back_kernel, base), [shape(n, HALF)] * 3, [pltpu.VMEM((n, HALF), WIDE)] * 3, 1,
        "attend_back", 12 * 10**9, spans, qkv, grad, probs, after=after,
    )


def tables_kernel(seg_ref, side_ref, valid_ref, spans, far_ref):
    n = seg_ref.shape[1]
    seg, side, valid = [z[...].astype(WIDE) for z in (seg_ref, side_ref, valid_ref)]
    live = jnp.sum(valid).astype(jnp.int32)
    for z in range(5):
        spans[4, z] = live
    for t in range(4):
        low = jnp.sum((seg < t).astype(WIDE)).astype(jnp.int32)
        high = jnp.sum((seg <= t).astype(WIDE)).astype(jnp.int32)
        width = jnp.max(jnp.where(seg == t, side, 1.0))
        small = high - low <= SMALL - 16
        start = low // 16 * 16
        at = jnp.minimum(start, jnp.where(small, n - SMALL, n - LARGE))
        key = jnp.minimum(start, n - WIN)
        kind = jnp.where((high > low) & (low < live), jnp.where(small, 1, 2), 0)
        for z, value in enumerate((low, high, at, key, kind)):
            spans[t, z] = value

        def places(first, shape_, dim):
            slot = lax.broadcasted_iota(jnp.int32, shape_, dim) + first
            place = (slot - low).astype(WIDE)
            row = jnp.floor((place + 0.5) / width)
            return (slot >= low) & (slot < high), row, place - row * width

        inside, row, col = places(at, (LARGE, 1), 0)
        inside_key, row_key, col_key = places(key, (1, WIN), 1)
        down, along = row - row_key, col - col_key
        far_ref[t] = jnp.where(inside & inside_key, jnp.sqrt(down * down + along * along), 1e12)


def tables(seg, side, valid):
    vmem, smem = [pl.BlockSpec(memory_space=z) for z in (pltpu.VMEM, pltpu.SMEM)]
    return pl.pallas_call(
        tables_kernel,
        in_specs=[vmem] * 3,
        out_specs=[smem, vmem],
        out_shape=[jax.ShapeDtypeStruct((5, 5), jnp.int32), jax.ShapeDtypeStruct((4, LARGE, WIN), WIDE)],
        compiler_params=pltpu.CompilerParams(vmem_limit_bytes=VMEM_BYTES),
        name="tables",
    )(seg, side, valid)


def bell(u):
    share = 0.5 + 0.5 * lax.erf(u * 0.7071067811865476)
    return u * share, share + u * (jnp.exp2(u * u * -0.7213475204444817) * 0.3989422804014327)


def up_kernel(x_ref, o0_ref, o1_ref, vec_ref, order_ref, own, other, mixed_ref, h_ref, a_ref, gl_ref, gp_ref, tmp):
    mixed_ref[...] = (
        nn(o0_ref[...], order_ref[:HALF, :]) + nn(o1_ref[...], order_ref[HALF:, :])
    ).astype(LOW)
    for col in (0, 384):
        part = slice(col, col + 384)
        h_ref[:, part] = x_ref[:, part].astype(WIDE) + nn(mixed_ref[...], both((own, other), 0, col, 384)) + vec_ref[2:3, part]
    gain, shift = vec_ref[3:4, :], vec_ref[4:5, :]

    def norm(rows, _):
        tmp[rows, :] = (normal(h_ref[rows, :])[0] * gain + shift).astype(LOW)

    over_rows(x_ref.shape[0], 144, norm)
    a_ref[...] = nn(tmp[...], order_ref[...]).astype(LOW)
    for col in range(0, FF, 384):
        k = 5 + col // D
        u = nn(a_ref[...], both((own, other), *divmod(col + D, WIDTH_TWO), 384)) + vec_ref[k : k + 1, col % D : col % D + 384]
        value, slope = bell(u)
        gl_ref[:, col : col + 384] = value.astype(LOW)
        gp_ref[:, col : col + 384] = slope.astype(LOW)


def upward(x, o, vec, order, two, after=()):
    n = x.shape[0]
    return whole_call(
        up_kernel, [shape(n, D), shape(n, D, WIDE), shape(n, D), shape(n, FF), shape(n, FF)],
        [pltpu.VMEM((n, D), LOW)], 0, "upward", 2 * n * D * (7 * D) * 2, x, *o, vec, order, *two,
        after=after,
    )


def down_kernel(place, vec_ref, gl_ref, gp_ref, dy_ref, h_ref, own, other, out_ref, dur_ref, vg_ref, wd, sem):
    def copies(b, piece, row):
        dst = pl.ds(pl.multiple_of(b * 96, 96), 96)
        return [
            pltpu.make_async_copy(
                piece.at[pl.ds(pl.multiple_of(row * 96 + side * (FF // 2), 96), 96), :],
                wd.at[dst, pl.ds(side * WIDTH_THREE, WIDTH_THREE)],
                sem,
            )
            for side in (0, 1)
        ]

    def begin(b, carry):
        p = place[b]
        pl.when(p < 16)(lambda: [z.start() for z in copies(b, own, p)] and None)
        pl.when(p >= 16)(lambda: [z.start() for z in copies(b, other, p - 16)] and None)
        return carry

    def finish(b, carry):
        for z in copies(b, own, 0):
            z.wait()
        return carry

    lax.fori_loop(0, 32, begin, 0)
    lax.fori_loop(0, 32, finish, 0)
    for col in range(0, FF, 384):
        part = slice(col, col + 384)
        du = nt(dy_ref[...], wd[part, :]) * gp_ref[:, part].astype(WIDE)
        dur_ref[:, part] = du.astype(LOW)
        k = col // D
        vg_ref[k : k + 1, col % D : col % D + 384] = jnp.sum(du, axis=0, keepdims=True)
    for col in (0, 384):
        part = slice(col, col + 384)
        out_ref[:, part] = (h_ref[:, part] + nn(gl_ref[...], wd[:, part]) + vec_ref[9:10, part]).astype(LOW)


def downward(place, vec, gl, gp, dy, h, three, after=()):
    n = h.shape[0]
    return whole_call(
        down_kernel, [shape(n, D), shape(n, FF), shape(8, D, WIDE)],
        [pltpu.VMEM((FF, D), LOW), pltpu.SemaphoreType.DMA], 1, "downward",
        2 * n * D * (8 * D), place, vec, gl, gp, dy, h, *three, anywhere=(6, 7), after=after,
    )


def hidden_kernel(vec_ref, order_ref, dur_ref, dy_ref, h_ref, own, other, dh_ref, dhr_ref, dor_ref, vg_ref, tmp):
    split = WIDTH_TWO - D
    for i, w in enumerate((own, other)):
        tmp[:, HALF * i : HALF * (i + 1)] = (
            nt(dur_ref[:, :split], w[:HALF, D:]) + nt(dur_ref[:, split:], w[HALF:, :])
        ).astype(LOW)
    dh_ref[...] = nt(tmp[...], order_ref[...])
    gain = vec_ref[3:4, :]

    def step(rows, sums):
        e = dh_ref[rows, :]
        dy = dy_ref[rows, :].astype(WIDE)
        n, rstd = normal(h_ref[rows, :])
        w = e * gain
        dh = dy + rstd * (w - jnp.mean(w, axis=-1, keepdims=True) - n * jnp.mean(w * n, axis=-1, keepdims=True))
        dh_ref[rows, :] = dh
        dhr_ref[rows, :] = dh.astype(LOW)
        return tuple(s + jnp.sum(z.reshape(-1, 8, D), axis=0) for s, z in zip(sums, (dh, e * n, e, dy)))

    zero = jnp.zeros((8, D), WIDE)
    sums = over_rows(h_ref.shape[0], 144, step, (zero,) * 4)
    for k, s in enumerate(sums):
        vg_ref[k : k + 1, :] = jnp.sum(s, axis=0, keepdims=True)
    for i, w in enumerate((own, other)):
        tmp[:, HALF * i : HALF * (i + 1)] = nt(dhr_ref[...], w[:HALF, :D]).astype(LOW)
    dor_ref[...] = nt(tmp[...], order_ref[...]).astype(LOW)


def hidden_grad(vec, order, dur, dy, h, two, after=()):
    n = h.shape[0]
    return whole_call(
        hidden_kernel, [shape(n, D, WIDE), shape(n, D), shape(n, D), shape(8, D, WIDE)],
        [pltpu.VMEM((n, D), LOW)], 0, "hidden_grad",
        2 * n * D * (7 * D), vec, order, dur, dy, h, *two, after=after,
    )


def down_grad_kernel(place, gl_ref, dy_ref, own, other):
    for c in range(8):
        t = tn(gl_ref[:, 384 * c : 384 * (c + 1)], dy_ref[...]).astype(LOW)
        for i in range(4):
            p = place[4 * c + i]

            def put(piece, row):
                for side in (0, 1):
                    rows = pl.ds(pl.multiple_of(row * 96 + side * (FF // 2), 96), 96)
                    piece[rows, :] = t[96 * i : 96 * (i + 1), side * WIDTH_THREE : (side + 1) * WIDTH_THREE]

            pl.when(p < 16)(lambda: put(own, p))
            pl.when(p >= 16)(lambda: put(other, p - 16))


def down_grad(place, gl, dy, after=()):
    n = dy.shape[0]
    return whole_call(down_grad_kernel, [shape(FF, WIDTH_THREE)] * 2, [], 1, "down_grad", 2 * n * D * FF, place, gl, dy, after=after)


def two_grad_kernel(mixed_ref, a_ref, dhr_ref, dur_ref, own, other):
    for col in range(0, D + FF, 384):
        left, right = (mixed_ref, dhr_ref[:, col : col + 384]) if col < D else (a_ref, dur_ref[:, col - D : col - D + 384])
        t = tn(left[...], right).astype(LOW)
        side, lo = divmod(col, WIDTH_TWO)
        own[HALF * side : HALF * (side + 1), lo : lo + 384] = t[:HALF]
        other[HALF * side : HALF * (side + 1), lo : lo + 384] = t[HALF:]


def two_grad(mixed, a, dhr, dur, after=()):
    n = a.shape[0]
    return whole_call(two_grad_kernel, [shape(D, WIDTH_TWO)] * 2, [], 0, "two_grad", 2 * n * D * (D + FF), mixed, a, dhr, dur,
                      after=after)


def one_grad_kernel(a_ref, *refs):
    halves, (own, other) = refs[:6], refs[6:]
    for i, half in enumerate(halves):
        t = tn(a_ref[...], half[...]).astype(LOW)
        side, lo = divmod(384 * i, CUT_ONE)
        own[HALF * side : HALF * (side + 1), lo : lo + 384] = t[:HALF]
        other[HALF * side : HALF * (side + 1), lo : lo + 384] = t[HALF:]


def one_grad(a, d, after=()):
    n = a.shape[0]
    return whole_call(one_grad_kernel, [shape(D, CUT_ONE)] * 2, [], 0, "one_grad", 2 * n * D * 3 * D, a, *d, after=after)


def input_back_kernel(order_ref, q0, q1, k0, k1, v0, v1, own, other, e_ref, tmp):
    for i, w in enumerate((own, other)):
        total = 0.0
        for j, d in enumerate((q0, q1, k0, k1, v0, v1)):
            side, lo = divmod(384 * j, CUT_ONE)
            total = total + nt(d[...], w[HALF * side : HALF * (side + 1), lo : lo + 384])
        tmp[:, HALF * i : HALF * (i + 1)] = total.astype(LOW)
    e_ref[...] = nt(tmp[...], order_ref[...])


def input_back(order, d, one, after=()):
    n = d[0].shape[0]
    return whole_call(
        input_back_kernel, [shape(n, D, WIDE)], [pltpu.VMEM((n, D), LOW)], 0, "input_back",
        2 * n * D * 4 * D, order, *d, *one, after=after,
    )[0]


def input_kernel(x_ref, vec_ref, e_ref, dh_ref, dx_ref, vg_ref):
    gain = vec_ref[0:1, :]

    def step(rows, sums):
        e = e_ref[rows, :]
        n, rstd = normal(x_ref[rows, :].astype(WIDE))
        w = e * gain
        dx_ref[rows, :] = dh_ref[rows, :] + rstd * (
            w - jnp.mean(w, axis=-1, keepdims=True) - n * jnp.mean(w * n, axis=-1, keepdims=True)
        )
        return tuple(s + jnp.sum(z.reshape(-1, 8, D), axis=0) for s, z in zip(sums, (e * n, e)))

    zero = jnp.zeros((8, D), WIDE)
    sums = over_rows(x_ref.shape[0], 144, step, (zero,) * 2)
    for k, s in enumerate(sums):
        vg_ref[k : k + 1, :] = jnp.sum(s, axis=0, keepdims=True)


def input_grad(x, vec, e, dh, after=()):
    n = x.shape[0]
    return whole_call(
        input_kernel, [shape(n, D, WIDE), shape(8, D, WIDE)], [], 0, "input_grad",
        2 * n * D * 3 * D, x, vec, e, dh, after=after,
    )


def near_kernel(a, b, c, d, left_ref, right_ref):
    cut = left_ref.shape[1]
    for out, lo in ((left_ref, 0), (right_ref, cut)):
        out[...] = jnp.concatenate([z[:, lo : lo + cut].astype(WIDE) for z in (a, b, c, d)], axis=0).astype(LOW)


def near_pieces(pieces, after=()):
    rows, cols = pieces[0].shape
    return whole_call(near_kernel, [shape(4 * rows, cols // 2)] * 2, [], 0, "near", 1, *pieces, after=after)


def first_kernel(left, got_left, right, got_right, left_ref, right_ref):
    rows = left.shape[0]
    for out, mine, got in ((left_ref, left, got_left), (right_ref, right, got_right)):
        out[:rows, :] = mine[...]
        out[rows:, :] = got[...]


def first_pieces(left, right, got, after=()):
    rows, cols = left.shape
    return whole_call(
        first_kernel, [shape(2 * rows, cols)] * 2, [], 0, "first", 1, left, got[0], right, got[1], after=after
    )


def second_kernel(left, got, right, far, own_ref):
    rows = left.shape[0]
    half = rows // 2
    own_ref[:rows, :] = left[...]
    own_ref[rows : 2 * rows, :] = got[...]
    for i in (0, 1):
        own_ref[2 * rows + 2 * i * half : 2 * rows + (2 * i + 1) * half, :] = right[i * half : (i + 1) * half, :]
        own_ref[2 * rows + (2 * i + 1) * half : 2 * rows + (2 * i + 2) * half, :] = far[i * half : (i + 1) * half, :]


def second_pieces(left, right, got, after=()):
    rows, cols = left.shape
    return whole_call(
        second_kernel, [shape(4 * rows, cols)], [], 0, "second", 1, left, got[0], right, got[1], after=after
    )[0]


def core_sum_kernel(own, got, left_keep, right_keep, left_out, right_out):
    half = left_keep.shape[0]
    rows = half // 2

    def total(lo, count):
        return own[lo : lo + count, :].astype(WIDE) + got[lo : lo + count, :].astype(WIDE)

    left_keep[...] = total(0, half)
    left_out[...] = total(half, half).astype(LOW)
    for i in (0, 1):
        lo = 2 * half + 2 * i * rows
        right_keep[i * rows : (i + 1) * rows, :] = total(lo, rows)
        right_out[i * rows : (i + 1) * rows, :] = total(lo + rows, rows).astype(LOW)


def core_sum(own, got, after=()):
    rows, cols = own.shape[0] // 4, own.shape[1]
    return whole_call(
        core_sum_kernel, [shape(rows, cols, WIDE)] * 2 + [shape(rows, cols)] * 2, [], 0, "core_sum", 1, own, got,
        after=after,
    )


def half_sum_kernel(left, got_left, right, got_right, left_keep, right_keep, left_out, right_out):
    rows = left_keep.shape[0]
    for mine, got, keep, out in ((left, got_left, left_keep, left_out), (right, got_right, right_keep, right_out)):
        keep[...] = mine[:rows, :] + got[:rows, :].astype(WIDE)
        out[...] = (mine[rows:, :] + got[rows:, :].astype(WIDE)).astype(LOW)


def half_sum(left, right, got, after=()):
    rows, cols = left.shape[0] // 2, left.shape[1]
    return whole_call(
        half_sum_kernel, [shape(rows, cols, WIDE)] * 2 + [shape(rows, cols)] * 2, [], 0, "half_sum", 1,
        left, got[0], right, got[1], after=after,
    )


def last_sum_kernel(left, got_left, right, got_right, keep, *outs):
    unit, cut = keep.shape[0], left.shape[1]
    for lo, mine, got in ((0, left, got_left), (cut, right, got_right)):
        total = mine[...] + got[...].astype(WIDE)
        keep[:, lo : lo + cut] = total[:unit]
        for i, out in enumerate(outs):
            out[:, lo : lo + cut] = total[unit * (i + 1) : unit * (i + 2)].astype(LOW)


def last_sum(left, right, got, after=()):
    unit, cols = left.shape[0] // 4, 2 * left.shape[1]
    return whole_call(
        last_sum_kernel, [shape(unit, cols, WIDE)] + [shape(unit, cols)] * 3, [], 0, "last_sum", 1,
        left, got[0], right, got[1], after=after,
    )


def swap(value, bits):
    pairs = [(i, i ^ bits) for i in range(32)]
    return lax.ppermute(value, AXES, pairs)


def tie(values, *first):
    return lax.optimization_barrier((tuple(values), first))[0]


class Flow:
    def __init__(self, steps):
        self.steps = steps
        self.next = next(steps)[:2]

    def issue(self, start=()):
        values, bits = self.next
        values = tie(values, start)
        self.got = tuple(swap(value, bit) for value, bit in zip(values, bits))
        return self.got

    def land(self, end=()):
        values, *bits = self.steps.send(tie(self.got, end))
        if values is None:
            return bits[0]
        self.next = (values, bits[0])
        return bits[1]


def spread(block):
    got = yield (block,) * 3, (8, 16, 24)
    left, right = near_pieces((block,) + got)
    got = yield (left, right), (2, 4), (left, right)
    left, right = first_pieces(left, right, got)
    got = yield (left, right), (4, 2), (left, right)
    own = second_pieces(left, right, got)
    got = yield (own,), (1,), (own,)
    yield None, (own, got[0])


def collect(pieces):
    (got,) = yield (pieces[1],), (1,)
    left, right, *out = ready = core_sum(pieces[0], got)
    got = yield out, (4, 2), tuple(ready)
    left, right, *out = ready = half_sum(left, right, got)
    got = yield out, (2, 4), tuple(ready)
    total, *out = ready = last_sum(left, right, got)
    got = yield out, (8, 16, 24), tuple(ready)
    yield None, (sum((z.astype(WIDE) for z in got), total),)


def collect_vec(blocks):
    half = blocks.shape[0] // 2
    (got,) = yield (blocks[half:],), (1,)
    blocks = blocks[:half] + got
    rows = half // 4
    got = yield [blocks[rows * k : rows * (k + 1)] for k in (1, 2, 3)], (2, 4, 6), (blocks,)
    blocks = sum(got, blocks[:rows])
    got = yield [blocks[k : k + 1] for k in (1, 2, 3)], (8, 16, 24), (blocks,)
    yield None, (sum(got, blocks[:1]).reshape(-1),)


def stack(whole):
    half, cut = whole.shape[0] // 2, whole.shape[1] // 2
    return tuple(jnp.concatenate([z[:, :cut], z[:, cut:]], axis=0) for z in (whole[:half], whole[half:]))


def unstack(pieces):
    half = pieces[0].shape[0] // 2
    return jnp.concatenate([jnp.concatenate([z[:half], z[half:]], axis=1) for z in pieces], axis=0)


class Whole:
    def __init__(self, result):
        self.result = result

    def issue(self, start=()):
        return ()

    def land(self, end=()):
        return self.result


def spread_any(block):
    return stack(lax.all_gather(block, AXES, axis=0, tiled=True))


def collect_any(pieces):
    return (lax.psum_scatter(unstack(pieces), AXES, scatter_dimension=0, tiled=True).astype(WIDE),)


def rearrange(whole, order, shards):
    return jnp.take(whole.reshape(shards, -1, whole.shape[1]), order, axis=0, mode="clip").reshape(whole.shape)


def adamw(master, moment_one, moment_two, gradient, step_rate, decay_rate):
    first_new = BETA_ONE * moment_one + (1.0 - BETA_ONE) * gradient
    second_new = BETA_TWO * moment_two + (1.0 - BETA_TWO) * gradient * gradient
    first_hat = first_new / (1.0 - BETA_ONE**STEP)
    second_hat = second_new / (1.0 - BETA_TWO**STEP)
    master_new = master - step_rate * (
        first_hat / (jnp.sqrt(second_hat) + ADAM_EPS) + decay_rate * master
    )
    return (first_new, second_new, master_new)


def local(
    tokens_in, cotangent, segments, tile_sides, valid_slots, owners,
    master_qkv, master_out, master_up, master_down, master_vec,
    first_qkv, first_out, first_up, first_down, first_vec,
    second_qkv, second_out, second_up, second_down, second_vec,
):
    shards = lax.axis_size(AXES)
    near = shards == 32
    unit = D // shards
    per_row = master_vec.shape[0] // unit
    share = master_vec.shape[0]
    ids = jnp.arange(shards, dtype=jnp.int32)
    if near:
        away = owners ^ lax.axis_index(AXES).astype(jnp.int32)
        place = (away >> 3) + 4 * ((away >> 1) & 1) + 8 * ((away >> 2) & 1) + 16 * (away & 1)
        place_down = place
    else:
        place = owners
        place_down = jnp.arange(32, dtype=jnp.int32)
    inverse = jnp.sum(ids[:, None] * (place[:, None] == ids[None, :]), axis=0)
    target = (place[:, None] * unit + jnp.arange(unit, dtype=jnp.int32)[None, :]).reshape(-1)
    order = (target[:, None] == jnp.arange(D, dtype=jnp.int32)[None, :]).astype(LOW)

    def gather(block):
        return Flow(spread(block)) if near else Whole(spread_any(block))

    def scatter(pieces):
        return Flow(collect(pieces)) if near else Whole(collect_any(pieces))

    vec_block = jnp.pad(master_vec.reshape(unit, per_row), ((0, 0), (0, 128 - per_row)))
    block_one = jnp.concatenate(
        [master_qkv[:, :CUT_ONE], vec_block, master_qkv[:, CUT_ONE:], jnp.zeros_like(vec_block)], axis=1
    )
    spans, far = tables(segments, tile_sides, valid_slots)
    slopes = LOG2E * jnp.exp2(-8.0 * (jnp.arange(HEADS, dtype=jnp.int32).astype(WIDE) + 1.0) / HEADS)
    one = gather(block_one.astype(LOW))
    two = gather(jnp.concatenate([master_out, master_up], axis=1).astype(LOW))
    if near:
        three = gather(master_down.astype(LOW))
    else:
        whole = lax.all_gather(master_down.astype(LOW), AXES, axis=0, tiled=True)
        three = Whole(stack(rearrange(whole, owners, shards)))
    one.issue()
    done = one.land((far, spans, slopes, order))
    one.issue(done)
    done = one.land()
    sent = one.issue(done) + two.issue(done)
    done = one.land()
    done = done + two.land(sent + done)
    one.issue(done)
    sent = two.issue(done)
    one = one.land()

    x = tokens_in[0]
    dy = cotangent[0]
    act_one, qkv, vec = project(x, order, one)
    done = two.land((qkv,))
    sent = two.issue(done) + three.issue(done)
    mixed_0, probs_0 = attend(0, qkv, far, spans, slopes, done)
    done = two.land((mixed_0,))
    done = done + three.land((mixed_0,) + sent + done)
    sent = two.issue(done) + three.issue(done)
    mixed_1, probs_1 = attend(3, qkv, far, spans, slopes, done + (mixed_0,))
    done = three.land((mixed_1,) + sent)
    two = two.land((mixed_1,) + sent)
    three.issue(done + two[1:])
    mixed, hidden, act_two, gelu, gelu_slope = upward(x, (mixed_0, mixed_1), vec, order, two, done)
    grad_three = down_grad(place_down, gelu, dy)
    done = three.land(tuple(grad_three))
    three.issue(done)
    three = three.land()
    if not near:
        back = jnp.sum(ids[:, None] * (owners[:, None] == ids[None, :]), axis=0)
        grad_three = stack(rearrange(unstack(grad_three), back, shards))
    flow_three = scatter(grad_three)
    flow_three.issue((three[1],))
    block_out, dur, sums_up = downward(place_down, vec, gelu, gelu_slope, dy, hidden, three)
    done = flow_three.land((dur,))
    flow_three.issue(done)
    dh, dh_low, dmixed, sums = hidden_grad(vec, order, dur, dy, hidden, two, done)
    grad_two = two_grad(mixed, act_two, dh_low, dur)
    done = flow_three.land(tuple(grad_two)) + tuple(grad_two)
    flow_two = scatter(grad_two)
    sent = flow_three.issue(done) + flow_two.issue(done)
    d0 = attend_back(0, qkv, dmixed, probs_0, spans, done)
    done = flow_three.land(tuple(d0) + sent) + flow_two.land(tuple(d0) + sent)
    sent = flow_three.issue(done) + flow_two.issue(done)
    d1 = attend_back(3, qkv, dmixed, probs_1, spans, done + tuple(d0))
    d = [z for pair in zip(d0, d1) for z in pair]
    grad_one = one_grad(act_one, d)
    dact = input_back(order, d, one, tuple(grad_one))
    done = (dact,) + tuple(grad_one) + sent
    sum_three, = flow_three.land(done)
    done = flow_two.land(done)
    flow_one = scatter(grad_one)
    sent = flow_one.issue(done) + flow_two.issue(done)
    tokens_grad, sums_one = input_grad(x, vec, dact, dh, done)
    vector_grad = jnp.concatenate([sums_one[:2], sums[:3], sums_up[:4], sums[3:4]], axis=0)
    blocks = jnp.take(vector_grad.reshape(shards, share), inverse, axis=0, mode="clip")
    if near:
        flow_vec = Flow(collect_vec(blocks))
    else:
        flow_vec = Whole((lax.psum_scatter(blocks.reshape(-1), AXES, scatter_dimension=0, tiled=True),))
    done = flow_one.land((blocks,) + sent) + flow_two.land((blocks,) + sent)
    sent = flow_one.issue(done) + flow_two.issue(done) + flow_vec.issue(done)
    upd_down = adamw(master_down, first_down, second_down, sum_three, RATE_MATRIX, DECAY_MATRIX)
    sent = sent + upd_down
    done = flow_one.land(sent) + flow_vec.land(sent)
    sum_two, = flow_two.land(sent)
    sent = flow_one.issue(done) + flow_vec.issue(done)
    done = flow_one.land(sent) + flow_vec.land(sent)
    sent = flow_one.issue(done) + flow_vec.issue(done)
    upd_out = adamw(master_out, first_out, second_out, sum_two[:, :D], RATE_MATRIX, DECAY_MATRIX)
    upd_up = adamw(master_up, first_up, second_up, sum_two[:, D:], RATE_MATRIX, DECAY_MATRIX)
    sum_one, = flow_one.land(sent + upd_out + upd_up)
    sum_vec, = flow_vec.land(sent + upd_out + upd_up)
    upd_qkv = adamw(master_qkv, first_qkv, second_qkv, sum_one, RATE_MATRIX, DECAY_MATRIX)
    upd_vec = adamw(master_vec, first_vec, second_vec, sum_vec, RATE_VECTOR, 0.0)
    return (
        (block_out[None], tokens_grad[None]) + upd_qkv + upd_out + upd_up + upd_down + upd_vec
    )


def solution(mesh):
    rows = P(AXES, None)
    flat = P(AXES)
    deep = P(AXES, None, None)
    stored = (rows,) * 4 + (flat,)
    in_specs = (deep,) * 2 + (rows,) * 3 + (P(),) + stored * 3
    out_specs = (deep,) * 2 + (rows,) * 12 + (flat,) * 3
    return jax.shard_map(local, mesh=mesh, in_specs=in_specs, out_specs=out_specs, check_vma=False)
```

```python
import functools

import jax
import jax.numpy as jnp
from jax import lax
from jax.experimental import pallas as pl
from jax.experimental.pallas import tpu as pltpu
from jax.sharding import PartitionSpec as P

D = 768
HEADS = 12
FF = 3072
STEP = 10
HALF = 384
WIN = 256
SMALL = 160
LARGE = 240
LOG2E = 1.4426950408889634
CUT_ONE = 1152
WIDTH_ONE = 1280
WIDTH_TWO = 1920
WIDTH_THREE = 384

EPSILON = 1e-05
BETA_ONE = 0.9
BETA_TWO = 0.999
ADAM_EPS = 1e-08
RATE_MATRIX = 0.05
DECAY_MATRIX = 0.05
RATE_VECTOR = 0.3

AXES = ("dp", "fsdp")
LOW = jnp.bfloat16
WIDE = jnp.float32
VMEM_BYTES = 12 * 2**20


def nn(left, right):
    return lax.dot_general(left, right, (((1,), (0,)), ((), ())), preferred_element_type=WIDE)


def nt(left, right):
    return lax.dot_general(left, right, (((1,), (1,)), ((), ())), preferred_element_type=WIDE)


def tn(left, right):
    return lax.dot_general(left, right, (((0,), (0,)), ((), ())), preferred_element_type=WIDE)


def shape(rows, cols, kind=LOW):
    return jax.ShapeDtypeStruct((rows, cols), kind)


def later(kernel, inputs, extra):
    return lambda *refs: kernel(*refs[:inputs], *refs[inputs + extra :])


def whole_call(kernel, outs, scratch, smem, name, flops, *args, anywhere=(), after=()):
    specs = []
    for i in range(len(args)):
        space = pltpu.SMEM if i < smem else pl.ANY if i in anywhere else pltpu.VMEM
        specs.append(pl.BlockSpec(memory_space=space))
    moved = sum(a.size * a.dtype.itemsize for a in args) + sum(o.size * o.dtype.itemsize for o in outs)
    return pl.pallas_call(
        later(kernel, len(args), len(after)),
        in_specs=specs + [pl.BlockSpec(memory_space=pl.ANY)] * len(after),
        out_specs=[pl.BlockSpec(memory_space=pltpu.VMEM)] * len(outs),
        out_shape=outs,
        scratch_shapes=scratch,
        compiler_params=pltpu.CompilerParams(vmem_limit_bytes=VMEM_BYTES),
        cost_estimate=pl.CostEstimate(flops=flops, bytes_accessed=moved, transcendentals=0),
        name=name,
    )(*args, *after)


def over_rows(count, step, body, init=None):
    return lax.fori_loop(0, count // step, lambda i, c: body(pl.ds(pl.multiple_of(i * step, step), step), c), init)


def normal(values):
    centre = values - jnp.mean(values, axis=-1, keepdims=True)
    rstd = lax.rsqrt(jnp.mean(centre * centre, axis=-1, keepdims=True) + EPSILON)
    return centre * rstd, rstd


def both(pair, side, lo, width):
    rows = slice(HALF * side, HALF * (side + 1))
    return jnp.concatenate([z[rows, lo : lo + width] for z in pair], axis=0)


def qkv_kernel(x_ref, order_ref, own, other, a_ref, qkv_ref, vec_ref, tmp, wide):
    moved = jnp.concatenate([z[:HALF, CUT_ONE:] for z in (own, other)], axis=0)
    wide[...] = nn(order_ref[...], moved)
    vec_ref[...] = jnp.zeros_like(vec_ref)
    for k in range(10):
        first = min(D * k // 10 // 8 * 8, D - 88)

        def tenths(rows):
            entry = lax.broadcasted_iota(jnp.int32, (rows, D), 1) + D * k
            tenth = (entry * 52429) >> 19
            return tenth, entry - 10 * tenth, lax.broadcasted_iota(jnp.int32, (rows, D), 0)

        _, column, row = tenths(128)
        picked = nn(wide[first : first + 88, :].astype(LOW), (row == column).astype(LOW))
        tenth, _, row = tenths(88)
        vec_ref[k : k + 1, :] = jnp.sum(jnp.where(row + first == tenth, picked, 0.0), axis=0, keepdims=True)
    gain, shift = vec_ref[0:1, :], vec_ref[1:2, :]

    def norm(rows, _):
        tmp[rows, :] = (normal(x_ref[rows, :].astype(WIDE))[0] * gain + shift).astype(LOW)

    over_rows(x_ref.shape[0], 144, norm)
    a_ref[...] = nn(tmp[...], order_ref[...]).astype(LOW)
    for col in range(0, 3 * D, 384):
        w = both((own, other), *divmod(col, CUT_ONE), 384)
        qkv_ref[:, col : col + 384] = nn(a_ref[...], w).astype(LOW)


def project(x, order, one, after=()):
    n = x.shape[0]
    return whole_call(
        qkv_kernel, [shape(n, D), shape(n, 3 * D), shape(16, D, WIDE)],
        [pltpu.VMEM((n, D), LOW), pltpu.VMEM((D, 128), WIDE)], 0, "project",
        2 * n * D * (4 * D), x, order, *one, after=after,
    )


def each_tile(spans, body):
    def step(t, carry):
        for kind, rows in ((1, SMALL), (2, LARGE)):

            @pl.when(spans[t, 4] == kind)
            def _():
                body(t, pl.multiple_of(spans[t, 2], 16), rows, pl.multiple_of(spans[t, 3], 16))

        return carry

    lax.fori_loop(0, 4, step, 0)


def padding_rows(spans, shape_):
    return lax.broadcasted_iota(jnp.int32, shape_, 0) >= spans[4, 0]


def own_half(values, e):
    lane = lax.broadcasted_iota(jnp.int32, values.shape, 1)
    return jnp.where((lane < 64) if e == 0 else (lane >= 64), values, jnp.zeros_like(values))


def attend_kernel(base, spans, slopes, qkv_ref, far_ref, o_ref, p_ref, acc):
    acc[...] = jnp.zeros_like(acc)

    def tile(t, at, count, key):
        rows, keys = pl.ds(at, count), pl.ds(key, WIN)
        row = lax.broadcasted_iota(jnp.int32, (count, 1), 0) + at
        inside = ((row >= spans[t, 0]) & (row < spans[t, 1])).astype(WIDE)
        far = far_ref[t, :count, :]
        for pair in range(3):
            col = (base + pair) * 128
            q, k, v = [qkv_ref[z, col + i * D : col + i * D + 128] for i, z in enumerate((rows, keys, keys))]
            out = None
            for e in range(2):
                s = nt(q, own_half(k, e)) * (0.125 * LOG2E) - slopes[2 * (base + pair) + e] * far
                p = jnp.exp2(s - jnp.max(s, axis=1, keepdims=True))
                p = (p * (inside / jnp.sum(p, axis=1, keepdims=True))).astype(LOW)
                p_ref[t, 2 * pair + e, :count, :] = p
                part = nn(p, own_half(v, e))
                out = part if out is None else out + part
            acc[rows, pair * 128 : pair * 128 + 128] += out

    each_tile(spans, tile)
    v = qkv_ref[:, base * 128 + 2 * D : base * 128 + 2 * D + HALF]
    o_ref[...] = jnp.where(padding_rows(spans, v.shape), v, acc[...].astype(LOW))


def attend(base, qkv, far, spans, slopes, after=()):
    n = qkv.shape[0]
    return whole_call(
        functools.partial(attend_kernel, base),
        [shape(n, HALF), jax.ShapeDtypeStruct((4, HEADS // 2, LARGE, WIN), LOW)],
        [pltpu.VMEM((n, HALF), WIDE)], 2, "attend", 9 * 10**9, spans, slopes, qkv, far, after=after,
    )


def attend_back_kernel(base, spans, qkv_ref, g_ref, p_ref, dq_ref, dk_ref, dv_ref, aq, ak, av):
    for acc in (aq, ak, av):
        acc[...] = jnp.zeros_like(acc)

    def tile(t, at, count, key):
        rows, keys = pl.ds(at, count), pl.ds(key, WIN)
        for pair in range(3):
            col = (base + pair) * 128
            q, k, v = [qkv_ref[z, col + i * D : col + i * D + 128] for i, z in enumerate((rows, keys, keys))]
            g = g_ref[rows, col : col + 128]
            sums = None
            for e in range(2):
                ge = own_half(g, e)
                p = p_ref[t, 2 * pair + e, :count, :]
                wide = p.astype(WIDE)
                d = wide * nt(ge * 0.125, v)
                d = (d - wide * jnp.sum(d, axis=1, keepdims=True)).astype(LOW)
                parts = (nn(d, own_half(k, e)), tn(d, own_half(q, e)), tn(p, ge))
                sums = parts if sums is None else tuple(a + b for a, b in zip(sums, parts))
            part = slice(pair * 128, pair * 128 + 128)
            aq[rows, part] += sums[0]
            ak[keys, part] += sums[1]
            av[keys, part] += sums[2]

    each_tile(spans, tile)
    dq_ref[...] = aq[...].astype(LOW)
    dk_ref[...] = ak[...].astype(LOW)
    g = g_ref[:, base * 128 : base * 128 + HALF]
    dv_ref[...] = jnp.where(padding_rows(spans, g.shape), g, av[...].astype(LOW))


def attend_back(base, qkv, grad, probs, spans, after=()):
    n = qkv.shape[0]
    return whole_call(
        functools.partial(attend_back_kernel, base), [shape(n, HALF)] * 3, [pltpu.VMEM((n, HALF), WIDE)] * 3, 1,
        "attend_back", 12 * 10**9, spans, qkv, grad, probs, after=after,
    )


def tables_kernel(seg_ref, side_ref, valid_ref, spans, far_ref):
    n = seg_ref.shape[1]
    seg, side, valid = [z[...].astype(WIDE) for z in (seg_ref, side_ref, valid_ref)]
    live = jnp.sum(valid).astype(jnp.int32)
    for z in range(5):
        spans[4, z] = live
    for t in range(4):
        low = jnp.sum((seg < t).astype(WIDE)).astype(jnp.int32)
        high = jnp.sum((seg <= t).astype(WIDE)).astype(jnp.int32)
        width = jnp.max(jnp.where(seg == t, side, 1.0))
        small = high - low <= SMALL - 16
        start = low // 16 * 16
        at = jnp.minimum(start, jnp.where(small, n - SMALL, n - LARGE))
        key = jnp.minimum(start, n - WIN)
        kind = jnp.where((high > low) & (low < live), jnp.where(small, 1, 2), 0)
        for z, value in enumerate((low, high, at, key, kind)):
            spans[t, z] = value

        def places(first, shape_, dim):
            slot = lax.broadcasted_iota(jnp.int32, shape_, dim) + first
            place = (slot - low).astype(WIDE)
            row = jnp.floor((place + 0.5) / width)
            return (slot >= low) & (slot < high), row, place - row * width

        inside, row, col = places(at, (LARGE, 1), 0)
        inside_key, row_key, col_key = places(key, (1, WIN), 1)
        down, along = row - row_key, col - col_key
        far_ref[t] = jnp.where(inside & inside_key, jnp.sqrt(down * down + along * along), 1e12)


def tables(seg, side, valid):
    vmem, smem = [pl.BlockSpec(memory_space=z) for z in (pltpu.VMEM, pltpu.SMEM)]
    return pl.pallas_call(
        tables_kernel,
        in_specs=[vmem] * 3,
        out_specs=[smem, vmem],
        out_shape=[jax.ShapeDtypeStruct((5, 5), jnp.int32), jax.ShapeDtypeStruct((4, LARGE, WIN), WIDE)],
        compiler_params=pltpu.CompilerParams(vmem_limit_bytes=VMEM_BYTES),
        name="tables",
    )(seg, side, valid)


def bell(u):
    share = 0.5 + 0.5 * lax.erf(u * 0.7071067811865476)
    return u * share, share + u * (jnp.exp2(u * u * -0.7213475204444817) * 0.3989422804014327)


def up_kernel(x_ref, o0_ref, o1_ref, vec_ref, order_ref, own, other, mixed_ref, h_ref, a_ref, gl_ref, gp_ref, tmp):
    mixed_ref[...] = (
        nn(o0_ref[...], order_ref[:HALF, :]) + nn(o1_ref[...], order_ref[HALF:, :])
    ).astype(LOW)
    for col in (0, 384):
        part = slice(col, col + 384)
        h_ref[:, part] = x_ref[:, part].astype(WIDE) + nn(mixed_ref[...], both((own, other), 0, col, 384)) + vec_ref[2:3, part]
    gain, shift = vec_ref[3:4, :], vec_ref[4:5, :]

    def norm(rows, _):
        tmp[rows, :] = (normal(h_ref[rows, :])[0] * gain + shift).astype(LOW)

    over_rows(x_ref.shape[0], 144, norm)
    a_ref[...] = nn(tmp[...], order_ref[...]).astype(LOW)
    for col in range(0, FF, 384):
        k = 5 + col // D
        u = nn(a_ref[...], both((own, other), *divmod(col + D, WIDTH_TWO), 384)) + vec_ref[k : k + 1, col % D : col % D + 384]
        value, slope = bell(u)
        gl_ref[:, col : col + 384] = value.astype(LOW)
        gp_ref[:, col : col + 384] = slope.astype(LOW)


def upward(x, o, vec, order, two, after=()):
    n = x.shape[0]
    return whole_call(
        up_kernel, [shape(n, D), shape(n, D, WIDE), shape(n, D), shape(n, FF), shape(n, FF)],
        [pltpu.VMEM((n, D), LOW)], 0, "upward", 2 * n * D * (7 * D) * 2, x, *o, vec, order, *two,
        after=after,
    )


def down_kernel(place, vec_ref, gl_ref, gp_ref, dy_ref, h_ref, own, other, out_ref, dur_ref, vg_ref, wd, sem):
    def copies(b, piece, row):
        dst = pl.ds(pl.multiple_of(b * 96, 96), 96)
        return [
            pltpu.make_async_copy(
                piece.at[pl.ds(pl.multiple_of(row * 96 + side * (FF // 2), 96), 96), :],
                wd.at[dst, pl.ds(side * WIDTH_THREE, WIDTH_THREE)],
                sem,
            )
            for side in (0, 1)
        ]

    def begin(b, carry):
        p = place[b]
        pl.when(p < 16)(lambda: [z.start() for z in copies(b, own, p)] and None)
        pl.when(p >= 16)(lambda: [z.start() for z in copies(b, other, p - 16)] and None)
        return carry

    def finish(b, carry):
        for z in copies(b, own, 0):
            z.wait()
        return carry

    lax.fori_loop(0, 32, begin, 0)
    lax.fori_loop(0, 32, finish, 0)
    for col in range(0, FF, 384):
        part = slice(col, col + 384)
        du = nt(dy_ref[...], wd[part, :]) * gp_ref[:, part].astype(WIDE)
        dur_ref[:, part] = du.astype(LOW)
        k = col // D
        vg_ref[k : k + 1, col % D : col % D + 384] = jnp.sum(du, axis=0, keepdims=True)
    for col in (0, 384):
        part = slice(col, col + 384)
        out_ref[:, part] = (h_ref[:, part] + nn(gl_ref[...], wd[:, part]) + vec_ref[9:10, part]).astype(LOW)


def downward(place, vec, gl, gp, dy, h, three, after=()):
    n = h.shape[0]
    return whole_call(
        down_kernel, [shape(n, D), shape(n, FF), shape(8, D, WIDE)],
        [pltpu.VMEM((FF, D), LOW), pltpu.SemaphoreType.DMA], 1, "downward",
        2 * n * D * (8 * D), place, vec, gl, gp, dy, h, *three, anywhere=(6, 7), after=after,
    )


def hidden_kernel(vec_ref, order_ref, dur_ref, dy_ref, h_ref, own, other, dh_ref, dhr_ref, dor_ref, vg_ref, tmp):
    split = WIDTH_TWO - D
    for i, w in enumerate((own, other)):
        tmp[:, HALF * i : HALF * (i + 1)] = (
            nt(dur_ref[:, :split], w[:HALF, D:]) + nt(dur_ref[:, split:], w[HALF:, :])
        ).astype(LOW)
    dh_ref[...] = nt(tmp[...], order_ref[...])
    gain = vec_ref[3:4, :]

    def step(rows, sums):
        e = dh_ref[rows, :]
        dy = dy_ref[rows, :].astype(WIDE)
        n, rstd = normal(h_ref[rows, :])
        w = e * gain
        dh = dy + rstd * (w - jnp.mean(w, axis=-1, keepdims=True) - n * jnp.mean(w * n, axis=-1, keepdims=True))
        dh_ref[rows, :] = dh
        dhr_ref[rows, :] = dh.astype(LOW)
        return tuple(s + jnp.sum(z.reshape(-1, 8, D), axis=0) for s, z in zip(sums, (dh, e * n, e, dy)))

    zero = jnp.zeros((8, D), WIDE)
    sums = over_rows(h_ref.shape[0], 144, step, (zero,) * 4)
    for k, s in enumerate(sums):
        vg_ref[k : k + 1, :] = jnp.sum(s, axis=0, keepdims=True)
    for i, w in enumerate((own, other)):
        tmp[:, HALF * i : HALF * (i + 1)] = nt(dhr_ref[...], w[:HALF, :D]).astype(LOW)
    dor_ref[...] = nt(tmp[...], order_ref[...]).astype(LOW)


def hidden_grad(vec, order, dur, dy, h, two, after=()):
    n = h.shape[0]
    return whole_call(
        hidden_kernel, [shape(n, D, WIDE), shape(n, D), shape(n, D), shape(8, D, WIDE)],
        [pltpu.VMEM((n, D), LOW)], 0, "hidden_grad",
        2 * n * D * (7 * D), vec, order, dur, dy, h, *two, after=after,
    )


def down_grad_kernel(place, gl_ref, dy_ref, own, other):
    for c in range(8):
        t = tn(gl_ref[:, 384 * c : 384 * (c + 1)], dy_ref[...]).astype(LOW)
        for i in range(4):
            p = place[4 * c + i]

            def put(piece, row):
                for side in (0, 1):
                    rows = pl.ds(pl.multiple_of(row * 96 + side * (FF // 2), 96), 96)
                    piece[rows, :] = t[96 * i : 96 * (i + 1), side * WIDTH_THREE : (side + 1) * WIDTH_THREE]

            pl.when(p < 16)(lambda: put(own, p))
            pl.when(p >= 16)(lambda: put(other, p - 16))


def down_grad(place, gl, dy, after=()):
    n = dy.shape[0]
    return whole_call(down_grad_kernel, [shape(FF, WIDTH_THREE)] * 2, [], 1, "down_grad", 2 * n * D * FF, place, gl, dy, after=after)


def two_grad_kernel(mixed_ref, a_ref, dhr_ref, dur_ref, own, other):
    for col in range(0, D + FF, 384):
        left, right = (mixed_ref, dhr_ref[:, col : col + 384]) if col < D else (a_ref, dur_ref[:, col - D : col - D + 384])
        t = tn(left[...], right).astype(LOW)
        side, lo = divmod(col, WIDTH_TWO)
        own[HALF * side : HALF * (side + 1), lo : lo + 384] = t[:HALF]
        other[HALF * side : HALF * (side + 1), lo : lo + 384] = t[HALF:]


def two_grad(mixed, a, dhr, dur, after=()):
    n = a.shape[0]
    return whole_call(two_grad_kernel, [shape(D, WIDTH_TWO)] * 2, [], 0, "two_grad", 2 * n * D * (D + FF), mixed, a, dhr, dur,
                      after=after)


def one_grad_kernel(a_ref, *refs):
    halves, (own, other) = refs[:6], refs[6:]
    for i, half in enumerate(halves):
        t = tn(a_ref[...], half[...]).astype(LOW)
        side, lo = divmod(384 * i, CUT_ONE)
        own[HALF * side : HALF * (side + 1), lo : lo + 384] = t[:HALF]
        other[HALF * side : HALF * (side + 1), lo : lo + 384] = t[HALF:]


def one_grad(a, d, after=()):
    n = a.shape[0]
    return whole_call(one_grad_kernel, [shape(D, CUT_ONE)] * 2, [], 0, "one_grad", 2 * n * D * 3 * D, a, *d, after=after)


def input_back_kernel(order_ref, q0, q1, k0, k1, v0, v1, own, other, e_ref, tmp):
    for i, w in enumerate((own, other)):
        total = 0.0
        for j, d in enumerate((q0, q1, k0, k1, v0, v1)):
            side, lo = divmod(384 * j, CUT_ONE)
            total = total + nt(d[...], w[HALF * side : HALF * (side + 1), lo : lo + 384])
        tmp[:, HALF * i : HALF * (i + 1)] = total.astype(LOW)
    e_ref[...] = nt(tmp[...], order_ref[...])


def input_back(order, d, one, after=()):
    n = d[0].shape[0]
    return whole_call(
        input_back_kernel, [shape(n, D, WIDE)], [pltpu.VMEM((n, D), LOW)], 0, "input_back",
        2 * n * D * 4 * D, order, *d, *one, after=after,
    )[0]


def input_kernel(x_ref, vec_ref, e_ref, dh_ref, dx_ref, vg_ref):
    gain = vec_ref[0:1, :]

    def step(rows, sums):
        e = e_ref[rows, :]
        n, rstd = normal(x_ref[rows, :].astype(WIDE))
        w = e * gain
        dx_ref[rows, :] = dh_ref[rows, :] + rstd * (
            w - jnp.mean(w, axis=-1, keepdims=True) - n * jnp.mean(w * n, axis=-1, keepdims=True)
        )
        return tuple(s + jnp.sum(z.reshape(-1, 8, D), axis=0) for s, z in zip(sums, (e * n, e)))

    zero = jnp.zeros((8, D), WIDE)
    sums = over_rows(x_ref.shape[0], 144, step, (zero,) * 2)
    for k, s in enumerate(sums):
        vg_ref[k : k + 1, :] = jnp.sum(s, axis=0, keepdims=True)


def input_grad(x, vec, e, dh, after=()):
    n = x.shape[0]
    return whole_call(
        input_kernel, [shape(n, D, WIDE), shape(8, D, WIDE)], [], 0, "input_grad",
        2 * n * D * 3 * D, x, vec, e, dh, after=after,
    )


def near_kernel(a, b, c, d, left_ref, right_ref):
    cut = left_ref.shape[1]
    for out, lo in ((left_ref, 0), (right_ref, cut)):
        out[...] = jnp.concatenate([z[:, lo : lo + cut].astype(WIDE) for z in (a, b, c, d)], axis=0).astype(LOW)


def near_pieces(pieces, after=()):
    rows, cols = pieces[0].shape
    return whole_call(near_kernel, [shape(4 * rows, cols // 2)] * 2, [], 0, "near", 1, *pieces, after=after)


def first_kernel(left, got_left, right, got_right, left_ref, right_ref):
    rows = left.shape[0]
    for out, mine, got in ((left_ref, left, got_left), (right_ref, right, got_right)):
        out[:rows, :] = mine[...]
        out[rows:, :] = got[...]


def first_pieces(left, right, got, after=()):
    rows, cols = left.shape
    return whole_call(
        first_kernel, [shape(2 * rows, cols)] * 2, [], 0, "first", 1, left, got[0], right, got[1], after=after
    )


def second_kernel(left, got, right, far, own_ref):
    rows = left.shape[0]
    half = rows // 2
    own_ref[:rows, :] = left[...]
    own_ref[rows : 2 * rows, :] = got[...]
    for i in (0, 1):
        own_ref[2 * rows + 2 * i * half : 2 * rows + (2 * i + 1) * half, :] = right[i * half : (i + 1) * half, :]
        own_ref[2 * rows + (2 * i + 1) * half : 2 * rows + (2 * i + 2) * half, :] = far[i * half : (i + 1) * half, :]


def second_pieces(left, right, got, after=()):
    rows, cols = left.shape
    return whole_call(
        second_kernel, [shape(4 * rows, cols)], [], 0, "second", 1, left, got[0], right, got[1], after=after
    )[0]


def core_sum_kernel(own, got, left_keep, right_keep, left_out, right_out):
    half = left_keep.shape[0]
    rows = half // 2

    def total(lo, count):
        return own[lo : lo + count, :].astype(WIDE) + got[lo : lo + count, :].astype(WIDE)

    left_keep[...] = total(0, half)
    left_out[...] = total(half, half).astype(LOW)
    for i in (0, 1):
        lo = 2 * half + 2 * i * rows
        right_keep[i * rows : (i + 1) * rows, :] = total(lo, rows)
        right_out[i * rows : (i + 1) * rows, :] = total(lo + rows, rows).astype(LOW)


def core_sum(own, got, after=()):
    rows, cols = own.shape[0] // 4, own.shape[1]
    return whole_call(
        core_sum_kernel, [shape(rows, cols, WIDE)] * 2 + [shape(rows, cols)] * 2, [], 0, "core_sum", 1, own, got,
        after=after,
    )


def half_sum_kernel(left, got_left, right, got_right, left_keep, right_keep, left_out, right_out):
    rows = left_keep.shape[0]
    for mine, got, keep, out in ((left, got_left, left_keep, left_out), (right, got_right, right_keep, right_out)):
        keep[...] = mine[:rows, :] + got[:rows, :].astype(WIDE)
        out[...] = (mine[rows:, :] + got[rows:, :].astype(WIDE)).astype(LOW)


def half_sum(left, right, got, after=()):
    rows, cols = left.shape[0] // 2, left.shape[1]
    return whole_call(
        half_sum_kernel, [shape(rows, cols, WIDE)] * 2 + [shape(rows, cols)] * 2, [], 0, "half_sum", 1,
        left, got[0], right, got[1], after=after,
    )


def last_sum_kernel(left, got_left, right, got_right, keep, *outs):
    unit, cut = keep.shape[0], left.shape[1]
    for lo, mine, got in ((0, left, got_left), (cut, right, got_right)):
        total = mine[...] + got[...].astype(WIDE)
        keep[:, lo : lo + cut] = total[:unit]
        for i, out in enumerate(outs):
            out[:, lo : lo + cut] = total[unit * (i + 1) : unit * (i + 2)].astype(LOW)


def last_sum(left, right, got, after=()):
    unit, cols = left.shape[0] // 4, 2 * left.shape[1]
    return whole_call(
        last_sum_kernel, [shape(unit, cols, WIDE)] + [shape(unit, cols)] * 3, [], 0, "last_sum", 1,
        left, got[0], right, got[1], after=after,
    )


def cast_kernel(values, out):
    out[...] = values[...].astype(LOW)


def cast(values, after=()):
    return whole_call(cast_kernel, [shape(*values.shape)], [], 0, "cast", 1, values, after=after)[0]


def vec_core_kernel(blocks, got, *outs):
    half = got.shape[0]
    total = blocks[:half, :] + got[...]
    rows = half // 4
    for k, out in enumerate(outs):
        out[...] = total[rows * k : rows * (k + 1), :]


def vec_core(blocks, got, after=()):
    rows, cols = got.shape
    return whole_call(
        vec_core_kernel, [shape(rows // 4, cols, WIDE)] * 4, [], 0, "vec_core", 1, blocks, got, after=after
    )


def vec_plane_kernel(mine, a, b, c, *outs):
    total = mine[...] + a[...] + b[...] + c[...]
    for k, out in enumerate(outs):
        out[...] = total[k : k + 1, :]


def vec_plane(mine, got, after=()):
    return whole_call(
        vec_plane_kernel, [shape(1, mine.shape[1], WIDE)] * 4, [], 0, "vec_plane", 1, mine, *got, after=after
    )


def swap(value, bits):
    pairs = [(i, i ^ bits) for i in range(32)]
    return lax.ppermute(value, AXES, pairs)


def tie(values, *first):
    return lax.optimization_barrier((tuple(values), first))[0]


class Flow:
    def __init__(self, steps):
        self.steps = steps
        self.next = next(steps)[:2]

    def issue(self, start=()):
        values, bits = self.next
        values = tie(values, start)
        self.got = tuple(swap(value, bit) for value, bit in zip(values, bits))
        return self.got

    def land(self, end=(), behind=()):
        values, *bits = self.steps.send((tie(self.got, end), tuple(behind)))
        if values is None:
            return bits[0]
        self.next = (values, bits[0])
        return bits[1]


def spread(block):
    got, behind = yield (block,) * 3, (8, 16, 24)
    left, right = near_pieces((block,) + got, behind)
    got, behind = yield (left, right), (2, 4), (left, right)
    left, right = first_pieces(left, right, got, behind)
    got, behind = yield (left, right), (4, 2), (left, right)
    own = second_pieces(left, right, got, behind)
    got, _ = yield (own,), (1,), (own,)
    yield None, (own, got[0])


def collect(pieces):
    (got,), behind = yield (pieces[1],), (1,)
    left, right, *out = ready = core_sum(pieces[0], got, behind)
    got, behind = yield out, (4, 2), tuple(ready)
    left, right, *out = ready = half_sum(left, right, got, behind)
    got, behind = yield out, (2, 4), tuple(ready)
    total, *out = ready = last_sum(left, right, got, behind)
    got, _ = yield out, (8, 16, 24), tuple(ready)
    yield None, (sum((z.astype(WIDE) for z in got), total),)


def collect_vec(blocks):
    (got,), behind = yield (blocks[blocks.shape[0] // 2 :],), (1,)
    mine, *out = ready = vec_core(blocks, got, behind)
    got, behind = yield out, (2, 4, 6), tuple(ready)
    mine, *out = ready = vec_plane(mine, got, behind)
    got, _ = yield out, (8, 16, 24), tuple(ready)
    yield None, (sum(got, mine).reshape(-1),)


def stack(whole):
    half, cut = whole.shape[0] // 2, whole.shape[1] // 2
    return tuple(jnp.concatenate([z[:, :cut], z[:, cut:]], axis=0) for z in (whole[:half], whole[half:]))


def unstack(pieces):
    half = pieces[0].shape[0] // 2
    return jnp.concatenate([jnp.concatenate([z[:half], z[half:]], axis=1) for z in pieces], axis=0)


class Whole:
    def __init__(self, result):
        self.result = result

    def issue(self, start=()):
        return ()

    def land(self, end=(), behind=()):
        return self.result


def spread_any(block):
    return stack(lax.all_gather(block, AXES, axis=0, tiled=True))


def collect_any(pieces):
    return (lax.psum_scatter(unstack(pieces), AXES, scatter_dimension=0, tiled=True).astype(WIDE),)


def rearrange(whole, order, shards):
    return jnp.take(whole.reshape(shards, -1, whole.shape[1]), order, axis=0, mode="clip").reshape(whole.shape)


def adamw(master, moment_one, moment_two, gradient, step_rate, decay_rate):
    first_new = BETA_ONE * moment_one + (1.0 - BETA_ONE) * gradient
    second_new = BETA_TWO * moment_two + (1.0 - BETA_TWO) * gradient * gradient
    first_hat = first_new / (1.0 - BETA_ONE**STEP)
    second_hat = second_new / (1.0 - BETA_TWO**STEP)
    master_new = master - step_rate * (
        first_hat / (jnp.sqrt(second_hat) + ADAM_EPS) + decay_rate * master
    )
    return (first_new, second_new, master_new)


def local(
    tokens_in, cotangent, segments, tile_sides, valid_slots, owners,
    master_qkv, master_out, master_up, master_down, master_vec,
    first_qkv, first_out, first_up, first_down, first_vec,
    second_qkv, second_out, second_up, second_down, second_vec,
):
    shards = lax.axis_size(AXES)
    near = shards == 32
    unit = D // shards
    per_row = master_vec.shape[0] // unit
    share = master_vec.shape[0]
    ids = jnp.arange(shards, dtype=jnp.int32)
    if near:
        away = owners ^ lax.axis_index(AXES).astype(jnp.int32)
        place = (away >> 3) + 4 * ((away >> 1) & 1) + 8 * ((away >> 2) & 1) + 16 * (away & 1)
        place_down = place
    else:
        place = owners
        place_down = jnp.arange(32, dtype=jnp.int32)
    inverse = jnp.sum(ids[:, None] * (place[:, None] == ids[None, :]), axis=0)
    target = (place[:, None] * unit + jnp.arange(unit, dtype=jnp.int32)[None, :]).reshape(-1)
    order = (target[:, None] == jnp.arange(D, dtype=jnp.int32)[None, :]).astype(LOW)

    def gather(block):
        return Flow(spread(block)) if near else Whole(spread_any(block))

    def scatter(pieces):
        return Flow(collect(pieces)) if near else Whole(collect_any(pieces))

    vec_block = jnp.pad(master_vec.reshape(unit, per_row), ((0, 0), (0, 128 - per_row)))
    block_one = jnp.concatenate(
        [master_qkv[:, :CUT_ONE], vec_block, master_qkv[:, CUT_ONE:], jnp.zeros_like(vec_block)], axis=1
    )
    spans, far = tables(segments, tile_sides, valid_slots)
    slopes = LOG2E * jnp.exp2(-8.0 * (jnp.arange(HEADS, dtype=jnp.int32).astype(WIDE) + 1.0) / HEADS)
    one = gather(block_one.astype(LOW))
    two = gather(jnp.concatenate([master_out, master_up], axis=1).astype(LOW))
    one.issue()
    done = one.land((far, spans, slopes, order))
    one.issue(done)
    done = one.land()
    sent = one.issue(done) + two.issue(done)
    done = one.land()
    done = done + two.land(sent + done)
    one.issue(done)
    sent = two.issue(done)
    one = one.land()

    x = tokens_in[0]
    dy = cotangent[0]
    act_one, qkv, vec = project(x, order, one)
    done = two.land((qkv,))
    if near:
        three = gather(master_down.astype(LOW))
    else:
        whole = lax.all_gather(master_down.astype(LOW), AXES, axis=0, tiled=True)
        three = Whole(stack(rearrange(whole, owners, shards)))
    two.issue(done)
    mixed_0, probs_0 = attend(0, qkv, far, spans, slopes, done)
    three.issue((mixed_0,))
    done = two.land((mixed_0,))
    done = done + three.land(done)
    sent = two.issue(done) + three.issue(done)
    mixed_1, probs_1 = attend(3, qkv, far, spans, slopes, done + (mixed_0,))
    done = three.land((mixed_1,) + sent)
    two = two.land((mixed_1,) + sent)
    three.issue(done + two[1:])
    mixed, hidden, act_two, gelu, gelu_slope = upward(x, (mixed_0, mixed_1), vec, order, two, done)
    grad_three = down_grad(place_down, gelu, dy)
    done = three.land(tuple(grad_three))
    three.issue(done)
    three = three.land()
    if not near:
        back = jnp.sum(ids[:, None] * (owners[:, None] == ids[None, :]), axis=0)
        grad_three = stack(rearrange(unstack(grad_three), back, shards))
    flow_three = scatter(grad_three)
    flow_three.issue((three[1],))
    block_out, dur, sums_up = downward(place_down, vec, gelu, gelu_slope, dy, hidden, three)
    done = flow_three.land((dur,))
    flow_three.issue(done)
    dh, dh_low, dmixed, sums = hidden_grad(vec, order, dur, dy, hidden, two, done)
    grad_two = two_grad(mixed, act_two, dh_low, dur)
    done = flow_three.land(tuple(grad_two)) + tuple(grad_two)
    flow_two = scatter(grad_two)
    sent = flow_three.issue(done) + flow_two.issue(done)
    d0 = attend_back(0, qkv, dmixed, probs_0, spans, done)
    done = flow_two.land(tuple(d0) + sent)
    done = done + flow_three.land(tuple(d0) + sent, done)
    sent = flow_two.issue(done) + flow_three.issue(done)
    d1 = attend_back(3, qkv, dmixed, probs_1, spans, done + tuple(d0))
    d = [z for pair in zip(d0, d1) for z in pair]
    grad_one = one_grad(act_one, d)
    dact = input_back(order, d, one, tuple(grad_one))
    done = (dact,) + tuple(grad_one) + sent
    sum_three, = flow_three.land(done)
    done = flow_two.land(done)
    flow_one = scatter(grad_one)
    sent = flow_one.issue(done) + flow_two.issue(done)
    tokens_grad, sums_one = input_grad(x, vec, dact, dh, done)
    vector_grad = jnp.concatenate([sums_one[:2], sums[:3], sums_up[:4], sums[3:4]], axis=0)
    blocks = jnp.take(vector_grad.reshape(shards, share), inverse, axis=0, mode="clip")
    if near:
        flow_vec = Flow(collect_vec(blocks))
    else:
        flow_vec = Whole((lax.psum_scatter(blocks.reshape(-1), AXES, scatter_dimension=0, tiled=True),))
    done = flow_one.land((blocks,) + sent) + flow_two.land((blocks,) + sent)
    sent = flow_one.issue(done) + flow_two.issue(done) + flow_vec.issue(done)
    done = flow_one.land(sent)
    sum_two, = flow_two.land(sent)
    first = flow_one.issue(done)[:1]
    flow_vec.land(done)
    flow_vec.issue(first)
    upd_down = adamw(master_down, first_down, second_down, sum_three, RATE_MATRIX, DECAY_MATRIX)
    done = flow_one.land()
    first = flow_one.issue(done)[:1]
    flow_vec.land(done)
    flow_vec.issue(first)
    upd_out = adamw(master_out, first_out, second_out, sum_two[:, :D], RATE_MATRIX, DECAY_MATRIX)
    upd_up = adamw(master_up, first_up, second_up, sum_two[:, D:], RATE_MATRIX, DECAY_MATRIX)
    sum_one, = flow_one.land(upd_out + upd_up)
    sum_vec, = flow_vec.land()
    upd_qkv = adamw(master_qkv, first_qkv, second_qkv, sum_one, RATE_MATRIX, DECAY_MATRIX)
    upd_vec = adamw(master_vec, first_vec, second_vec, sum_vec, RATE_VECTOR, 0.0)
    return (
        (block_out[None], tokens_grad[None]) + upd_qkv + upd_out + upd_up + upd_down + upd_vec
    )


def solution(mesh):
    rows = P(AXES, None)
    flat = P(AXES)
    deep = P(AXES, None, None)
    stored = (rows,) * 4 + (flat,)
    in_specs = (deep,) * 2 + (rows,) * 3 + (P(),) + stored * 3
    out_specs = (deep,) * 2 + (rows,) * 12 + (flat,) * 3
    return jax.shard_map(local, mesh=mesh, in_specs=in_specs, out_specs=out_specs, check_vma=False)
```

```python
import functools

import jax
import jax.numpy as jnp
from jax import lax
from jax.experimental import pallas as pl
from jax.experimental.pallas import tpu as pltpu
from jax.sharding import PartitionSpec as P

D = 768
HEADS = 12
FF = 3072
STEP = 10
HALF = 384
WIN = 256
SMALL = 160
LARGE = 240
LOG2E = 1.4426950408889634
CUT_ONE = 1152
WIDTH_ONE = 1280
WIDTH_TWO = 1920
WIDTH_THREE = 384

EPSILON = 1e-05
BETA_ONE = 0.9
BETA_TWO = 0.999
ADAM_EPS = 1e-08
RATE_MATRIX = 0.05
DECAY_MATRIX = 0.05
RATE_VECTOR = 0.3

AXES = ("dp", "fsdp")
LOW = jnp.bfloat16
WIDE = jnp.float32
VMEM_BYTES = 12 * 2**20


def nn(left, right):
    return lax.dot_general(left, right, (((1,), (0,)), ((), ())), preferred_element_type=WIDE)


def nt(left, right):
    return lax.dot_general(left, right, (((1,), (1,)), ((), ())), preferred_element_type=WIDE)


def tn(left, right):
    return lax.dot_general(left, right, (((0,), (0,)), ((), ())), preferred_element_type=WIDE)


def shape(rows, cols, kind=LOW):
    return jax.ShapeDtypeStruct((rows, cols), kind)


def later(kernel, inputs, extra):
    return lambda *refs: kernel(*refs[:inputs], *refs[inputs + extra :])


def whole_call(kernel, outs, scratch, smem, name, flops, *args, anywhere=(), after=()):
    specs = []
    for i in range(len(args)):
        space = pltpu.SMEM if i < smem else pl.ANY if i in anywhere else pltpu.VMEM
        specs.append(pl.BlockSpec(memory_space=space))
    moved = sum(a.size * a.dtype.itemsize for a in args) + sum(o.size * o.dtype.itemsize for o in outs)
    return pl.pallas_call(
        later(kernel, len(args), len(after)),
        in_specs=specs + [pl.BlockSpec(memory_space=pl.ANY)] * len(after),
        out_specs=[pl.BlockSpec(memory_space=pltpu.VMEM)] * len(outs),
        out_shape=outs,
        scratch_shapes=scratch,
        compiler_params=pltpu.CompilerParams(vmem_limit_bytes=VMEM_BYTES),
        cost_estimate=pl.CostEstimate(flops=flops, bytes_accessed=moved, transcendentals=0),
        name=name,
    )(*args, *after)


def over_rows(count, step, body, init=None):
    return lax.fori_loop(0, count // step, lambda i, c: body(pl.ds(pl.multiple_of(i * step, step), step), c), init)


def normal(values):
    centre = values - jnp.mean(values, axis=-1, keepdims=True)
    rstd = lax.rsqrt(jnp.mean(centre * centre, axis=-1, keepdims=True) + EPSILON)
    return centre * rstd, rstd


def both(pair, side, lo, width):
    rows = slice(HALF * side, HALF * (side + 1))
    return jnp.concatenate([z[rows, lo : lo + width] for z in pair], axis=0)


def qkv_kernel(x_ref, order_ref, own, other, a_ref, qkv_ref, vec_ref, tmp, wide):
    moved = jnp.concatenate([z[:HALF, CUT_ONE:] for z in (own, other)], axis=0)
    wide[...] = nn(order_ref[...], moved)
    vec_ref[...] = jnp.zeros_like(vec_ref)
    for k in range(10):
        first = min(D * k // 10 // 8 * 8, D - 88)

        def tenths(rows):
            entry = lax.broadcasted_iota(jnp.int32, (rows, D), 1) + D * k
            tenth = (entry * 52429) >> 19
            return tenth, entry - 10 * tenth, lax.broadcasted_iota(jnp.int32, (rows, D), 0)

        _, column, row = tenths(128)
        picked = nn(wide[first : first + 88, :].astype(LOW), (row == column).astype(LOW))
        tenth, _, row = tenths(88)
        vec_ref[k : k + 1, :] = jnp.sum(jnp.where(row + first == tenth, picked, 0.0), axis=0, keepdims=True)
    gain, shift = vec_ref[0:1, :], vec_ref[1:2, :]

    def norm(rows, _):
        tmp[rows, :] = (normal(x_ref[rows, :].astype(WIDE))[0] * gain + shift).astype(LOW)

    over_rows(x_ref.shape[0], 144, norm)
    a_ref[...] = nn(tmp[...], order_ref[...]).astype(LOW)
    for col in range(0, 3 * D, 384):
        w = both((own, other), *divmod(col, CUT_ONE), 384)
        qkv_ref[:, col : col + 384] = nn(a_ref[...], w).astype(LOW)


def project(x, order, one, after=()):
    n = x.shape[0]
    return whole_call(
        qkv_kernel, [shape(n, D), shape(n, 3 * D), shape(16, D, WIDE)],
        [pltpu.VMEM((n, D), LOW), pltpu.VMEM((D, 128), WIDE)], 0, "project",
        2 * n * D * (4 * D), x, order, *one, after=after,
    )


def each_tile(spans, body):
    def step(t, carry):
        for kind, rows in ((1, SMALL), (2, LARGE)):

            @pl.when(spans[t, 4] == kind)
            def _():
                body(t, pl.multiple_of(spans[t, 2], 16), rows, pl.multiple_of(spans[t, 3], 16))

        return carry

    lax.fori_loop(0, 4, step, 0)


def padding_rows(spans, shape_):
    return lax.broadcasted_iota(jnp.int32, shape_, 0) >= spans[4, 0]


def own_half(values, e):
    lane = lax.broadcasted_iota(jnp.int32, values.shape, 1)
    return jnp.where((lane < 64) if e == 0 else (lane >= 64), values, jnp.zeros_like(values))


def attend_kernel(base, spans, slopes, qkv_ref, far_ref, o_ref, p_ref, acc):
    acc[...] = jnp.zeros_like(acc)

    def tile(t, at, count, key):
        rows, keys = pl.ds(at, count), pl.ds(key, WIN)
        row = lax.broadcasted_iota(jnp.int32, (count, 1), 0) + at
        inside = ((row >= spans[t, 0]) & (row < spans[t, 1])).astype(WIDE)
        far = far_ref[t, :count, :]
        for pair in range(3):
            col = (base + pair) * 128
            q, k, v = [qkv_ref[z, col + i * D : col + i * D + 128] for i, z in enumerate((rows, keys, keys))]
            out = None
            for e in range(2):
                s = nt(q, own_half(k, e)) * (0.125 * LOG2E) - slopes[2 * (base + pair) + e] * far
                p = jnp.exp2(s - jnp.max(s, axis=1, keepdims=True))
                p = (p * (inside / jnp.sum(p, axis=1, keepdims=True))).astype(LOW)
                p_ref[t, 2 * pair + e, :count, :] = p
                part = nn(p, own_half(v, e))
                out = part if out is None else out + part
            acc[rows, pair * 128 : pair * 128 + 128] += out

    each_tile(spans, tile)
    v = qkv_ref[:, base * 128 + 2 * D : base * 128 + 2 * D + HALF]
    o_ref[...] = jnp.where(padding_rows(spans, v.shape), v, acc[...].astype(LOW))


def attend(base, qkv, far, spans, slopes, after=()):
    n = qkv.shape[0]
    return whole_call(
        functools.partial(attend_kernel, base),
        [shape(n, HALF), jax.ShapeDtypeStruct((4, HEADS // 2, LARGE, WIN), LOW)],
        [pltpu.VMEM((n, HALF), WIDE)], 2, "attend", 9 * 10**9, spans, slopes, qkv, far, after=after,
    )


def attend_back_kernel(base, spans, qkv_ref, g_ref, p_ref, dq_ref, dk_ref, dv_ref, aq, ak, av):
    for acc in (aq, ak, av):
        acc[...] = jnp.zeros_like(acc)

    def tile(t, at, count, key):
        rows, keys = pl.ds(at, count), pl.ds(key, WIN)
        for pair in range(3):
            col = (base + pair) * 128
            q, k, v = [qkv_ref[z, col + i * D : col + i * D + 128] for i, z in enumerate((rows, keys, keys))]
            g = g_ref[rows, col : col + 128]
            sums = None
            for e in range(2):
                ge = own_half(g, e)
                p = p_ref[t, 2 * pair + e, :count, :]
                wide = p.astype(WIDE)
                d = wide * nt(ge * 0.125, v)
                d = (d - wide * jnp.sum(d, axis=1, keepdims=True)).astype(LOW)
                parts = (nn(d, own_half(k, e)), tn(d, own_half(q, e)), tn(p, ge))
                sums = parts if sums is None else tuple(a + b for a, b in zip(sums, parts))
            part = slice(pair * 128, pair * 128 + 128)
            aq[rows, part] += sums[0]
            ak[keys, part] += sums[1]
            av[keys, part] += sums[2]

    each_tile(spans, tile)
    dq_ref[...] = aq[...].astype(LOW)
    dk_ref[...] = ak[...].astype(LOW)
    g = g_ref[:, base * 128 : base * 128 + HALF]
    dv_ref[...] = jnp.where(padding_rows(spans, g.shape), g, av[...].astype(LOW))


def attend_back(base, qkv, grad, probs, spans, after=()):
    n = qkv.shape[0]
    return whole_call(
        functools.partial(attend_back_kernel, base), [shape(n, HALF)] * 3, [pltpu.VMEM((n, HALF), WIDE)] * 3, 1,
        "attend_back", 12 * 10**9, spans, qkv, grad, probs, after=after,
    )


def tables_kernel(seg_ref, side_ref, valid_ref, spans, far_ref):
    n = seg_ref.shape[1]
    seg, side, valid = [z[...].astype(WIDE) for z in (seg_ref, side_ref, valid_ref)]
    live = jnp.sum(valid).astype(jnp.int32)
    for z in range(5):
        spans[4, z] = live
    for t in range(4):
        low = jnp.sum((seg < t).astype(WIDE)).astype(jnp.int32)
        high = jnp.sum((seg <= t).astype(WIDE)).astype(jnp.int32)
        width = jnp.max(jnp.where(seg == t, side, 1.0))
        small = high - low <= SMALL - 16
        start = low // 16 * 16
        at = jnp.minimum(start, jnp.where(small, n - SMALL, n - LARGE))
        key = jnp.minimum(start, n - WIN)
        kind = jnp.where((high > low) & (low < live), jnp.where(small, 1, 2), 0)
        for z, value in enumerate((low, high, at, key, kind)):
            spans[t, z] = value

        def places(first, shape_, dim):
            slot = lax.broadcasted_iota(jnp.int32, shape_, dim) + first
            place = (slot - low).astype(WIDE)
            row = jnp.floor((place + 0.5) / width)
            return (slot >= low) & (slot < high), row, place - row * width

        inside, row, col = places(at, (LARGE, 1), 0)
        inside_key, row_key, col_key = places(key, (1, WIN), 1)
        down, along = row - row_key, col - col_key
        far_ref[t] = jnp.where(inside & inside_key, jnp.sqrt(down * down + along * along), 1e12)


def tables(seg, side, valid):
    vmem, smem = [pl.BlockSpec(memory_space=z) for z in (pltpu.VMEM, pltpu.SMEM)]
    return pl.pallas_call(
        tables_kernel,
        in_specs=[vmem] * 3,
        out_specs=[smem, vmem],
        out_shape=[jax.ShapeDtypeStruct((5, 5), jnp.int32), jax.ShapeDtypeStruct((4, LARGE, WIN), WIDE)],
        compiler_params=pltpu.CompilerParams(vmem_limit_bytes=VMEM_BYTES),
        name="tables",
    )(seg, side, valid)


def bell(u):
    share = 0.5 + 0.5 * lax.erf(u * 0.7071067811865476)
    return u * share, share + u * (jnp.exp2(u * u * -0.7213475204444817) * 0.3989422804014327)


def up_kernel(x_ref, o0_ref, o1_ref, vec_ref, order_ref, own, other, mixed_ref, h_ref, a_ref, gl_ref, gp_ref, tmp):
    mixed_ref[...] = (
        nn(o0_ref[...], order_ref[:HALF, :]) + nn(o1_ref[...], order_ref[HALF:, :])
    ).astype(LOW)
    for col in (0, 384):
        part = slice(col, col + 384)
        h_ref[:, part] = x_ref[:, part].astype(WIDE) + nn(mixed_ref[...], both((own, other), 0, col, 384)) + vec_ref[2:3, part]
    gain, shift = vec_ref[3:4, :], vec_ref[4:5, :]

    def norm(rows, _):
        tmp[rows, :] = (normal(h_ref[rows, :])[0] * gain + shift).astype(LOW)

    over_rows(x_ref.shape[0], 144, norm)
    a_ref[...] = nn(tmp[...], order_ref[...]).astype(LOW)
    for col in range(0, FF, 384):
        k = 5 + col // D
        u = nn(a_ref[...], both((own, other), *divmod(col + D, WIDTH_TWO), 384)) + vec_ref[k : k + 1, col % D : col % D + 384]
        value, slope = bell(u)
        gl_ref[:, col : col + 384] = value.astype(LOW)
        gp_ref[:, col : col + 384] = slope.astype(LOW)


def upward(x, o, vec, order, two, after=()):
    n = x.shape[0]
    return whole_call(
        up_kernel, [shape(n, D), shape(n, D, WIDE), shape(n, D), shape(n, FF), shape(n, FF)],
        [pltpu.VMEM((n, D), LOW)], 0, "upward", 2 * n * D * (7 * D) * 2, x, *o, vec, order, *two,
        after=after,
    )


def fetch_down(place, own, other, wd, sem):
    def copies(b, piece, row):
        dst = pl.ds(pl.multiple_of(b * 96, 96), 96)
        return [
            pltpu.make_async_copy(
                piece.at[pl.ds(pl.multiple_of(row * 96 + side * (FF // 2), 96), 96), :],
                wd.at[dst, pl.ds(side * WIDTH_THREE, WIDTH_THREE)],
                sem,
            )
            for side in (0, 1)
        ]

    def begin(b, carry):
        p = place[b]
        pl.when(p < 16)(lambda: [z.start() for z in copies(b, own, p)] and None)
        pl.when(p >= 16)(lambda: [z.start() for z in copies(b, other, p - 16)] and None)
        return carry

    def finish(b, carry):
        for z in copies(b, own, 0):
            z.wait()
        return carry

    lax.fori_loop(0, 32, begin, 0)
    lax.fori_loop(0, 32, finish, 0)


def down_kernel(place, gp_ref, dy_ref, own, other, dur_ref, vg_ref, wd, sem):
    fetch_down(place, own, other, wd, sem)
    for col in range(0, FF, 384):
        part = slice(col, col + 384)
        du = nt(dy_ref[...], wd[part, :]) * gp_ref[:, part].astype(WIDE)
        dur_ref[:, part] = du.astype(LOW)
        k = col // D
        vg_ref[k : k + 1, col % D : col % D + 384] = jnp.sum(du, axis=0, keepdims=True)


def down_back(place, gp, dy, three, after=()):
    n = dy.shape[0]
    return whole_call(
        down_kernel, [shape(n, FF), shape(8, D, WIDE)], [pltpu.VMEM((FF, D), LOW), pltpu.SemaphoreType.DMA], 1,
        "down_back", 2 * n * D * (4 * D), place, gp, dy, *three, anywhere=(3, 4), after=after,
    )


def down_out_kernel(place, vec_ref, gl_ref, h_ref, own, other, out_ref, wd, sem):
    fetch_down(place, own, other, wd, sem)
    for col in (0, 384):
        part = slice(col, col + 384)
        out_ref[:, part] = (h_ref[:, part] + nn(gl_ref[...], wd[:, part]) + vec_ref[9:10, part]).astype(LOW)


def down_out(place, vec, gl, h, three, after=()):
    n = h.shape[0]
    return whole_call(
        down_out_kernel, [shape(n, D)], [pltpu.VMEM((FF, D), LOW), pltpu.SemaphoreType.DMA], 1,
        "down_out", 2 * n * D * (4 * D), place, vec, gl, h, *three, anywhere=(4, 5), after=after,
    )[0]


def hidden_kernel(vec_ref, order_ref, dur_ref, dy_ref, h_ref, own, other, dh_ref, dhr_ref, dor_ref, vg_ref, tmp):
    split = WIDTH_TWO - D
    for i, w in enumerate((own, other)):
        tmp[:, HALF * i : HALF * (i + 1)] = (
            nt(dur_ref[:, :split], w[:HALF, D:]) + nt(dur_ref[:, split:], w[HALF:, :])
        ).astype(LOW)
    dh_ref[...] = nt(tmp[...], order_ref[...])
    gain = vec_ref[3:4, :]

    def step(rows, sums):
        e = dh_ref[rows, :]
        dy = dy_ref[rows, :].astype(WIDE)
        n, rstd = normal(h_ref[rows, :])
        w = e * gain
        dh = dy + rstd * (w - jnp.mean(w, axis=-1, keepdims=True) - n * jnp.mean(w * n, axis=-1, keepdims=True))
        dh_ref[rows, :] = dh
        dhr_ref[rows, :] = dh.astype(LOW)
        return tuple(s + jnp.sum(z.reshape(-1, 8, D), axis=0) for s, z in zip(sums, (dh, e * n, e, dy)))

    zero = jnp.zeros((8, D), WIDE)
    sums = over_rows(h_ref.shape[0], 144, step, (zero,) * 4)
    for k, s in enumerate(sums):
        vg_ref[k : k + 1, :] = jnp.sum(s, axis=0, keepdims=True)
    for i, w in enumerate((own, other)):
        tmp[:, HALF * i : HALF * (i + 1)] = nt(dhr_ref[...], w[:HALF, :D]).astype(LOW)
    dor_ref[...] = nt(tmp[...], order_ref[...]).astype(LOW)


def hidden_grad(vec, order, dur, dy, h, two, after=()):
    n = h.shape[0]
    return whole_call(
        hidden_kernel, [shape(n, D, WIDE), shape(n, D), shape(n, D), shape(8, D, WIDE)],
        [pltpu.VMEM((n, D), LOW)], 0, "hidden_grad",
        2 * n * D * (7 * D), vec, order, dur, dy, h, *two, after=after,
    )


def down_grad_kernel(place, gl_ref, dy_ref, own, other):
    for c in range(8):
        t = tn(gl_ref[:, 384 * c : 384 * (c + 1)], dy_ref[...]).astype(LOW)
        for i in range(4):
            p = place[4 * c + i]

            def put(piece, row):
                for side in (0, 1):
                    rows = pl.ds(pl.multiple_of(row * 96 + side * (FF // 2), 96), 96)
                    piece[rows, :] = t[96 * i : 96 * (i + 1), side * WIDTH_THREE : (side + 1) * WIDTH_THREE]

            pl.when(p < 16)(lambda: put(own, p))
            pl.when(p >= 16)(lambda: put(other, p - 16))


def down_grad(place, gl, dy, after=()):
    n = dy.shape[0]
    return whole_call(down_grad_kernel, [shape(FF, WIDTH_THREE)] * 2, [], 1, "down_grad", 2 * n * D * FF, place, gl, dy, after=after)


def two_grad_kernel(mixed_ref, a_ref, dhr_ref, dur_ref, own, other):
    for col in range(0, D + FF, 384):
        left, right = (mixed_ref, dhr_ref[:, col : col + 384]) if col < D else (a_ref, dur_ref[:, col - D : col - D + 384])
        t = tn(left[...], right).astype(LOW)
        side, lo = divmod(col, WIDTH_TWO)
        own[HALF * side : HALF * (side + 1), lo : lo + 384] = t[:HALF]
        other[HALF * side : HALF * (side + 1), lo : lo + 384] = t[HALF:]


def two_grad(mixed, a, dhr, dur, after=()):
    n = a.shape[0]
    return whole_call(two_grad_kernel, [shape(D, WIDTH_TWO)] * 2, [], 0, "two_grad", 2 * n * D * (D + FF), mixed, a, dhr, dur,
                      after=after)


def one_grad_kernel(a_ref, order_ref, first_ref, mid_ref, up_ref, *refs):
    halves, (own, other, wide) = refs[:6], refs[6:]
    wide[...] = jnp.zeros_like(wide)
    rows = [first_ref[0:1, :], first_ref[1:2, :]] + [mid_ref[i : i + 1, :] for i in range(3)]
    rows = rows + [up_ref[i : i + 1, :] for i in range(4)] + [mid_ref[3:4, :]]
    for k, values in enumerate(rows):
        first = min(D * k // 10 // 8 * 8, D - 88)
        entry = lax.broadcasted_iota(jnp.int32, (88, D), 1) + D * k
        row = lax.broadcasted_iota(jnp.int32, (88, D), 0) + first
        spread_out = jnp.where(row == (entry * 52429) >> 19, values, 0.0).astype(LOW)
        entry = lax.broadcasted_iota(jnp.int32, (D, 128), 0) + D * k
        column = entry - 10 * ((entry * 52429) >> 19)
        pick = (lax.broadcasted_iota(jnp.int32, (D, 128), 1) == column).astype(LOW)
        wide[first : first + 88, :] += nn(spread_out, pick)
    moved = tn(order_ref[...], wide[...].astype(LOW)).astype(LOW)
    for i, out in enumerate((own, other)):
        out[:HALF, CUT_ONE:] = moved[HALF * i : HALF * (i + 1), :]
        out[HALF:, CUT_ONE:] = jnp.zeros((HALF, WIDTH_ONE - CUT_ONE), LOW)
    for i, half in enumerate(halves):
        t = tn(a_ref[...], half[...]).astype(LOW)
        side, lo = divmod(384 * i, CUT_ONE)
        own[HALF * side : HALF * (side + 1), lo : lo + 384] = t[:HALF]
        other[HALF * side : HALF * (side + 1), lo : lo + 384] = t[HALF:]


def one_grad(a, order, sums, d, after=()):
    n = a.shape[0]
    return whole_call(
        one_grad_kernel, [shape(D, WIDTH_ONE)] * 2, [pltpu.VMEM((D, 128), WIDE)], 0, "one_grad",
        2 * n * D * 3 * D, a, order, *sums, *d, after=after,
    )


def input_back_kernel(order_ref, q0, q1, k0, k1, v0, v1, own, other, e_ref, tmp):
    for i, w in enumerate((own, other)):
        total = 0.0
        for j, d in enumerate((q0, q1, k0, k1, v0, v1)):
            side, lo = divmod(384 * j, CUT_ONE)
            total = total + nt(d[...], w[HALF * side : HALF * (side + 1), lo : lo + 384])
        tmp[:, HALF * i : HALF * (i + 1)] = total.astype(LOW)
    e_ref[...] = nt(tmp[...], order_ref[...])


def input_back(order, d, one, after=()):
    n = d[0].shape[0]
    return whole_call(
        input_back_kernel, [shape(n, D, WIDE)], [pltpu.VMEM((n, D), LOW)], 0, "input_back",
        2 * n * D * 4 * D, order, *d, *one, after=after,
    )[0]


def input_kernel(x_ref, vec_ref, e_ref, dh_ref, dx_ref, vg_ref):
    gain = vec_ref[0:1, :]

    def step(rows, sums):
        e = e_ref[rows, :]
        n, rstd = normal(x_ref[rows, :].astype(WIDE))
        w = e * gain
        dx_ref[rows, :] = dh_ref[rows, :] + rstd * (
            w - jnp.mean(w, axis=-1, keepdims=True) - n * jnp.mean(w * n, axis=-1, keepdims=True)
        )
        return tuple(s + jnp.sum(z.reshape(-1, 8, D), axis=0) for s, z in zip(sums, (e * n, e)))

    zero = jnp.zeros((8, D), WIDE)
    sums = over_rows(x_ref.shape[0], 144, step, (zero,) * 2)
    for k, s in enumerate(sums):
        vg_ref[k : k + 1, :] = jnp.sum(s, axis=0, keepdims=True)


def input_grad(x, vec, e, dh, after=()):
    n = x.shape[0]
    return whole_call(
        input_kernel, [shape(n, D, WIDE), shape(8, D, WIDE)], [], 0, "input_grad",
        2 * n * D * 3 * D, x, vec, e, dh, after=after,
    )


def near_kernel(a, b, c, d, left_ref, right_ref):
    cut = left_ref.shape[1]
    for out, lo in ((left_ref, 0), (right_ref, cut)):
        out[...] = jnp.concatenate([z[:, lo : lo + cut].astype(WIDE) for z in (a, b, c, d)], axis=0).astype(LOW)


def near_pieces(pieces, after=()):
    rows, cols = pieces[0].shape
    return whole_call(near_kernel, [shape(4 * rows, cols // 2)] * 2, [], 0, "near", 1, *pieces, after=after)


def first_kernel(left, got_left, right, got_right, left_ref, right_ref):
    rows = left.shape[0]
    for out, mine, got in ((left_ref, left, got_left), (right_ref, right, got_right)):
        out[:rows, :] = mine[...]
        out[rows:, :] = got[...]


def first_pieces(left, right, got, after=()):
    rows, cols = left.shape
    return whole_call(
        first_kernel, [shape(2 * rows, cols)] * 2, [], 0, "first", 1, left, got[0], right, got[1], after=after
    )


def second_kernel(left, got, right, far, own_ref):
    rows = left.shape[0]
    half = rows // 2
    own_ref[:rows, :] = left[...]
    own_ref[rows : 2 * rows, :] = got[...]
    for i in (0, 1):
        own_ref[2 * rows + 2 * i * half : 2 * rows + (2 * i + 1) * half, :] = right[i * half : (i + 1) * half, :]
        own_ref[2 * rows + (2 * i + 1) * half : 2 * rows + (2 * i + 2) * half, :] = far[i * half : (i + 1) * half, :]


def second_pieces(left, right, got, after=()):
    rows, cols = left.shape
    return whole_call(
        second_kernel, [shape(4 * rows, cols)], [], 0, "second", 1, left, got[0], right, got[1], after=after
    )[0]


def core_sum_kernel(own, got, left_keep, right_keep, left_out, right_out):
    half = left_keep.shape[0]
    rows = half // 2

    def total(lo, count):
        return own[lo : lo + count, :].astype(WIDE) + got[lo : lo + count, :].astype(WIDE)

    left_keep[...] = total(0, half)
    left_out[...] = total(half, half).astype(LOW)
    for i in (0, 1):
        lo = 2 * half + 2 * i * rows
        right_keep[i * rows : (i + 1) * rows, :] = total(lo, rows)
        right_out[i * rows : (i + 1) * rows, :] = total(lo + rows, rows).astype(LOW)


def core_sum(own, got, after=()):
    rows, cols = own.shape[0] // 4, own.shape[1]
    return whole_call(
        core_sum_kernel, [shape(rows, cols, WIDE)] * 2 + [shape(rows, cols)] * 2, [], 0, "core_sum", 1, own, got,
        after=after,
    )


def half_sum_kernel(left, got_left, right, got_right, left_keep, right_keep, left_out, right_out):
    rows = left_keep.shape[0]
    for mine, got, keep, out in ((left, got_left, left_keep, left_out), (right, got_right, right_keep, right_out)):
        keep[...] = mine[:rows, :] + got[:rows, :].astype(WIDE)
        out[...] = (mine[rows:, :] + got[rows:, :].astype(WIDE)).astype(LOW)


def half_sum(left, right, got, after=()):
    rows, cols = left.shape[0] // 2, left.shape[1]
    return whole_call(
        half_sum_kernel, [shape(rows, cols, WIDE)] * 2 + [shape(rows, cols)] * 2, [], 0, "half_sum", 1,
        left, got[0], right, got[1], after=after,
    )


def last_sum_kernel(left, got_left, right, got_right, keep, *outs):
    unit, cut = keep.shape[0], left.shape[1]
    for lo, mine, got in ((0, left, got_left), (cut, right, got_right)):
        total = mine[...] + got[...].astype(WIDE)
        keep[:, lo : lo + cut] = total[:unit]
        for i, out in enumerate(outs):
            out[:, lo : lo + cut] = total[unit * (i + 1) : unit * (i + 2)].astype(LOW)


def last_sum(left, right, got, after=()):
    unit, cols = left.shape[0] // 4, 2 * left.shape[1]
    return whole_call(
        last_sum_kernel, [shape(unit, cols, WIDE)] + [shape(unit, cols)] * 3, [], 0, "last_sum", 1,
        left, got[0], right, got[1], after=after,
    )


def swap(value, bits):
    pairs = [(i, i ^ bits) for i in range(32)]
    return lax.ppermute(value, AXES, pairs)


def tie(values, *first):
    return lax.optimization_barrier((tuple(values), first))[0]


class Flow:
    def __init__(self, steps):
        self.steps = steps
        self.next = next(steps)[:2]

    def issue(self, start=()):
        values, bits = self.next
        values = tie(values, start)
        self.got = tuple(swap(value, bit) for value, bit in zip(values, bits))
        return self.got

    def land(self, end=()):
        values, *bits = self.steps.send(tie(self.got, end))
        if values is None:
            return bits[0]
        self.next = (values, bits[0])
        return bits[1]


def spread(block):
    got = yield (block,) * 3, (8, 16, 24)
    left, right = near_pieces((block,) + got)
    got = yield (left, right), (2, 4), (left, right)
    left, right = first_pieces(left, right, got)
    got = yield (left, right), (4, 2), (left, right)
    own = second_pieces(left, right, got)
    got = yield (own,), (1,), (own,)
    yield None, (own, got[0])


def collect(pieces):
    (got,) = yield (pieces[1],), (1,)
    left, right, *out = ready = core_sum(pieces[0], got)
    got = yield out, (4, 2), tuple(ready)
    left, right, *out = ready = half_sum(left, right, got)
    got = yield out, (2, 4), tuple(ready)
    total, *out = ready = last_sum(left, right, got)
    got = yield out, (8, 16, 24), tuple(ready)
    yield None, (sum((z.astype(WIDE) for z in got), total),)


def stack(whole):
    half, cut = whole.shape[0] // 2, whole.shape[1] // 2
    return tuple(jnp.concatenate([z[:, :cut], z[:, cut:]], axis=0) for z in (whole[:half], whole[half:]))


def unstack(pieces):
    half = pieces[0].shape[0] // 2
    return jnp.concatenate([jnp.concatenate([z[:half], z[half:]], axis=1) for z in pieces], axis=0)


class Whole:
    def __init__(self, result):
        self.result = result

    def issue(self, start=()):
        return ()

    def land(self, end=()):
        return self.result


def spread_any(block):
    return stack(lax.all_gather(block, AXES, axis=0, tiled=True))


def collect_any(pieces):
    return (lax.psum_scatter(unstack(pieces), AXES, scatter_dimension=0, tiled=True).astype(WIDE),)


def rearrange(whole, order, shards):
    return jnp.take(whole.reshape(shards, -1, whole.shape[1]), order, axis=0, mode="clip").reshape(whole.shape)


def adamw(master, moment_one, moment_two, gradient, step_rate, decay_rate):
    first_new = BETA_ONE * moment_one + (1.0 - BETA_ONE) * gradient
    second_new = BETA_TWO * moment_two + (1.0 - BETA_TWO) * gradient * gradient
    first_hat = first_new / (1.0 - BETA_ONE**STEP)
    second_hat = second_new / (1.0 - BETA_TWO**STEP)
    master_new = master - step_rate * (
        first_hat / (jnp.sqrt(second_hat) + ADAM_EPS) + decay_rate * master
    )
    return (first_new, second_new, master_new)


def local(
    tokens_in, cotangent, segments, tile_sides, valid_slots, owners,
    master_qkv, master_out, master_up, master_down, master_vec,
    first_qkv, first_out, first_up, first_down, first_vec,
    second_qkv, second_out, second_up, second_down, second_vec,
):
    shards = lax.axis_size(AXES)
    near = shards == 32
    unit = D // shards
    per_row = master_vec.shape[0] // unit
    ids = jnp.arange(shards, dtype=jnp.int32)
    if near:
        away = owners ^ lax.axis_index(AXES).astype(jnp.int32)
        place = (away >> 3) + 4 * ((away >> 1) & 1) + 8 * ((away >> 2) & 1) + 16 * (away & 1)
        place_down = place
    else:
        place = owners
        place_down = jnp.arange(32, dtype=jnp.int32)
    target = (place[:, None] * unit + jnp.arange(unit, dtype=jnp.int32)[None, :]).reshape(-1)
    order = (target[:, None] == jnp.arange(D, dtype=jnp.int32)[None, :]).astype(LOW)

    def gather(block):
        return Flow(spread(block)) if near else Whole(spread_any(block))

    def scatter(pieces):
        return Flow(collect(pieces)) if near else Whole(collect_any(pieces))

    vec_block = jnp.pad(master_vec.reshape(unit, per_row), ((0, 0), (0, 128 - per_row)))
    block_one = jnp.concatenate(
        [master_qkv[:, :CUT_ONE], vec_block, master_qkv[:, CUT_ONE:], jnp.zeros_like(vec_block)], axis=1
    )
    spans, far = tables(segments, tile_sides, valid_slots)
    slopes = LOG2E * jnp.exp2(-8.0 * (jnp.arange(HEADS, dtype=jnp.int32).astype(WIDE) + 1.0) / HEADS)
    one = gather(block_one.astype(LOW))
    two = gather(jnp.concatenate([master_out, master_up], axis=1).astype(LOW))
    if near:
        three = gather(master_down.astype(LOW))
    else:
        whole = lax.all_gather(master_down.astype(LOW), AXES, axis=0, tiled=True)
        three = Whole(stack(rearrange(whole, owners, shards)))
    one.issue()
    done = one.land((far, spans, slopes, order))
    one.issue(done)
    done = one.land()
    sent = one.issue(done) + two.issue(done)
    done = one.land()
    done = done + two.land(sent + done)
    one.issue(done)
    sent = two.issue(done)
    one = one.land()

    x = tokens_in[0]
    dy = cotangent[0]
    act_one, qkv, vec = project(x, order, one)
    done = two.land((qkv,))
    sent = two.issue(done) + three.issue(done)
    mixed_0, probs_0 = attend(0, qkv, far, spans, slopes, done)
    done = two.land((mixed_0,))
    done = done + three.land((mixed_0,) + sent + done)
    sent = two.issue(done) + three.issue(done)
    mixed_1, probs_1 = attend(3, qkv, far, spans, slopes, done + (mixed_0,))
    done = three.land((mixed_1,) + sent)
    two = two.land((mixed_1,) + sent)
    three.issue(done + two[1:])
    mixed, hidden, act_two, gelu, gelu_slope = upward(x, (mixed_0, mixed_1), vec, order, two, done)
    grad_three = down_grad(place_down, gelu, dy)
    done = three.land(tuple(grad_three))
    three.issue(done)
    three = three.land()
    if not near:
        back = jnp.sum(ids[:, None] * (owners[:, None] == ids[None, :]), axis=0)
        grad_three = stack(rearrange(unstack(grad_three), back, shards))
    flow_three = scatter(grad_three)
    flow_three.issue((three[1],))
    dur, sums_up = down_back(place_down, gelu_slope, dy, three)
    done = flow_three.land((dur,))
    flow_three.issue(done)
    dh, dh_low, dmixed, sums = hidden_grad(vec, order, dur, dy, hidden, two, done)
    grad_two = two_grad(mixed, act_two, dh_low, dur)
    done = flow_three.land(tuple(grad_two)) + tuple(grad_two)
    flow_two = scatter(grad_two)
    sent = flow_three.issue(done) + flow_two.issue(done)
    d0 = attend_back(0, qkv, dmixed, probs_0, spans, done)
    done = flow_three.land(tuple(d0) + sent) + flow_two.land(tuple(d0) + sent)
    sent = flow_three.issue(done) + flow_two.issue(done)
    d1 = attend_back(3, qkv, dmixed, probs_1, spans, done + tuple(d0))
    d = [z for pair in zip(d0, d1) for z in pair]
    dact = input_back(order, d, one)
    tokens_grad, sums_one = input_grad(x, vec, dact, dh)
    grad_one = one_grad(act_one, order, (sums_one, sums, sums_up), d)
    done = tuple(grad_one) + sent
    sum_three, = flow_three.land(done)
    done = flow_two.land(done)
    flow_one = scatter(grad_one)
    sent = flow_one.issue(done) + flow_two.issue(done)
    block_out = down_out(place_down, vec, gelu, hidden, three, done)
    done = flow_one.land((block_out,) + sent) + flow_two.land((block_out,) + sent)
    sent = flow_one.issue(done) + flow_two.issue(done)
    upd_down = adamw(master_down, first_down, second_down, sum_three, RATE_MATRIX, DECAY_MATRIX)
    sent = sent + upd_down
    done = flow_one.land(sent)
    sum_two, = flow_two.land(sent)
    flow_one.issue(done)
    upd_out = adamw(master_out, first_out, second_out, sum_two[:, :D], RATE_MATRIX, DECAY_MATRIX)
    upd_up = adamw(master_up, first_up, second_up, sum_two[:, D:], RATE_MATRIX, DECAY_MATRIX)
    done = flow_one.land(upd_out)
    flow_one.issue(done)
    sum_one, = flow_one.land(upd_up)
    sum_vec = sum_one[:, CUT_ONE : CUT_ONE + per_row].reshape(-1)
    sum_one = jnp.concatenate([sum_one[:, :CUT_ONE], sum_one[:, WIDTH_ONE : WIDTH_ONE + CUT_ONE]], axis=1)
    upd_qkv = adamw(master_qkv, first_qkv, second_qkv, sum_one, RATE_MATRIX, DECAY_MATRIX)
    upd_vec = adamw(master_vec, first_vec, second_vec, sum_vec, RATE_VECTOR, 0.0)
    return (
        (block_out[None], tokens_grad[None]) + upd_qkv + upd_out + upd_up + upd_down + upd_vec
    )


def solution(mesh):
    rows = P(AXES, None)
    flat = P(AXES)
    deep = P(AXES, None, None)
    stored = (rows,) * 4 + (flat,)
    in_specs = (deep,) * 2 + (rows,) * 3 + (P(),) + stored * 3
    out_specs = (deep,) * 2 + (rows,) * 12 + (flat,) * 3
    return jax.shard_map(local, mesh=mesh, in_specs=in_specs, out_specs=out_specs, check_vma=False)
```

```python
import functools

import jax
import jax.numpy as jnp
from jax import lax
from jax.experimental import pallas as pl
from jax.experimental.pallas import tpu as pltpu
from jax.sharding import PartitionSpec as P

D = 768
HEADS = 12
FF = 3072
STEP = 10
HALF = 384
WIN = 256
SMALL = 160
LARGE = 240
LOG2E = 1.4426950408889634
CUT_ONE = 1152
WIDTH_ONE = 1280
WIDTH_TWO = 1920
WIDTH_THREE = 384

EPSILON = 1e-05
BETA_ONE = 0.9
BETA_TWO = 0.999
ADAM_EPS = 1e-08
RATE_MATRIX = 0.05
DECAY_MATRIX = 0.05
RATE_VECTOR = 0.3

AXES = ("dp", "fsdp")
LOW = jnp.bfloat16
WIDE = jnp.float32
VMEM_BYTES = 7 * 2**20


def nn(left, right):
    return lax.dot_general(left, right, (((1,), (0,)), ((), ())), preferred_element_type=WIDE)


def nt(left, right):
    return lax.dot_general(left, right, (((1,), (1,)), ((), ())), preferred_element_type=WIDE)


def tn(left, right):
    return lax.dot_general(left, right, (((0,), (0,)), ((), ())), preferred_element_type=WIDE)


def shape(rows, cols, kind=LOW):
    return jax.ShapeDtypeStruct((rows, cols), kind)


def later(kernel, inputs, extra):
    return lambda *refs: kernel(*refs[:inputs], *refs[inputs + extra :])


def whole_call(kernel, outs, scratch, smem, name, flops, *args, anywhere=(), after=()):
    specs = []
    for i in range(len(args)):
        space = pltpu.SMEM if i < smem else pl.ANY if i in anywhere else pltpu.VMEM
        specs.append(pl.BlockSpec(memory_space=space))
    moved = sum(a.size * a.dtype.itemsize for a in args) + sum(o.size * o.dtype.itemsize for o in outs)
    return pl.pallas_call(
        later(kernel, len(args), len(after)),
        in_specs=specs + [pl.BlockSpec(memory_space=pl.ANY)] * len(after),
        out_specs=[pl.BlockSpec(memory_space=pltpu.VMEM)] * len(outs),
        out_shape=outs,
        scratch_shapes=scratch,
        compiler_params=pltpu.CompilerParams(vmem_limit_bytes=VMEM_BYTES),
        cost_estimate=pl.CostEstimate(flops=flops, bytes_accessed=moved, transcendentals=0),
        name=name,
    )(*args, *after)


def over_rows(count, step, body, init=None):
    return lax.fori_loop(0, count // step, lambda i, c: body(pl.ds(pl.multiple_of(i * step, step), step), c), init)


def normal(values):
    centre = values - jnp.mean(values, axis=-1, keepdims=True)
    rstd = lax.rsqrt(jnp.mean(centre * centre, axis=-1, keepdims=True) + EPSILON)
    return centre * rstd, rstd


def both(pair, side, lo, width):
    rows = slice(HALF * side, HALF * (side + 1))
    return jnp.concatenate([z[rows, lo : lo + width] for z in pair], axis=0)


def normal_kernel(x_ref, n_ref):
    def norm(rows, _):
        n_ref[rows, :] = normal(x_ref[rows, :].astype(WIDE))[0]

    over_rows(x_ref.shape[0], 144, norm)


def normalized(x):
    return whole_call(normal_kernel, [shape(*x.shape, WIDE)], [], 0, "normalized", 1, x)[0]


def qkv_kernel(n_ref, order_ref, own, other, a_ref, qkv_ref, vec_ref, tmp, wide):
    moved = jnp.concatenate([z[:HALF, CUT_ONE:] for z in (own, other)], axis=0)
    wide[...] = nn(order_ref[...], moved)
    vec_ref[...] = jnp.zeros_like(vec_ref)
    for k in range(10):
        first = min(D * k // 10 // 8 * 8, D - 88)

        def tenths(rows):
            entry = lax.broadcasted_iota(jnp.int32, (rows, D), 1) + D * k
            tenth = (entry * 52429) >> 19
            return tenth, entry - 10 * tenth, lax.broadcasted_iota(jnp.int32, (rows, D), 0)

        _, column, row = tenths(128)
        picked = nn(wide[first : first + 88, :].astype(LOW), (row == column).astype(LOW))
        tenth, _, row = tenths(88)
        vec_ref[k : k + 1, :] = jnp.sum(jnp.where(row + first == tenth, picked, 0.0), axis=0, keepdims=True)
    gain, shift = vec_ref[0:1, :], vec_ref[1:2, :]

    def norm(rows, _):
        tmp[rows, :] = (n_ref[rows, :] * gain + shift).astype(LOW)

    over_rows(n_ref.shape[0], 144, norm)
    a_ref[...] = nn(tmp[...], order_ref[...]).astype(LOW)
    for col in range(0, 3 * D, 384):
        w = both((own, other), *divmod(col, CUT_ONE), 384)
        qkv_ref[:, col : col + 384] = nn(a_ref[...], w).astype(LOW)


def project(normed, order, one, after=()):
    n = normed.shape[0]
    return whole_call(
        qkv_kernel, [shape(n, D), shape(n, 3 * D), shape(16, D, WIDE)],
        [pltpu.VMEM((n, D), LOW), pltpu.VMEM((D, 128), WIDE)], 0, "project",
        2 * n * D * (4 * D), normed, order, *one, after=after,
    )


def each_tile(spans, body):
    def step(t, carry):
        for kind, rows in ((1, SMALL), (2, LARGE)):

            @pl.when(spans[t, 4] == kind)
            def _():
                body(t, pl.multiple_of(spans[t, 2], 16), rows, pl.multiple_of(spans[t, 3], 16))

        return carry

    lax.fori_loop(0, 4, step, 0)


def padding_rows(spans, shape_):
    return lax.broadcasted_iota(jnp.int32, shape_, 0) >= spans[4, 0]


def own_half(values, e):
    lane = lax.broadcasted_iota(jnp.int32, values.shape, 1)
    return jnp.where((lane < 64) if e == 0 else (lane >= 64), values, jnp.zeros_like(values))


def attend_kernel(base, spans, slopes, qkv_ref, far_ref, o_ref, p_ref, acc):
    acc[...] = jnp.zeros_like(acc)

    def tile(t, at, count, key):
        rows, keys = pl.ds(at, count), pl.ds(key, WIN)
        row = lax.broadcasted_iota(jnp.int32, (count, 1), 0) + at
        inside = ((row >= spans[t, 0]) & (row < spans[t, 1])).astype(WIDE)
        far = far_ref[t, :count, :]
        for pair in range(3):
            col = (base + pair) * 128
            q, k, v = [qkv_ref[z, col + i * D : col + i * D + 128] for i, z in enumerate((rows, keys, keys))]
            out = None
            for e in range(2):
                s = nt(q, own_half(k, e)) * (0.125 * LOG2E) - slopes[2 * (base + pair) + e] * far
                p = jnp.exp2(s - jnp.max(s, axis=1, keepdims=True))
                p = (p * (inside / jnp.sum(p, axis=1, keepdims=True))).astype(LOW)
                p_ref[t, 2 * pair + e, :count, :] = p
                part = nn(p, own_half(v, e))
                out = part if out is None else out + part
            acc[rows, pair * 128 : pair * 128 + 128] += out

    each_tile(spans, tile)
    v = qkv_ref[:, base * 128 + 2 * D : base * 128 + 2 * D + HALF]
    o_ref[...] = jnp.where(padding_rows(spans, v.shape), v, acc[...].astype(LOW))


def attend(base, qkv, far, spans, slopes, after=()):
    n = qkv.shape[0]
    return whole_call(
        functools.partial(attend_kernel, base),
        [shape(n, HALF), jax.ShapeDtypeStruct((4, HEADS // 2, LARGE, WIN), LOW)],
        [pltpu.VMEM((n, HALF), WIDE)], 2, "attend", 9 * 10**9, spans, slopes, qkv, far, after=after,
    )


def attend_back_kernel(base, spans, qkv_ref, g_ref, p_ref, dq_ref, dk_ref, dv_ref, aq, ak, av):
    for acc in (aq, ak, av):
        acc[...] = jnp.zeros_like(acc)

    def tile(t, at, count, key):
        rows, keys = pl.ds(at, count), pl.ds(key, WIN)
        for pair in range(3):
            col = (base + pair) * 128
            q, k, v = [qkv_ref[z, col + i * D : col + i * D + 128] for i, z in enumerate((rows, keys, keys))]
            g = g_ref[rows, col : col + 128]
            sums = None
            for e in range(2):
                ge = own_half(g, e)
                p = p_ref[t, 2 * pair + e, :count, :]
                wide = p.astype(WIDE)
                d = wide * nt(ge * 0.125, v)
                d = (d - wide * jnp.sum(d, axis=1, keepdims=True)).astype(LOW)
                parts = (nn(d, own_half(k, e)), tn(d, own_half(q, e)), tn(p, ge))
                sums = parts if sums is None else tuple(a + b for a, b in zip(sums, parts))
            part = slice(pair * 128, pair * 128 + 128)
            aq[rows, part] += sums[0]
            ak[keys, part] += sums[1]
            av[keys, part] += sums[2]

    each_tile(spans, tile)
    dq_ref[...] = aq[...].astype(LOW)
    dk_ref[...] = ak[...].astype(LOW)
    g = g_ref[:, base * 128 : base * 128 + HALF]
    dv_ref[...] = jnp.where(padding_rows(spans, g.shape), g, av[...].astype(LOW))


def attend_back(base, qkv, grad, probs, spans, after=()):
    n = qkv.shape[0]
    return whole_call(
        functools.partial(attend_back_kernel, base), [shape(n, HALF)] * 3, [pltpu.VMEM((n, HALF), WIDE)] * 3, 1,
        "attend_back", 12 * 10**9, spans, qkv, grad, probs, after=after,
    )


def tables_kernel(seg_ref, side_ref, valid_ref, spans, far_ref):
    n = seg_ref.shape[1]
    seg, side, valid = [z[...].astype(WIDE) for z in (seg_ref, side_ref, valid_ref)]
    live = jnp.sum(valid).astype(jnp.int32)
    for z in range(5):
        spans[4, z] = live
    for t in range(4):
        low = jnp.sum((seg < t).astype(WIDE)).astype(jnp.int32)
        high = jnp.sum((seg <= t).astype(WIDE)).astype(jnp.int32)
        width = jnp.max(jnp.where(seg == t, side, 1.0))
        small = high - low <= SMALL - 16
        start = low // 16 * 16
        at = jnp.minimum(start, jnp.where(small, n - SMALL, n - LARGE))
        key = jnp.minimum(start, n - WIN)
        kind = jnp.where((high > low) & (low < live), jnp.where(small, 1, 2), 0)
        for z, value in enumerate((low, high, at, key, kind)):
            spans[t, z] = value

        def places(first, shape_, dim):
            slot = lax.broadcasted_iota(jnp.int32, shape_, dim) + first
            place = (slot - low).astype(WIDE)
            row = jnp.floor((place + 0.5) / width)
            return (slot >= low) & (slot < high), row, place - row * width

        inside, row, col = places(at, (LARGE, 1), 0)
        inside_key, row_key, col_key = places(key, (1, WIN), 1)
        down, along = row - row_key, col - col_key
        far_ref[t] = jnp.where(inside & inside_key, jnp.sqrt(down * down + along * along), 1e12)


def tables(seg, side, valid):
    vmem, smem = [pl.BlockSpec(memory_space=z) for z in (pltpu.VMEM, pltpu.SMEM)]
    return pl.pallas_call(
        tables_kernel,
        in_specs=[vmem] * 3,
        out_specs=[smem, vmem],
        out_shape=[jax.ShapeDtypeStruct((5, 5), jnp.int32), jax.ShapeDtypeStruct((4, LARGE, WIN), WIDE)],
        compiler_params=pltpu.CompilerParams(vmem_limit_bytes=VMEM_BYTES),
        name="tables",
    )(seg, side, valid)


def bell(u):
    share = 0.5 + 0.5 * lax.erf(u * 0.7071067811865476)
    return u * share, share + u * (jnp.exp2(u * u * -0.7213475204444817) * 0.3989422804014327)


def up_kernel(x_ref, o0_ref, o1_ref, vec_ref, order_ref, own, other, mixed_ref, h_ref, a_ref, gl_ref, gp_ref, tmp):
    mixed_ref[...] = (
        nn(o0_ref[...], order_ref[:HALF, :]) + nn(o1_ref[...], order_ref[HALF:, :])
    ).astype(LOW)
    for col in (0, 384):
        part = slice(col, col + 384)
        h_ref[:, part] = x_ref[:, part].astype(WIDE) + nn(mixed_ref[...], both((own, other), 0, col, 384)) + vec_ref[2:3, part]
    gain, shift = vec_ref[3:4, :], vec_ref[4:5, :]

    def norm(rows, _):
        tmp[rows, :] = (normal(h_ref[rows, :])[0] * gain + shift).astype(LOW)

    over_rows(x_ref.shape[0], 144, norm)
    a_ref[...] = nn(tmp[...], order_ref[...]).astype(LOW)
    for col in range(0, FF, 384):
        k = 5 + col // D
        u = nn(a_ref[...], both((own, other), *divmod(col + D, WIDTH_TWO), 384)) + vec_ref[k : k + 1, col % D : col % D + 384]
        value, slope = bell(u)
        gl_ref[:, col : col + 384] = value.astype(LOW)
        gp_ref[:, col : col + 384] = slope.astype(LOW)


def upward(x, o, vec, order, two, after=()):
    n = x.shape[0]
    return whole_call(
        up_kernel, [shape(n, D), shape(n, D, WIDE), shape(n, D), shape(n, FF), shape(n, FF)],
        [pltpu.VMEM((n, D), LOW)], 0, "upward", 2 * n * D * (7 * D) * 2, x, *o, vec, order, *two,
        after=after,
    )


def fetch_down(place, own, other, wd, sem):
    def copies(b, piece, row):
        dst = pl.ds(pl.multiple_of(b * 96, 96), 96)
        return [
            pltpu.make_async_copy(
                piece.at[pl.ds(pl.multiple_of(row * 96 + side * (FF // 2), 96), 96), :],
                wd.at[dst, pl.ds(side * WIDTH_THREE, WIDTH_THREE)],
                sem,
            )
            for side in (0, 1)
        ]

    def begin(b, carry):
        p = place[b]
        pl.when(p < 16)(lambda: [z.start() for z in copies(b, own, p)] and None)
        pl.when(p >= 16)(lambda: [z.start() for z in copies(b, other, p - 16)] and None)
        return carry

    def finish(b, carry):
        for z in copies(b, own, 0):
            z.wait()
        return carry

    lax.fori_loop(0, 32, begin, 0)
    lax.fori_loop(0, 32, finish, 0)


def down_kernel(place, gp_ref, dy_ref, own, other, dur_ref, vg_ref, wd, sem):
    fetch_down(place, own, other, wd, sem)
    for col in range(0, FF, 384):
        part = slice(col, col + 384)
        du = nt(dy_ref[...], wd[part, :]) * gp_ref[:, part].astype(WIDE)
        dur_ref[:, part] = du.astype(LOW)
        k = col // D
        vg_ref[k : k + 1, col % D : col % D + 384] = jnp.sum(du, axis=0, keepdims=True)


def down_back(place, gp, dy, three, after=()):
    n = dy.shape[0]
    return whole_call(
        down_kernel, [shape(n, FF), shape(8, D, WIDE)], [pltpu.VMEM((FF, D), LOW), pltpu.SemaphoreType.DMA], 1,
        "down_back", 2 * n * D * (4 * D), place, gp, dy, *three, anywhere=(3, 4), after=after,
    )


def down_out_kernel(place, vec_ref, gl_ref, h_ref, own, other, out_ref, wd, sem):
    fetch_down(place, own, other, wd, sem)
    for col in (0, 384):
        part = slice(col, col + 384)
        out_ref[:, part] = (h_ref[:, part] + nn(gl_ref[...], wd[:, part]) + vec_ref[9:10, part]).astype(LOW)


def down_out(place, vec, gl, h, three, after=()):
    n = h.shape[0]
    return whole_call(
        down_out_kernel, [shape(n, D)], [pltpu.VMEM((FF, D), LOW), pltpu.SemaphoreType.DMA], 1,
        "down_out", 2 * n * D * (4 * D), place, vec, gl, h, *three, anywhere=(4, 5), after=after,
    )[0]


def hidden_kernel(vec_ref, order_ref, dur_ref, dy_ref, h_ref, own, other, dh_ref, dhr_ref, dor_ref, vg_ref, tmp):
    split = WIDTH_TWO - D
    for i, w in enumerate((own, other)):
        tmp[:, HALF * i : HALF * (i + 1)] = (
            nt(dur_ref[:, :split], w[:HALF, D:]) + nt(dur_ref[:, split:], w[HALF:, :])
        ).astype(LOW)
    dh_ref[...] = nt(tmp[...], order_ref[...])
    gain = vec_ref[3:4, :]

    def step(rows, sums):
        e = dh_ref[rows, :]
        dy = dy_ref[rows, :].astype(WIDE)
        n, rstd = normal(h_ref[rows, :])
        w = e * gain
        dh = dy + rstd * (w - jnp.mean(w, axis=-1, keepdims=True) - n * jnp.mean(w * n, axis=-1, keepdims=True))
        dh_ref[rows, :] = dh
        dhr_ref[rows, :] = dh.astype(LOW)
        return tuple(s + jnp.sum(z.reshape(-1, 8, D), axis=0) for s, z in zip(sums, (dh, e * n, e, dy)))

    zero = jnp.zeros((8, D), WIDE)
    sums = over_rows(h_ref.shape[0], 144, step, (zero,) * 4)
    for k, s in enumerate(sums):
        vg_ref[k : k + 1, :] = jnp.sum(s, axis=0, keepdims=True)
    for i, w in enumerate((own, other)):
        tmp[:, HALF * i : HALF * (i + 1)] = nt(dhr_ref[...], w[:HALF, :D]).astype(LOW)
    dor_ref[...] = nt(tmp[...], order_ref[...]).astype(LOW)


def hidden_grad(vec, order, dur, dy, h, two, after=()):
    n = h.shape[0]
    return whole_call(
        hidden_kernel, [shape(n, D, WIDE), shape(n, D), shape(n, D), shape(8, D, WIDE)],
        [pltpu.VMEM((n, D), LOW)], 0, "hidden_grad",
        2 * n * D * (7 * D), vec, order, dur, dy, h, *two, after=after,
    )


def down_grad_kernel(place, gl_ref, dy_ref, own, other):
    for c in range(8):
        t = tn(gl_ref[:, 384 * c : 384 * (c + 1)], dy_ref[...]).astype(LOW)
        for i in range(4):
            p = place[4 * c + i]

            def put(piece, row):
                for side in (0, 1):
                    rows = pl.ds(pl.multiple_of(row * 96 + side * (FF // 2), 96), 96)
                    piece[rows, :] = t[96 * i : 96 * (i + 1), side * WIDTH_THREE : (side + 1) * WIDTH_THREE]

            pl.when(p < 16)(lambda: put(own, p))
            pl.when(p >= 16)(lambda: put(other, p - 16))


def down_grad(place, gl, dy, after=()):
    n = dy.shape[0]
    return whole_call(down_grad_kernel, [shape(FF, WIDTH_THREE)] * 2, [], 1, "down_grad", 2 * n * D * FF, place, gl, dy, after=after)


def two_grad_kernel(mixed_ref, a_ref, dhr_ref, dur_ref, own, other):
    for col in range(0, D + FF, 384):
        left, right = (mixed_ref, dhr_ref[:, col : col + 384]) if col < D else (a_ref, dur_ref[:, col - D : col - D + 384])
        t = tn(left[...], right).astype(LOW)
        side, lo = divmod(col, WIDTH_TWO)
        own[HALF * side : HALF * (side + 1), lo : lo + 384] = t[:HALF]
        other[HALF * side : HALF * (side + 1), lo : lo + 384] = t[HALF:]


def two_grad(mixed, a, dhr, dur, after=()):
    n = a.shape[0]
    return whole_call(two_grad_kernel, [shape(D, WIDTH_TWO)] * 2, [], 0, "two_grad", 2 * n * D * (D + FF), mixed, a, dhr, dur,
                      after=after)


def one_grad_kernel(a_ref, order_ref, first_ref, mid_ref, up_ref, *refs):
    halves, (own, other, wide) = refs[:6], refs[6:]
    wide[...] = jnp.zeros_like(wide)
    rows = [first_ref[0:1, :], first_ref[1:2, :]] + [mid_ref[i : i + 1, :] for i in range(3)]
    rows = rows + [up_ref[i : i + 1, :] for i in range(4)] + [mid_ref[3:4, :]]
    for k, values in enumerate(rows):
        first = min(D * k // 10 // 8 * 8, D - 88)
        entry = lax.broadcasted_iota(jnp.int32, (88, D), 1) + D * k
        row = lax.broadcasted_iota(jnp.int32, (88, D), 0) + first
        spread_out = jnp.where(row == (entry * 52429) >> 19, values, 0.0).astype(LOW)
        entry = lax.broadcasted_iota(jnp.int32, (D, 128), 0) + D * k
        column = entry - 10 * ((entry * 52429) >> 19)
        pick = (lax.broadcasted_iota(jnp.int32, (D, 128), 1) == column).astype(LOW)
        wide[first : first + 88, :] += nn(spread_out, pick)
    moved = tn(order_ref[...], wide[...].astype(LOW)).astype(LOW)
    for i, out in enumerate((own, other)):
        out[:HALF, CUT_ONE:] = moved[HALF * i : HALF * (i + 1), :]
        out[HALF:, CUT_ONE:] = jnp.zeros((HALF, WIDTH_ONE - CUT_ONE), LOW)
    for i, half in enumerate(halves):
        t = tn(a_ref[...], half[...]).astype(LOW)
        side, lo = divmod(384 * i, CUT_ONE)
        own[HALF * side : HALF * (side + 1), lo : lo + 384] = t[:HALF]
        other[HALF * side : HALF * (side + 1), lo : lo + 384] = t[HALF:]


def one_grad(a, order, sums, d, after=()):
    n = a.shape[0]
    return whole_call(
        one_grad_kernel, [shape(D, WIDTH_ONE)] * 2, [pltpu.VMEM((D, 128), WIDE)], 0, "one_grad",
        2 * n * D * 3 * D, a, order, *sums, *d, after=after,
    )


def input_back_kernel(order_ref, q0, q1, k0, k1, v0, v1, own, other, e_ref, tmp):
    for i, w in enumerate((own, other)):
        total = 0.0
        for j, d in enumerate((q0, q1, k0, k1, v0, v1)):
            side, lo = divmod(384 * j, CUT_ONE)
            total = total + nt(d[...], w[HALF * side : HALF * (side + 1), lo : lo + 384])
        tmp[:, HALF * i : HALF * (i + 1)] = total.astype(LOW)
    e_ref[...] = nt(tmp[...], order_ref[...])


def input_back(order, d, one, after=()):
    n = d[0].shape[0]
    return whole_call(
        input_back_kernel, [shape(n, D, WIDE)], [pltpu.VMEM((n, D), LOW)], 0, "input_back",
        2 * n * D * 4 * D, order, *d, *one, after=after,
    )[0]


def input_kernel(x_ref, vec_ref, e_ref, dh_ref, dx_ref, vg_ref):
    gain = vec_ref[0:1, :]

    def step(rows, sums):
        e = e_ref[rows, :]
        n, rstd = normal(x_ref[rows, :].astype(WIDE))
        w = e * gain
        dx_ref[rows, :] = dh_ref[rows, :] + rstd * (
            w - jnp.mean(w, axis=-1, keepdims=True) - n * jnp.mean(w * n, axis=-1, keepdims=True)
        )
        return tuple(s + jnp.sum(z.reshape(-1, 8, D), axis=0) for s, z in zip(sums, (e * n, e)))

    zero = jnp.zeros((8, D), WIDE)
    sums = over_rows(x_ref.shape[0], 144, step, (zero,) * 2)
    for k, s in enumerate(sums):
        vg_ref[k : k + 1, :] = jnp.sum(s, axis=0, keepdims=True)


def input_grad(x, vec, e, dh, after=()):
    n = x.shape[0]
    return whole_call(
        input_kernel, [shape(n, D, WIDE), shape(8, D, WIDE)], [], 0, "input_grad",
        2 * n * D * 3 * D, x, vec, e, dh, after=after,
    )


def near_kernel(a, b, c, d, left_ref, right_ref):
    cut = left_ref.shape[1]
    for out, lo in ((left_ref, 0), (right_ref, cut)):
        out[...] = jnp.concatenate([z[:, lo : lo + cut].astype(WIDE) for z in (a, b, c, d)], axis=0).astype(LOW)


def near_pieces(pieces, after=()):
    rows, cols = pieces[0].shape
    return whole_call(near_kernel, [shape(4 * rows, cols // 2)] * 2, [], 0, "near", 1, *pieces, after=after)


def first_kernel(left, got_left, right, got_right, left_ref, right_ref):
    rows = left.shape[0]
    for out, mine, got in ((left_ref, left, got_left), (right_ref, right, got_right)):
        out[:rows, :] = mine[...]
        out[rows:, :] = got[...]


def first_pieces(left, right, got, after=()):
    rows, cols = left.shape
    return whole_call(
        first_kernel, [shape(2 * rows, cols)] * 2, [], 0, "first", 1, left, got[0], right, got[1], after=after
    )


def second_kernel(left, got, right, far, own_ref):
    rows = left.shape[0]
    half = rows // 2
    own_ref[:rows, :] = left[...]
    own_ref[rows : 2 * rows, :] = got[...]
    for i in (0, 1):
        own_ref[2 * rows + 2 * i * half : 2 * rows + (2 * i + 1) * half, :] = right[i * half : (i + 1) * half, :]
        own_ref[2 * rows + (2 * i + 1) * half : 2 * rows + (2 * i + 2) * half, :] = far[i * half : (i + 1) * half, :]


def second_pieces(left, right, got, after=()):
    rows, cols = left.shape
    return whole_call(
        second_kernel, [shape(4 * rows, cols)], [], 0, "second", 1, left, got[0], right, got[1], after=after
    )[0]


def core_sum_kernel(own, got, left_keep, right_keep, left_out, right_out):
    half = left_keep.shape[0]
    rows = half // 2

    def total(lo, count):
        return own[lo : lo + count, :].astype(WIDE) + got[lo : lo + count, :].astype(WIDE)

    left_keep[...] = total(0, half)
    left_out[...] = total(half, half).astype(LOW)
    for i in (0, 1):
        lo = 2 * half + 2 * i * rows
        right_keep[i * rows : (i + 1) * rows, :] = total(lo, rows)
        right_out[i * rows : (i + 1) * rows, :] = total(lo + rows, rows).astype(LOW)


def core_sum(own, got, after=()):
    rows, cols = own.shape[0] // 4, own.shape[1]
    return whole_call(
        core_sum_kernel, [shape(rows, cols, WIDE)] * 2 + [shape(rows, cols)] * 2, [], 0, "core_sum", 1, own, got,
        after=after,
    )


def half_sum_kernel(left, got_left, right, got_right, left_keep, right_keep, left_out, right_out):
    rows = left_keep.shape[0]
    for mine, got, keep, out in ((left, got_left, left_keep, left_out), (right, got_right, right_keep, right_out)):
        keep[...] = mine[:rows, :] + got[:rows, :].astype(WIDE)
        out[...] = (mine[rows:, :] + got[rows:, :].astype(WIDE)).astype(LOW)


def half_sum(left, right, got, after=()):
    rows, cols = left.shape[0] // 2, left.shape[1]
    return whole_call(
        half_sum_kernel, [shape(rows, cols, WIDE)] * 2 + [shape(rows, cols)] * 2, [], 0, "half_sum", 1,
        left, got[0], right, got[1], after=after,
    )


def last_sum_kernel(left, got_left, right, got_right, keep, *outs):
    unit, cut = keep.shape[0], left.shape[1]
    for lo, mine, got in ((0, left, got_left), (cut, right, got_right)):
        total = mine[...] + got[...].astype(WIDE)
        keep[:, lo : lo + cut] = total[:unit]
        for i, out in enumerate(outs):
            out[:, lo : lo + cut] = total[unit * (i + 1) : unit * (i + 2)].astype(LOW)


def last_sum(left, right, got, after=()):
    unit, cols = left.shape[0] // 4, 2 * left.shape[1]
    return whole_call(
        last_sum_kernel, [shape(unit, cols, WIDE)] + [shape(unit, cols)] * 3, [], 0, "last_sum", 1,
        left, got[0], right, got[1], after=after,
    )


def swap(value, bits):
    pairs = [(i, i ^ bits) for i in range(32)]
    return lax.ppermute(value, AXES, pairs)


def tie(values, *first):
    return lax.optimization_barrier((tuple(values), first))[0]


class Flow:
    def __init__(self, steps):
        self.steps = steps
        self.next = next(steps)[:2]

    def issue(self, start=()):
        values, bits = self.next
        values = tie(values, start)
        self.got = tuple(swap(value, bit) for value, bit in zip(values, bits))
        return self.got

    def land(self, end=()):
        values, *bits = self.steps.send(tie(self.got, end))
        if values is None:
            return bits[0]
        self.next = (values, bits[0])
        return bits[1]


def spread(block):
    got = yield (block,) * 3, (8, 16, 24)
    left, right = near_pieces((block,) + got)
    got = yield (left, right), (2, 4), (left, right)
    left, right = first_pieces(left, right, got)
    got = yield (left, right), (4, 2), (left, right)
    own = second_pieces(left, right, got)
    got = yield (own,), (1,), (own,)
    yield None, (own, got[0])


def collect(pieces):
    (got,) = yield (pieces[1],), (1,)
    left, right, *out = ready = core_sum(pieces[0], got)
    got = yield out, (4, 2), tuple(ready)
    left, right, *out = ready = half_sum(left, right, got)
    got = yield out, (2, 4), tuple(ready)
    total, *out = ready = last_sum(left, right, got)
    got = yield out, (8, 16, 24), tuple(ready)
    yield None, (sum((z.astype(WIDE) for z in got), total),)


def stack(whole):
    half, cut = whole.shape[0] // 2, whole.shape[1] // 2
    return tuple(jnp.concatenate([z[:, :cut], z[:, cut:]], axis=0) for z in (whole[:half], whole[half:]))


def unstack(pieces):
    half = pieces[0].shape[0] // 2
    return jnp.concatenate([jnp.concatenate([z[:half], z[half:]], axis=1) for z in pieces], axis=0)


class Whole:
    def __init__(self, result):
        self.result = result

    def issue(self, start=()):
        return ()

    def land(self, end=()):
        return self.result


def spread_any(block):
    return stack(lax.all_gather(block, AXES, axis=0, tiled=True))


def collect_any(pieces):
    return (lax.psum_scatter(unstack(pieces), AXES, scatter_dimension=0, tiled=True).astype(WIDE),)


def rearrange(whole, order, shards):
    return jnp.take(whole.reshape(shards, -1, whole.shape[1]), order, axis=0, mode="clip").reshape(whole.shape)


def adamw(master, moment_one, moment_two, gradient, step_rate, decay_rate):
    first_new = BETA_ONE * moment_one + (1.0 - BETA_ONE) * gradient
    second_new = BETA_TWO * moment_two + (1.0 - BETA_TWO) * gradient * gradient
    first_hat = first_new / (1.0 - BETA_ONE**STEP)
    second_hat = second_new / (1.0 - BETA_TWO**STEP)
    master_new = master - step_rate * (
        first_hat / (jnp.sqrt(second_hat) + ADAM_EPS) + decay_rate * master
    )
    return (first_new, second_new, master_new)


def local(
    tokens_in, cotangent, segments, tile_sides, valid_slots, owners,
    master_qkv, master_out, master_up, master_down, master_vec,
    first_qkv, first_out, first_up, first_down, first_vec,
    second_qkv, second_out, second_up, second_down, second_vec,
):
    shards = lax.axis_size(AXES)
    near = shards == 32
    unit = D // shards
    per_row = master_vec.shape[0] // unit
    ids = jnp.arange(shards, dtype=jnp.int32)
    if near:
        away = owners ^ lax.axis_index(AXES).astype(jnp.int32)
        place = (away >> 3) + 4 * ((away >> 1) & 1) + 8 * ((away >> 2) & 1) + 16 * (away & 1)
        place_down = place
    else:
        place = owners
        place_down = jnp.arange(32, dtype=jnp.int32)
    target = (place[:, None] * unit + jnp.arange(unit, dtype=jnp.int32)[None, :]).reshape(-1)
    order = (target[:, None] == jnp.arange(D, dtype=jnp.int32)[None, :]).astype(LOW)

    def gather(block):
        return Flow(spread(block)) if near else Whole(spread_any(block))

    def scatter(pieces):
        return Flow(collect(pieces)) if near else Whole(collect_any(pieces))

    vec_block = jnp.pad(master_vec.reshape(unit, per_row), ((0, 0), (0, 128 - per_row)))
    block_one = jnp.concatenate(
        [master_qkv[:, :CUT_ONE], vec_block, master_qkv[:, CUT_ONE:], jnp.zeros_like(vec_block)], axis=1
    )
    spans, far = tables(segments, tile_sides, valid_slots)
    slopes = LOG2E * jnp.exp2(-8.0 * (jnp.arange(HEADS, dtype=jnp.int32).astype(WIDE) + 1.0) / HEADS)
    one = gather(block_one.astype(LOW))
    two = gather(jnp.concatenate([master_out, master_up], axis=1).astype(LOW))
    if near:
        three = gather(master_down.astype(LOW))
    else:
        whole = lax.all_gather(master_down.astype(LOW), AXES, axis=0, tiled=True)
        three = Whole(stack(rearrange(whole, owners, shards)))
    one.issue()
    normed = normalized(tokens_in[0])
    done = one.land((far, spans, slopes, order, normed))
    one.issue(done)
    done = one.land()
    sent = one.issue(done) + two.issue(done)
    done = one.land()
    done = done + two.land(sent + done)
    one.issue(done)
    sent = two.issue(done)
    one = one.land()

    x = tokens_in[0]
    dy = cotangent[0]
    act_one, qkv, vec = project(normed, order, one)
    done = two.land((qkv,))
    sent = two.issue(done) + three.issue(done)
    mixed_0, probs_0 = attend(0, qkv, far, spans, slopes, done)
    done = two.land((mixed_0,))
    done = done + three.land((mixed_0,) + sent + done)
    sent = two.issue(done) + three.issue(done)
    mixed_1, probs_1 = attend(3, qkv, far, spans, slopes, done + (mixed_0,))
    done = three.land((mixed_1,) + sent)
    two = two.land((mixed_1,) + sent)
    three.issue(done + two[1:])
    mixed, hidden, act_two, gelu, gelu_slope = upward(x, (mixed_0, mixed_1), vec, order, two, done)
    grad_three = down_grad(place_down, gelu, dy)
    done = three.land(tuple(grad_three))
    three.issue(done)
    three = three.land()
    if not near:
        back = jnp.sum(ids[:, None] * (owners[:, None] == ids[None, :]), axis=0)
        grad_three = stack(rearrange(unstack(grad_three), back, shards))
    flow_three = scatter(grad_three)
    flow_three.issue((three[1],))
    dur, sums_up = down_back(place_down, gelu_slope, dy, three)
    done = flow_three.land((dur,))
    flow_three.issue(done)
    dh, dh_low, dmixed, sums = hidden_grad(vec, order, dur, dy, hidden, two, done)
    grad_two = two_grad(mixed, act_two, dh_low, dur)
    done = flow_three.land(tuple(grad_two)) + tuple(grad_two)
    flow_two = scatter(grad_two)
    sent = flow_three.issue(done) + flow_two.issue(done)
    d0 = attend_back(0, qkv, dmixed, probs_0, spans, done)
    done = flow_three.land(tuple(d0) + sent) + flow_two.land(tuple(d0) + sent)
    sent = flow_three.issue(done) + flow_two.issue(done)
    d1 = attend_back(3, qkv, dmixed, probs_1, spans, done + tuple(d0))
    d = [z for pair in zip(d0, d1) for z in pair]
    dact = input_back(order, d, one)
    tokens_grad, sums_one = input_grad(x, vec, dact, dh)
    grad_one = one_grad(act_one, order, (sums_one, sums, sums_up), d)
    done = tuple(grad_one) + sent
    sum_three, = flow_three.land(done)
    done = flow_two.land(done)
    flow_one = scatter(grad_one)
    sent = flow_one.issue(done) + flow_two.issue(done)
    block_out = down_out(place_down, vec, gelu, hidden, three, done)
    done = flow_one.land((block_out,) + sent) + flow_two.land((block_out,) + sent)
    sent = flow_one.issue(done) + flow_two.issue(done)
    upd_down = adamw(master_down, first_down, second_down, sum_three, RATE_MATRIX, DECAY_MATRIX)
    sent = sent + upd_down
    done = flow_one.land(sent)
    sum_two, = flow_two.land(sent)
    flow_one.issue(done)
    upd_out = adamw(master_out, first_out, second_out, sum_two[:, :D], RATE_MATRIX, DECAY_MATRIX)
    upd_up = adamw(master_up, first_up, second_up, sum_two[:, D:], RATE_MATRIX, DECAY_MATRIX)
    done = flow_one.land(upd_out)
    flow_one.issue(done)
    sum_one, = flow_one.land(upd_up)
    sum_vec = sum_one[:, CUT_ONE : CUT_ONE + per_row].reshape(-1)
    sum_one = jnp.concatenate([sum_one[:, :CUT_ONE], sum_one[:, WIDTH_ONE : WIDTH_ONE + CUT_ONE]], axis=1)
    upd_qkv = adamw(master_qkv, first_qkv, second_qkv, sum_one, RATE_MATRIX, DECAY_MATRIX)
    upd_vec = adamw(master_vec, first_vec, second_vec, sum_vec, RATE_VECTOR, 0.0)
    return (
        (block_out[None], tokens_grad[None]) + upd_qkv + upd_out + upd_up + upd_down + upd_vec
    )


def solution(mesh):
    rows = P(AXES, None)
    flat = P(AXES)
    deep = P(AXES, None, None)
    stored = (rows,) * 4 + (flat,)
    in_specs = (deep,) * 2 + (rows,) * 3 + (P(),) + stored * 3
    out_specs = (deep,) * 2 + (rows,) * 12 + (flat,) * 3
    return jax.shard_map(local, mesh=mesh, in_specs=in_specs, out_specs=out_specs, check_vma=False)
```

```python
import functools

import jax
import jax.numpy as jnp
from jax import lax
from jax.experimental import pallas as pl
from jax.experimental.pallas import tpu as pltpu
from jax.sharding import PartitionSpec as P

D = 768
HEADS = 12
FF = 3072
STEP = 10
HALF = 384
WIN = 256
SMALL = 160
LARGE = 240
LOG2E = 1.4426950408889634
CUT_ONE = 1152
WIDTH_ONE = 1280
WIDTH_TWO = 1920
WIDTH_THREE = 384

EPSILON = 1e-05
BETA_ONE = 0.9
BETA_TWO = 0.999
ADAM_EPS = 1e-08
RATE_MATRIX = 0.05
DECAY_MATRIX = 0.05
RATE_VECTOR = 0.3

AXES = ("dp", "fsdp")
LOW = jnp.bfloat16
WIDE = jnp.float32
VMEM_BYTES = 10 * 2**20


def nn(left, right):
    return lax.dot_general(left, right, (((1,), (0,)), ((), ())), preferred_element_type=WIDE)


def nt(left, right):
    return lax.dot_general(left, right, (((1,), (1,)), ((), ())), preferred_element_type=WIDE)


def tn(left, right):
    return lax.dot_general(left, right, (((0,), (0,)), ((), ())), preferred_element_type=WIDE)


def shape(rows, cols, kind=LOW):
    return jax.ShapeDtypeStruct((rows, cols), kind)


def later(kernel, inputs, extra):
    return lambda *refs: kernel(*refs[:inputs], *refs[inputs + extra :])


def whole_call(kernel, outs, scratch, smem, name, flops, *args, anywhere=(), after=()):
    specs = []
    for i in range(len(args)):
        space = pltpu.SMEM if i < smem else pl.ANY if i in anywhere else pltpu.VMEM
        specs.append(pl.BlockSpec(memory_space=space))
    moved = sum(a.size * a.dtype.itemsize for a in args) + sum(o.size * o.dtype.itemsize for o in outs)
    return pl.pallas_call(
        later(kernel, len(args), len(after)),
        in_specs=specs + [pl.BlockSpec(memory_space=pl.ANY)] * len(after),
        out_specs=[pl.BlockSpec(memory_space=pltpu.VMEM)] * len(outs),
        out_shape=outs,
        scratch_shapes=scratch,
        compiler_params=pltpu.CompilerParams(vmem_limit_bytes=VMEM_BYTES),
        cost_estimate=pl.CostEstimate(flops=flops, bytes_accessed=moved, transcendentals=0),
        name=name,
    )(*args, *after)


def over_rows(count, step, body, init=None):
    return lax.fori_loop(0, count // step, lambda i, c: body(pl.ds(pl.multiple_of(i * step, step), step), c), init)


def normal(values):
    centre = values - jnp.mean(values, axis=-1, keepdims=True)
    rstd = lax.rsqrt(jnp.mean(centre * centre, axis=-1, keepdims=True) + EPSILON)
    return centre * rstd, rstd


def both(pair, side, lo, width):
    rows = slice(HALF * side, HALF * (side + 1))
    return jnp.concatenate([z[rows, lo : lo + width] for z in pair], axis=0)


def normal_kernel(x_ref, n_ref):
    def norm(rows, _):
        n_ref[rows, :] = normal(x_ref[rows, :].astype(WIDE))[0]

    over_rows(x_ref.shape[0], 144, norm)


def normalized(x):
    return whole_call(normal_kernel, [shape(*x.shape, WIDE)], [], 0, "normalized", 1, x)[0]


def qkv_kernel(n_ref, order_ref, own, other, a_ref, qkv_ref, vec_ref, tmp, wide):
    moved = jnp.concatenate([z[:HALF, CUT_ONE:] for z in (own, other)], axis=0)
    wide[...] = nn(order_ref[...], moved)
    vec_ref[...] = jnp.zeros_like(vec_ref)
    for k in range(10):
        first = min(D * k // 10 // 8 * 8, D - 88)

        def tenths(rows):
            entry = lax.broadcasted_iota(jnp.int32, (rows, D), 1) + D * k
            tenth = (entry * 52429) >> 19
            return tenth, entry - 10 * tenth, lax.broadcasted_iota(jnp.int32, (rows, D), 0)

        _, column, row = tenths(128)
        picked = nn(wide[first : first + 88, :].astype(LOW), (row == column).astype(LOW))
        tenth, _, row = tenths(88)
        vec_ref[k : k + 1, :] = jnp.sum(jnp.where(row + first == tenth, picked, 0.0), axis=0, keepdims=True)
    gain, shift = vec_ref[0:1, :], vec_ref[1:2, :]

    def norm(rows, _):
        tmp[rows, :] = (n_ref[rows, :] * gain + shift).astype(LOW)

    over_rows(n_ref.shape[0], 144, norm)
    a_ref[...] = nn(tmp[...], order_ref[...]).astype(LOW)
    for col in range(0, 3 * D, 384):
        w = both((own, other), *divmod(col, CUT_ONE), 384)
        qkv_ref[:, col : col + 384] = nn(a_ref[...], w).astype(LOW)


def project(normed, order, one, after=()):
    n = normed.shape[0]
    return whole_call(
        qkv_kernel, [shape(n, D), shape(n, 3 * D), shape(16, D, WIDE)],
        [pltpu.VMEM((n, D), LOW), pltpu.VMEM((D, 128), WIDE)], 0, "project",
        2 * n * D * (4 * D), normed, order, *one, after=after,
    )


def each_tile(spans, body):
    def step(t, carry):
        for kind, rows in ((1, SMALL), (2, LARGE)):

            @pl.when(spans[t, 4] == kind)
            def _():
                body(t, pl.multiple_of(spans[t, 2], 16), rows, pl.multiple_of(spans[t, 3], 16))

        return carry

    lax.fori_loop(0, 4, step, 0)


def padding_rows(spans, shape_):
    return lax.broadcasted_iota(jnp.int32, shape_, 0) >= spans[4, 0]


def own_half(values, e):
    lane = lax.broadcasted_iota(jnp.int32, values.shape, 1)
    return jnp.where((lane < 64) if e == 0 else (lane >= 64), values, jnp.zeros_like(values))


def attend_kernel(base, spans, slopes, qkv_ref, far_ref, o_ref, p_ref, acc):
    acc[...] = jnp.zeros_like(acc)

    def tile(t, at, count, key):
        rows, keys = pl.ds(at, count), pl.ds(key, WIN)
        row = lax.broadcasted_iota(jnp.int32, (count, 1), 0) + at
        inside = ((row >= spans[t, 0]) & (row < spans[t, 1])).astype(WIDE)
        far = far_ref[t, :count, :]
        for pair in range(3):
            col = (base + pair) * 128
            q, k, v = [qkv_ref[z, col + i * D : col + i * D + 128] for i, z in enumerate((rows, keys, keys))]
            out = None
            for e in range(2):
                s = nt(q, own_half(k, e)) * (0.125 * LOG2E) - slopes[2 * (base + pair) + e] * far
                p = jnp.exp2(s - jnp.max(s, axis=1, keepdims=True))
                p = (p * (inside / jnp.sum(p, axis=1, keepdims=True))).astype(LOW)
                p_ref[t, 2 * pair + e, :count, :] = p
                part = nn(p, own_half(v, e))
                out = part if out is None else out + part
            acc[rows, pair * 128 : pair * 128 + 128] += out

    each_tile(spans, tile)
    v = qkv_ref[:, base * 128 + 2 * D : base * 128 + 2 * D + HALF]
    o_ref[...] = jnp.where(padding_rows(spans, v.shape), v, acc[...].astype(LOW))


def attend(base, qkv, far, spans, slopes, after=()):
    n = qkv.shape[0]
    return whole_call(
        functools.partial(attend_kernel, base),
        [shape(n, HALF), jax.ShapeDtypeStruct((4, HEADS // 2, LARGE, WIN), LOW)],
        [pltpu.VMEM((n, HALF), WIDE)], 2, "attend", 9 * 10**9, spans, slopes, qkv, far, after=after,
    )


def attend_back_kernel(base, spans, qkv_ref, g_ref, p_ref, dq_ref, dk_ref, dv_ref, aq, ak, av):
    for acc in (aq, ak, av):
        acc[...] = jnp.zeros_like(acc)

    def tile(t, at, count, key):
        rows, keys = pl.ds(at, count), pl.ds(key, WIN)
        for pair in range(3):
            col = (base + pair) * 128
            q, k, v = [qkv_ref[z, col + i * D : col + i * D + 128] for i, z in enumerate((rows, keys, keys))]
            g = g_ref[rows, col : col + 128]
            sums = None
            for e in range(2):
                ge = own_half(g, e)
                p = p_ref[t, 2 * pair + e, :count, :]
                wide = p.astype(WIDE)
                d = wide * nt(ge * 0.125, v)
                d = (d - wide * jnp.sum(d, axis=1, keepdims=True)).astype(LOW)
                parts = (nn(d, own_half(k, e)), tn(d, own_half(q, e)), tn(p, ge))
                sums = parts if sums is None else tuple(a + b for a, b in zip(sums, parts))
            part = slice(pair * 128, pair * 128 + 128)
            aq[rows, part] += sums[0]
            ak[keys, part] += sums[1]
            av[keys, part] += sums[2]

    each_tile(spans, tile)
    dq_ref[...] = aq[...].astype(LOW)
    dk_ref[...] = ak[...].astype(LOW)
    g = g_ref[:, base * 128 : base * 128 + HALF]
    dv_ref[...] = jnp.where(padding_rows(spans, g.shape), g, av[...].astype(LOW))


def attend_back(base, qkv, grad, probs, spans, after=()):
    n = qkv.shape[0]
    return whole_call(
        functools.partial(attend_back_kernel, base), [shape(n, HALF)] * 3, [pltpu.VMEM((n, HALF), WIDE)] * 3, 1,
        "attend_back", 12 * 10**9, spans, qkv, grad, probs, after=after,
    )


def tables_kernel(seg_ref, side_ref, valid_ref, spans, far_ref):
    n = seg_ref.shape[1]
    seg, side, valid = [z[...].astype(WIDE) for z in (seg_ref, side_ref, valid_ref)]
    live = jnp.sum(valid).astype(jnp.int32)
    for z in range(5):
        spans[4, z] = live
    for t in range(4):
        low = jnp.sum((seg < t).astype(WIDE)).astype(jnp.int32)
        high = jnp.sum((seg <= t).astype(WIDE)).astype(jnp.int32)
        width = jnp.max(jnp.where(seg == t, side, 1.0))
        small = high - low <= SMALL - 16
        start = low // 16 * 16
        at = jnp.minimum(start, jnp.where(small, n - SMALL, n - LARGE))
        key = jnp.minimum(start, n - WIN)
        kind = jnp.where((high > low) & (low < live), jnp.where(small, 1, 2), 0)
        for z, value in enumerate((low, high, at, key, kind)):
            spans[t, z] = value

        def places(first, shape_, dim):
            slot = lax.broadcasted_iota(jnp.int32, shape_, dim) + first
            place = (slot - low).astype(WIDE)
            row = jnp.floor((place + 0.5) / width)
            return (slot >= low) & (slot < high), row, place - row * width

        inside, row, col = places(at, (LARGE, 1), 0)
        inside_key, row_key, col_key = places(key, (1, WIN), 1)
        down, along = row - row_key, col - col_key
        far_ref[t] = jnp.where(inside & inside_key, jnp.sqrt(down * down + along * along), 1e12)


def tables(seg, side, valid):
    vmem, smem = [pl.BlockSpec(memory_space=z) for z in (pltpu.VMEM, pltpu.SMEM)]
    return pl.pallas_call(
        tables_kernel,
        in_specs=[vmem] * 3,
        out_specs=[smem, vmem],
        out_shape=[jax.ShapeDtypeStruct((5, 5), jnp.int32), jax.ShapeDtypeStruct((4, LARGE, WIN), WIDE)],
        compiler_params=pltpu.CompilerParams(vmem_limit_bytes=VMEM_BYTES),
        name="tables",
    )(seg, side, valid)


def bell(u):
    share = 0.5 + 0.5 * lax.erf(u * 0.7071067811865476)
    return u * share, share + u * (jnp.exp2(u * u * -0.7213475204444817) * 0.3989422804014327)


def up_kernel(x_ref, o0_ref, o1_ref, vec_ref, order_ref, own, other, mixed_ref, h_ref, a_ref, gl_ref, gp_ref, tmp):
    mixed_ref[...] = (
        nn(o0_ref[...], order_ref[:HALF, :]) + nn(o1_ref[...], order_ref[HALF:, :])
    ).astype(LOW)
    for col in (0, 384):
        part = slice(col, col + 384)
        h_ref[:, part] = x_ref[:, part].astype(WIDE) + nn(mixed_ref[...], both((own, other), 0, col, 384)) + vec_ref[2:3, part]
    gain, shift = vec_ref[3:4, :], vec_ref[4:5, :]

    def norm(rows, _):
        tmp[rows, :] = (normal(h_ref[rows, :])[0] * gain + shift).astype(LOW)

    over_rows(x_ref.shape[0], 144, norm)
    a_ref[...] = nn(tmp[...], order_ref[...]).astype(LOW)
    for col in range(0, FF, 384):
        k = 5 + col // D
        u = nn(a_ref[...], both((own, other), *divmod(col + D, WIDTH_TWO), 384)) + vec_ref[k : k + 1, col % D : col % D + 384]
        value, slope = bell(u)
        gl_ref[:, col : col + 384] = value.astype(LOW)
        gp_ref[:, col : col + 384] = slope.astype(LOW)


def upward(x, o, vec, order, two, after=()):
    n = x.shape[0]
    return whole_call(
        up_kernel, [shape(n, D), shape(n, D, WIDE), shape(n, D), shape(n, FF), shape(n, FF)],
        [pltpu.VMEM((n, D), LOW)], 0, "upward", 2 * n * D * (7 * D) * 2, x, *o, vec, order, *two,
        after=after,
    )


def fetch_down(block_of, own, other, wd):
    for p in range(32):
        dst = pl.ds(pl.multiple_of(block_of[p] * 96, 96), 96)
        piece = own if p < 16 else other
        for side in (0, 1):
            lo = p % 16 * 96 + side * (FF // 2)
            wd[dst, side * WIDTH_THREE : (side + 1) * WIDTH_THREE] = piece[lo : lo + 96, :]


def down_kernel(block_of, gp_ref, dy_ref, own, other, dur_ref, vg_ref, wd):
    fetch_down(block_of, own, other, wd)
    for col in range(0, FF, 384):
        part = slice(col, col + 384)
        du = nt(dy_ref[...], wd[part, :]) * gp_ref[:, part].astype(WIDE)
        dur_ref[:, part] = du.astype(LOW)
        k = col // D
        vg_ref[k : k + 1, col % D : col % D + 384] = jnp.sum(du, axis=0, keepdims=True)


def down_back(block_of, gp, dy, three, after=()):
    n = dy.shape[0]
    return whole_call(
        down_kernel, [shape(n, FF), shape(8, D, WIDE)], [pltpu.VMEM((FF, D), LOW)], 1,
        "down_back", 2 * n * D * (4 * D), block_of, gp, dy, *three, after=after,
    )


def down_out_kernel(block_of, vec_ref, gl_ref, h_ref, own, other, out_ref, wd):
    fetch_down(block_of, own, other, wd)
    for col in (0, 384):
        part = slice(col, col + 384)
        out_ref[:, part] = (h_ref[:, part] + nn(gl_ref[...], wd[:, part]) + vec_ref[9:10, part]).astype(LOW)


def down_out(block_of, vec, gl, h, three, after=()):
    n = h.shape[0]
    return whole_call(
        down_out_kernel, [shape(n, D)], [pltpu.VMEM((FF, D), LOW)], 1,
        "down_out", 2 * n * D * (4 * D), block_of, vec, gl, h, *three, after=after,
    )[0]


def hidden_kernel(vec_ref, order_ref, dur_ref, dy_ref, h_ref, own, other, dh_ref, dhr_ref, dor_ref, vg_ref, tmp):
    split = WIDTH_TWO - D
    for i, w in enumerate((own, other)):
        tmp[:, HALF * i : HALF * (i + 1)] = (
            nt(dur_ref[:, :split], w[:HALF, D:]) + nt(dur_ref[:, split:], w[HALF:, :])
        ).astype(LOW)
    dh_ref[...] = nt(tmp[...], order_ref[...])
    gain = vec_ref[3:4, :]

    def step(rows, sums):
        e = dh_ref[rows, :]
        dy = dy_ref[rows, :].astype(WIDE)
        n, rstd = normal(h_ref[rows, :])
        w = e * gain
        dh = dy + rstd * (w - jnp.mean(w, axis=-1, keepdims=True) - n * jnp.mean(w * n, axis=-1, keepdims=True))
        dh_ref[rows, :] = dh
        dhr_ref[rows, :] = dh.astype(LOW)
        return tuple(s + jnp.sum(z.reshape(-1, 8, D), axis=0) for s, z in zip(sums, (dh, e * n, e, dy)))

    zero = jnp.zeros((8, D), WIDE)
    sums = over_rows(h_ref.shape[0], 144, step, (zero,) * 4)
    for k, s in enumerate(sums):
        vg_ref[k : k + 1, :] = jnp.sum(s, axis=0, keepdims=True)
    for i, w in enumerate((own, other)):
        tmp[:, HALF * i : HALF * (i + 1)] = nt(dhr_ref[...], w[:HALF, :D]).astype(LOW)
    dor_ref[...] = nt(tmp[...], order_ref[...]).astype(LOW)


def hidden_grad(vec, order, dur, dy, h, two, after=()):
    n = h.shape[0]
    return whole_call(
        hidden_kernel, [shape(n, D, WIDE), shape(n, D), shape(n, D), shape(8, D, WIDE)],
        [pltpu.VMEM((n, D), LOW)], 0, "hidden_grad",
        2 * n * D * (7 * D), vec, order, dur, dy, h, *two, after=after,
    )


def down_grad_kernel(block_of, gl_ref, dy_ref, own, other, all_ref):
    for col in range(0, FF, 384):
        all_ref[col : col + 384, :] = tn(gl_ref[:, col : col + 384], dy_ref[...]).astype(LOW)
    for p in range(32):
        src = pl.ds(pl.multiple_of(block_of[p] * 96, 96), 96)
        piece = own if p < 16 else other
        for side in (0, 1):
            lo = p % 16 * 96 + side * (FF // 2)
            piece[lo : lo + 96, :] = all_ref[src, side * WIDTH_THREE : (side + 1) * WIDTH_THREE]


def down_grad(block_of, gl, dy, after=()):
    n = dy.shape[0]
    return whole_call(
        down_grad_kernel, [shape(FF, WIDTH_THREE)] * 2, [pltpu.VMEM((FF, D), LOW)], 1, "down_grad",
        2 * n * D * FF, block_of, gl, dy, after=after,
    )


def two_grad_kernel(mixed_ref, a_ref, dhr_ref, dur_ref, own, other):
    for col in range(0, D + FF, 384):
        left, right = (mixed_ref, dhr_ref[:, col : col + 384]) if col < D else (a_ref, dur_ref[:, col - D : col - D + 384])
        t = tn(left[...], right).astype(LOW)
        side, lo = divmod(col, WIDTH_TWO)
        own[HALF * side : HALF * (side + 1), lo : lo + 384] = t[:HALF]
        other[HALF * side : HALF * (side + 1), lo : lo + 384] = t[HALF:]


def two_grad(mixed, a, dhr, dur, after=()):
    n = a.shape[0]
    return whole_call(two_grad_kernel, [shape(D, WIDTH_TWO)] * 2, [], 0, "two_grad", 2 * n * D * (D + FF), mixed, a, dhr, dur,
                      after=after)


def one_grad_kernel(a_ref, order_ref, first_ref, mid_ref, up_ref, *refs):
    halves, (own, other, wide) = refs[:6], refs[6:]
    wide[...] = jnp.zeros_like(wide)
    rows = [first_ref[0:1, :], first_ref[1:2, :]] + [mid_ref[i : i + 1, :] for i in range(3)]
    rows = rows + [up_ref[i : i + 1, :] for i in range(4)] + [mid_ref[3:4, :]]
    for k, values in enumerate(rows):
        first = min(D * k // 10 // 8 * 8, D - 88)
        entry = lax.broadcasted_iota(jnp.int32, (88, D), 1) + D * k
        row = lax.broadcasted_iota(jnp.int32, (88, D), 0) + first
        spread_out = jnp.where(row == (entry * 52429) >> 19, values, 0.0).astype(LOW)
        entry = lax.broadcasted_iota(jnp.int32, (D, 128), 0) + D * k
        column = entry - 10 * ((entry * 52429) >> 19)
        pick = (lax.broadcasted_iota(jnp.int32, (D, 128), 1) == column).astype(LOW)
        wide[first : first + 88, :] += nn(spread_out, pick)
    moved = tn(order_ref[...], wide[...].astype(LOW)).astype(LOW)
    for i, out in enumerate((own, other)):
        out[:HALF, CUT_ONE:] = moved[HALF * i : HALF * (i + 1), :]
        out[HALF:, CUT_ONE:] = jnp.zeros((HALF, WIDTH_ONE - CUT_ONE), LOW)
    for i, half in enumerate(halves):
        t = tn(a_ref[...], half[...]).astype(LOW)
        side, lo = divmod(384 * i, CUT_ONE)
        own[HALF * side : HALF * (side + 1), lo : lo + 384] = t[:HALF]
        other[HALF * side : HALF * (side + 1), lo : lo + 384] = t[HALF:]


def one_grad(a, order, sums, d, after=()):
    n = a.shape[0]
    return whole_call(
        one_grad_kernel, [shape(D, WIDTH_ONE)] * 2, [pltpu.VMEM((D, 128), WIDE)], 0, "one_grad",
        2 * n * D * 3 * D, a, order, *sums, *d, after=after,
    )


def input_back_kernel(order_ref, q0, q1, k0, k1, v0, v1, own, other, e_ref, tmp):
    for i, w in enumerate((own, other)):
        total = 0.0
        for j, d in enumerate((q0, q1, k0, k1, v0, v1)):
            side, lo = divmod(384 * j, CUT_ONE)
            total = total + nt(d[...], w[HALF * side : HALF * (side + 1), lo : lo + 384])
        tmp[:, HALF * i : HALF * (i + 1)] = total.astype(LOW)
    e_ref[...] = nt(tmp[...], order_ref[...])


def input_back(order, d, one, after=()):
    n = d[0].shape[0]
    return whole_call(
        input_back_kernel, [shape(n, D, WIDE)], [pltpu.VMEM((n, D), LOW)], 0, "input_back",
        2 * n * D * 4 * D, order, *d, *one, after=after,
    )[0]


def input_kernel(x_ref, vec_ref, e_ref, dh_ref, dx_ref, vg_ref):
    gain = vec_ref[0:1, :]

    def step(rows, sums):
        e = e_ref[rows, :]
        n, rstd = normal(x_ref[rows, :].astype(WIDE))
        w = e * gain
        dx_ref[rows, :] = dh_ref[rows, :] + rstd * (
            w - jnp.mean(w, axis=-1, keepdims=True) - n * jnp.mean(w * n, axis=-1, keepdims=True)
        )
        return tuple(s + jnp.sum(z.reshape(-1, 8, D), axis=0) for s, z in zip(sums, (e * n, e)))

    zero = jnp.zeros((8, D), WIDE)
    sums = over_rows(x_ref.shape[0], 144, step, (zero,) * 2)
    for k, s in enumerate(sums):
        vg_ref[k : k + 1, :] = jnp.sum(s, axis=0, keepdims=True)


def input_grad(x, vec, e, dh, after=()):
    n = x.shape[0]
    return whole_call(
        input_kernel, [shape(n, D, WIDE), shape(8, D, WIDE)], [], 0, "input_grad",
        2 * n * D * 3 * D, x, vec, e, dh, after=after,
    )


def near_kernel(a, b, c, d, left_ref, right_ref):
    cut = left_ref.shape[1]
    for out, lo in ((left_ref, 0), (right_ref, cut)):
        out[...] = jnp.concatenate([z[:, lo : lo + cut].astype(WIDE) for z in (a, b, c, d)], axis=0).astype(LOW)


def near_pieces(pieces, after=()):
    rows, cols = pieces[0].shape
    return whole_call(near_kernel, [shape(4 * rows, cols // 2)] * 2, [], 0, "near", 1, *pieces, after=after)


def first_kernel(left, got_left, right, got_right, left_ref, right_ref):
    rows = left.shape[0]
    for out, mine, got in ((left_ref, left, got_left), (right_ref, right, got_right)):
        out[:rows, :] = mine[...]
        out[rows:, :] = got[...]


def first_pieces(left, right, got, after=()):
    rows, cols = left.shape
    return whole_call(
        first_kernel, [shape(2 * rows, cols)] * 2, [], 0, "first", 1, left, got[0], right, got[1], after=after
    )


def second_kernel(left, got, right, far, own_ref):
    rows = left.shape[0]
    half = rows // 2
    own_ref[:rows, :] = left[...]
    own_ref[rows : 2 * rows, :] = got[...]
    for i in (0, 1):
        own_ref[2 * rows + 2 * i * half : 2 * rows + (2 * i + 1) * half, :] = right[i * half : (i + 1) * half, :]
        own_ref[2 * rows + (2 * i + 1) * half : 2 * rows + (2 * i + 2) * half, :] = far[i * half : (i + 1) * half, :]


def second_pieces(left, right, got, after=()):
    rows, cols = left.shape
    return whole_call(
        second_kernel, [shape(4 * rows, cols)], [], 0, "second", 1, left, got[0], right, got[1], after=after
    )[0]


def core_sum_kernel(own, got, left_keep, right_keep, left_out, right_out):
    half = left_keep.shape[0]
    rows = half // 2

    def total(lo, count):
        return own[lo : lo + count, :].astype(WIDE) + got[lo : lo + count, :].astype(WIDE)

    left_keep[...] = total(0, half)
    left_out[...] = total(half, half).astype(LOW)
    for i in (0, 1):
        lo = 2 * half + 2 * i * rows
        right_keep[i * rows : (i + 1) * rows, :] = total(lo, rows)
        right_out[i * rows : (i + 1) * rows, :] = total(lo + rows, rows).astype(LOW)


def core_sum(own, got, after=()):
    rows, cols = own.shape[0] // 4, own.shape[1]
    return whole_call(
        core_sum_kernel, [shape(rows, cols, WIDE)] * 2 + [shape(rows, cols)] * 2, [], 0, "core_sum", 1, own, got,
        after=after,
    )


def half_sum_kernel(left, got_left, right, got_right, left_keep, right_keep, left_out, right_out):
    rows = left_keep.shape[0]
    for mine, got, keep, out in ((left, got_left, left_keep, left_out), (right, got_right, right_keep, right_out)):
        keep[...] = mine[:rows, :] + got[:rows, :].astype(WIDE)
        out[...] = (mine[rows:, :] + got[rows:, :].astype(WIDE)).astype(LOW)


def half_sum(left, right, got, after=()):
    rows, cols = left.shape[0] // 2, left.shape[1]
    return whole_call(
        half_sum_kernel, [shape(rows, cols, WIDE)] * 2 + [shape(rows, cols)] * 2, [], 0, "half_sum", 1,
        left, got[0], right, got[1], after=after,
    )


def last_sum_kernel(left, got_left, right, got_right, keep, *outs):
    unit, cut = keep.shape[0], left.shape[1]
    for lo, mine, got in ((0, left, got_left), (cut, right, got_right)):
        total = mine[...] + got[...].astype(WIDE)
        keep[:, lo : lo + cut] = total[:unit]
        for i, out in enumerate(outs):
            out[:, lo : lo + cut] = total[unit * (i + 1) : unit * (i + 2)].astype(LOW)


def last_sum(left, right, got, after=()):
    unit, cols = left.shape[0] // 4, 2 * left.shape[1]
    return whole_call(
        last_sum_kernel, [shape(unit, cols, WIDE)] + [shape(unit, cols)] * 3, [], 0, "last_sum", 1,
        left, got[0], right, got[1], after=after,
    )


def swap(value, bits):
    pairs = [(i, i ^ bits) for i in range(32)]
    return lax.ppermute(value, AXES, pairs)


def tie(values, *first):
    return lax.optimization_barrier((tuple(values), first))[0]


class Flow:
    def __init__(self, steps):
        self.steps = steps
        self.next = next(steps)[:2]

    def issue(self, start=()):
        values, bits = self.next
        values = tie(values, start)
        self.got = tuple(swap(value, bit) for value, bit in zip(values, bits))
        return self.got

    def land(self, end=()):
        values, *bits = self.steps.send(tie(self.got, end))
        if values is None:
            return bits[0]
        self.next = (values, bits[0])
        return bits[1]


def spread(block):
    got = yield (block,) * 3, (8, 16, 24)
    left, right = near_pieces((block,) + got)
    got = yield (left, right), (2, 4), (left, right)
    left, right = first_pieces(left, right, got)
    got = yield (left, right), (4, 2), (left, right)
    own = second_pieces(left, right, got)
    got = yield (own,), (1,), (own,)
    yield None, (own, got[0])


def collect(pieces):
    (got,) = yield (pieces[1],), (1,)
    left, right, *out = ready = core_sum(pieces[0], got)
    got = yield out, (4, 2), tuple(ready)
    left, right, *out = ready = half_sum(left, right, got)
    got = yield out, (2, 4), tuple(ready)
    total, *out = ready = last_sum(left, right, got)
    got = yield out, (8, 16, 24), tuple(ready)
    yield None, (sum((z.astype(WIDE) for z in got), total),)


def stack(whole):
    half, cut = whole.shape[0] // 2, whole.shape[1] // 2
    return tuple(jnp.concatenate([z[:, :cut], z[:, cut:]], axis=0) for z in (whole[:half], whole[half:]))


def unstack(pieces):
    half = pieces[0].shape[0] // 2
    return jnp.concatenate([jnp.concatenate([z[:half], z[half:]], axis=1) for z in pieces], axis=0)


class Whole:
    def __init__(self, result):
        self.result = result

    def issue(self, start=()):
        return ()

    def land(self, end=()):
        return self.result


def spread_any(block):
    return stack(lax.all_gather(block, AXES, axis=0, tiled=True))


def collect_any(pieces):
    return (lax.psum_scatter(unstack(pieces), AXES, scatter_dimension=0, tiled=True).astype(WIDE),)


def rearrange(whole, order, shards):
    return jnp.take(whole.reshape(shards, -1, whole.shape[1]), order, axis=0, mode="clip").reshape(whole.shape)


def adamw(master, moment_one, moment_two, gradient, step_rate, decay_rate):
    first_new = BETA_ONE * moment_one + (1.0 - BETA_ONE) * gradient
    second_new = BETA_TWO * moment_two + (1.0 - BETA_TWO) * gradient * gradient
    first_hat = first_new / (1.0 - BETA_ONE**STEP)
    second_hat = second_new / (1.0 - BETA_TWO**STEP)
    master_new = master - step_rate * (
        first_hat / (jnp.sqrt(second_hat) + ADAM_EPS) + decay_rate * master
    )
    return (first_new, second_new, master_new)


def local(
    tokens_in, cotangent, segments, tile_sides, valid_slots, owners,
    master_qkv, master_out, master_up, master_down, master_vec,
    first_qkv, first_out, first_up, first_down, first_vec,
    second_qkv, second_out, second_up, second_down, second_vec,
):
    shards = lax.axis_size(AXES)
    near = shards == 32
    unit = D // shards
    per_row = master_vec.shape[0] // unit
    ids = jnp.arange(shards, dtype=jnp.int32)
    if near:
        away = owners ^ lax.axis_index(AXES).astype(jnp.int32)
        place = (away >> 3) + 4 * ((away >> 1) & 1) + 8 * ((away >> 2) & 1) + 16 * (away & 1)
        places = jnp.arange(32, dtype=jnp.int32)
        block_of = jnp.sum(places[:, None] * (place[:, None] == places[None, :]), axis=0)
    else:
        place = owners
        block_of = jnp.arange(32, dtype=jnp.int32)
    target = (place[:, None] * unit + jnp.arange(unit, dtype=jnp.int32)[None, :]).reshape(-1)
    order = (target[:, None] == jnp.arange(D, dtype=jnp.int32)[None, :]).astype(LOW)

    def gather(block):
        return Flow(spread(block)) if near else Whole(spread_any(block))

    def scatter(pieces):
        return Flow(collect(pieces)) if near else Whole(collect_any(pieces))

    vec_block = jnp.pad(master_vec.reshape(unit, per_row), ((0, 0), (0, 128 - per_row)))
    block_one = jnp.concatenate(
        [master_qkv[:, :CUT_ONE], vec_block, master_qkv[:, CUT_ONE:], jnp.zeros_like(vec_block)], axis=1
    )
    spans, far = tables(segments, tile_sides, valid_slots)
    slopes = LOG2E * jnp.exp2(-8.0 * (jnp.arange(HEADS, dtype=jnp.int32).astype(WIDE) + 1.0) / HEADS)
    one = gather(block_one.astype(LOW))
    two = gather(jnp.concatenate([master_out, master_up], axis=1).astype(LOW))
    if near:
        three = gather(master_down.astype(LOW))
    else:
        whole = lax.all_gather(master_down.astype(LOW), AXES, axis=0, tiled=True)
        three = Whole(stack(rearrange(whole, owners, shards)))
    one.issue()
    normed = normalized(tokens_in[0])
    done = one.land((far, spans, slopes, order, normed))
    one.issue(done)
    done = one.land()
    sent = one.issue(done) + two.issue(done)
    done = one.land()
    done = done + two.land(sent + done)
    one.issue(done)
    sent = two.issue(done)
    one = one.land()

    x = tokens_in[0]
    dy = cotangent[0]
    act_one, qkv, vec = project(normed, order, one)
    done = two.land((qkv,))
    sent = two.issue(done) + three.issue(done)
    mixed_0, probs_0 = attend(0, qkv, far, spans, slopes, done)
    done = two.land((mixed_0,))
    done = done + three.land((mixed_0,) + sent + done)
    sent = two.issue(done) + three.issue(done)
    mixed_1, probs_1 = attend(3, qkv, far, spans, slopes, done + (mixed_0,))
    done = three.land((mixed_1,) + sent)
    two = two.land((mixed_1,) + sent)
    three.issue(done + two[1:])
    mixed, hidden, act_two, gelu, gelu_slope = upward(x, (mixed_0, mixed_1), vec, order, two, done)
    grad_three = down_grad(block_of, gelu, dy)
    done = three.land(tuple(grad_three))
    three.issue(done)
    three = three.land()
    if not near:
        back = jnp.sum(ids[:, None] * (owners[:, None] == ids[None, :]), axis=0)
        grad_three = stack(rearrange(unstack(grad_three), back, shards))
    flow_three = scatter(grad_three)
    flow_three.issue((three[1],))
    dur, sums_up = down_back(block_of, gelu_slope, dy, three)
    done = flow_three.land((dur,))
    flow_three.issue(done)
    dh, dh_low, dmixed, sums = hidden_grad(vec, order, dur, dy, hidden, two, done)
    grad_two = two_grad(mixed, act_two, dh_low, dur)
    done = flow_three.land(tuple(grad_two)) + tuple(grad_two)
    flow_two = scatter(grad_two)
    sent = flow_three.issue(done) + flow_two.issue(done)
    d0 = attend_back(0, qkv, dmixed, probs_0, spans, done)
    done = flow_three.land(tuple(d0) + sent) + flow_two.land(tuple(d0) + sent)
    sent = flow_three.issue(done) + flow_two.issue(done)
    d1 = attend_back(3, qkv, dmixed, probs_1, spans, done + tuple(d0))
    d = [z for pair in zip(d0, d1) for z in pair]
    dact = input_back(order, d, one)
    tokens_grad, sums_one = input_grad(x, vec, dact, dh)
    grad_one = one_grad(act_one, order, (sums_one, sums, sums_up), d)
    done = tuple(grad_one) + sent
    sum_three, = flow_three.land(done)
    done = flow_two.land(done)
    flow_one = scatter(grad_one)
    sent = flow_one.issue(done) + flow_two.issue(done)
    block_out = down_out(block_of, vec, gelu, hidden, three, done)
    done = flow_one.land((block_out,) + sent) + flow_two.land((block_out,) + sent)
    sent = flow_one.issue(done) + flow_two.issue(done)
    upd_down = adamw(master_down, first_down, second_down, sum_three, RATE_MATRIX, DECAY_MATRIX)
    sent = sent + upd_down
    done = flow_one.land(sent)
    sum_two, = flow_two.land(sent)
    flow_one.issue(done)
    upd_out = adamw(master_out, first_out, second_out, sum_two[:, :D], RATE_MATRIX, DECAY_MATRIX)
    upd_up = adamw(master_up, first_up, second_up, sum_two[:, D:], RATE_MATRIX, DECAY_MATRIX)
    done = flow_one.land(upd_out)
    flow_one.issue(done)
    sum_one, = flow_one.land(upd_up)
    sum_vec = sum_one[:, CUT_ONE : CUT_ONE + per_row].reshape(-1)
    sum_one = jnp.concatenate([sum_one[:, :CUT_ONE], sum_one[:, WIDTH_ONE : WIDTH_ONE + CUT_ONE]], axis=1)
    upd_qkv = adamw(master_qkv, first_qkv, second_qkv, sum_one, RATE_MATRIX, DECAY_MATRIX)
    upd_vec = adamw(master_vec, first_vec, second_vec, sum_vec, RATE_VECTOR, 0.0)
    return (
        (block_out[None], tokens_grad[None]) + upd_qkv + upd_out + upd_up + upd_down + upd_vec
    )


def solution(mesh):
    rows = P(AXES, None)
    flat = P(AXES)
    deep = P(AXES, None, None)
    stored = (rows,) * 4 + (flat,)
    in_specs = (deep,) * 2 + (rows,) * 3 + (P(),) + stored * 3
    out_specs = (deep,) * 2 + (rows,) * 12 + (flat,) * 3
    return jax.shard_map(local, mesh=mesh, in_specs=in_specs, out_specs=out_specs, check_vma=False)
```

```python
import functools

import jax
import jax.numpy as jnp
from jax import lax
from jax.experimental import pallas as pl
from jax.experimental.pallas import tpu as pltpu
from jax.sharding import PartitionSpec as P

D = 768
HEADS = 12
FF = 3072
STEP = 10
HALF = 384
WIN = 256
SMALL = 160
LARGE = 240
LOG2E = 1.4426950408889634
CUT_ONE = 1152
WIDTH_ONE = 1280
WIDTH_TWO = 1920
WIDTH_THREE = 384

EPSILON = 1e-05
BETA_ONE = 0.9
BETA_TWO = 0.999
ADAM_EPS = 1e-08
RATE_MATRIX = 0.05
DECAY_MATRIX = 0.05
RATE_VECTOR = 0.3

AXES = ("dp", "fsdp")
LOW = jnp.bfloat16
WIDE = jnp.float32
VMEM_BYTES = 8 * 2**20


def nn(left, right):
    return lax.dot_general(left, right, (((1,), (0,)), ((), ())), preferred_element_type=WIDE)


def nt(left, right):
    return lax.dot_general(left, right, (((1,), (1,)), ((), ())), preferred_element_type=WIDE)


def tn(left, right):
    return lax.dot_general(left, right, (((0,), (0,)), ((), ())), preferred_element_type=WIDE)


def shape(rows, cols, kind=LOW):
    return jax.ShapeDtypeStruct((rows, cols), kind)


def later(kernel, inputs, extra):
    return lambda *refs: kernel(*refs[:inputs], *refs[inputs + extra :])


def whole_call(kernel, outs, scratch, smem, name, flops, *args, anywhere=(), after=()):
    specs = []
    for i in range(len(args)):
        space = pltpu.SMEM if i < smem else pl.ANY if i in anywhere else pltpu.VMEM
        specs.append(pl.BlockSpec(memory_space=space))
    moved = sum(a.size * a.dtype.itemsize for a in args) + sum(o.size * o.dtype.itemsize for o in outs)
    return pl.pallas_call(
        later(kernel, len(args), len(after)),
        in_specs=specs + [pl.BlockSpec(memory_space=pl.ANY)] * len(after),
        out_specs=[pl.BlockSpec(memory_space=pltpu.VMEM)] * len(outs),
        out_shape=outs,
        scratch_shapes=scratch,
        compiler_params=pltpu.CompilerParams(vmem_limit_bytes=VMEM_BYTES),
        cost_estimate=pl.CostEstimate(flops=flops, bytes_accessed=moved, transcendentals=0),
        name=name,
    )(*args, *after)


def over_rows(count, step, body, init=None):
    return lax.fori_loop(0, count // step, lambda i, c: body(pl.ds(pl.multiple_of(i * step, step), step), c), init)


def normal(values):
    centre = values - jnp.mean(values, axis=-1, keepdims=True)
    rstd = lax.rsqrt(jnp.mean(centre * centre, axis=-1, keepdims=True) + EPSILON)
    return centre * rstd, rstd


def both(pair, side, lo, width):
    rows = slice(HALF * side, HALF * (side + 1))
    return jnp.concatenate([z[rows, lo : lo + width] for z in pair], axis=0)


def normal_kernel(x_ref, n_ref):
    def norm(rows, _):
        n_ref[rows, :] = normal(x_ref[rows, :].astype(WIDE))[0]

    over_rows(x_ref.shape[0], 144, norm)


def normalized(x):
    return whole_call(normal_kernel, [shape(*x.shape, WIDE)], [], 0, "normalized", 1, x)[0]


def qkv_kernel(n_ref, order_ref, own, other, a_ref, qkv_ref, vec_ref, tmp, wide):
    moved = jnp.concatenate([z[:HALF, CUT_ONE:] for z in (own, other)], axis=0)
    wide[...] = nn(order_ref[...], moved)
    vec_ref[...] = jnp.zeros_like(vec_ref)
    for k in range(10):
        first = min(D * k // 10 // 8 * 8, D - 88)

        def tenths(rows):
            entry = lax.broadcasted_iota(jnp.int32, (rows, D), 1) + D * k
            tenth = (entry * 52429) >> 19
            return tenth, entry - 10 * tenth, lax.broadcasted_iota(jnp.int32, (rows, D), 0)

        _, column, row = tenths(128)
        picked = nn(wide[first : first + 88, :].astype(LOW), (row == column).astype(LOW))
        tenth, _, row = tenths(88)
        vec_ref[k : k + 1, :] = jnp.sum(jnp.where(row + first == tenth, picked, 0.0), axis=0, keepdims=True)
    gain, shift = vec_ref[0:1, :], vec_ref[1:2, :]

    def norm(rows, _):
        tmp[rows, :] = (n_ref[rows, :] * gain + shift).astype(LOW)

    over_rows(n_ref.shape[0], 144, norm)
    a_ref[...] = nn(tmp[...], order_ref[...]).astype(LOW)
    for col in range(0, 3 * D, 384):
        w = both((own, other), *divmod(col, CUT_ONE), 384)
        qkv_ref[:, col : col + 384] = nn(a_ref[...], w).astype(LOW)


def project(normed, order, one, after=()):
    n = normed.shape[0]
    return whole_call(
        qkv_kernel, [shape(n, D), shape(n, 3 * D), shape(16, D, WIDE)],
        [pltpu.VMEM((n, D), LOW), pltpu.VMEM((D, 128), WIDE)], 0, "project",
        2 * n * D * (4 * D), normed, order, *one, after=after,
    )


def each_tile(spans, body):
    def step(t, carry):
        for kind, rows in ((1, SMALL), (2, LARGE)):

            @pl.when(spans[t, 4] == kind)
            def _():
                body(t, pl.multiple_of(spans[t, 2], 16), rows, pl.multiple_of(spans[t, 3], 16))

        return carry

    lax.fori_loop(0, 4, step, 0)


def padding_rows(spans, shape_):
    return lax.broadcasted_iota(jnp.int32, shape_, 0) >= spans[4, 0]


def own_half(values, e):
    lane = lax.broadcasted_iota(jnp.int32, values.shape, 1)
    return jnp.where((lane < 64) if e == 0 else (lane >= 64), values, jnp.zeros_like(values))


def attend_kernel(base, spans, slopes, qkv_ref, far_ref, o_ref, p_ref, acc):
    acc[...] = jnp.zeros_like(acc)

    def tile(t, at, count, key):
        rows, keys = pl.ds(at, count), pl.ds(key, WIN)
        row = lax.broadcasted_iota(jnp.int32, (count, 1), 0) + at
        inside = ((row >= spans[t, 0]) & (row < spans[t, 1])).astype(WIDE)
        far = far_ref[t, :count, :]
        for pair in range(3):
            col = (base + pair) * 128
            q, k, v = [qkv_ref[z, col + i * D : col + i * D + 128] for i, z in enumerate((rows, keys, keys))]
            out = None
            for e in range(2):
                s = nt(q, own_half(k, e)) * (0.125 * LOG2E) - slopes[2 * (base + pair) + e] * far
                p = jnp.exp2(s - jnp.max(s, axis=1, keepdims=True))
                p = (p * (inside / jnp.sum(p, axis=1, keepdims=True))).astype(LOW)
                p_ref[t, 2 * pair + e, :count, :] = p
                part = nn(p, own_half(v, e))
                out = part if out is None else out + part
            acc[rows, pair * 128 : pair * 128 + 128] += out

    each_tile(spans, tile)
    v = qkv_ref[:, base * 128 + 2 * D : base * 128 + 2 * D + HALF]
    o_ref[...] = jnp.where(padding_rows(spans, v.shape), v, acc[...].astype(LOW))


def attend(base, qkv, far, spans, slopes, after=()):
    n = qkv.shape[0]
    return whole_call(
        functools.partial(attend_kernel, base),
        [shape(n, HALF), jax.ShapeDtypeStruct((4, HEADS // 2, LARGE, WIN), LOW)],
        [pltpu.VMEM((n, HALF), WIDE)], 2, "attend", 9 * 10**9, spans, slopes, qkv, far, after=after,
    )


def attend_back_kernel(base, spans, qkv_ref, g_ref, p_ref, dq_ref, dk_ref, dv_ref, aq, ak, av):
    for acc in (aq, ak, av):
        acc[...] = jnp.zeros_like(acc)

    def tile(t, at, count, key):
        rows, keys = pl.ds(at, count), pl.ds(key, WIN)
        for pair in range(3):
            col = (base + pair) * 128
            q, k, v = [qkv_ref[z, col + i * D : col + i * D + 128] for i, z in enumerate((rows, keys, keys))]
            g = g_ref[rows, col : col + 128]
            sums = None
            for e in range(2):
                ge = own_half(g, e)
                p = p_ref[t, 2 * pair + e, :count, :]
                wide = p.astype(WIDE)
                d = wide * nt(ge * 0.125, v)
                d = (d - wide * jnp.sum(d, axis=1, keepdims=True)).astype(LOW)
                parts = (nn(d, own_half(k, e)), tn(d, own_half(q, e)), tn(p, ge))
                sums = parts if sums is None else tuple(a + b for a, b in zip(sums, parts))
            part = slice(pair * 128, pair * 128 + 128)
            aq[rows, part] += sums[0]
            ak[keys, part] += sums[1]
            av[keys, part] += sums[2]

    each_tile(spans, tile)
    dq_ref[...] = aq[...].astype(LOW)
    dk_ref[...] = ak[...].astype(LOW)
    g = g_ref[:, base * 128 : base * 128 + HALF]
    dv_ref[...] = jnp.where(padding_rows(spans, g.shape), g, av[...].astype(LOW))


def attend_back(base, qkv, grad, probs, spans, after=()):
    n = qkv.shape[0]
    return whole_call(
        functools.partial(attend_back_kernel, base), [shape(n, HALF)] * 3, [pltpu.VMEM((n, HALF), WIDE)] * 3, 1,
        "attend_back", 12 * 10**9, spans, qkv, grad, probs, after=after,
    )


def tables_kernel(seg_ref, side_ref, valid_ref, spans, far_ref):
    n = seg_ref.shape[1]
    seg, side, valid = [z[...].astype(WIDE) for z in (seg_ref, side_ref, valid_ref)]
    live = jnp.sum(valid).astype(jnp.int32)
    for z in range(5):
        spans[4, z] = live
    for t in range(4):
        low = jnp.sum((seg < t).astype(WIDE)).astype(jnp.int32)
        high = jnp.sum((seg <= t).astype(WIDE)).astype(jnp.int32)
        width = jnp.max(jnp.where(seg == t, side, 1.0))
        small = high - low <= SMALL - 16
        start = low // 16 * 16
        at = jnp.minimum(start, jnp.where(small, n - SMALL, n - LARGE))
        key = jnp.minimum(start, n - WIN)
        kind = jnp.where((high > low) & (low < live), jnp.where(small, 1, 2), 0)
        for z, value in enumerate((low, high, at, key, kind)):
            spans[t, z] = value

        def places(first, shape_, dim):
            slot = lax.broadcasted_iota(jnp.int32, shape_, dim) + first
            place = (slot - low).astype(WIDE)
            row = jnp.floor((place + 0.5) / width)
            return (slot >= low) & (slot < high), row, place - row * width

        inside, row, col = places(at, (LARGE, 1), 0)
        inside_key, row_key, col_key = places(key, (1, WIN), 1)
        down, along = row - row_key, col - col_key
        far_ref[t] = jnp.where(inside & inside_key, jnp.sqrt(down * down + along * along), 1e12)


def tables(seg, side, valid):
    vmem, smem = [pl.BlockSpec(memory_space=z) for z in (pltpu.VMEM, pltpu.SMEM)]
    return pl.pallas_call(
        tables_kernel,
        in_specs=[vmem] * 3,
        out_specs=[smem, vmem],
        out_shape=[jax.ShapeDtypeStruct((5, 5), jnp.int32), jax.ShapeDtypeStruct((4, LARGE, WIN), WIDE)],
        compiler_params=pltpu.CompilerParams(vmem_limit_bytes=VMEM_BYTES),
        name="tables",
    )(seg, side, valid)


def bell(u):
    share = 0.5 + 0.5 * lax.erf(u * 0.7071067811865476)
    return u * share, share + u * (jnp.exp2(u * u * -0.7213475204444817) * 0.3989422804014327)


def up_kernel(x_ref, o0_ref, o1_ref, vec_ref, order_ref, own, other, mixed_ref, h_ref, a_ref, gl_ref, gp_ref, tmp):
    mixed_ref[...] = (
        nn(o0_ref[...], order_ref[:HALF, :]) + nn(o1_ref[...], order_ref[HALF:, :])
    ).astype(LOW)
    for col in (0, 384):
        part = slice(col, col + 384)
        h_ref[:, part] = x_ref[:, part].astype(WIDE) + nn(mixed_ref[...], both((own, other), 0, col, 384)) + vec_ref[2:3, part]
    gain, shift = vec_ref[3:4, :], vec_ref[4:5, :]

    def norm(rows, _):
        tmp[rows, :] = (normal(h_ref[rows, :])[0] * gain + shift).astype(LOW)

    over_rows(x_ref.shape[0], 144, norm)
    a_ref[...] = nn(tmp[...], order_ref[...]).astype(LOW)
    for col in range(0, FF, 384):
        k = 5 + col // D
        u = nn(a_ref[...], both((own, other), *divmod(col + D, WIDTH_TWO), 384)) + vec_ref[k : k + 1, col % D : col % D + 384]
        value, slope = bell(u)
        gl_ref[:, col : col + 384] = value.astype(LOW)
        gp_ref[:, col : col + 384] = slope.astype(LOW)


def upward(x, o, vec, order, two, after=()):
    n = x.shape[0]
    return whole_call(
        up_kernel, [shape(n, D), shape(n, D, WIDE), shape(n, D), shape(n, FF), shape(n, FF)],
        [pltpu.VMEM((n, D), LOW)], 0, "upward", 2 * n * D * (7 * D) * 2, x, *o, vec, order, *two,
        after=after,
    )


def fetch_down(block_of, own, other, wd):
    for p in range(32):
        dst = pl.ds(pl.multiple_of(block_of[p] * 96, 96), 96)
        piece = own if p < 16 else other
        for side in (0, 1):
            lo = p % 16 * 96 + side * (FF // 2)
            wd[dst, side * WIDTH_THREE : (side + 1) * WIDTH_THREE] = piece[lo : lo + 96, :]


def down_kernel(block_of, gp_ref, dy_ref, own, other, dur_ref, vg_ref, wd):
    fetch_down(block_of, own, other, wd)
    for col in range(0, FF, 384):
        part = slice(col, col + 384)
        du = nt(dy_ref[...], wd[part, :]) * gp_ref[:, part].astype(WIDE)
        dur_ref[:, part] = du.astype(LOW)
        k = col // D
        vg_ref[k : k + 1, col % D : col % D + 384] = jnp.sum(du, axis=0, keepdims=True)


def down_back(block_of, gp, dy, three, after=()):
    n = dy.shape[0]
    return whole_call(
        down_kernel, [shape(n, FF), shape(8, D, WIDE)], [pltpu.VMEM((FF, D), LOW)], 1,
        "down_back", 2 * n * D * (4 * D), block_of, gp, dy, *three, after=after,
    )


def down_out_kernel(block_of, vec_ref, gl_ref, h_ref, own, other, out_ref, wd):
    fetch_down(block_of, own, other, wd)
    for col in (0, 384):
        part = slice(col, col + 384)
        out_ref[:, part] = (h_ref[:, part] + nn(gl_ref[...], wd[:, part]) + vec_ref[9:10, part]).astype(LOW)


def down_out(block_of, vec, gl, h, three, after=()):
    n = h.shape[0]
    return whole_call(
        down_out_kernel, [shape(n, D)], [pltpu.VMEM((FF, D), LOW)], 1,
        "down_out", 2 * n * D * (4 * D), block_of, vec, gl, h, *three, after=after,
    )[0]


def hidden_kernel(vec_ref, order_ref, dur_ref, dy_ref, h_ref, own, other, dh_ref, dhr_ref, dor_ref, vg_ref, tmp):
    split = WIDTH_TWO - D
    for i, w in enumerate((own, other)):
        tmp[:, HALF * i : HALF * (i + 1)] = (
            nt(dur_ref[:, :split], w[:HALF, D:]) + nt(dur_ref[:, split:], w[HALF:, :])
        ).astype(LOW)
    dh_ref[...] = nt(tmp[...], order_ref[...])
    gain = vec_ref[3:4, :]

    def step(rows, sums):
        e = dh_ref[rows, :]
        dy = dy_ref[rows, :].astype(WIDE)
        n, rstd = normal(h_ref[rows, :])
        w = e * gain
        dh = dy + rstd * (w - jnp.mean(w, axis=-1, keepdims=True) - n * jnp.mean(w * n, axis=-1, keepdims=True))
        dh_ref[rows, :] = dh
        dhr_ref[rows, :] = dh.astype(LOW)
        return tuple(s + jnp.sum(z.reshape(-1, 8, D), axis=0) for s, z in zip(sums, (dh, e * n, e, dy)))

    zero = jnp.zeros((8, D), WIDE)
    sums = over_rows(h_ref.shape[0], 144, step, (zero,) * 4)
    for k, s in enumerate(sums):
        vg_ref[k : k + 1, :] = jnp.sum(s, axis=0, keepdims=True)
    for i, w in enumerate((own, other)):
        tmp[:, HALF * i : HALF * (i + 1)] = nt(dhr_ref[...], w[:HALF, :D]).astype(LOW)
    dor_ref[...] = nt(tmp[...], order_ref[...]).astype(LOW)


def hidden_grad(vec, order, dur, dy, h, two, after=()):
    n = h.shape[0]
    return whole_call(
        hidden_kernel, [shape(n, D, WIDE), shape(n, D), shape(n, D), shape(8, D, WIDE)],
        [pltpu.VMEM((n, D), LOW)], 0, "hidden_grad",
        2 * n * D * (7 * D), vec, order, dur, dy, h, *two, after=after,
    )


def down_grad_kernel(block_of, gl_ref, dy_ref, own, other, all_ref):
    for col in range(0, FF, 384):
        all_ref[col : col + 384, :] = tn(gl_ref[:, col : col + 384], dy_ref[...]).astype(LOW)
    for p in range(32):
        src = pl.ds(pl.multiple_of(block_of[p] * 96, 96), 96)
        piece = own if p < 16 else other
        for side in (0, 1):
            lo = p % 16 * 96 + side * (FF // 2)
            piece[lo : lo + 96, :] = all_ref[src, side * WIDTH_THREE : (side + 1) * WIDTH_THREE]


def down_grad(block_of, gl, dy, after=()):
    n = dy.shape[0]
    return whole_call(
        down_grad_kernel, [shape(FF, WIDTH_THREE)] * 2, [pltpu.VMEM((FF, D), LOW)], 1, "down_grad",
        2 * n * D * FF, block_of, gl, dy, after=after,
    )


def two_grad_kernel(mixed_ref, a_ref, dhr_ref, dur_ref, own, other):
    for col in range(0, D + FF, 384):
        left, right = (mixed_ref, dhr_ref[:, col : col + 384]) if col < D else (a_ref, dur_ref[:, col - D : col - D + 384])
        t = tn(left[...], right).astype(LOW)
        side, lo = divmod(col, WIDTH_TWO)
        own[HALF * side : HALF * (side + 1), lo : lo + 384] = t[:HALF]
        other[HALF * side : HALF * (side + 1), lo : lo + 384] = t[HALF:]


def two_grad(mixed, a, dhr, dur, after=()):
    n = a.shape[0]
    return whole_call(two_grad_kernel, [shape(D, WIDTH_TWO)] * 2, [], 0, "two_grad", 2 * n * D * (D + FF), mixed, a, dhr, dur,
                      after=after)


def one_grad_kernel(a_ref, order_ref, first_ref, mid_ref, up_ref, *refs):
    halves, (own, other, wide) = refs[:6], refs[6:]
    wide[...] = jnp.zeros_like(wide)
    rows = [first_ref[0:1, :], first_ref[1:2, :]] + [mid_ref[i : i + 1, :] for i in range(3)]
    rows = rows + [up_ref[i : i + 1, :] for i in range(4)] + [mid_ref[3:4, :]]
    for k, values in enumerate(rows):
        first = min(D * k // 10 // 8 * 8, D - 88)
        entry = lax.broadcasted_iota(jnp.int32, (88, D), 1) + D * k
        row = lax.broadcasted_iota(jnp.int32, (88, D), 0) + first
        spread_out = jnp.where(row == (entry * 52429) >> 19, values, 0.0).astype(LOW)
        entry = lax.broadcasted_iota(jnp.int32, (D, 128), 0) + D * k
        column = entry - 10 * ((entry * 52429) >> 19)
        pick = (lax.broadcasted_iota(jnp.int32, (D, 128), 1) == column).astype(LOW)
        wide[first : first + 88, :] += nn(spread_out, pick)
    moved = tn(order_ref[...], wide[...].astype(LOW)).astype(LOW)
    for i, out in enumerate((own, other)):
        out[:HALF, CUT_ONE:] = moved[HALF * i : HALF * (i + 1), :]
        out[HALF:, CUT_ONE:] = jnp.zeros((HALF, WIDTH_ONE - CUT_ONE), LOW)
    for i, half in enumerate(halves):
        t = tn(a_ref[...], half[...]).astype(LOW)
        side, lo = divmod(384 * i, CUT_ONE)
        own[HALF * side : HALF * (side + 1), lo : lo + 384] = t[:HALF]
        other[HALF * side : HALF * (side + 1), lo : lo + 384] = t[HALF:]


def one_grad(a, order, sums, d, after=()):
    n = a.shape[0]
    return whole_call(
        one_grad_kernel, [shape(D, WIDTH_ONE)] * 2, [pltpu.VMEM((D, 128), WIDE)], 0, "one_grad",
        2 * n * D * 3 * D, a, order, *sums, *d, after=after,
    )


def input_back_kernel(order_ref, q0, q1, k0, k1, v0, v1, own, other, e_ref, tmp):
    for i, w in enumerate((own, other)):
        total = 0.0
        for j, d in enumerate((q0, q1, k0, k1, v0, v1)):
            side, lo = divmod(384 * j, CUT_ONE)
            total = total + nt(d[...], w[HALF * side : HALF * (side + 1), lo : lo + 384])
        tmp[:, HALF * i : HALF * (i + 1)] = total.astype(LOW)
    e_ref[...] = nt(tmp[...], order_ref[...])


def input_back(order, d, one, after=()):
    n = d[0].shape[0]
    return whole_call(
        input_back_kernel, [shape(n, D, WIDE)], [pltpu.VMEM((n, D), LOW)], 0, "input_back",
        2 * n * D * 4 * D, order, *d, *one, after=after,
    )[0]


def input_kernel(x_ref, vec_ref, e_ref, dh_ref, dx_ref, vg_ref):
    gain = vec_ref[0:1, :]

    def step(rows, sums):
        e = e_ref[rows, :]
        n, rstd = normal(x_ref[rows, :].astype(WIDE))
        w = e * gain
        dx_ref[rows, :] = dh_ref[rows, :] + rstd * (
            w - jnp.mean(w, axis=-1, keepdims=True) - n * jnp.mean(w * n, axis=-1, keepdims=True)
        )
        return tuple(s + jnp.sum(z.reshape(-1, 8, D), axis=0) for s, z in zip(sums, (e * n, e)))

    zero = jnp.zeros((8, D), WIDE)
    sums = over_rows(x_ref.shape[0], 144, step, (zero,) * 2)
    for k, s in enumerate(sums):
        vg_ref[k : k + 1, :] = jnp.sum(s, axis=0, keepdims=True)


def input_grad(x, vec, e, dh, after=()):
    n = x.shape[0]
    return whole_call(
        input_kernel, [shape(n, D, WIDE), shape(8, D, WIDE)], [], 0, "input_grad",
        2 * n * D * 3 * D, x, vec, e, dh, after=after,
    )


def near_kernel(a, b, c, d, left_ref, right_ref):
    cut = left_ref.shape[1]
    for out, lo in ((left_ref, 0), (right_ref, cut)):
        out[...] = jnp.concatenate([z[:, lo : lo + cut].astype(WIDE) for z in (a, b, c, d)], axis=0).astype(LOW)


def near_pieces(pieces, after=()):
    rows, cols = pieces[0].shape
    return whole_call(near_kernel, [shape(4 * rows, cols // 2)] * 2, [], 0, "near", 1, *pieces, after=after)


def first_kernel(left, got_left, right, got_right, left_ref, right_ref):
    rows = left.shape[0]
    for out, mine, got in ((left_ref, left, got_left), (right_ref, right, got_right)):
        out[:rows, :] = mine[...]
        out[rows:, :] = got[...]


def first_pieces(left, right, got, after=()):
    rows, cols = left.shape
    return whole_call(
        first_kernel, [shape(2 * rows, cols)] * 2, [], 0, "first", 1, left, got[0], right, got[1], after=after
    )


def second_kernel(left, got, right, far, own_ref):
    rows = left.shape[0]
    half = rows // 2
    own_ref[:rows, :] = left[...]
    own_ref[rows : 2 * rows, :] = got[...]
    for i in (0, 1):
        own_ref[2 * rows + 2 * i * half : 2 * rows + (2 * i + 1) * half, :] = right[i * half : (i + 1) * half, :]
        own_ref[2 * rows + (2 * i + 1) * half : 2 * rows + (2 * i + 2) * half, :] = far[i * half : (i + 1) * half, :]


def second_pieces(left, right, got, after=()):
    rows, cols = left.shape
    return whole_call(
        second_kernel, [shape(4 * rows, cols)], [], 0, "second", 1, left, got[0], right, got[1], after=after
    )[0]


def core_sum_kernel(own, got, left_keep, right_keep, left_out, right_out):
    half = left_keep.shape[0]
    rows = half // 2

    def total(lo, count):
        return own[lo : lo + count, :].astype(WIDE) + got[lo : lo + count, :].astype(WIDE)

    left_keep[...] = total(0, half)
    left_out[...] = total(half, half).astype(LOW)
    for i in (0, 1):
        lo = 2 * half + 2 * i * rows
        right_keep[i * rows : (i + 1) * rows, :] = total(lo, rows)
        right_out[i * rows : (i + 1) * rows, :] = total(lo + rows, rows).astype(LOW)


def core_sum(own, got, after=()):
    rows, cols = own.shape[0] // 4, own.shape[1]
    return whole_call(
        core_sum_kernel, [shape(rows, cols, WIDE)] * 2 + [shape(rows, cols)] * 2, [], 0, "core_sum", 1, own, got,
        after=after,
    )


def half_sum_kernel(left, got_left, right, got_right, left_keep, right_keep, left_out, right_out):
    rows = left_keep.shape[0]
    for mine, got, keep, out in ((left, got_left, left_keep, left_out), (right, got_right, right_keep, right_out)):
        keep[...] = mine[:rows, :] + got[:rows, :].astype(WIDE)
        out[...] = (mine[rows:, :] + got[rows:, :].astype(WIDE)).astype(LOW)


def half_sum(left, right, got, after=()):
    rows, cols = left.shape[0] // 2, left.shape[1]
    return whole_call(
        half_sum_kernel, [shape(rows, cols, WIDE)] * 2 + [shape(rows, cols)] * 2, [], 0, "half_sum", 1,
        left, got[0], right, got[1], after=after,
    )


def last_sum_kernel(left, got_left, right, got_right, keep, *outs):
    unit, cut = keep.shape[0], left.shape[1]
    for lo, mine, got in ((0, left, got_left), (cut, right, got_right)):
        total = mine[...] + got[...].astype(WIDE)
        keep[:, lo : lo + cut] = total[:unit]
        for i, out in enumerate(outs):
            out[:, lo : lo + cut] = total[unit * (i + 1) : unit * (i + 2)].astype(LOW)


def last_sum(left, right, got, after=()):
    unit, cols = left.shape[0] // 4, 2 * left.shape[1]
    return whole_call(
        last_sum_kernel, [shape(unit, cols, WIDE)] + [shape(unit, cols)] * 3, [], 0, "last_sum", 1,
        left, got[0], right, got[1], after=after,
    )


def swap(value, bits):
    pairs = [(i, i ^ bits) for i in range(32)]
    return lax.ppermute(value, AXES, pairs)


def tie(values, *first):
    return lax.optimization_barrier((tuple(values), first))[0]


class Flow:
    def __init__(self, steps):
        self.steps = steps
        self.next = next(steps)[:2]

    def issue(self, start=()):
        values, bits = self.next
        values = tie(values, start)
        self.got = tuple(swap(value, bit) for value, bit in zip(values, bits))
        return self.got

    def land(self, end=()):
        values, *bits = self.steps.send(tie(self.got, end))
        if values is None:
            return bits[0]
        self.next = (values, bits[0])
        return bits[1]


def spread(block):
    got = yield (block,) * 3, (8, 16, 24)
    left, right = near_pieces((block,) + got)
    got = yield (left, right), (2, 4), (left, right)
    left, right = first_pieces(left, right, got)
    got = yield (left, right), (4, 2), (left, right)
    own = second_pieces(left, right, got)
    got = yield (own,), (1,), (own,)
    yield None, (own, got[0])


def collect(pieces):
    (got,) = yield (pieces[1],), (1,)
    left, right, *out = ready = core_sum(pieces[0], got)
    got = yield out, (4, 2), tuple(ready)
    left, right, *out = ready = half_sum(left, right, got)
    got = yield out, (2, 4), tuple(ready)
    total, *out = ready = last_sum(left, right, got)
    got = yield out, (8, 16, 24), tuple(ready)
    yield None, (sum((z.astype(WIDE) for z in got), total),)


def stack(whole):
    half, cut = whole.shape[0] // 2, whole.shape[1] // 2
    return tuple(jnp.concatenate([z[:, :cut], z[:, cut:]], axis=0) for z in (whole[:half], whole[half:]))


def unstack(pieces):
    half = pieces[0].shape[0] // 2
    return jnp.concatenate([jnp.concatenate([z[:half], z[half:]], axis=1) for z in pieces], axis=0)


class Whole:
    def __init__(self, result):
        self.result = result

    def issue(self, start=()):
        return ()

    def land(self, end=()):
        return self.result


def spread_any(block):
    return stack(lax.all_gather(block, AXES, axis=0, tiled=True))


def collect_any(pieces):
    return (lax.psum_scatter(unstack(pieces), AXES, scatter_dimension=0, tiled=True).astype(WIDE),)


def rearrange(whole, order, shards):
    return jnp.take(whole.reshape(shards, -1, whole.shape[1]), order, axis=0, mode="clip").reshape(whole.shape)


def adamw(master, moment_one, moment_two, gradient, step_rate, decay_rate):
    first_new = BETA_ONE * moment_one + (1.0 - BETA_ONE) * gradient
    second_new = BETA_TWO * moment_two + (1.0 - BETA_TWO) * gradient * gradient
    first_hat = first_new / (1.0 - BETA_ONE**STEP)
    second_hat = second_new / (1.0 - BETA_TWO**STEP)
    master_new = master - step_rate * (
        first_hat / (jnp.sqrt(second_hat) + ADAM_EPS) + decay_rate * master
    )
    return (first_new, second_new, master_new)


def local(
    tokens_in, cotangent, segments, tile_sides, valid_slots, owners,
    master_qkv, master_out, master_up, master_down, master_vec,
    first_qkv, first_out, first_up, first_down, first_vec,
    second_qkv, second_out, second_up, second_down, second_vec,
):
    shards = lax.axis_size(AXES)
    near = shards == 32
    unit = D // shards
    per_row = master_vec.shape[0] // unit
    ids = jnp.arange(shards, dtype=jnp.int32)
    if near:
        away = owners ^ lax.axis_index(AXES).astype(jnp.int32)
        place = (away >> 3) + 4 * ((away >> 1) & 1) + 8 * ((away >> 2) & 1) + 16 * (away & 1)
        places = jnp.arange(32, dtype=jnp.int32)
        block_of = jnp.sum(places[:, None] * (place[:, None] == places[None, :]), axis=0)
    else:
        place = owners
        block_of = jnp.arange(32, dtype=jnp.int32)
    target = (place[:, None] * unit + jnp.arange(unit, dtype=jnp.int32)[None, :]).reshape(-1)
    order = (target[:, None] == jnp.arange(D, dtype=jnp.int32)[None, :]).astype(LOW)

    def gather(block):
        return Flow(spread(block)) if near else Whole(spread_any(block))

    def scatter(pieces):
        return Flow(collect(pieces)) if near else Whole(collect_any(pieces))

    vec_block = jnp.pad(master_vec.reshape(unit, per_row), ((0, 0), (0, 128 - per_row)))
    block_one = jnp.concatenate(
        [master_qkv[:, :CUT_ONE], vec_block, master_qkv[:, CUT_ONE:], jnp.zeros_like(vec_block)], axis=1
    )
    spans, far = tables(segments, tile_sides, valid_slots)
    slopes = LOG2E * jnp.exp2(-8.0 * (jnp.arange(HEADS, dtype=jnp.int32).astype(WIDE) + 1.0) / HEADS)
    one = gather(block_one.astype(LOW))
    two = gather(jnp.concatenate([master_out, master_up], axis=1).astype(LOW))
    if near:
        three = gather(master_down.astype(LOW))
    else:
        whole = lax.all_gather(master_down.astype(LOW), AXES, axis=0, tiled=True)
        three = Whole(stack(rearrange(whole, owners, shards)))
    one.issue()
    normed = normalized(tokens_in[0])
    done = one.land((far, spans, slopes, order, normed))
    one.issue(done)
    done = one.land()
    sent = one.issue(done) + two.issue(done)
    done = one.land()
    done = done + two.land(sent + done)
    one.issue(done)
    sent = two.issue(done)
    one = one.land()

    x = tokens_in[0]
    dy = cotangent[0]
    act_one, qkv, vec = project(normed, order, one)
    done = two.land((qkv,))
    sent = two.issue(done) + three.issue(done)
    mixed_0, probs_0 = attend(0, qkv, far, spans, slopes, done)
    done = two.land((mixed_0,))
    done = done + three.land((mixed_0,) + sent + done)
    sent = two.issue(done) + three.issue(done)
    mixed_1, probs_1 = attend(3, qkv, far, spans, slopes, done + (mixed_0,))
    done = three.land((mixed_1,) + sent)
    two = two.land((mixed_1,) + sent)
    three.issue(done + two[1:])
    mixed, hidden, act_two, gelu, gelu_slope = upward(x, (mixed_0, mixed_1), vec, order, two, done)
    grad_three = down_grad(block_of, gelu, dy)
    done = three.land(tuple(grad_three))
    three.issue(done)
    three = three.land()
    if not near:
        back = jnp.sum(ids[:, None] * (owners[:, None] == ids[None, :]), axis=0)
        grad_three = stack(rearrange(unstack(grad_three), back, shards))
    flow_three = scatter(grad_three)
    flow_three.issue()
    dur, sums_up = down_back(block_of, gelu_slope, dy, three)
    done = flow_three.land((dur,))
    flow_three.issue(done)
    dh, dh_low, dmixed, sums = hidden_grad(vec, order, dur, dy, hidden, two, done)
    grad_two = two_grad(mixed, act_two, dh_low, dur)
    done = flow_three.land(tuple(grad_two)) + tuple(grad_two)
    flow_two = scatter(grad_two)
    sent = flow_three.issue(done) + flow_two.issue(done)
    d0 = attend_back(0, qkv, dmixed, probs_0, spans, done)
    done = flow_three.land(tuple(d0) + sent) + flow_two.land(tuple(d0) + sent)
    sent = flow_three.issue(done) + flow_two.issue(done)
    d1 = attend_back(3, qkv, dmixed, probs_1, spans, done + tuple(d0))
    d = [z for pair in zip(d0, d1) for z in pair]
    dact = input_back(order, d, one)
    tokens_grad, sums_one = input_grad(x, vec, dact, dh)
    grad_one = one_grad(act_one, order, (sums_one, sums, sums_up), d)
    done = tuple(grad_one) + sent
    sum_three, = flow_three.land(done)
    done = flow_two.land(done)
    flow_one = scatter(grad_one)
    sent = flow_one.issue(done) + flow_two.issue(done)
    block_out = down_out(block_of, vec, gelu, hidden, three, done)
    done = flow_one.land((block_out,) + sent) + flow_two.land((block_out,) + sent)
    sent = flow_one.issue(done) + flow_two.issue(done)
    upd_down = adamw(master_down, first_down, second_down, sum_three, RATE_MATRIX, DECAY_MATRIX)
    sent = sent + upd_down
    done = flow_one.land(sent)
    sum_two, = flow_two.land(sent)
    flow_one.issue(done)
    upd_out = adamw(master_out, first_out, second_out, sum_two[:, :D], RATE_MATRIX, DECAY_MATRIX)
    upd_up = adamw(master_up, first_up, second_up, sum_two[:, D:], RATE_MATRIX, DECAY_MATRIX)
    done = flow_one.land(upd_out)
    flow_one.issue(done)
    sum_one, = flow_one.land(upd_up)
    sum_vec = sum_one[:, CUT_ONE : CUT_ONE + per_row].reshape(-1)
    sum_one = jnp.concatenate([sum_one[:, :CUT_ONE], sum_one[:, WIDTH_ONE : WIDTH_ONE + CUT_ONE]], axis=1)
    upd_qkv = adamw(master_qkv, first_qkv, second_qkv, sum_one, RATE_MATRIX, DECAY_MATRIX)
    upd_vec = adamw(master_vec, first_vec, second_vec, sum_vec, RATE_VECTOR, 0.0)
    return (
        (block_out[None], tokens_grad[None]) + upd_qkv + upd_out + upd_up + upd_down + upd_vec
    )


def solution(mesh):
    rows = P(AXES, None)
    flat = P(AXES)
    deep = P(AXES, None, None)
    stored = (rows,) * 4 + (flat,)
    in_specs = (deep,) * 2 + (rows,) * 3 + (P(),) + stored * 3
    out_specs = (deep,) * 2 + (rows,) * 12 + (flat,) * 3
    return jax.shard_map(local, mesh=mesh, in_specs=in_specs, out_specs=out_specs, check_vma=False)
```

```python
import functools

import jax
import jax.numpy as jnp
from jax import lax
from jax.experimental import pallas as pl
from jax.experimental.pallas import tpu as pltpu
from jax.sharding import PartitionSpec as P

D = 768
HEADS = 12
FF = 3072
STEP = 10
HALF = 384
WIN = 256
SMALL = 160
LARGE = 240
LOG2E = 1.4426950408889634
CUT_ONE = 1152
WIDTH_ONE = 1280
WIDTH_TWO = 1920
WIDTH_THREE = 384

EPSILON = 1e-05
BETA_ONE = 0.9
BETA_TWO = 0.999
ADAM_EPS = 1e-08
RATE_MATRIX = 0.05
DECAY_MATRIX = 0.05
RATE_VECTOR = 0.3

AXES = ("dp", "fsdp")
LOW = jnp.bfloat16
WIDE = jnp.float32
VMEM_BYTES = 8 * 2**20


def nn(left, right):
    return lax.dot_general(left, right, (((1,), (0,)), ((), ())), preferred_element_type=WIDE)


def nt(left, right):
    return lax.dot_general(left, right, (((1,), (1,)), ((), ())), preferred_element_type=WIDE)


def tn(left, right):
    return lax.dot_general(left, right, (((0,), (0,)), ((), ())), preferred_element_type=WIDE)


def shape(rows, cols, kind=LOW):
    return jax.ShapeDtypeStruct((rows, cols), kind)


def later(kernel, inputs, extra):
    return lambda *refs: kernel(*refs[:inputs], *refs[inputs + extra :])


def whole_call(kernel, outs, scratch, smem, name, flops, *args, anywhere=(), after=()):
    specs = []
    for i in range(len(args)):
        space = pltpu.SMEM if i < smem else pl.ANY if i in anywhere else pltpu.VMEM
        specs.append(pl.BlockSpec(memory_space=space))
    moved = sum(a.size * a.dtype.itemsize for a in args) + sum(o.size * o.dtype.itemsize for o in outs)
    return pl.pallas_call(
        later(kernel, len(args), len(after)),
        in_specs=specs + [pl.BlockSpec(memory_space=pl.ANY)] * len(after),
        out_specs=[pl.BlockSpec(memory_space=pltpu.VMEM)] * len(outs),
        out_shape=outs,
        scratch_shapes=scratch,
        compiler_params=pltpu.CompilerParams(vmem_limit_bytes=VMEM_BYTES),
        cost_estimate=pl.CostEstimate(flops=flops, bytes_accessed=moved, transcendentals=0),
        name=name,
    )(*args, *after)


def over_rows(count, step, body, init=None):
    return lax.fori_loop(0, count // step, lambda i, c: body(pl.ds(pl.multiple_of(i * step, step), step), c), init)


def normal(values):
    centre = values - jnp.mean(values, axis=-1, keepdims=True)
    rstd = lax.rsqrt(jnp.mean(centre * centre, axis=-1, keepdims=True) + EPSILON)
    return centre * rstd, rstd


def both(pair, side, lo, width):
    rows = slice(HALF * side, HALF * (side + 1))
    return jnp.concatenate([z[rows, lo : lo + width] for z in pair], axis=0)


def normal_kernel(x_ref, n_ref):
    def norm(rows, _):
        n_ref[rows, :] = normal(x_ref[rows, :].astype(WIDE))[0]

    over_rows(x_ref.shape[0], 144, norm)


def normalized(x):
    return whole_call(normal_kernel, [shape(*x.shape, WIDE)], [], 0, "normalized", 1, x)[0]


def qkv_kernel(n_ref, order_ref, own, other, a_ref, qkv_ref, vec_ref, tmp, wide):
    moved = jnp.concatenate([z[:HALF, CUT_ONE:] for z in (own, other)], axis=0)
    wide[...] = nn(order_ref[...], moved)
    vec_ref[...] = jnp.zeros_like(vec_ref)
    for k in range(10):
        first = min(D * k // 10 // 8 * 8, D - 88)

        def tenths(rows):
            entry = lax.broadcasted_iota(jnp.int32, (rows, D), 1) + D * k
            tenth = (entry * 52429) >> 19
            return tenth, entry - 10 * tenth, lax.broadcasted_iota(jnp.int32, (rows, D), 0)

        _, column, row = tenths(128)
        picked = nn(wide[first : first + 88, :].astype(LOW), (row == column).astype(LOW))
        tenth, _, row = tenths(88)
        vec_ref[k : k + 1, :] = jnp.sum(jnp.where(row + first == tenth, picked, 0.0), axis=0, keepdims=True)
    gain, shift = vec_ref[0:1, :], vec_ref[1:2, :]

    def norm(rows, _):
        tmp[rows, :] = (n_ref[rows, :] * gain + shift).astype(LOW)

    over_rows(n_ref.shape[0], 144, norm)
    a_ref[...] = nn(tmp[...], order_ref[...]).astype(LOW)
    for col in range(0, 3 * D, 384):
        w = both((own, other), *divmod(col, CUT_ONE), 384)
        qkv_ref[:, col : col + 384] = nn(a_ref[...], w).astype(LOW)


def project(normed, order, one, after=()):
    n = normed.shape[0]
    return whole_call(
        qkv_kernel, [shape(n, D), shape(n, 3 * D), shape(16, D, WIDE)],
        [pltpu.VMEM((n, D), LOW), pltpu.VMEM((D, 128), WIDE)], 0, "project",
        2 * n * D * (4 * D), normed, order, *one, after=after,
    )


def each_tile(spans, body):
    def step(t, carry):
        for kind, rows in ((1, SMALL), (2, LARGE)):

            @pl.when(spans[t, 4] == kind)
            def _():
                body(t, pl.multiple_of(spans[t, 2], 16), rows, pl.multiple_of(spans[t, 3], 16))

        return carry

    lax.fori_loop(0, 4, step, 0)


def padding_rows(spans, shape_):
    return lax.broadcasted_iota(jnp.int32, shape_, 0) >= spans[4, 0]


def own_half(values, e):
    lane = lax.broadcasted_iota(jnp.int32, values.shape, 1)
    return jnp.where((lane < 64) if e == 0 else (lane >= 64), values, jnp.zeros_like(values))


def attend_kernel(base, spans, slopes, qkv_ref, far_ref, o_ref, p_ref, acc):
    acc[...] = jnp.zeros_like(acc)

    def tile(t, at, count, key):
        rows, keys = pl.ds(at, count), pl.ds(key, WIN)
        row = lax.broadcasted_iota(jnp.int32, (count, 1), 0) + at
        inside = ((row >= spans[t, 0]) & (row < spans[t, 1])).astype(WIDE)
        far = far_ref[t, :count, :]
        for pair in range(3):
            col = (base + pair) * 128
            q, k, v = [qkv_ref[z, col + i * D : col + i * D + 128] for i, z in enumerate((rows, keys, keys))]
            out = None
            for e in range(2):
                s = nt(q, own_half(k, e)) * (0.125 * LOG2E) - slopes[2 * (base + pair) + e] * far
                p = jnp.exp2(s - jnp.max(s, axis=1, keepdims=True))
                p = (p * (inside / jnp.sum(p, axis=1, keepdims=True))).astype(LOW)
                p_ref[t, 2 * pair + e, :count, :] = p
                part = nn(p, own_half(v, e))
                out = part if out is None else out + part
            acc[rows, pair * 128 : pair * 128 + 128] += out

    each_tile(spans, tile)
    v = qkv_ref[:, base * 128 + 2 * D : base * 128 + 2 * D + HALF]
    o_ref[...] = jnp.where(padding_rows(spans, v.shape), v, acc[...].astype(LOW))


def attend(base, qkv, far, spans, slopes, after=()):
    n = qkv.shape[0]
    return whole_call(
        functools.partial(attend_kernel, base),
        [shape(n, HALF), jax.ShapeDtypeStruct((4, HEADS // 2, LARGE, WIN), LOW)],
        [pltpu.VMEM((n, HALF), WIDE)], 2, "attend", 9 * 10**9, spans, slopes, qkv, far, after=after,
    )


def attend_back_kernel(base, spans, qkv_ref, g_ref, p_ref, dq_ref, dk_ref, dv_ref, aq, ak, av):
    for acc in (aq, ak, av):
        acc[...] = jnp.zeros_like(acc)

    def tile(t, at, count, key):
        rows, keys = pl.ds(at, count), pl.ds(key, WIN)
        for pair in range(3):
            col = (base + pair) * 128
            q, k, v = [qkv_ref[z, col + i * D : col + i * D + 128] for i, z in enumerate((rows, keys, keys))]
            g = g_ref[rows, col : col + 128]
            sums = None
            for e in range(2):
                ge = own_half(g, e)
                p = p_ref[t, 2 * pair + e, :count, :]
                wide = p.astype(WIDE)
                d = wide * nt(ge * 0.125, v)
                d = (d - wide * jnp.sum(d, axis=1, keepdims=True)).astype(LOW)
                parts = (nn(d, own_half(k, e)), tn(d, own_half(q, e)), tn(p, ge))
                sums = parts if sums is None else tuple(a + b for a, b in zip(sums, parts))
            part = slice(pair * 128, pair * 128 + 128)
            aq[rows, part] += sums[0]
            ak[keys, part] += sums[1]
            av[keys, part] += sums[2]

    each_tile(spans, tile)
    dq_ref[...] = aq[...].astype(LOW)
    dk_ref[...] = ak[...].astype(LOW)
    g = g_ref[:, base * 128 : base * 128 + HALF]
    dv_ref[...] = jnp.where(padding_rows(spans, g.shape), g, av[...].astype(LOW))


def attend_back(base, qkv, grad, probs, spans, after=()):
    n = qkv.shape[0]
    return whole_call(
        functools.partial(attend_back_kernel, base), [shape(n, HALF)] * 3, [pltpu.VMEM((n, HALF), WIDE)] * 3, 1,
        "attend_back", 12 * 10**9, spans, qkv, grad, probs, after=after,
    )


def tables_kernel(seg_ref, side_ref, valid_ref, spans, far_ref):
    n = seg_ref.shape[1]
    seg, side, valid = [z[...].astype(WIDE) for z in (seg_ref, side_ref, valid_ref)]
    live = jnp.sum(valid).astype(jnp.int32)
    for z in range(5):
        spans[4, z] = live
    for t in range(4):
        low = jnp.sum((seg < t).astype(WIDE)).astype(jnp.int32)
        high = jnp.sum((seg <= t).astype(WIDE)).astype(jnp.int32)
        width = jnp.max(jnp.where(seg == t, side, 1.0))
        small = high - low <= SMALL - 16
        start = low // 16 * 16
        at = jnp.minimum(start, jnp.where(small, n - SMALL, n - LARGE))
        key = jnp.minimum(start, n - WIN)
        kind = jnp.where((high > low) & (low < live), jnp.where(small, 1, 2), 0)
        for z, value in enumerate((low, high, at, key, kind)):
            spans[t, z] = value

        def places(first, shape_, dim):
            slot = lax.broadcasted_iota(jnp.int32, shape_, dim) + first
            place = (slot - low).astype(WIDE)
            row = jnp.floor((place + 0.5) / width)
            return (slot >= low) & (slot < high), row, place - row * width

        inside, row, col = places(at, (LARGE, 1), 0)
        inside_key, row_key, col_key = places(key, (1, WIN), 1)
        down, along = row - row_key, col - col_key
        far_ref[t] = jnp.where(inside & inside_key, jnp.sqrt(down * down + along * along), 1e12)


def tables(seg, side, valid):
    vmem, smem = [pl.BlockSpec(memory_space=z) for z in (pltpu.VMEM, pltpu.SMEM)]
    return pl.pallas_call(
        tables_kernel,
        in_specs=[vmem] * 3,
        out_specs=[smem, vmem],
        out_shape=[jax.ShapeDtypeStruct((5, 5), jnp.int32), jax.ShapeDtypeStruct((4, LARGE, WIN), WIDE)],
        compiler_params=pltpu.CompilerParams(vmem_limit_bytes=VMEM_BYTES),
        name="tables",
    )(seg, side, valid)


def bell(u):
    share = 0.5 + 0.5 * lax.erf(u * 0.7071067811865476)
    return u * share, share + u * (jnp.exp2(u * u * -0.7213475204444817) * 0.3989422804014327)


def up_kernel(x_ref, o0_ref, o1_ref, vec_ref, order_ref, own, other, mixed_ref, h_ref, a_ref, gl_ref, gp_ref, tmp):
    mixed_ref[...] = (
        nn(o0_ref[...], order_ref[:HALF, :]) + nn(o1_ref[...], order_ref[HALF:, :])
    ).astype(LOW)
    for col in (0, 384):
        part = slice(col, col + 384)
        h_ref[:, part] = x_ref[:, part].astype(WIDE) + nn(mixed_ref[...], both((own, other), 0, col, 384)) + vec_ref[2:3, part]
    gain, shift = vec_ref[3:4, :], vec_ref[4:5, :]

    def norm(rows, _):
        tmp[rows, :] = (normal(h_ref[rows, :])[0] * gain + shift).astype(LOW)

    over_rows(x_ref.shape[0], 144, norm)
    a_ref[...] = nn(tmp[...], order_ref[...]).astype(LOW)
    for col in range(0, FF, 384):
        k = 5 + col // D
        u = nn(a_ref[...], both((own, other), *divmod(col + D, WIDTH_TWO), 384)) + vec_ref[k : k + 1, col % D : col % D + 384]
        value, slope = bell(u)
        gl_ref[:, col : col + 384] = value.astype(LOW)
        gp_ref[:, col : col + 384] = slope.astype(LOW)


def upward(x, o, vec, order, two, after=()):
    n = x.shape[0]
    return whole_call(
        up_kernel, [shape(n, D), shape(n, D, WIDE), shape(n, D), shape(n, FF), shape(n, FF)],
        [pltpu.VMEM((n, D), LOW)], 0, "upward", 2 * n * D * (7 * D) * 2, x, *o, vec, order, *two,
        after=after,
    )


def fetch_down(block_of, own, other, wd):
    for p in range(32):
        dst = pl.ds(pl.multiple_of(block_of[p] * 96, 96), 96)
        piece = own if p < 16 else other
        for side in (0, 1):
            lo = p % 16 * 96 + side * (FF // 2)
            wd[dst, side * WIDTH_THREE : (side + 1) * WIDTH_THREE] = piece[lo : lo + 96, :]


def down_kernel(block_of, gp_ref, dy_ref, own, other, dur_ref, vg_ref, wd):
    fetch_down(block_of, own, other, wd)
    for col in range(0, FF, 384):
        part = slice(col, col + 384)
        du = nt(dy_ref[...], wd[part, :]) * gp_ref[:, part].astype(WIDE)
        dur_ref[:, part] = du.astype(LOW)
        k = col // D
        vg_ref[k : k + 1, col % D : col % D + 384] = jnp.sum(du, axis=0, keepdims=True)


def down_back(block_of, gp, dy, three, after=()):
    n = dy.shape[0]
    return whole_call(
        down_kernel, [shape(n, FF), shape(8, D, WIDE)], [pltpu.VMEM((FF, D), LOW)], 1,
        "down_back", 2 * n * D * (4 * D), block_of, gp, dy, *three, after=after,
    )


def down_out_kernel(block_of, vec_ref, gl_ref, h_ref, own, other, out_ref, wd):
    fetch_down(block_of, own, other, wd)
    for col in (0, 384):
        part = slice(col, col + 384)
        out_ref[:, part] = (h_ref[:, part] + nn(gl_ref[...], wd[:, part]) + vec_ref[9:10, part]).astype(LOW)


def down_out(block_of, vec, gl, h, three, after=()):
    n = h.shape[0]
    return whole_call(
        down_out_kernel, [shape(n, D)], [pltpu.VMEM((FF, D), LOW)], 1,
        "down_out", 2 * n * D * (4 * D), block_of, vec, gl, h, *three, after=after,
    )[0]


def hidden_kernel(vec_ref, order_ref, dur_ref, dy_ref, h_ref, own, other, dh_ref, dhr_ref, dor_ref, vg_ref, tmp):
    split = WIDTH_TWO - D
    for i, w in enumerate((own, other)):
        tmp[:, HALF * i : HALF * (i + 1)] = (
            nt(dur_ref[:, :split], w[:HALF, D:]) + nt(dur_ref[:, split:], w[HALF:, :])
        ).astype(LOW)
    dh_ref[...] = nt(tmp[...], order_ref[...])
    gain = vec_ref[3:4, :]

    def step(rows, sums):
        e = dh_ref[rows, :]
        dy = dy_ref[rows, :].astype(WIDE)
        n, rstd = normal(h_ref[rows, :])
        w = e * gain
        dh = dy + rstd * (w - jnp.mean(w, axis=-1, keepdims=True) - n * jnp.mean(w * n, axis=-1, keepdims=True))
        dh_ref[rows, :] = dh
        dhr_ref[rows, :] = dh.astype(LOW)
        return tuple(s + jnp.sum(z.reshape(-1, 8, D), axis=0) for s, z in zip(sums, (dh, e * n, e, dy)))

    zero = jnp.zeros((8, D), WIDE)
    sums = over_rows(h_ref.shape[0], 144, step, (zero,) * 4)
    for k, s in enumerate(sums):
        vg_ref[k : k + 1, :] = jnp.sum(s, axis=0, keepdims=True)
    for i, w in enumerate((own, other)):
        tmp[:, HALF * i : HALF * (i + 1)] = nt(dhr_ref[...], w[:HALF, :D]).astype(LOW)
    dor_ref[...] = nt(tmp[...], order_ref[...]).astype(LOW)


def hidden_grad(vec, order, dur, dy, h, two, after=()):
    n = h.shape[0]
    return whole_call(
        hidden_kernel, [shape(n, D, WIDE), shape(n, D), shape(n, D), shape(8, D, WIDE)],
        [pltpu.VMEM((n, D), LOW)], 0, "hidden_grad",
        2 * n * D * (7 * D), vec, order, dur, dy, h, *two, after=after,
    )


def down_grad_kernel(block_of, gl_ref, dy_ref, own, other, all_ref):
    for col in range(0, FF, 384):
        all_ref[col : col + 384, :] = tn(gl_ref[:, col : col + 384], dy_ref[...]).astype(LOW)
    for p in range(32):
        src = pl.ds(pl.multiple_of(block_of[p] * 96, 96), 96)
        piece = own if p < 16 else other
        for side in (0, 1):
            lo = p % 16 * 96 + side * (FF // 2)
            piece[lo : lo + 96, :] = all_ref[src, side * WIDTH_THREE : (side + 1) * WIDTH_THREE]


def down_grad(block_of, gl, dy, after=()):
    n = dy.shape[0]
    return whole_call(
        down_grad_kernel, [shape(FF, WIDTH_THREE)] * 2, [pltpu.VMEM((FF, D), LOW)], 1, "down_grad",
        2 * n * D * FF, block_of, gl, dy, after=after,
    )


def two_grad_kernel(mixed_ref, a_ref, dhr_ref, dur_ref, own, other):
    for col in range(0, D + FF, 384):
        left, right = (mixed_ref, dhr_ref[:, col : col + 384]) if col < D else (a_ref, dur_ref[:, col - D : col - D + 384])
        t = tn(left[...], right).astype(LOW)
        side, lo = divmod(col, WIDTH_TWO)
        own[HALF * side : HALF * (side + 1), lo : lo + 384] = t[:HALF]
        other[HALF * side : HALF * (side + 1), lo : lo + 384] = t[HALF:]


def two_grad(mixed, a, dhr, dur, after=()):
    n = a.shape[0]
    return whole_call(two_grad_kernel, [shape(D, WIDTH_TWO)] * 2, [], 0, "two_grad", 2 * n * D * (D + FF), mixed, a, dhr, dur,
                      after=after)


def one_grad_kernel(a_ref, order_ref, first_ref, mid_ref, up_ref, *refs):
    halves, (own, other, wide) = refs[:6], refs[6:]
    wide[...] = jnp.zeros_like(wide)
    rows = [first_ref[0:1, :], first_ref[1:2, :]] + [mid_ref[i : i + 1, :] for i in range(3)]
    rows = rows + [up_ref[i : i + 1, :] for i in range(4)] + [mid_ref[3:4, :]]
    for k, values in enumerate(rows):
        first = min(D * k // 10 // 8 * 8, D - 88)
        entry = lax.broadcasted_iota(jnp.int32, (88, D), 1) + D * k
        row = lax.broadcasted_iota(jnp.int32, (88, D), 0) + first
        spread_out = jnp.where(row == (entry * 52429) >> 19, values, 0.0).astype(LOW)
        entry = lax.broadcasted_iota(jnp.int32, (D, 128), 0) + D * k
        column = entry - 10 * ((entry * 52429) >> 19)
        pick = (lax.broadcasted_iota(jnp.int32, (D, 128), 1) == column).astype(LOW)
        wide[first : first + 88, :] += nn(spread_out, pick)
    moved = tn(order_ref[...], wide[...].astype(LOW)).astype(LOW)
    for i, out in enumerate((own, other)):
        out[:HALF, CUT_ONE:] = moved[HALF * i : HALF * (i + 1), :]
        out[HALF:, CUT_ONE:] = jnp.zeros((HALF, WIDTH_ONE - CUT_ONE), LOW)
    for i, half in enumerate(halves):
        t = tn(a_ref[...], half[...]).astype(LOW)
        side, lo = divmod(384 * i, CUT_ONE)
        own[HALF * side : HALF * (side + 1), lo : lo + 384] = t[:HALF]
        other[HALF * side : HALF * (side + 1), lo : lo + 384] = t[HALF:]


def one_grad(a, order, sums, d, after=()):
    n = a.shape[0]
    return whole_call(
        one_grad_kernel, [shape(D, WIDTH_ONE)] * 2, [pltpu.VMEM((D, 128), WIDE)], 0, "one_grad",
        2 * n * D * 3 * D, a, order, *sums, *d, after=after,
    )


def input_back_kernel(order_ref, q0, q1, k0, k1, v0, v1, own, other, e_ref, tmp):
    for i, w in enumerate((own, other)):
        total = 0.0
        for j, d in enumerate((q0, q1, k0, k1, v0, v1)):
            side, lo = divmod(384 * j, CUT_ONE)
            total = total + nt(d[...], w[HALF * side : HALF * (side + 1), lo : lo + 384])
        tmp[:, HALF * i : HALF * (i + 1)] = total.astype(LOW)
    e_ref[...] = nt(tmp[...], order_ref[...])


def input_back(order, d, one, after=()):
    n = d[0].shape[0]
    return whole_call(
        input_back_kernel, [shape(n, D, WIDE)], [pltpu.VMEM((n, D), LOW)], 0, "input_back",
        2 * n * D * 4 * D, order, *d, *one, after=after,
    )[0]


def input_kernel(x_ref, vec_ref, e_ref, dh_ref, dx_ref, vg_ref):
    gain = vec_ref[0:1, :]

    def step(rows, sums):
        e = e_ref[rows, :]
        n, rstd = normal(x_ref[rows, :].astype(WIDE))
        w = e * gain
        dx_ref[rows, :] = dh_ref[rows, :] + rstd * (
            w - jnp.mean(w, axis=-1, keepdims=True) - n * jnp.mean(w * n, axis=-1, keepdims=True)
        )
        return tuple(s + jnp.sum(z.reshape(-1, 8, D), axis=0) for s, z in zip(sums, (e * n, e)))

    zero = jnp.zeros((8, D), WIDE)
    sums = over_rows(x_ref.shape[0], 144, step, (zero,) * 2)
    for k, s in enumerate(sums):
        vg_ref[k : k + 1, :] = jnp.sum(s, axis=0, keepdims=True)


def input_grad(x, vec, e, dh, after=()):
    n = x.shape[0]
    return whole_call(
        input_kernel, [shape(n, D, WIDE), shape(8, D, WIDE)], [], 0, "input_grad",
        2 * n * D * 3 * D, x, vec, e, dh, after=after,
    )


def near_kernel(a, b, c, d, left_ref, right_ref):
    cut = left_ref.shape[1]
    for out, lo in ((left_ref, 0), (right_ref, cut)):
        out[...] = jnp.concatenate([z[:, lo : lo + cut].astype(WIDE) for z in (a, b, c, d)], axis=0).astype(LOW)


def near_pieces(pieces, after=()):
    rows, cols = pieces[0].shape
    return whole_call(near_kernel, [shape(4 * rows, cols // 2)] * 2, [], 0, "near", 1, *pieces, after=after)


def first_kernel(left, got_left, right, got_right, left_ref, right_ref):
    rows = left.shape[0]
    for out, mine, got in ((left_ref, left, got_left), (right_ref, right, got_right)):
        out[:rows, :] = mine[...]
        out[rows:, :] = got[...]


def first_pieces(left, right, got, after=()):
    rows, cols = left.shape
    return whole_call(
        first_kernel, [shape(2 * rows, cols)] * 2, [], 0, "first", 1, left, got[0], right, got[1], after=after
    )


def second_kernel(left, got, right, far, own_ref):
    rows = left.shape[0]
    half = rows // 2
    own_ref[:rows, :] = left[...]
    own_ref[rows : 2 * rows, :] = got[...]
    for i in (0, 1):
        own_ref[2 * rows + 2 * i * half : 2 * rows + (2 * i + 1) * half, :] = right[i * half : (i + 1) * half, :]
        own_ref[2 * rows + (2 * i + 1) * half : 2 * rows + (2 * i + 2) * half, :] = far[i * half : (i + 1) * half, :]


def second_pieces(left, right, got, after=()):
    rows, cols = left.shape
    return whole_call(
        second_kernel, [shape(4 * rows, cols)], [], 0, "second", 1, left, got[0], right, got[1], after=after
    )[0]


def core_sum_kernel(own, got, left_keep, right_keep, left_out, right_out):
    half = left_keep.shape[0]
    rows = half // 2

    def total(lo, count):
        return own[lo : lo + count, :].astype(WIDE) + got[lo : lo + count, :].astype(WIDE)

    left_keep[...] = total(0, half)
    left_out[...] = total(half, half).astype(LOW)
    for i in (0, 1):
        lo = 2 * half + 2 * i * rows
        right_keep[i * rows : (i + 1) * rows, :] = total(lo, rows)
        right_out[i * rows : (i + 1) * rows, :] = total(lo + rows, rows).astype(LOW)


def core_sum(own, got, after=()):
    rows, cols = own.shape[0] // 4, own.shape[1]
    return whole_call(
        core_sum_kernel, [shape(rows, cols, WIDE)] * 2 + [shape(rows, cols)] * 2, [], 0, "core_sum", 1, own, got,
        after=after,
    )


def half_sum_kernel(left, got_left, right, got_right, left_keep, right_keep, left_out, right_out):
    rows = left_keep.shape[0]
    for mine, got, keep, out in ((left, got_left, left_keep, left_out), (right, got_right, right_keep, right_out)):
        keep[...] = mine[:rows, :] + got[:rows, :].astype(WIDE)
        out[...] = (mine[rows:, :] + got[rows:, :].astype(WIDE)).astype(LOW)


def half_sum(left, right, got, after=()):
    rows, cols = left.shape[0] // 2, left.shape[1]
    return whole_call(
        half_sum_kernel, [shape(rows, cols, WIDE)] * 2 + [shape(rows, cols)] * 2, [], 0, "half_sum", 1,
        left, got[0], right, got[1], after=after,
    )


def last_sum_kernel(left, got_left, right, got_right, keep, *outs):
    unit, cut = keep.shape[0], left.shape[1]
    for lo, mine, got in ((0, left, got_left), (cut, right, got_right)):
        total = mine[...] + got[...].astype(WIDE)
        keep[:, lo : lo + cut] = total[:unit]
        for i, out in enumerate(outs):
            out[:, lo : lo + cut] = total[unit * (i + 1) : unit * (i + 2)].astype(LOW)


def last_sum(left, right, got, after=()):
    unit, cols = left.shape[0] // 4, 2 * left.shape[1]
    return whole_call(
        last_sum_kernel, [shape(unit, cols, WIDE)] + [shape(unit, cols)] * 3, [], 0, "last_sum", 1,
        left, got[0], right, got[1], after=after,
    )


def swap(value, bits):
    pairs = [(i, i ^ bits) for i in range(32)]
    return lax.ppermute(value, AXES, pairs)


def tie(values, *first):
    return lax.optimization_barrier((tuple(values), first))[0]


class Flow:
    def __init__(self, steps):
        self.steps = steps
        self.next = next(steps)[:2]

    def issue(self, start=()):
        values, bits = self.next
        values = tie(values, start)
        self.got = tuple(swap(value, bit) for value, bit in zip(values, bits))
        return self.got

    def land(self, end=()):
        values, *bits = self.steps.send(tie(self.got, end))
        if values is None:
            return bits[0]
        self.next = (values, bits[0])
        return bits[1]


def spread(block):
    got = yield (block,) * 3, (8, 16, 24)
    left, right = near_pieces((block,) + got)
    got = yield (left, right), (2, 4), (left, right)
    left, right = first_pieces(left, right, got)
    got = yield (left, right), (4, 2), (left, right)
    own = second_pieces(left, right, got)
    got = yield (own,), (1,), (own,)
    yield None, (own, got[0])


def collect(pieces):
    (got,) = yield (pieces[1],), (1,)
    left, right, *out = ready = core_sum(pieces[0], got)
    got = yield out, (4, 2), tuple(ready)
    left, right, *out = ready = half_sum(left, right, got)
    got = yield out, (2, 4), tuple(ready)
    total, *out = ready = last_sum(left, right, got)
    got = yield out, (8, 16, 24), tuple(ready)
    yield None, (sum((z.astype(WIDE) for z in got), total),)


def stack(whole):
    half, cut = whole.shape[0] // 2, whole.shape[1] // 2
    return tuple(jnp.concatenate([z[:, :cut], z[:, cut:]], axis=0) for z in (whole[:half], whole[half:]))


def unstack(pieces):
    half = pieces[0].shape[0] // 2
    return jnp.concatenate([jnp.concatenate([z[:half], z[half:]], axis=1) for z in pieces], axis=0)


class Whole:
    def __init__(self, result):
        self.result = result

    def issue(self, start=()):
        return ()

    def land(self, end=()):
        return self.result


def spread_any(block):
    return stack(lax.all_gather(block, AXES, axis=0, tiled=True))


def collect_any(pieces):
    return (lax.psum_scatter(unstack(pieces), AXES, scatter_dimension=0, tiled=True).astype(WIDE),)


def rearrange(whole, order, shards):
    return jnp.take(whole.reshape(shards, -1, whole.shape[1]), order, axis=0, mode="clip").reshape(whole.shape)


def adamw(master, moment_one, moment_two, gradient, step_rate, decay_rate):
    first_new = BETA_ONE * moment_one + (1.0 - BETA_ONE) * gradient
    second_new = BETA_TWO * moment_two + (1.0 - BETA_TWO) * gradient * gradient
    first_hat = first_new / (1.0 - BETA_ONE**STEP)
    second_hat = second_new / (1.0 - BETA_TWO**STEP)
    master_new = master - step_rate * (
        first_hat / (jnp.sqrt(second_hat) + ADAM_EPS) + decay_rate * master
    )
    return (first_new, second_new, master_new)


def local(
    tokens_in, cotangent, segments, tile_sides, valid_slots, owners,
    master_qkv, master_out, master_up, master_down, master_vec,
    first_qkv, first_out, first_up, first_down, first_vec,
    second_qkv, second_out, second_up, second_down, second_vec,
):
    shards = lax.axis_size(AXES)
    near = shards == 32
    unit = D // shards
    per_row = master_vec.shape[0] // unit
    ids = jnp.arange(shards, dtype=jnp.int32)
    if near:
        away = owners ^ lax.axis_index(AXES).astype(jnp.int32)
        place = (away >> 3) + 4 * ((away >> 1) & 1) + 8 * ((away >> 2) & 1) + 16 * (away & 1)
        places = jnp.arange(32, dtype=jnp.int32)
        block_of = jnp.sum(places[:, None] * (place[:, None] == places[None, :]), axis=0)
    else:
        place = owners
        block_of = jnp.arange(32, dtype=jnp.int32)
    target = (place[:, None] * unit + jnp.arange(unit, dtype=jnp.int32)[None, :]).reshape(-1)
    order = (target[:, None] == jnp.arange(D, dtype=jnp.int32)[None, :]).astype(LOW)

    def gather(block):
        return Flow(spread(block)) if near else Whole(spread_any(block))

    def scatter(pieces):
        return Flow(collect(pieces)) if near else Whole(collect_any(pieces))

    vec_block = jnp.pad(master_vec.reshape(unit, per_row), ((0, 0), (0, 128 - per_row)))
    block_one = jnp.concatenate(
        [master_qkv[:, :CUT_ONE], vec_block, master_qkv[:, CUT_ONE:], jnp.zeros_like(vec_block)], axis=1
    )
    spans, far = tables(segments, tile_sides, valid_slots)
    slopes = LOG2E * jnp.exp2(-8.0 * (jnp.arange(HEADS, dtype=jnp.int32).astype(WIDE) + 1.0) / HEADS)
    one = gather(block_one.astype(LOW))
    two = gather(jnp.concatenate([master_out, master_up], axis=1).astype(LOW))
    if near:
        three = gather(master_down.astype(LOW))
    else:
        whole = lax.all_gather(master_down.astype(LOW), AXES, axis=0, tiled=True)
        three = Whole(stack(rearrange(whole, owners, shards)))
    one.issue()
    normed = normalized(tokens_in[0])
    done = one.land((far, spans, slopes, order, normed))
    one.issue(done)
    done = one.land()
    sent = one.issue(done) + two.issue(done)
    done = one.land()
    done = done + two.land(sent + done)
    one.issue(done)
    sent = two.issue(done)
    one = one.land()

    x = tokens_in[0]
    dy = cotangent[0]
    act_one, qkv, vec = project(normed, order, one)
    done = two.land((qkv,))
    two.issue(done)
    mixed_0, probs_0 = attend(0, qkv, far, spans, slopes, done)
    three.issue((mixed_0,))
    done = two.land((mixed_0,))
    done = done + three.land(done)
    sent = two.issue(done) + three.issue(done)
    mixed_1, probs_1 = attend(3, qkv, far, spans, slopes, done + (mixed_0,))
    done = three.land((mixed_1,) + sent)
    two = two.land((mixed_1,) + sent)
    three.issue(done + two[1:])
    mixed, hidden, act_two, gelu, gelu_slope = upward(x, (mixed_0, mixed_1), vec, order, two, done)
    grad_three = down_grad(block_of, gelu, dy)
    done = three.land(tuple(grad_three))
    three.issue(done)
    three = three.land()
    if not near:
        back = jnp.sum(ids[:, None] * (owners[:, None] == ids[None, :]), axis=0)
        grad_three = stack(rearrange(unstack(grad_three), back, shards))
    flow_three = scatter(grad_three)
    flow_three.issue()
    dur, sums_up = down_back(block_of, gelu_slope, dy, three)
    done = flow_three.land((dur,))
    flow_three.issue(done)
    dh, dh_low, dmixed, sums = hidden_grad(vec, order, dur, dy, hidden, two, done)
    grad_two = two_grad(mixed, act_two, dh_low, dur)
    done = flow_three.land(tuple(grad_two)) + tuple(grad_two)
    flow_two = scatter(grad_two)
    sent = flow_three.issue(done) + flow_two.issue(done)
    d0 = attend_back(0, qkv, dmixed, probs_0, spans, done)
    done = flow_three.land(tuple(d0) + sent) + flow_two.land(tuple(d0) + sent)
    sent = flow_three.issue(done) + flow_two.issue(done)
    d1 = attend_back(3, qkv, dmixed, probs_1, spans, done + tuple(d0))
    d = [z for pair in zip(d0, d1) for z in pair]
    dact = input_back(order, d, one)
    tokens_grad, sums_one = input_grad(x, vec, dact, dh)
    grad_one = one_grad(act_one, order, (sums_one, sums, sums_up), d)
    done = tuple(grad_one) + sent
    sum_three, = flow_three.land(done)
    done = flow_two.land(done)
    flow_one = scatter(grad_one)
    sent = flow_one.issue(done) + flow_two.issue(done)
    block_out = down_out(block_of, vec, gelu, hidden, three, done)
    done = flow_one.land((block_out,) + sent) + flow_two.land((block_out,) + sent)
    sent = flow_one.issue(done) + flow_two.issue(done)
    upd_down = adamw(master_down, first_down, second_down, sum_three, RATE_MATRIX, DECAY_MATRIX)
    sent = sent + upd_down
    done = flow_one.land(sent)
    sum_two, = flow_two.land(sent)
    flow_one.issue(done)
    upd_out = adamw(master_out, first_out, second_out, sum_two[:, :D], RATE_MATRIX, DECAY_MATRIX)
    upd_up = adamw(master_up, first_up, second_up, sum_two[:, D:], RATE_MATRIX, DECAY_MATRIX)
    done = flow_one.land(upd_out)
    flow_one.issue(done)
    sum_one, = flow_one.land(upd_up)
    sum_vec = sum_one[:, CUT_ONE : CUT_ONE + per_row].reshape(-1)
    sum_one = jnp.concatenate([sum_one[:, :CUT_ONE], sum_one[:, WIDTH_ONE : WIDTH_ONE + CUT_ONE]], axis=1)
    upd_qkv = adamw(master_qkv, first_qkv, second_qkv, sum_one, RATE_MATRIX, DECAY_MATRIX)
    upd_vec = adamw(master_vec, first_vec, second_vec, sum_vec, RATE_VECTOR, 0.0)
    return (
        (block_out[None], tokens_grad[None]) + upd_qkv + upd_out + upd_up + upd_down + upd_vec
    )


def solution(mesh):
    rows = P(AXES, None)
    flat = P(AXES)
    deep = P(AXES, None, None)
    stored = (rows,) * 4 + (flat,)
    in_specs = (deep,) * 2 + (rows,) * 3 + (P(),) + stored * 3
    out_specs = (deep,) * 2 + (rows,) * 12 + (flat,) * 3
    return jax.shard_map(local, mesh=mesh, in_specs=in_specs, out_specs=out_specs, check_vma=False)
```

```python
import functools

import jax
import jax.numpy as jnp
from jax import lax
from jax.experimental import pallas as pl
from jax.experimental.pallas import tpu as pltpu
from jax.sharding import PartitionSpec as P

D = 768
HEADS = 12
FF = 3072
STEP = 10
HALF = 384
WIN = 256
SMALL = 160
LARGE = 240
LOG2E = 1.4426950408889634
CUT_ONE = 1152
WIDTH_ONE = 1280
WIDTH_TWO = 1920
WIDTH_THREE = 384

EPSILON = 1e-05
BETA_ONE = 0.9
BETA_TWO = 0.999
ADAM_EPS = 1e-08
RATE_MATRIX = 0.05
DECAY_MATRIX = 0.05
RATE_VECTOR = 0.3

AXES = ("dp", "fsdp")
LOW = jnp.bfloat16
WIDE = jnp.float32
VMEM_BYTES = 10 * 2**20


def nn(left, right):
    return lax.dot_general(left, right, (((1,), (0,)), ((), ())), preferred_element_type=WIDE)


def nt(left, right):
    return lax.dot_general(left, right, (((1,), (1,)), ((), ())), preferred_element_type=WIDE)


def tn(left, right):
    return lax.dot_general(left, right, (((0,), (0,)), ((), ())), preferred_element_type=WIDE)


def shape(rows, cols, kind=LOW):
    return jax.ShapeDtypeStruct((rows, cols), kind)


def later(kernel, inputs, extra):
    return lambda *refs: kernel(*refs[:inputs], *refs[inputs + extra :])


def whole_call(kernel, outs, scratch, smem, name, flops, *args, anywhere=(), after=()):
    specs = []
    for i in range(len(args)):
        space = pltpu.SMEM if i < smem else pl.ANY if i in anywhere else pltpu.VMEM
        specs.append(pl.BlockSpec(memory_space=space))
    moved = sum(a.size * a.dtype.itemsize for a in args) + sum(o.size * o.dtype.itemsize for o in outs)
    return pl.pallas_call(
        later(kernel, len(args), len(after)),
        in_specs=specs + [pl.BlockSpec(memory_space=pl.ANY)] * len(after),
        out_specs=[pl.BlockSpec(memory_space=pltpu.VMEM)] * len(outs),
        out_shape=outs,
        scratch_shapes=scratch,
        compiler_params=pltpu.CompilerParams(vmem_limit_bytes=VMEM_BYTES),
        cost_estimate=pl.CostEstimate(flops=flops, bytes_accessed=moved, transcendentals=0),
        name=name,
    )(*args, *after)


def over_rows(count, step, body, init=None):
    return lax.fori_loop(0, count // step, lambda i, c: body(pl.ds(pl.multiple_of(i * step, step), step), c), init)


def normal(values):
    centre = values - jnp.mean(values, axis=-1, keepdims=True)
    rstd = lax.rsqrt(jnp.mean(centre * centre, axis=-1, keepdims=True) + EPSILON)
    return centre * rstd, rstd


def both(pair, side, lo, width):
    rows = slice(HALF * side, HALF * (side + 1))
    return jnp.concatenate([z[rows, lo : lo + width] for z in pair], axis=0)


def normal_kernel(x_ref, n_ref):
    def norm(rows, _):
        n_ref[rows, :] = normal(x_ref[rows, :].astype(WIDE))[0]

    over_rows(x_ref.shape[0], 144, norm)


def normalized(x):
    return whole_call(normal_kernel, [shape(*x.shape, WIDE)], [], 0, "normalized", 1, x)[0]


def qkv_kernel(n_ref, order_ref, own, other, a_ref, qkv_ref, vec_ref, tmp, wide):
    moved = jnp.concatenate([z[:HALF, CUT_ONE:] for z in (own, other)], axis=0)
    wide[...] = nn(order_ref[...], moved)
    vec_ref[...] = jnp.zeros_like(vec_ref)
    for k in range(10):
        first = min(D * k // 10 // 8 * 8, D - 88)

        def tenths(rows):
            entry = lax.broadcasted_iota(jnp.int32, (rows, D), 1) + D * k
            tenth = (entry * 52429) >> 19
            return tenth, entry - 10 * tenth, lax.broadcasted_iota(jnp.int32, (rows, D), 0)

        _, column, row = tenths(128)
        picked = nn(wide[first : first + 88, :].astype(LOW), (row == column).astype(LOW))
        tenth, _, row = tenths(88)
        vec_ref[k : k + 1, :] = jnp.sum(jnp.where(row + first == tenth, picked, 0.0), axis=0, keepdims=True)
    gain, shift = vec_ref[0:1, :], vec_ref[1:2, :]

    def norm(rows, _):
        tmp[rows, :] = (n_ref[rows, :] * gain + shift).astype(LOW)

    over_rows(n_ref.shape[0], 144, norm)
    a_ref[...] = nn(tmp[...], order_ref[...]).astype(LOW)
    for col in range(0, 3 * D, 384):
        w = both((own, other), *divmod(col, CUT_ONE), 384)
        qkv_ref[:, col : col + 384] = nn(a_ref[...], w).astype(LOW)


def project(normed, order, one, after=()):
    n = normed.shape[0]
    return whole_call(
        qkv_kernel, [shape(n, D), shape(n, 3 * D), shape(16, D, WIDE)],
        [pltpu.VMEM((n, D), LOW), pltpu.VMEM((D, 128), WIDE)], 0, "project",
        2 * n * D * (4 * D), normed, order, *one, after=after,
    )


def each_tile(spans, body):
    def step(t, carry):
        for kind, rows in ((1, SMALL), (2, LARGE)):

            @pl.when(spans[t, 4] == kind)
            def _():
                body(t, pl.multiple_of(spans[t, 2], 16), rows, pl.multiple_of(spans[t, 3], 16))

        return carry

    lax.fori_loop(0, 4, step, 0)


def padding_rows(spans, shape_):
    return lax.broadcasted_iota(jnp.int32, shape_, 0) >= spans[4, 0]


def own_half(values, e):
    lane = lax.broadcasted_iota(jnp.int32, values.shape, 1)
    return jnp.where((lane < 64) if e == 0 else (lane >= 64), values, jnp.zeros_like(values))


def attend_kernel(base, spans, slopes, qkv_ref, far_ref, o_ref, p_ref, acc):
    acc[...] = jnp.zeros_like(acc)

    def tile(t, at, count, key):
        rows, keys = pl.ds(at, count), pl.ds(key, WIN)
        row = lax.broadcasted_iota(jnp.int32, (count, 1), 0) + at
        inside = ((row >= spans[t, 0]) & (row < spans[t, 1])).astype(WIDE)
        far = far_ref[t, :count, :]
        for pair in range(3):
            col = (base + pair) * 128
            q, k, v = [qkv_ref[z, col + i * D : col + i * D + 128] for i, z in enumerate((rows, keys, keys))]
            out = None
            for e in range(2):
                s = nt(q, own_half(k, e)) * (0.125 * LOG2E) - slopes[2 * (base + pair) + e] * far
                p = jnp.exp2(s - jnp.max(s, axis=1, keepdims=True))
                p = (p * (inside / jnp.sum(p, axis=1, keepdims=True))).astype(LOW)
                p_ref[t, 2 * pair + e, :count, :] = p
                part = nn(p, own_half(v, e))
                out = part if out is None else out + part
            acc[rows, pair * 128 : pair * 128 + 128] += out

    each_tile(spans, tile)
    v = qkv_ref[:, base * 128 + 2 * D : base * 128 + 2 * D + HALF]
    o_ref[...] = jnp.where(padding_rows(spans, v.shape), v, acc[...].astype(LOW))


def attend(base, qkv, far, spans, slopes, after=()):
    n = qkv.shape[0]
    return whole_call(
        functools.partial(attend_kernel, base),
        [shape(n, HALF), jax.ShapeDtypeStruct((4, HEADS // 2, LARGE, WIN), LOW)],
        [pltpu.VMEM((n, HALF), WIDE)], 2, "attend", 9 * 10**9, spans, slopes, qkv, far, after=after,
    )


def attend_back_kernel(base, spans, qkv_ref, g_ref, p_ref, dq_ref, dk_ref, dv_ref, aq, ak, av):
    for acc in (aq, ak, av):
        acc[...] = jnp.zeros_like(acc)

    def tile(t, at, count, key):
        rows, keys = pl.ds(at, count), pl.ds(key, WIN)
        for pair in range(3):
            col = (base + pair) * 128
            q, k, v = [qkv_ref[z, col + i * D : col + i * D + 128] for i, z in enumerate((rows, keys, keys))]
            g = g_ref[rows, col : col + 128]
            sums = None
            for e in range(2):
                ge = own_half(g, e)
                p = p_ref[t, 2 * pair + e, :count, :]
                wide = p.astype(WIDE)
                d = wide * nt(ge * 0.125, v)
                d = (d - wide * jnp.sum(d, axis=1, keepdims=True)).astype(LOW)
                parts = (nn(d, own_half(k, e)), tn(d, own_half(q, e)), tn(p, ge))
                sums = parts if sums is None else tuple(a + b for a, b in zip(sums, parts))
            part = slice(pair * 128, pair * 128 + 128)
            aq[rows, part] += sums[0]
            ak[keys, part] += sums[1]
            av[keys, part] += sums[2]

    each_tile(spans, tile)
    dq_ref[...] = aq[...].astype(LOW)
    dk_ref[...] = ak[...].astype(LOW)
    g = g_ref[:, base * 128 : base * 128 + HALF]
    dv_ref[...] = jnp.where(padding_rows(spans, g.shape), g, av[...].astype(LOW))


def attend_back(base, qkv, grad, probs, spans, after=()):
    n = qkv.shape[0]
    return whole_call(
        functools.partial(attend_back_kernel, base), [shape(n, HALF)] * 3, [pltpu.VMEM((n, HALF), WIDE)] * 3, 1,
        "attend_back", 12 * 10**9, spans, qkv, grad, probs, after=after,
    )


def tables_kernel(seg_ref, side_ref, valid_ref, spans, far_ref):
    n = seg_ref.shape[1]
    seg, side, valid = [z[...].astype(WIDE) for z in (seg_ref, side_ref, valid_ref)]
    live = jnp.sum(valid).astype(jnp.int32)
    for z in range(5):
        spans[4, z] = live
    for t in range(4):
        low = jnp.sum((seg < t).astype(WIDE)).astype(jnp.int32)
        high = jnp.sum((seg <= t).astype(WIDE)).astype(jnp.int32)
        width = jnp.max(jnp.where(seg == t, side, 1.0))
        small = high - low <= SMALL - 16
        start = low // 16 * 16
        at = jnp.minimum(start, jnp.where(small, n - SMALL, n - LARGE))
        key = jnp.minimum(start, n - WIN)
        kind = jnp.where((high > low) & (low < live), jnp.where(small, 1, 2), 0)
        for z, value in enumerate((low, high, at, key, kind)):
            spans[t, z] = value

        def places(first, shape_, dim):
            slot = lax.broadcasted_iota(jnp.int32, shape_, dim) + first
            place = (slot - low).astype(WIDE)
            row = jnp.floor((place + 0.5) / width)
            return (slot >= low) & (slot < high), row, place - row * width

        inside, row, col = places(at, (LARGE, 1), 0)
        inside_key, row_key, col_key = places(key, (1, WIN), 1)
        down, along = row - row_key, col - col_key
        far_ref[t] = jnp.where(inside & inside_key, jnp.sqrt(down * down + along * along), 1e12)


def tables(seg, side, valid):
    vmem, smem = [pl.BlockSpec(memory_space=z) for z in (pltpu.VMEM, pltpu.SMEM)]
    return pl.pallas_call(
        tables_kernel,
        in_specs=[vmem] * 3,
        out_specs=[smem, vmem],
        out_shape=[jax.ShapeDtypeStruct((5, 5), jnp.int32), jax.ShapeDtypeStruct((4, LARGE, WIN), WIDE)],
        compiler_params=pltpu.CompilerParams(vmem_limit_bytes=VMEM_BYTES),
        name="tables",
    )(seg, side, valid)


def bell(u):
    share = 0.5 + 0.5 * lax.erf(u * 0.7071067811865476)
    return u * share, share + u * (jnp.exp2(u * u * -0.7213475204444817) * 0.3989422804014327)


def up_kernel(x_ref, o0_ref, o1_ref, vec_ref, order_ref, own, other, mixed_ref, h_ref, a_ref, gl_ref, gp_ref, tmp):
    mixed_ref[...] = (
        nn(o0_ref[...], order_ref[:HALF, :]) + nn(o1_ref[...], order_ref[HALF:, :])
    ).astype(LOW)
    for col in (0, 384):
        part = slice(col, col + 384)
        h_ref[:, part] = x_ref[:, part].astype(WIDE) + nn(mixed_ref[...], both((own, other), 0, col, 384)) + vec_ref[2:3, part]
    gain, shift = vec_ref[3:4, :], vec_ref[4:5, :]

    def norm(rows, _):
        tmp[rows, :] = (normal(h_ref[rows, :])[0] * gain + shift).astype(LOW)

    over_rows(x_ref.shape[0], 144, norm)
    a_ref[...] = nn(tmp[...], order_ref[...]).astype(LOW)
    for col in range(0, FF, 384):
        k = 5 + col // D
        u = nn(a_ref[...], both((own, other), *divmod(col + D, WIDTH_TWO), 384)) + vec_ref[k : k + 1, col % D : col % D + 384]
        value, slope = bell(u)
        gl_ref[:, col : col + 384] = value.astype(LOW)
        gp_ref[:, col : col + 384] = slope.astype(LOW)


def upward(x, o, vec, order, two, after=()):
    n = x.shape[0]
    return whole_call(
        up_kernel, [shape(n, D), shape(n, D, WIDE), shape(n, D), shape(n, FF), shape(n, FF)],
        [pltpu.VMEM((n, D), LOW)], 0, "upward", 2 * n * D * (7 * D) * 2, x, *o, vec, order, *two,
        after=after,
    )


def fetch_down(block_of, own, other, wd):
    for p in range(32):
        dst = pl.ds(pl.multiple_of(block_of[p] * 96, 96), 96)
        piece = own if p < 16 else other
        for side in (0, 1):
            lo = p % 16 * 96 + side * (FF // 2)
            wd[dst, side * WIDTH_THREE : (side + 1) * WIDTH_THREE] = piece[lo : lo + 96, :]


def down_kernel(block_of, gp_ref, dy_ref, own, other, dur_ref, vg_ref, wd):
    fetch_down(block_of, own, other, wd)
    for col in range(0, FF, 384):
        part = slice(col, col + 384)
        du = nt(dy_ref[...], wd[part, :]) * gp_ref[:, part].astype(WIDE)
        dur_ref[:, part] = du.astype(LOW)
        k = col // D
        vg_ref[k : k + 1, col % D : col % D + 384] = jnp.sum(du, axis=0, keepdims=True)


def down_back(block_of, gp, dy, three, after=()):
    n = dy.shape[0]
    return whole_call(
        down_kernel, [shape(n, FF), shape(8, D, WIDE)], [pltpu.VMEM((FF, D), LOW)], 1,
        "down_back", 2 * n * D * (4 * D), block_of, gp, dy, *three, after=after,
    )


def down_out_kernel(block_of, vec_ref, gl_ref, h_ref, own, other, out_ref, wd):
    fetch_down(block_of, own, other, wd)
    for col in (0, 384):
        part = slice(col, col + 384)
        out_ref[:, part] = (h_ref[:, part] + nn(gl_ref[...], wd[:, part]) + vec_ref[9:10, part]).astype(LOW)


def down_out(block_of, vec, gl, h, three, after=()):
    n = h.shape[0]
    return whole_call(
        down_out_kernel, [shape(n, D)], [pltpu.VMEM((FF, D), LOW)], 1,
        "down_out", 2 * n * D * (4 * D), block_of, vec, gl, h, *three, after=after,
    )[0]


def hidden_kernel(vec_ref, order_ref, dur_ref, dy_ref, h_ref, own, other, dh_ref, dhr_ref, dor_ref, vg_ref, tmp):
    split = WIDTH_TWO - D
    for i, w in enumerate((own, other)):
        tmp[:, HALF * i : HALF * (i + 1)] = (
            nt(dur_ref[:, :split], w[:HALF, D:]) + nt(dur_ref[:, split:], w[HALF:, :])
        ).astype(LOW)
    dh_ref[...] = nt(tmp[...], order_ref[...])
    gain = vec_ref[3:4, :]

    def step(rows, sums):
        e = dh_ref[rows, :]
        dy = dy_ref[rows, :].astype(WIDE)
        n, rstd = normal(h_ref[rows, :])
        w = e * gain
        dh = dy + rstd * (w - jnp.mean(w, axis=-1, keepdims=True) - n * jnp.mean(w * n, axis=-1, keepdims=True))
        dh_ref[rows, :] = dh
        dhr_ref[rows, :] = dh.astype(LOW)
        return tuple(s + jnp.sum(z.reshape(-1, 8, D), axis=0) for s, z in zip(sums, (dh, e * n, e, dy)))

    zero = jnp.zeros((8, D), WIDE)
    sums = over_rows(h_ref.shape[0], 144, step, (zero,) * 4)
    for k, s in enumerate(sums):
        vg_ref[k : k + 1, :] = jnp.sum(s, axis=0, keepdims=True)
    for i, w in enumerate((own, other)):
        tmp[:, HALF * i : HALF * (i + 1)] = nt(dhr_ref[...], w[:HALF, :D]).astype(LOW)
    dor_ref[...] = nt(tmp[...], order_ref[...]).astype(LOW)


def hidden_grad(vec, order, dur, dy, h, two, after=()):
    n = h.shape[0]
    return whole_call(
        hidden_kernel, [shape(n, D, WIDE), shape(n, D), shape(n, D), shape(8, D, WIDE)],
        [pltpu.VMEM((n, D), LOW)], 0, "hidden_grad",
        2 * n * D * (7 * D), vec, order, dur, dy, h, *two, after=after,
    )


def down_grad_kernel(block_of, gl_ref, dy_ref, own, other, all_ref):
    for col in range(0, FF, 384):
        all_ref[col : col + 384, :] = tn(gl_ref[:, col : col + 384], dy_ref[...]).astype(LOW)
    for p in range(32):
        src = pl.ds(pl.multiple_of(block_of[p] * 96, 96), 96)
        piece = own if p < 16 else other
        for side in (0, 1):
            lo = p % 16 * 96 + side * (FF // 2)
            piece[lo : lo + 96, :] = all_ref[src, side * WIDTH_THREE : (side + 1) * WIDTH_THREE]


def down_grad(block_of, gl, dy, after=()):
    n = dy.shape[0]
    return whole_call(
        down_grad_kernel, [shape(FF, WIDTH_THREE)] * 2, [pltpu.VMEM((FF, D), LOW)], 1, "down_grad",
        2 * n * D * FF, block_of, gl, dy, after=after,
    )


def two_grad_kernel(mixed_ref, a_ref, dhr_ref, dur_ref, own, other):
    for col, width in ((0, 768), (768, 384), (1152, 768), (1920, 640), (2560, 640), (3200, 640)):
        left, right = (mixed_ref, dhr_ref) if col < D else (a_ref, dur_ref[:, col - D : col - D + width])
        t = tn(left[...], right[...]).astype(LOW)
        side, lo = divmod(col, WIDTH_TWO)
        own[HALF * side : HALF * (side + 1), lo : lo + width] = t[:HALF]
        other[HALF * side : HALF * (side + 1), lo : lo + width] = t[HALF:]


def two_grad(mixed, a, dhr, dur, after=()):
    n = a.shape[0]
    return whole_call(two_grad_kernel, [shape(D, WIDTH_TWO)] * 2, [], 0, "two_grad", 2 * n * D * (D + FF), mixed, a, dhr, dur,
                      after=after)


def one_grad_kernel(a_ref, order_ref, first_ref, mid_ref, up_ref, *refs):
    halves, (own, other, wide) = refs[:6], refs[6:]
    wide[...] = jnp.zeros_like(wide)
    rows = [first_ref[0:1, :], first_ref[1:2, :]] + [mid_ref[i : i + 1, :] for i in range(3)]
    rows = rows + [up_ref[i : i + 1, :] for i in range(4)] + [mid_ref[3:4, :]]
    for k, values in enumerate(rows):
        first = min(D * k // 10 // 8 * 8, D - 88)
        entry = lax.broadcasted_iota(jnp.int32, (88, D), 1) + D * k
        row = lax.broadcasted_iota(jnp.int32, (88, D), 0) + first
        spread_out = jnp.where(row == (entry * 52429) >> 19, values, 0.0).astype(LOW)
        entry = lax.broadcasted_iota(jnp.int32, (D, 128), 0) + D * k
        column = entry - 10 * ((entry * 52429) >> 19)
        pick = (lax.broadcasted_iota(jnp.int32, (D, 128), 1) == column).astype(LOW)
        wide[first : first + 88, :] += nn(spread_out, pick)
    moved = tn(order_ref[...], wide[...].astype(LOW)).astype(LOW)
    for i, out in enumerate((own, other)):
        out[:HALF, CUT_ONE:] = moved[HALF * i : HALF * (i + 1), :]
        out[HALF:, CUT_ONE:] = jnp.zeros((HALF, WIDTH_ONE - CUT_ONE), LOW)
    for i, half in enumerate(halves):
        t = tn(a_ref[...], half[...]).astype(LOW)
        side, lo = divmod(384 * i, CUT_ONE)
        own[HALF * side : HALF * (side + 1), lo : lo + 384] = t[:HALF]
        other[HALF * side : HALF * (side + 1), lo : lo + 384] = t[HALF:]


def one_grad(a, order, sums, d, after=()):
    n = a.shape[0]
    return whole_call(
        one_grad_kernel, [shape(D, WIDTH_ONE)] * 2, [pltpu.VMEM((D, 128), WIDE)], 0, "one_grad",
        2 * n * D * 3 * D, a, order, *sums, *d, after=after,
    )


def input_back_kernel(order_ref, q0, q1, k0, k1, v0, v1, own, other, e_ref, tmp):
    for i, w in enumerate((own, other)):
        total = 0.0
        for j, d in enumerate((q0, q1, k0, k1, v0, v1)):
            side, lo = divmod(384 * j, CUT_ONE)
            total = total + nt(d[...], w[HALF * side : HALF * (side + 1), lo : lo + 384])
        tmp[:, HALF * i : HALF * (i + 1)] = total.astype(LOW)
    e_ref[...] = nt(tmp[...], order_ref[...])


def input_back(order, d, one, after=()):
    n = d[0].shape[0]
    return whole_call(
        input_back_kernel, [shape(n, D, WIDE)], [pltpu.VMEM((n, D), LOW)], 0, "input_back",
        2 * n * D * 4 * D, order, *d, *one, after=after,
    )[0]


def input_kernel(x_ref, vec_ref, e_ref, dh_ref, dx_ref, vg_ref):
    gain = vec_ref[0:1, :]

    def step(rows, sums):
        e = e_ref[rows, :]
        n, rstd = normal(x_ref[rows, :].astype(WIDE))
        w = e * gain
        dx_ref[rows, :] = dh_ref[rows, :] + rstd * (
            w - jnp.mean(w, axis=-1, keepdims=True) - n * jnp.mean(w * n, axis=-1, keepdims=True)
        )
        return tuple(s + jnp.sum(z.reshape(-1, 8, D), axis=0) for s, z in zip(sums, (e * n, e)))

    zero = jnp.zeros((8, D), WIDE)
    sums = over_rows(x_ref.shape[0], 144, step, (zero,) * 2)
    for k, s in enumerate(sums):
        vg_ref[k : k + 1, :] = jnp.sum(s, axis=0, keepdims=True)


def input_grad(x, vec, e, dh, after=()):
    n = x.shape[0]
    return whole_call(
        input_kernel, [shape(n, D, WIDE), shape(8, D, WIDE)], [], 0, "input_grad",
        2 * n * D * 3 * D, x, vec, e, dh, after=after,
    )


def near_kernel(a, b, c, d, left_ref, right_ref):
    cut = left_ref.shape[1]
    for out, lo in ((left_ref, 0), (right_ref, cut)):
        out[...] = jnp.concatenate([z[:, lo : lo + cut].astype(WIDE) for z in (a, b, c, d)], axis=0).astype(LOW)


def near_pieces(pieces, after=()):
    rows, cols = pieces[0].shape
    return whole_call(near_kernel, [shape(4 * rows, cols // 2)] * 2, [], 0, "near", 1, *pieces, after=after)


def first_kernel(left, got_left, right, got_right, left_ref, right_ref):
    rows = left.shape[0]
    for out, mine, got in ((left_ref, left, got_left), (right_ref, right, got_right)):
        out[:rows, :] = mine[...]
        out[rows:, :] = got[...]


def first_pieces(left, right, got, after=()):
    rows, cols = left.shape
    return whole_call(
        first_kernel, [shape(2 * rows, cols)] * 2, [], 0, "first", 1, left, got[0], right, got[1], after=after
    )


def second_kernel(left, got, right, far, own_ref):
    rows = left.shape[0]
    half = rows // 2
    own_ref[:rows, :] = left[...]
    own_ref[rows : 2 * rows, :] = got[...]
    for i in (0, 1):
        own_ref[2 * rows + 2 * i * half : 2 * rows + (2 * i + 1) * half, :] = right[i * half : (i + 1) * half, :]
        own_ref[2 * rows + (2 * i + 1) * half : 2 * rows + (2 * i + 2) * half, :] = far[i * half : (i + 1) * half, :]


def second_pieces(left, right, got, after=()):
    rows, cols = left.shape
    return whole_call(
        second_kernel, [shape(4 * rows, cols)], [], 0, "second", 1, left, got[0], right, got[1], after=after
    )[0]


def core_sum_kernel(own, got, left_keep, right_keep, left_out, right_out):
    half = left_keep.shape[0]
    rows = half // 2

    def total(lo, count):
        return own[lo : lo + count, :].astype(WIDE) + got[lo : lo + count, :].astype(WIDE)

    left_keep[...] = total(0, half)
    left_out[...] = total(half, half).astype(LOW)
    for i in (0, 1):
        lo = 2 * half + 2 * i * rows
        right_keep[i * rows : (i + 1) * rows, :] = total(lo, rows)
        right_out[i * rows : (i + 1) * rows, :] = total(lo + rows, rows).astype(LOW)


def core_sum(own, got, after=()):
    rows, cols = own.shape[0] // 4, own.shape[1]
    return whole_call(
        core_sum_kernel, [shape(rows, cols, WIDE)] * 2 + [shape(rows, cols)] * 2, [], 0, "core_sum", 1, own, got,
        after=after,
    )


def half_sum_kernel(left, got_left, right, got_right, left_keep, right_keep, left_out, right_out):
    rows = left_keep.shape[0]
    for mine, got, keep, out in ((left, got_left, left_keep, left_out), (right, got_right, right_keep, right_out)):
        keep[...] = mine[:rows, :] + got[:rows, :].astype(WIDE)
        out[...] = (mine[rows:, :] + got[rows:, :].astype(WIDE)).astype(LOW)


def half_sum(left, right, got, after=()):
    rows, cols = left.shape[0] // 2, left.shape[1]
    return whole_call(
        half_sum_kernel, [shape(rows, cols, WIDE)] * 2 + [shape(rows, cols)] * 2, [], 0, "half_sum", 1,
        left, got[0], right, got[1], after=after,
    )


def last_sum_kernel(left, got_left, right, got_right, keep, *outs):
    unit, cut = keep.shape[0], left.shape[1]
    for lo, mine, got in ((0, left, got_left), (cut, right, got_right)):
        total = mine[...] + got[...].astype(WIDE)
        keep[:, lo : lo + cut] = total[:unit]
        for i, out in enumerate(outs):
            out[:, lo : lo + cut] = total[unit * (i + 1) : unit * (i + 2)].astype(LOW)


def last_sum(left, right, got, after=()):
    unit, cols = left.shape[0] // 4, 2 * left.shape[1]
    return whole_call(
        last_sum_kernel, [shape(unit, cols, WIDE)] + [shape(unit, cols)] * 3, [], 0, "last_sum", 1,
        left, got[0], right, got[1], after=after,
    )


def swap(value, bits):
    pairs = [(i, i ^ bits) for i in range(32)]
    return lax.ppermute(value, AXES, pairs)


def tie(values, *first):
    return lax.optimization_barrier((tuple(values), first))[0]


class Flow:
    def __init__(self, steps):
        self.steps = steps
        self.next = next(steps)[:2]

    def issue(self, start=()):
        values, bits = self.next
        values = tie(values, start)
        self.got = tuple(swap(value, bit) for value, bit in zip(values, bits))
        return self.got

    def land(self, end=()):
        values, *bits = self.steps.send(tie(self.got, end))
        if values is None:
            return bits[0]
        self.next = (values, bits[0])
        return bits[1]


def spread(block):
    got = yield (block,) * 3, (8, 16, 24)
    left, right = near_pieces((block,) + got)
    got = yield (left, right), (2, 4), (left, right)
    left, right = first_pieces(left, right, got)
    got = yield (left, right), (4, 2), (left, right)
    own = second_pieces(left, right, got)
    got = yield (own,), (1,), (own,)
    yield None, (own, got[0])


def collect(pieces):
    (got,) = yield (pieces[1],), (1,)
    left, right, *out = ready = core_sum(pieces[0], got)
    got = yield out, (4, 2), tuple(ready)
    left, right, *out = ready = half_sum(left, right, got)
    got = yield out, (2, 4), tuple(ready)
    total, *out = ready = last_sum(left, right, got)
    got = yield out, (8, 16, 24), tuple(ready)
    yield None, (sum((z.astype(WIDE) for z in got), total),)


def stack(whole):
    half, cut = whole.shape[0] // 2, whole.shape[1] // 2
    return tuple(jnp.concatenate([z[:, :cut], z[:, cut:]], axis=0) for z in (whole[:half], whole[half:]))


def unstack(pieces):
    half = pieces[0].shape[0] // 2
    return jnp.concatenate([jnp.concatenate([z[:half], z[half:]], axis=1) for z in pieces], axis=0)


class Whole:
    def __init__(self, result):
        self.result = result

    def issue(self, start=()):
        return ()

    def land(self, end=()):
        return self.result


def spread_any(block):
    return stack(lax.all_gather(block, AXES, axis=0, tiled=True))


def collect_any(pieces):
    return (lax.psum_scatter(unstack(pieces), AXES, scatter_dimension=0, tiled=True).astype(WIDE),)


def rearrange(whole, order, shards):
    return jnp.take(whole.reshape(shards, -1, whole.shape[1]), order, axis=0, mode="clip").reshape(whole.shape)


def adamw(master, moment_one, moment_two, gradient, step_rate, decay_rate):
    first_new = BETA_ONE * moment_one + (1.0 - BETA_ONE) * gradient
    second_new = BETA_TWO * moment_two + (1.0 - BETA_TWO) * gradient * gradient
    first_hat = first_new / (1.0 - BETA_ONE**STEP)
    second_hat = second_new / (1.0 - BETA_TWO**STEP)
    master_new = master - step_rate * (
        first_hat / (jnp.sqrt(second_hat) + ADAM_EPS) + decay_rate * master
    )
    return (first_new, second_new, master_new)


def local(
    tokens_in, cotangent, segments, tile_sides, valid_slots, owners,
    master_qkv, master_out, master_up, master_down, master_vec,
    first_qkv, first_out, first_up, first_down, first_vec,
    second_qkv, second_out, second_up, second_down, second_vec,
):
    shards = lax.axis_size(AXES)
    near = shards == 32
    unit = D // shards
    per_row = master_vec.shape[0] // unit
    ids = jnp.arange(shards, dtype=jnp.int32)
    if near:
        away = owners ^ lax.axis_index(AXES).astype(jnp.int32)
        place = (away >> 3) + 4 * ((away >> 1) & 1) + 8 * ((away >> 2) & 1) + 16 * (away & 1)
        places = jnp.arange(32, dtype=jnp.int32)
        block_of = jnp.sum(places[:, None] * (place[:, None] == places[None, :]), axis=0)
    else:
        place = owners
        block_of = jnp.arange(32, dtype=jnp.int32)
    target = (place[:, None] * unit + jnp.arange(unit, dtype=jnp.int32)[None, :]).reshape(-1)
    order = (target[:, None] == jnp.arange(D, dtype=jnp.int32)[None, :]).astype(LOW)

    def gather(block):
        return Flow(spread(block)) if near else Whole(spread_any(block))

    def scatter(pieces):
        return Flow(collect(pieces)) if near else Whole(collect_any(pieces))

    vec_block = jnp.pad(master_vec.reshape(unit, per_row), ((0, 0), (0, 128 - per_row)))
    block_one = jnp.concatenate(
        [master_qkv[:, :CUT_ONE], vec_block, master_qkv[:, CUT_ONE:], jnp.zeros_like(vec_block)], axis=1
    )
    spans, far = tables(segments, tile_sides, valid_slots)
    slopes = LOG2E * jnp.exp2(-8.0 * (jnp.arange(HEADS, dtype=jnp.int32).astype(WIDE) + 1.0) / HEADS)
    one = gather(block_one.astype(LOW))
    two = gather(jnp.concatenate([master_out, master_up], axis=1).astype(LOW))
    if near:
        three = gather(master_down.astype(LOW))
    else:
        whole = lax.all_gather(master_down.astype(LOW), AXES, axis=0, tiled=True)
        three = Whole(stack(rearrange(whole, owners, shards)))
    one.issue()
    normed = normalized(tokens_in[0])
    done = one.land((far, spans, slopes, order, normed))
    one.issue(done)
    done = one.land()
    sent = one.issue(done) + two.issue(done)
    done = one.land()
    done = done + two.land(sent + done)
    one.issue(done)
    sent = two.issue(done)
    one = one.land()

    x = tokens_in[0]
    dy = cotangent[0]
    act_one, qkv, vec = project(normed, order, one)
    done = two.land((qkv,))
    sent = two.issue(done) + three.issue(done)
    mixed_0, probs_0 = attend(0, qkv, far, spans, slopes, done)
    done = two.land((mixed_0,))
    done = done + three.land((mixed_0,) + sent + done)
    sent = two.issue(done) + three.issue(done)
    mixed_1, probs_1 = attend(3, qkv, far, spans, slopes, done + (mixed_0,))
    done = three.land((mixed_1,) + sent)
    two = two.land((mixed_1,) + sent)
    three.issue(done + two[1:])
    mixed, hidden, act_two, gelu, gelu_slope = upward(x, (mixed_0, mixed_1), vec, order, two, done)
    grad_three = down_grad(block_of, gelu, dy)
    done = three.land(tuple(grad_three))
    three.issue(done)
    three = three.land()
    if not near:
        back = jnp.sum(ids[:, None] * (owners[:, None] == ids[None, :]), axis=0)
        grad_three = stack(rearrange(unstack(grad_three), back, shards))
    flow_three = scatter(grad_three)
    flow_three.issue((three[1],))
    dur, sums_up = down_back(block_of, gelu_slope, dy, three)
    done = flow_three.land((dur,))
    flow_three.issue(done)
    dh, dh_low, dmixed, sums = hidden_grad(vec, order, dur, dy, hidden, two, done)
    grad_two = two_grad(mixed, act_two, dh_low, dur)
    done = flow_three.land(tuple(grad_two)) + tuple(grad_two)
    flow_two = scatter(grad_two)
    sent = flow_three.issue(done) + flow_two.issue(done)
    d0 = attend_back(0, qkv, dmixed, probs_0, spans, done)
    done = flow_three.land(tuple(d0) + sent) + flow_two.land(tuple(d0) + sent)
    sent = flow_three.issue(done) + flow_two.issue(done)
    d1 = attend_back(3, qkv, dmixed, probs_1, spans, done + tuple(d0))
    d = [z for pair in zip(d0, d1) for z in pair]
    dact = input_back(order, d, one)
    tokens_grad, sums_one = input_grad(x, vec, dact, dh)
    grad_one = one_grad(act_one, order, (sums_one, sums, sums_up), d)
    done = tuple(grad_one) + sent
    sum_three, = flow_three.land(done)
    done = flow_two.land(done)
    flow_one = scatter(grad_one)
    sent = flow_one.issue(done) + flow_two.issue(done)
    block_out = down_out(block_of, vec, gelu, hidden, three, done)
    done = flow_one.land((block_out,) + sent) + flow_two.land((block_out,) + sent)
    sent = flow_one.issue(done) + flow_two.issue(done)
    upd_down = adamw(master_down, first_down, second_down, sum_three, RATE_MATRIX, DECAY_MATRIX)
    sent = sent + upd_down
    done = flow_one.land(sent)
    sum_two, = flow_two.land(sent)
    flow_one.issue(done)
    upd_out = adamw(master_out, first_out, second_out, sum_two[:, :D], RATE_MATRIX, DECAY_MATRIX)
    upd_up = adamw(master_up, first_up, second_up, sum_two[:, D:], RATE_MATRIX, DECAY_MATRIX)
    done = flow_one.land(upd_out)
    flow_one.issue(done)
    sum_one, = flow_one.land(upd_up)
    sum_vec = sum_one[:, CUT_ONE : CUT_ONE + per_row].reshape(-1)
    sum_one = jnp.concatenate([sum_one[:, :CUT_ONE], sum_one[:, WIDTH_ONE : WIDTH_ONE + CUT_ONE]], axis=1)
    upd_qkv = adamw(master_qkv, first_qkv, second_qkv, sum_one, RATE_MATRIX, DECAY_MATRIX)
    upd_vec = adamw(master_vec, first_vec, second_vec, sum_vec, RATE_VECTOR, 0.0)
    return (
        (block_out[None], tokens_grad[None]) + upd_qkv + upd_out + upd_up + upd_down + upd_vec
    )


def solution(mesh):
    rows = P(AXES, None)
    flat = P(AXES)
    deep = P(AXES, None, None)
    stored = (rows,) * 4 + (flat,)
    in_specs = (deep,) * 2 + (rows,) * 3 + (P(),) + stored * 3
    out_specs = (deep,) * 2 + (rows,) * 12 + (flat,) * 3
    return jax.shard_map(local, mesh=mesh, in_specs=in_specs, out_specs=out_specs, check_vma=False)
```
